32 devices in a mesh: dp: 16 (over z, y, core), expert: 2 (over x).
Axes of the slice: x: 2, y: 2, z: 4, core: 2. Of those that a mesh axis runs over, the one named last changes fastest.
Arguments:
- hidden_in: bfloat16 [2, 16384, 768], P(None, ('dp', 'expert')), may hold values from -6 to 6
- out_grad: bfloat16 [2, 16384, 768], P(None, ('dp', 'expert')), may hold values from -6 to 6
- places: int32 [2, 16, 1024], P(None, 'dp'), may hold values from 0 to 1023, as said below
- lengths: int32 [2, 16, 2], P(None, 'dp'), may hold values from 0 to 1024, as said below
- routes: int32 [2, 16384, 1], P(None, ('dp', 'expert')), may hold values from 0 to 1; in each aligned block of 512 rows (0 to 511, 512 to 1023, ..., all dimensions but the last counted through in order) at most 272 rows name the same one
- norm1_gain: bfloat16 [768], P('dp'), may hold values from 0.5 to 1.5
- w_query: bfloat16 [768, 768], P('dp'), may hold values from -0.21875 to 0.21875
- w_key: bfloat16 [768, 768], P('dp'), may hold values from -0.21875 to 0.21875
- w_value: bfloat16 [768, 768], P('dp'), may hold values from -0.21875 to 0.21875
- w_output: bfloat16 [768, 768], P('dp'), may hold values from -1.75 to 1.75
- rel_table: bfloat16 [32, 12], P('dp'), may hold values from -4 to 4
- norm2_gain: bfloat16 [768], P('dp'), may hold values from 0.5 to 1.5
- w_router: bfloat16 [768, 2], P('dp'), may hold values from -0.15625 to 0.15625
- w_in: bfloat16 [2, 768, 3072], P('expert', 'dp'), may hold values from -0.21875 to 0.21875
- w_out: bfloat16 [2, 3072, 768], P('expert', 'dp'), may hold values from -0.625 to 0.625
Outputs:
- layer_out: bfloat16 [2, 16384, 768], P(None, ('dp', 'expert'))
- in_grad: float32 [2, 16384, 768], P(None, ('dp', 'expert'))
- norm1_gain_grad: float32 [768], P('dp')
- w_query_grad: float32 [768, 768], P('dp')
- w_key_grad: float32 [768, 768], P('dp')
- w_value_grad: float32 [768, 768], P('dp')
- w_output_grad: float32 [768, 768], P('dp')
- rel_table_grad: float32 [32, 12], P('dp')
- norm2_gain_grad: float32 [768], P('dp')
- w_router_grad: float32 [768, 2], P('dp')
- w_in_grad: float32 [2, 768, 3072], P('expert', 'dp')
- w_out_grad: float32 [2, 3072, 768], P('expert', 'dp')
The draws below stay inside these ranges and needn't reach their ends.
Inputs may be any that keep to these rules, and one draw needn't show every extreme that they name: `routes`: in each aligned block of 512 rows (one device's tokens of one micro-batch) no expert is named more than 272 times, and in some blocks one is named exactly 272 times. `places`: for each micro-batch and group the entries are a permutation of the packed positions; rows k of the 2 devices of a group hold the positions k * 2 to k * 2 + 1 in some order. Each row sums to 1024; lengths may be 0; in each draw one length is exactly 1024.
All inputs are finite; a program needn't handle non-finite values.
Results may differ from the reference program's by a relative error of at most 0.028.
Values may be sent and summed in bfloat16 or wider, within the bound.
No kernel may reach another device: no remote copies, remote signals or barrier semaphores. Data moves between devices by JAX's collectives and lax.ppermute only.
A program may use at most 176 MiB of HBM per device.

```python
import math
from functools import partial
import jax
import jax.numpy as jnp
import numpy as np
from jax import lax

D = 768
HEADS = 12
HEAD_DIM = 64
FF = 3072
BUCKETS = 32
MICRO = 2
SEQ_MAX = 1024
EXPERTS = 2
GROUP = 1024
TOK_DEV = 512
TOKENS = 16384
SEQS = 2
CAP = 272
N_DP = 16
N_EXPERT = 2


def draw_places(key, part):
    key = jax.random.fold_in(key, 11)
    ranking = jax.random.randint(key, (MICRO, N_DP, TOK_DEV, N_EXPERT), 0, 1 << 20)
    ranking = ranking * N_EXPERT + jnp.arange(N_EXPERT, dtype=jnp.int32)
    ordering = jnp.argsort(ranking, axis=-1).astype(jnp.int32)
    rounds_base = jnp.arange(TOK_DEV, dtype=jnp.int32)[:, None] * N_EXPERT
    placed = ordering + rounds_base
    placed = jnp.transpose(placed, (0, 1, 3, 2)).reshape(MICRO, N_DP, GROUP)
    return placed


def draw_lengths(key, part):
    key = jax.random.fold_in(key, 23)
    offset_key, choice_key = jax.random.split(key)
    seq_base = GROUP // SEQS
    half_span = SEQ_MAX // 4
    offsets = jax.random.randint(offset_key, (MICRO, N_DP, SEQS - 1), 1 - half_span, half_span)
    boundaries = jnp.arange(1, SEQS, dtype=jnp.int32) * seq_base + offsets
    chosen = jax.random.randint(choice_key, (), 0, MICRO * N_DP)
    row_ids = jnp.arange(MICRO * N_DP, dtype=jnp.int32).reshape(MICRO, N_DP)
    picked = (row_ids == chosen)[:, :, None] & (jnp.arange(SEQS - 1, dtype=jnp.int32) == 0)[None, None, :]
    boundaries = jnp.where(picked, 2 * seq_base, boundaries)
    boundaries = lax.cummax(boundaries, axis=2)
    boundaries = jnp.clip(boundaries, 0, GROUP)
    zeros_col = jnp.zeros((MICRO, N_DP, 1), jnp.int32)
    group_col = jnp.full((MICRO, N_DP, 1), GROUP, jnp.int32)
    bounds_all = jnp.concatenate([zeros_col, boundaries, group_col], axis=2)
    return bounds_all[:, :, 1:] - bounds_all[:, :, :-1]


def shard_levels(key, shape, cuts, smallest, largest):
    loudness, own = 1.0, jax.random.fold_in(key, 6)
    for position, blocks in cuts:
        draws = jnp.exp(jax.random.uniform(jax.random.fold_in(own, position), (blocks,), jnp.float32, smallest / len(cuts), largest / len(cuts)))
        loudness = loudness * jnp.repeat(draws, shape[position] // blocks).reshape([-1 if axis == position else 1 for axis in range(len(shape))])
    return loudness


def routed_block(rng, own, number, rows, number_of, top, limit, skew):
    sequence = jax.random.permutation(rng, number_of)
    crowded, common = shares(number_of, rows * top, limit, skew, True), shares(number_of, rows * top, limit, skew, False)
    places = jnp.arange(number_of)

    def named(tallies, turn):
        used = int((tallies > 0).sum())
        fixed = max(1, used // 4)
        moved = fixed + (places - fixed + turn * (used - fixed)) % max(1, number_of - fixed)
        return jnp.zeros((number_of,), jnp.int32).at[sequence[jnp.where(places < fixed, places, moved)]].set(jnp.asarray(tallies, jnp.int32))

    tallies = jnp.where(number % 4 == 0, named(crowded, number // 4), named(common, number - number // 4 - 1))
    mixed = jax.random.permutation(jax.random.fold_in(own, 3), number_of)
    donor, taker = mixed[0:number_of // 2 * 2:2], mixed[1:number_of // 2 * 2:2]
    room = jnp.minimum(tallies[donor] - 1, limit - tallies[taker]) // 2
    room = jnp.where((donor == sequence[0]) | (taker == sequence[0]) | (tallies[taker] == 0), 0, jnp.maximum(room, 0))
    moved = jax.random.randint(jax.random.fold_in(own, 4), (number_of // 2,), 0, 1 << 20) % (room + 1)
    tallies = tallies.at[donor].add(-moved).at[taker].add(moved)
    members = jnp.searchsorted(jnp.cumsum(tallies), jnp.arange(rows * top), side="right").astype(jnp.int32)
    listing = members.reshape(top, rows).T
    listing = listing[jax.random.permutation(jax.random.fold_in(own, 1), rows)]
    turn = jax.random.randint(jax.random.fold_in(own, 2), (rows, 1), 0, top)
    return jnp.take_along_axis(listing, (jnp.arange(top)[None, :] + turn) % top, axis=1)


def shares(count, total, most, slope, full):
    loads = [(1 << 20) // math.isqrt(standing ** slope) + 1 for standing in range(1, count + 1)]
    largest = most if full else min(most, max(-(-total // count), total * loads[0] // sum(loads)))
    least = 1 if total - largest >= count - 1 else 0
    given, surplus = [largest] + [least] * (count - 1), total - largest - least * (count - 1)
    while surplus > 0:
        movable = [i for i in range(1, count) if given[i] < largest] or [i for i in range(1, count) if given[i] < most]
        whole, budget = sum([loads[i] for i in movable]), surplus
        for i in movable:
            extra = min(most - given[i], max(1, budget * loads[i] // whole), surplus)
            given[i] = given[i] + extra
            surplus = surplus - extra
    return np.array(given)


def centred(rng, shape, deviation, limit, cuts=(), kind=jnp.bfloat16):
    loudness = shard_levels(rng, shape, cuts, -0.22, 0.18) if cuts else 1.0
    values = jax.random.normal(rng, shape, jnp.float32) * deviation * loudness
    return jnp.minimum(jnp.maximum(values, -limit), limit).astype(kind)


def setup_inputs(seed: int = 0) -> dict:
    key_list = jax.random.split(jax.random.key(seed), 16)
    hidden_in = centred(key_list[0], (MICRO, TOKENS, D), 1.0, 6.0, ((1, 32),))
    out_grad = centred(key_list[1], (MICRO, TOKENS, D), 1.0, 6.0, ((1, 32),))
    places = draw_places(jax.random.fold_in(key_list[15], 71), 0)
    lengths = draw_lengths(jax.random.fold_in(key_list[15], 71), 0)
    routes_keys = jax.random.split(jax.random.fold_in(key_list[4], 1), MICRO * TOKENS // TOK_DEV)
    routes_turns = jax.random.permutation(jax.random.fold_in(key_list[4], 3), MICRO * TOKENS // TOK_DEV)
    routes = jax.vmap(lambda own, number: routed_block(jax.random.fold_in(key_list[4], 2), own, number, TOK_DEV, EXPERTS, 1, CAP, 2))(routes_keys, routes_turns).reshape((MICRO, TOKENS, 1))
    norm1_gain = jnp.clip(1.0 + 0.1 * jax.random.normal(key_list[5], (D,), jnp.float32), 0.5, 1.5).astype(jnp.bfloat16)
    w_query = centred(key_list[6], (D, D), D ** -0.5, 0.21875, ((0, 16),))
    w_key = centred(key_list[7], (D, D), D ** -0.5, 0.21875, ((0, 16),))
    w_value = centred(key_list[8], (D, D), D ** -0.5, 0.21875, ((0, 16),))
    w_output = centred(key_list[9], (D, D), (D // 64) ** -0.5, 1.75, ((0, 16),))
    rel_table = centred(key_list[10], (BUCKETS, HEADS), 1.0, 4.0, ((0, 16),))
    norm2_gain = jnp.clip(1.0 + 0.1 * jax.random.normal(key_list[11], (D,), jnp.float32), 0.5, 1.5).astype(jnp.bfloat16)
    w_router = centred(key_list[12], (D, EXPERTS), (2 * D) ** -0.5, 0.15625, ((0, 16),))
    w_in = centred(key_list[13], (EXPERTS, D, FF), D ** -0.5, 0.21875, ((0, 2), (1, 16)))
    w_out = centred(key_list[14], (EXPERTS, FF, D), (FF // 32) ** -0.5, 0.625, ((0, 2), (1, 16)))
    return {"hidden_in": hidden_in, "out_grad": out_grad, "places": places, "lengths": lengths, "routes": routes, "norm1_gain": norm1_gain, "w_query": w_query, "w_key": w_key, "w_value": w_value, "w_output": w_output, "rel_table": rel_table, "norm2_gain": norm2_gain, "w_router": w_router, "w_in": w_in, "w_out": w_out}


@jax.custom_vjp
def low(v):
    return lax.optimization_barrier(v.astype(jnp.bfloat16)).astype(jnp.float32)

@jax.custom_vjp
def low_back(v):
    return v

def low_keep(v):
    return (low(v), None)

def low_pass(kept, grad):
    return (grad,)

def back_keep(v):
    return (v, None)

def back_low(kept, grad):
    return (low(grad),)
low.defvjp(low_keep, low_pass)
low_back.defvjp(back_keep, back_low)
bucket_edges = (1, 2, 3, 4, 5, 6, 7, 8, 12, 16, 23, 32, 46, 64, 91)
epsilon = 1e-06
masked_score = -1000000000.0
precise = lax.Precision.HIGHEST

def norm_rows(rows, gain):
    mean_square = lax.optimization_barrier(jnp.mean(rows * rows, axis=-1, keepdims=True))
    return rows * lax.rsqrt(mean_square + epsilon) * gain

def bucket_ids(query_pos, key_pos):
    offset = key_pos[None, :] - query_pos[:, None]
    distance = jnp.abs(offset)
    levels = jnp.zeros(offset.shape, jnp.int32)
    for edge_value in bucket_edges:
        levels = levels + (distance >= edge_value).astype(jnp.int32)
    return levels + 16 * (offset > 0).astype(jnp.int32)

def segment_ids(positions, lengths_row):
    seq_ends = jnp.cumsum(lengths_row)[:-1]
    return lax.optimization_barrier(jnp.sum((positions[:, None] >= seq_ends[None, :]).astype(jnp.int32), axis=1))

def softmax_rows(scores):
    row_max = lax.optimization_barrier(jnp.max(scores, axis=-1, keepdims=True))
    shifted = jnp.exp(scores - row_max)
    return shifted / lax.optimization_barrier(jnp.sum(shifted, axis=-1, keepdims=True))

def attend_group(normed, positions, lengths_row, w_query, w_key, w_value, w_output, rel_table):
    queries = low(low_back(jnp.dot(normed, w_query, precision=precise)))
    keys_all = low(low_back(jnp.dot(normed, w_key, precision=precise)))
    values_all = low(low_back(jnp.dot(normed, w_value, precision=precise)))
    query_heads = queries.reshape(GROUP, HEADS, HEAD_DIM)
    key_heads = keys_all.reshape(GROUP, HEADS, HEAD_DIM)
    value_heads = values_all.reshape(GROUP, HEADS, HEAD_DIM)
    bucket_grid = bucket_ids(positions, positions)
    pos_bias = jnp.transpose(jnp.take(rel_table, bucket_grid, axis=0), (2, 0, 1))
    raw_scores = jnp.einsum('ahd,bhd->hab', query_heads, key_heads, precision=precise) * HEAD_DIM ** (-0.5) + pos_bias
    raw_scores = low_back(raw_scores)
    segment = segment_ids(positions, lengths_row)
    same_seq = segment[:, None] == segment[None, :]
    scores = jnp.where(same_seq[None], raw_scores, masked_score)
    attn_probs = low(softmax_rows(scores))
    attended = jnp.einsum('hab,bhd->ahd', attn_probs, value_heads, precision=precise).reshape(GROUP, D)
    attended = low(low_back(attended))
    return low_back(jnp.dot(attended, w_output, precision=precise))

def expert_block(rows, inner_weight, outer_weight):
    pre_act = low_back(jnp.dot(rows, inner_weight, precision=precise))
    hidden = low(jax.nn.gelu(pre_act, approximate=True))
    return low(low_back(jnp.dot(hidden, outer_weight, precision=precise)))

def layer_forward(hidden_all, norm1_gain, w_query, w_key, w_value, w_output, rel_table, norm2_gain, w_router, w_in, w_out, places, lengths, routes):
    attend = jax.checkpoint(attend_group)
    run_expert = jax.checkpoint(expert_block)
    outputs = []
    for batch_idx in range(MICRO):
        tokens_f = hidden_all[batch_idx]
        normed_one = low(norm_rows(tokens_f, norm1_gain))
        grouped = normed_one.reshape(N_DP, GROUP, D)
        attn_out = lax.map(lambda operand: attend(operand[0], operand[1], operand[2], w_query, w_key, w_value, w_output, rel_table), (grouped, places[batch_idx], lengths[batch_idx]))
        resid_mid = tokens_f + attn_out.reshape(TOKENS, D)
        normed_two = low(norm_rows(resid_mid, norm2_gain))
        logits = jnp.dot(normed_two, w_router, precision=precise)
        gate_all = softmax_rows(logits)
        chosen = routes[batch_idx, :, 0]
        picked = chosen[:, None] == jnp.arange(EXPERTS, dtype=jnp.int32)[None, :]
        gate_prob = lax.optimization_barrier(jnp.sum(jnp.where(picked, gate_all, 0.0), axis=1))
        counts = picked.astype(jnp.int32).reshape(N_DP * N_EXPERT, TOK_DEV, EXPERTS)
        earlier = jnp.cumsum(counts, axis=1) - counts
        slot_idx = lax.optimization_barrier(jnp.sum(earlier * counts, axis=2)).reshape(TOKENS)
        token_idx = jnp.arange(TOKENS, dtype=jnp.int32)
        group_idx = token_idx // GROUP
        source_idx = token_idx % GROUP // TOK_DEV
        target = ((chosen * N_DP + group_idx) * N_EXPERT + source_idx) * CAP + slot_idx
        buffer = jnp.zeros((EXPERTS * N_DP * N_EXPERT * CAP, D), jnp.float32).at[target].set(normed_two)
        buffer = low_back(buffer).reshape(EXPERTS, N_DP * N_EXPERT * CAP, D)
        expert_out = lax.map(lambda operand: run_expert(operand[0], operand[1], operand[2]), (buffer, w_in, w_out))
        returned = expert_out.reshape(EXPERTS * N_DP * N_EXPERT * CAP, D)[target]
        outputs.append(resid_mid + gate_prob[:, None] * returned)
    return jnp.stack(outputs)

def reference(hidden_in, out_grad, places, lengths, routes, norm1_gain, w_query, w_key, w_value, w_output, rel_table, norm2_gain, w_router, w_in, w_out):
    floats = tuple((array.astype(jnp.float32) for array in (hidden_in, norm1_gain, w_query, w_key, w_value, w_output, rel_table, norm2_gain, w_router, w_in, w_out)))
    bound_layer = partial(layer_forward, places=places, lengths=lengths, routes=routes)
    result, pullback = jax.vjp(bound_layer, *floats)
    gradients = pullback(out_grad.astype(jnp.float32))
    return (result.astype(jnp.bfloat16), gradients[0], gradients[1], gradients[2], gradients[3], gradients[4], gradients[5], gradients[6], gradients[7], gradients[8], gradients[9], gradients[10])
```

```python
import functools

import jax
import jax.numpy as jnp
from jax import lax
from jax.experimental import pallas as pl
from jax.experimental.pallas import tpu as pltpu
from jax.sharding import PartitionSpec as P

bucket_edges = (1, 2, 3, 4, 5, 6, 7, 8, 12, 16, 23, 32, 46, 64, 91)
levels_all = len(bucket_edges) + 1
epsilon = 1e-06
masked_score = -1000000000.0
precise = lax.Precision.HIGHEST
float32 = jnp.float32
bfloat = jnp.bfloat16
tile = 128
vmem_bytes = 56 * 1024 * 1024


def params():
    return pltpu.CompilerParams(vmem_limit_bytes=vmem_bytes)


def dot_nn(left, right):
    return lax.dot_general(left, right, (((1,), (0,)), ((), ())), preferred_element_type=float32)


def dot_nt(left, right):
    return lax.dot_general(left, right, (((1,), (1,)), ((), ())), preferred_element_type=float32)


def dot_tn(left, right):
    return lax.dot_general(left, right, (((0,), (0,)), ((), ())), preferred_element_type=float32)


def norm_rows(rows, gain):
    mean_square = jnp.mean(rows * rows, axis=-1, keepdims=True)
    return rows * lax.rsqrt(mean_square + epsilon) * gain


def norm_back(rows, gain, grad):
    scale = lax.rsqrt(jnp.mean(rows * rows, axis=-1, keepdims=True) + epsilon)
    unit = rows * scale
    weighted = grad * gain
    inner = jnp.mean(weighted * unit, axis=-1, keepdims=True)
    return scale * (weighted - unit * inner), grad * unit


def bucket_of(offset):
    distance = jnp.abs(offset)
    levels = jnp.zeros(offset.shape, jnp.int32)
    for edge_value in bucket_edges:
        levels = levels + (distance >= edge_value).astype(jnp.int32)
    return levels + levels_all * (offset > 0).astype(jnp.int32)


def near_shift(tiles):
    return min(1, tiles - 1)


def bias_kernel(stride, reach, table_ref, out_ref):
    row = lax.broadcasted_iota(jnp.int32, (tile, tile), 0)
    lane = lax.broadcasted_iota(jnp.int32, (tile, tile), 1)
    heads = out_ref.shape[0]
    for shift in range(-reach, reach + 1):
        for step in range(2 * stride - 1):
            ids = bucket_of(stride * (tile * shift + lane - row) + step - (stride - 1))
            columns = slice((shift + reach) * tile, (shift + reach + 1) * tile)
            for head in range(heads):
                values = jnp.broadcast_to(table_ref[head : head + 1, :], (tile, tile))
                out_ref[head, step, :, columns] = jnp.take_along_axis(values, ids, axis=1)


def bias_tiles(table, stride, tiles):
    heads = table.shape[1]
    reach = near_shift(tiles)
    lanes = jnp.pad(table.astype(float32).T, ((0, 0), (0, tile - table.shape[0])))
    return pl.pallas_call(
        functools.partial(bias_kernel, stride, reach),
        out_shape=jax.ShapeDtypeStruct(
            (heads, 2 * stride - 1, tile, (2 * reach + 1) * tile), float32
        ),
        compiler_params=params(),
        name="bias_tiles",
    )(lanes)


def attend_kernel(
    stride, head_dim, far_ref, q_ref, k_ref, v_ref, info_ref, bias_ref, probs_ref, out_ref
):
    pair = pl.program_id(0)
    rows_all = q_ref.shape[0]
    tiles = rows_all // tile
    reach = near_shift(tiles)
    per = tile // head_dim
    lane = lax.broadcasted_iota(jnp.int32, (tile, tile), 1)
    for block in range(tiles):
        rows = slice(block * tile, (block + 1) * tile)
        place = info_ref[rows, 0:1]
        low = info_ref[rows, 1:2]
        high = info_ref[rows, 2:3]
        queries = q_ref[rows, :]
        joined = None
        for sub in range(per):
            head = pair * per + sub
            inside = (lane >= sub * head_dim) & (lane < (sub + 1) * head_dim)
            own = jnp.where(inside, queries, jnp.zeros_like(queries))
            raw = dot_nt(own, k_ref[...])
            pieces = []
            top = None
            for part in range(stride):
                for col in range(tiles):
                    start = part * rows_all + col * tile
                    piece = raw[:, start : start + tile]
                    shift = col - block
                    if shift < -reach:
                        piece = piece + far_ref[0, head]
                    elif shift > reach:
                        piece = piece + far_ref[1, head]
                    else:
                        columns = slice((shift + reach) * tile, (shift + reach + 1) * tile)
                        bias = bias_ref[sub, part + stride - 1, :, columns]
                        for other in range(1, stride):
                            bias = jnp.where(
                                place == other,
                                bias_ref[sub, part - other + stride - 1, :, columns],
                                bias,
                            )
                        piece = piece + bias
                    position = stride * (col * tile + lane) + part
                    piece = jnp.where(
                        (position >= low) & (position < high), piece, masked_score
                    )
                    pieces.append(piece)
                    top = piece if top is None else jnp.maximum(top, piece)
            row_max = jnp.max(top, axis=-1, keepdims=True)
            total = None
            for idx, piece in enumerate(pieces):
                pieces[idx] = jnp.exp(piece - row_max)
                total = pieces[idx] if total is None else total + pieces[idx]
            inverse = 1.0 / jnp.sum(total, axis=-1, keepdims=True)
            low_probs = jnp.concatenate(
                [(piece * inverse).astype(bfloat) for piece in pieces], axis=1
            )
            probs_ref[sub, rows, :] = low_probs
            result = dot_nn(low_probs, v_ref[...])
            joined = result if joined is None else jnp.where(inside, result, joined)
        out_ref[rows, :] = joined.astype(bfloat)


def attend(queries, keys, values, info, bias, far, head_dim, stride):
    rows_all, width = queries.shape
    keys_all = keys.shape[0]
    per = tile // head_dim
    heads = width // head_dim
    return pl.pallas_call(
        functools.partial(attend_kernel, stride, head_dim),
        grid=(width // tile,),
        in_specs=[
            pl.BlockSpec(memory_space=pltpu.SMEM),
            pl.BlockSpec((rows_all, tile), lambda i: (0, i)),
            pl.BlockSpec((keys_all, tile), lambda i: (0, i)),
            pl.BlockSpec((keys_all, tile), lambda i: (0, i)),
            pl.BlockSpec(info.shape, lambda i: (0, 0)),
            pl.BlockSpec((per,) + bias.shape[1:], lambda i: (i, 0, 0, 0)),
        ],
        out_specs=[
            pl.BlockSpec((per, rows_all, keys_all), lambda i: (i, 0, 0)),
            pl.BlockSpec((rows_all, tile), lambda i: (0, i)),
        ],
        out_shape=[
            jax.ShapeDtypeStruct((heads, rows_all, keys_all), bfloat),
            jax.ShapeDtypeStruct((rows_all, width), bfloat),
        ],
        compiler_params=params(),
        cost_estimate=pl.CostEstimate(
            flops=16 * rows_all * keys_all * width,
            bytes_accessed=2 * heads * rows_all * keys_all,
            transcendentals=heads * rows_all * keys_all,
        ),
        name="attend",
    )(far, queries, keys, values, info, bias)


def attend_back_kernel(
    stride,
    head_dim,
    scale,
    probs_ref,
    grad_ref,
    out_ref,
    q_ref,
    k_ref,
    v_ref,
    info_ref,
    dq_ref,
    dk_ref,
    dv_ref,
    dbias_ref,
    dfar_ref,
    ds_ref,
):
    rows_all = q_ref.shape[0]
    tiles = rows_all // tile
    reach = near_shift(tiles)
    per = tile // head_dim
    lane = lax.broadcasted_iota(jnp.int32, (tile, tile), 1)
    queries_t = q_ref[...].T
    grads_t = grad_ref[...].T
    dbias_ref[...] = jnp.zeros_like(dbias_ref)
    dfar_ref[...] = jnp.zeros_like(dfar_ref)
    dk_parts = []
    dv_parts = []
    for sub in range(per):
        inside = (lane >= sub * head_dim) & (lane < (sub + 1) * head_dim)
        for block in range(tiles):
            rows = slice(block * tile, (block + 1) * tile)
            place = info_ref[rows, 0:1]
            grads = grad_ref[rows, :]
            own = jnp.where(inside, grads, jnp.zeros_like(grads))
            row_dot = jnp.sum(
                own.astype(float32) * out_ref[rows, :].astype(float32), axis=-1, keepdims=True
            )
            raw = dot_nt(own, v_ref[...])
            pieces = []
            for part in range(stride):
                for col in range(tiles):
                    start = part * rows_all + col * tile
                    piece = probs_ref[sub, rows, start : start + tile].astype(float32) * (
                        raw[:, start : start + tile] - row_dot
                    )
                    shift = col - block
                    if shift < -reach:
                        dfar_ref[sub, 0] += piece
                    elif shift > reach:
                        dfar_ref[sub, 1] += piece
                    else:
                        columns = slice((shift + reach) * tile, (shift + reach + 1) * tile)
                        for other in range(stride):
                            dbias_ref[sub, part - other + stride - 1, :, columns] += jnp.where(
                                place == other, piece, 0.0
                            )
                    pieces.append(piece.astype(bfloat))
            low_grads = jnp.concatenate(pieces, axis=1)
            ds_ref[rows, :] = low_grads
            result = dot_nn(low_grads, k_ref[...]) * scale
            if sub == 0:
                dq_ref[rows, :] = result.astype(bfloat)
            else:
                dq_ref[rows, :] = jnp.where(inside, result.astype(bfloat), dq_ref[rows, :])
        dims = slice(sub * head_dim, (sub + 1) * head_dim)
        dk_parts.append(dot_nn(queries_t[dims, :], ds_ref[...]))
        dv_parts.append(dot_nn(grads_t[dims, :], probs_ref[sub]))
    dk_ref[...] = jnp.concatenate(dk_parts, axis=0).T.astype(bfloat)
    dv_ref[...] = jnp.concatenate(dv_parts, axis=0).T.astype(bfloat)


def attend_back(probs, grads, outs, queries, keys, values, info, head_dim, stride, bias_shape):
    rows_all, width = queries.shape
    keys_all = keys.shape[0]
    per = tile // head_dim
    heads = width // head_dim
    row_spec = pl.BlockSpec((rows_all, tile), lambda i: (0, i))
    key_spec = pl.BlockSpec((keys_all, tile), lambda i: (0, i))
    return pl.pallas_call(
        functools.partial(attend_back_kernel, stride, head_dim, head_dim ** (-0.5)),
        grid=(width // tile,),
        in_specs=[
            pl.BlockSpec((per, rows_all, keys_all), lambda i: (i, 0, 0)),
            row_spec,
            row_spec,
            row_spec,
            key_spec,
            key_spec,
            pl.BlockSpec(info.shape, lambda i: (0, 0)),
        ],
        out_specs=[
            row_spec,
            key_spec,
            key_spec,
            pl.BlockSpec((per,) + bias_shape[1:], lambda i: (i, 0, 0, 0)),
            pl.BlockSpec((per, 2, tile, tile), lambda i: (i, 0, 0, 0)),
        ],
        out_shape=[
            jax.ShapeDtypeStruct((rows_all, width), bfloat),
            jax.ShapeDtypeStruct((keys_all, width), bfloat),
            jax.ShapeDtypeStruct((keys_all, width), bfloat),
            jax.ShapeDtypeStruct(bias_shape, float32),
            jax.ShapeDtypeStruct((heads, 2, tile, tile), float32),
        ],
        scratch_shapes=[pltpu.VMEM((rows_all, keys_all), bfloat)],
        compiler_params=params(),
        cost_estimate=pl.CostEstimate(
            flops=32 * rows_all * keys_all * width,
            bytes_accessed=2 * heads * rows_all * keys_all,
            transcendentals=0,
        ),
        name="attend_back",
    )(probs, grads, outs, queries, keys, values, info)


def expert_kernel(
    count, slots, width, chunk, inner_ref, outer_ref, *refs
):
    blocks = refs[:count]
    results = refs[count : 2 * count]
    hidden_ref, grad_pre_ref, rows_ref, grads_ref, sum_ref, back_ref = refs[2 * count :]
    turn = pl.program_id(0)

    @pl.when(turn == 0)
    def _():
        for idx in range(count):
            rows = slice(idx * slots, (idx + 1) * slots)
            rows_ref[rows, :] = blocks[idx][:, :width]
            grads_ref[rows, :] = blocks[idx][:, width:]

    inner = inner_ref[...].reshape(width, width)
    outer = outer_ref[...].reshape(width, width)
    rows = rows_ref[...]
    grads = grads_ref[...]
    root = 0.7978845608028654
    for start in range(0, width, chunk):
        columns = slice(start, start + chunk)
        pre = dot_nn(rows, inner[:, columns])
        grad_hidden = dot_nt(grads, outer[columns, :])
        square = pre * pre
        curve = jnp.tanh(root * pre * (1.0 + 0.044715 * square))
        half = 0.5 * (1.0 + curve)
        slope = half + (0.5 * root) * pre * (1.0 - curve * curve) * (1.0 + 0.134145 * square)
        hidden_ref[:, columns] = (pre * half).astype(bfloat)
        grad_pre_ref[:, columns] = (grad_hidden * slope).astype(bfloat)
    product = dot_nn(hidden_ref[...], outer)
    product_back = dot_nt(grad_pre_ref[...], inner)

    @pl.when(turn == 0)
    def _():
        sum_ref[...] = product
        back_ref[...] = product_back

    @pl.when(turn > 0)
    def _():
        sum_ref[...] += product
        back_ref[...] += product_back

    @pl.when(turn == pl.num_programs(0) - 1)
    def _():
        for idx in range(count):
            span = slice(idx * slots, (idx + 1) * slots)
            results[idx][:, :width] = sum_ref[span, :].astype(bfloat)
            results[idx][:, width:] = back_ref[span, :].astype(bfloat)


def run_expert(weights, blocks, width):
    (inner, inner_spec), (outer, outer_spec), turns = weights
    count = len(blocks)
    slots = blocks[0].shape[0]
    total = count * slots
    whole = pl.BlockSpec((slots, 2 * width), lambda i: (0, 0))
    chunk = pl.BlockSpec((total, width), lambda i: (0, i))
    outs = pl.pallas_call(
        functools.partial(expert_kernel, count, slots, width, 256),
        grid=(turns,),
        in_specs=[inner_spec, outer_spec] + [whole] * count,
        out_specs=[whole] * count + [chunk, chunk],
        out_shape=[jax.ShapeDtypeStruct((slots, 2 * width), bfloat)] * count
        + [jax.ShapeDtypeStruct((total, turns * width), bfloat)] * 2,
        scratch_shapes=[
            pltpu.VMEM((total, width), bfloat),
            pltpu.VMEM((total, width), bfloat),
            pltpu.VMEM((total, width), float32),
            pltpu.VMEM((total, width), float32),
        ],
        compiler_params=params(),
        cost_estimate=pl.CostEstimate(
            flops=8 * total * width * width * turns,
            bytes_accessed=4 * width * width * turns,
            transcendentals=total * width * turns,
        ),
        name="run_expert",
    )(inner, outer, *blocks)
    return outs[:count], outs[count], outs[count + 1]


def expert_grad_kernel(batches, count, slots, width, second, *refs):
    groups = [refs[idx * count : (idx + 1) * count] for idx in range(batches)]
    wide = refs[batches * count : batches * count + batches]
    out_ref, rows_ref = refs[-2], refs[-1]
    half = slice(width, 2 * width) if second else slice(0, width)

    @pl.when(pl.program_id(0) == 0)
    def _():
        for batch in range(batches):
            for idx in range(count):
                start = (batch * count + idx) * slots
                rows_ref[start : start + slots, :] = groups[batch][idx][:, half]

    total = None
    span = count * slots
    for batch in range(batches):
        rows = rows_ref[batch * span : (batch + 1) * span, :]
        if second:
            term = dot_tn(wide[batch][...], rows)
        else:
            term = dot_tn(rows, wide[batch][...])
        total = term if total is None else total + term
    out_ref[...] = total.astype(bfloat).reshape(out_ref.shape)


def expert_grad(groups, wide, width, second, out_shape, out_spec, buffer=None):
    batches = len(groups)
    count = len(groups[0])
    slots = groups[0][0].shape[0]
    total = count * slots
    turns = wide[0].shape[1] // width
    kernel = functools.partial(expert_grad_kernel, batches, count, slots, width, second)
    in_specs = [pl.BlockSpec((slots, 2 * width), lambda i: (0, 0))] * (batches * count)
    in_specs = in_specs + [pl.BlockSpec((total, width), lambda i: (0, i))] * batches
    operands = [block for group in groups for block in group] + list(wide)
    aliases = {}
    body = kernel
    if buffer is not None:
        in_specs = [pl.BlockSpec(memory_space=pl.ANY)] + in_specs
        operands = [buffer] + operands
        aliases = {0: 0}

        def body(*refs):
            kernel(*refs[1:])

    return pl.pallas_call(
        body,
        grid=(turns,),
        in_specs=in_specs,
        out_specs=out_spec,
        out_shape=jax.ShapeDtypeStruct(out_shape, bfloat),
        scratch_shapes=[pltpu.VMEM((batches * total, width), bfloat)],
        input_output_aliases=aliases,
        compiler_params=params(),
        cost_estimate=pl.CostEstimate(
            flops=2 * batches * total * width * width * turns,
            bytes_accessed=4 * width * width * turns,
            transcendentals=0,
        ),
        name="expert_grad_outer" if second else "expert_grad_inner",
    )(*operands)


def on_device(
    hidden_in,
    out_grad,
    places,
    lengths,
    routes,
    norm1_gain,
    w_query,
    w_key,
    w_value,
    w_output,
    rel_table,
    norm2_gain,
    w_router,
    w_in,
    w_out,
):
    batches, rows_own, width = hidden_in.shape
    heads = rel_table.shape[1]
    head_dim = width // heads
    scale = head_dim ** (-0.5)
    shards = lax.axis_size("dp")
    members = lax.axis_size("expert")
    me = lax.axis_index("expert")
    experts = w_router.shape[1]
    hidden_width = w_in.shape[2]
    turns = hidden_width // width
    tiles = rows_own // tile
    depth = width // shards
    depth_out = hidden_width // shards
    table_rows = rel_table.shape[0]
    capacity = max(2, rows_own * 17 // (experts * 16))
    slots = -(-capacity // 16) * 16

    def around(step):
        return [(idx, (idx + step) % members) for idx in range(members)]

    hidden_from = [hidden_in] + [
        lax.ppermute(hidden_in, "expert", around(step)) for step in range(1, members)
    ]

    small = jnp.concatenate(
        [
            norm1_gain.reshape(-1),
            norm2_gain.reshape(-1),
            w_router.reshape(-1),
            rel_table.reshape(-1),
        ]
    )
    small_used = small.shape[0]
    small_rows = -(-small_used // width)
    small_pad = -(-small_rows // 16) * 16
    small = jnp.pad(small, (0, small_pad * width - small_used)).reshape(small_pad, width)
    first = lax.all_gather(
        jnp.concatenate([w_query, w_key, w_value, small], axis=0), "dp", axis=0, tiled=False
    )
    inner_parts = [w_in[0, :, idx * width : (idx + 1) * width] for idx in range(turns)]
    second_own = jnp.concatenate(inner_parts + [w_out[0], w_output], axis=0)
    second_own, _ = lax.optimization_barrier((second_own, first))
    second = lax.all_gather(second_own, "dp", axis=0, tiled=False)

    query_w = first[:, :depth].reshape(width, width)
    key_w = first[:, depth : 2 * depth].reshape(width, width)
    value_w = first[:, 2 * depth : 3 * depth].reshape(width, width)
    small_all = first[:, 3 * depth :].reshape(shards, small_pad * width)
    gain_one = small_all[:, :depth].reshape(width).astype(float32)
    gain_two = small_all[:, depth : 2 * depth].reshape(width).astype(float32)
    router_end = 2 * depth + depth * experts
    router_w = small_all[:, 2 * depth : router_end].reshape(width, experts)
    table = small_all[:, router_end:small_used].reshape(shards * table_rows, heads)
    output_w = second[:, turns * depth + depth_out :].reshape(width, width)

    direct = depth % 16 == 0 and turns * depth == depth_out and shards % turns == 0
    if direct:
        group = shards // turns
        inner_spec = pl.BlockSpec((shards, depth, width), lambda i: (0, i, 0))
        outer_spec = pl.BlockSpec((group, depth_out, width), lambda i: (i, 1, 0))
        weights = ((second, inner_spec), (second, outer_spec), turns)
    else:
        inner_w = second[:, : turns * depth].reshape(shards, turns, depth, width)
        inner_w = jnp.transpose(inner_w, (1, 0, 2, 3)).reshape(turns, width, width)
        outer_w = second[:, turns * depth : turns * depth + depth_out].reshape(
            turns, width, width
        )
        plain = pl.BlockSpec((1, width, width), lambda i: (i, 0, 0))
        weights = ((inner_w, plain), (outer_w, plain), turns)

    places_in = places[:, 0].reshape(batches, members, rows_own)
    offsets = places_in - members * jnp.arange(rows_own, dtype=jnp.int32)[None, None]
    offset_from = [
        jnp.take(offsets, jnp.mod(me - step, members), axis=1) for step in range(members)
    ]

    def by_place(parts):
        ordered = []
        for place in range(members):
            rows = parts[0]
            for step in range(1, members):
                rows = jnp.where((offset_from[step] == place)[..., None], parts[step], rows)
            ordered.append(rows)
        return jnp.concatenate(ordered, axis=1)

    def of_member(ordered, batch, step):
        rows = ordered[:rows_own]
        for place in range(1, members):
            rows = jnp.where(
                (offset_from[step][batch] == place)[:, None],
                ordered[place * rows_own : (place + 1) * rows_own],
                rows,
            )
        return rows

    ends = jnp.cumsum(lengths[:, 0], axis=-1)[:, :-1]
    position_own = offset_from[0] + members * jnp.arange(rows_own, dtype=jnp.int32)[None]
    past = position_own[:, :, None] >= ends[:, None, :]
    low = jnp.max(jnp.where(past, ends[:, None, :], 0), axis=-1)
    high = jnp.min(jnp.where(past, members * rows_own, ends[:, None, :]), axis=-1)
    info = jnp.stack([offset_from[0], low, high], axis=-1)
    info = jnp.pad(info, ((0, 0), (0, 0), (0, 5)))

    chosen = routes[:, :, 0]
    picked = chosen[:, :, None] == jnp.arange(experts, dtype=jnp.int32)
    counts = picked.astype(jnp.int32)
    slot = jnp.sum((jnp.cumsum(counts, axis=1) - counts) * counts, axis=2)
    target = jnp.mod(chosen - me, members) * slots + slot
    dispatch = (
        jnp.arange(members * slots, dtype=jnp.int32)[None, :, None] == target[:, None, :]
    ).astype(bfloat)

    ordered_in = by_place(hidden_from)
    ordered_f = ordered_in.astype(float32)
    own_f = hidden_in.astype(float32)
    normed_all = norm_rows(ordered_f, gain_one).astype(bfloat)
    normed_own = norm_rows(own_f, gain_one).astype(bfloat)
    flat_all = normed_all.reshape(batches * members * rows_own, width)
    flat_own = normed_own.reshape(batches * rows_own, width)
    queries = (dot_nn(flat_own, query_w).astype(bfloat) * bfloat(scale)).reshape(
        batches, rows_own, width
    )
    keys = dot_nn(flat_all, key_w).astype(bfloat).reshape(batches, members * rows_own, width)
    values = dot_nn(flat_all, value_w).astype(bfloat).reshape(batches, members * rows_own, width)
    bias = bias_tiles(table, members, tiles)
    table_f = table.astype(float32)
    far = jnp.stack([table_f[levels_all - 1], table_f[2 * levels_all - 1]])

    probs = []
    attended = []
    resid_mid = []
    normed_two = []
    gate_all = []
    gate = []
    blocks = []
    for batch in range(batches):
        kept, joined = attend(
            queries[batch], keys[batch], values[batch], info[batch], bias, far, head_dim, members
        )
        probs.append(kept)
        attended.append(joined)
        mid = own_f[batch] + dot_nn(joined, output_w)
        normed = norm_rows(mid, gain_two).astype(bfloat)
        logits = dot_nn(normed, router_w)
        shifted = jnp.exp(logits - jnp.max(logits, axis=-1, keepdims=True))
        router_probs = shifted / jnp.sum(shifted, axis=-1, keepdims=True)
        gate_own = jnp.sum(jnp.where(picked[batch], router_probs, 0.0), axis=1, keepdims=True)
        grad_expert = (gate_own * out_grad[batch].astype(float32)).astype(bfloat)
        outgoing = dot_nn(
            dispatch[batch], jnp.concatenate([normed, grad_expert], axis=1)
        ).astype(bfloat)
        received = [outgoing[:slots]]
        for step in range(1, members):
            received.append(
                lax.ppermute(
                    outgoing[step * slots : (step + 1) * slots], "expert", around(step)
                )
            )
        resid_mid.append(mid)
        normed_two.append(normed)
        gate_all.append(router_probs)
        gate.append(gate_own)
        blocks.append(received)

    returned = []
    hidden = []
    grad_pre = []
    for batch in range(batches):
        results, hidden_rows, grad_rows = run_expert(weights, blocks[batch], width)
        hidden.append(hidden_rows)
        grad_pre.append(grad_rows)
        back = [results[0]]
        for step in range(1, members):
            back.append(lax.ppermute(results[step], "expert", around(-step)))
        returned.append(jnp.concatenate(back, axis=0))

    if direct:
        buffer_shape = (shards, turns * depth + depth_out, width)
        buffer = expert_grad(
            blocks,
            grad_pre,
            width,
            False,
            buffer_shape,
            pl.BlockSpec((shards, depth, width), lambda i: (0, i, 0)),
        )
        buffer = expert_grad(
            blocks,
            hidden,
            width,
            True,
            buffer_shape,
            pl.BlockSpec((group, depth_out, width), lambda i: (i, 1, 0)),
            buffer,
        )
    else:
        plain_shape = (turns, width, width)
        inner_g = expert_grad(blocks, grad_pre, width, False, plain_shape, plain)
        outer_g = expert_grad(blocks, hidden, width, True, plain_shape, plain)
        inner_g = jnp.transpose(inner_g.reshape(turns, shards, depth, width), (1, 0, 2, 3))
        buffer = jnp.concatenate(
            [
                inner_g.reshape(shards, turns * depth, width),
                outer_g.reshape(shards, depth_out, width),
            ],
            axis=1,
        )
    expert_sum = lax.psum_scatter(buffer, "dp", scatter_dimension=0, tiled=False)

    layer_rows = []
    input_rows = []
    grad_attn_rows = []
    grad_q_rows = []
    grad_k_rows = []
    grad_v_rows = []
    grad_gain_one = 0.0
    grad_gain_two = 0.0
    grad_router = 0.0
    grad_bias = 0.0
    grad_far = 0.0
    router_f = router_w.astype(float32)
    for batch in range(batches):
        home = dot_tn(dispatch[batch], returned[batch])
        expert_back = home[:, :width]
        grad_output = out_grad[batch].astype(float32)
        layer_rows.append((resid_mid[batch] + gate[batch] * expert_back).astype(bfloat))
        grad_gate = jnp.sum(grad_output * expert_back, axis=1, keepdims=True)
        grad_logits = (grad_gate * gate[batch]) * (
            jnp.where(picked[batch], 1.0, 0.0) - gate_all[batch]
        )
        grad_normed = home[:, width:] + lax.dot_general(
            grad_logits, router_f, (((1,), (1,)), ((), ())), precision=precise
        )
        grad_router = grad_router + lax.dot_general(
            normed_two[batch].astype(float32),
            grad_logits,
            (((0,), (0,)), ((), ())),
            precision=precise,
        )
        grad_resid, gain_terms = norm_back(resid_mid[batch], gain_two, grad_normed)
        grad_gain_two = grad_gain_two + jnp.sum(gain_terms, axis=0)
        grad_mid = grad_output + grad_resid
        grad_attn = grad_mid.astype(bfloat)
        grad_attn_rows.append(grad_attn)
        grad_attended = dot_nt(grad_attn, output_w).astype(bfloat)
        grad_q, grad_k, grad_v, bias_terms, far_terms = attend_back(
            probs[batch],
            grad_attended,
            attended[batch],
            queries[batch],
            keys[batch],
            values[batch],
            info[batch],
            head_dim,
            members,
            bias.shape,
        )
        grad_q_rows.append(grad_q)
        grad_k_rows.append(grad_k)
        grad_v_rows.append(grad_v)
        grad_bias = grad_bias + bias_terms
        grad_far = grad_far + far_terms
        grad_ordered = dot_nt(grad_k, key_w) + dot_nt(grad_v, value_w)
        grad_own = dot_nt(grad_q, query_w)
        home_rows = of_member(grad_ordered, batch, 0)
        for step in range(1, members):
            sent = of_member(grad_ordered, batch, step).astype(bfloat)
            home_rows = home_rows + lax.ppermute(sent, "expert", around(-step)).astype(float32)
        grad_tokens, _ = norm_back(own_f[batch], gain_one, grad_own + home_rows)
        input_rows.append(grad_mid + grad_tokens)
        _, terms_all = norm_back(ordered_f[batch], gain_one, grad_ordered)
        _, terms_own = norm_back(own_f[batch], gain_one, grad_own)
        grad_gain_one = grad_gain_one + jnp.sum(terms_all, axis=0) + jnp.sum(terms_own, axis=0)

    def flat(rows):
        return jnp.concatenate(rows, axis=0)

    grad_wo = dot_tn(flat(attended), flat(grad_attn_rows))
    grad_wq = dot_tn(flat_own, flat(grad_q_rows))
    grad_wk = dot_tn(flat_all, flat(grad_k_rows))
    grad_wv = dot_tn(flat_all, flat(grad_v_rows))

    steps = 2 * members - 1
    reach = near_shift(tiles)
    shape = (steps, tile, (2 * reach + 1) * tile)
    delta = (
        members
        * (
            lax.broadcasted_iota(jnp.int32, shape, 2)
            - reach * tile
            - lax.broadcasted_iota(jnp.int32, shape, 1)
        )
        + lax.broadcasted_iota(jnp.int32, shape, 0)
        - (members - 1)
    )
    buckets = shards * table_rows
    onehot = (
        bucket_of(delta)[None] == jnp.arange(buckets, dtype=jnp.int32)[:, None, None, None]
    ).astype(bfloat)
    grad_table = jnp.einsum(
        "hsab,ksab->kh", grad_bias.astype(bfloat), onehot, preferred_element_type=float32
    )
    far_sum = jnp.sum(grad_far, axis=(2, 3))
    grad_table = grad_table.at[levels_all - 1].add(far_sum[:, 0])
    grad_table = grad_table.at[2 * levels_all - 1].add(far_sum[:, 1])

    small_grad = jnp.concatenate(
        [
            grad_gain_one.reshape(shards, depth),
            grad_gain_two.reshape(shards, depth),
            grad_router.reshape(shards, depth * experts),
            grad_table.reshape(shards, table_rows * heads),
        ],
        axis=1,
    )
    small_grad = jnp.pad(small_grad, ((0, 0), (0, small_pad * width - small_used)))
    dense = jnp.concatenate(
        [
            grad_wq.astype(bfloat).reshape(shards, depth, width),
            grad_wk.astype(bfloat).reshape(shards, depth, width),
            grad_wv.astype(bfloat).reshape(shards, depth, width),
            grad_wo.astype(bfloat).reshape(shards, depth, width),
            small_grad.astype(bfloat).reshape(shards, small_pad, width),
        ],
        axis=1,
    )
    dense, _ = lax.optimization_barrier((dense, expert_sum))
    dense_part = lax.psum_scatter(dense, "dp", scatter_dimension=0, tiled=False)
    dense_sum = dense_part.astype(float32)
    for step in range(1, members):
        dense_sum = dense_sum + lax.ppermute(dense_part, "expert", around(step)).astype(float32)

    expert_f = expert_sum.astype(float32)
    inner_sum = jnp.concatenate(
        [expert_f[idx * depth : (idx + 1) * depth] for idx in range(turns)], axis=1
    )[None]
    outer_sum = expert_f[turns * depth :][None]
    small_sum = dense_sum[4 * depth :].reshape(-1)
    return (
        jnp.stack(layer_rows),
        jnp.stack(input_rows),
        small_sum[:depth],
        dense_sum[:depth],
        dense_sum[depth : 2 * depth],
        dense_sum[2 * depth : 3 * depth],
        dense_sum[3 * depth : 4 * depth],
        small_sum[router_end:small_used].reshape(table_rows, heads),
        small_sum[depth : 2 * depth],
        small_sum[2 * depth : router_end].reshape(depth, experts),
        inner_sum,
        outer_sum,
    )


def solution(mesh):
    return jax.shard_map(
        on_device,
        mesh=mesh,
        in_specs=(
            P(None, ("dp", "expert"), None),
            P(None, ("dp", "expert"), None),
            P(None, "dp", None),
            P(None, "dp", None),
            P(None, ("dp", "expert"), None),
            P("dp"),
            P("dp", None),
            P("dp", None),
            P("dp", None),
            P("dp", None),
            P("dp", None),
            P("dp"),
            P("dp", None),
            P("expert", "dp", None),
            P("expert", "dp", None),
        ),
        out_specs=(
            P(None, ("dp", "expert"), None),
            P(None, ("dp", "expert"), None),
            P("dp"),
            P("dp", None),
            P("dp", None),
            P("dp", None),
            P("dp", None),
            P("dp", None),
            P("dp"),
            P("dp", None),
            P("expert", "dp", None),
            P("expert", "dp", None),
        ),
        check_vma=False,
    )
```

```python
import functools

import jax
import jax.numpy as jnp
from jax import lax
from jax.experimental import pallas as pl
from jax.experimental.pallas import tpu as pltpu
from jax.sharding import PartitionSpec as P

bucket_edges = (1, 2, 3, 4, 5, 6, 7, 8, 12, 16, 23, 32, 46, 64, 91)
levels_all = len(bucket_edges) + 1
epsilon = 1e-06
masked_score = -1000000000.0
precise = lax.Precision.HIGHEST
float32 = jnp.float32
bfloat = jnp.bfloat16
tile = 128
vmem_bytes = 56 * 1024 * 1024


def params():
    return pltpu.CompilerParams(vmem_limit_bytes=vmem_bytes)


def dot_nn(left, right):
    return lax.dot_general(left, right, (((1,), (0,)), ((), ())), preferred_element_type=float32)


def dot_nt(left, right):
    return lax.dot_general(left, right, (((1,), (1,)), ((), ())), preferred_element_type=float32)


def dot_tn(left, right):
    return lax.dot_general(left, right, (((0,), (0,)), ((), ())), preferred_element_type=float32)


def norm_rows(rows, gain):
    mean_square = jnp.mean(rows * rows, axis=-1, keepdims=True)
    return rows * lax.rsqrt(mean_square + epsilon) * gain


def norm_back(rows, gain, grad):
    scale = lax.rsqrt(jnp.mean(rows * rows, axis=-1, keepdims=True) + epsilon)
    unit = rows * scale
    weighted = grad * gain
    inner = jnp.mean(weighted * unit, axis=-1, keepdims=True)
    return scale * (weighted - unit * inner), grad * unit


def bucket_of(offset):
    distance = jnp.abs(offset)
    levels = jnp.zeros(offset.shape, jnp.int32)
    for edge_value in bucket_edges:
        levels = levels + (distance >= edge_value).astype(jnp.int32)
    return levels + levels_all * (offset > 0).astype(jnp.int32)


def near_shift(tiles):
    return min(1, tiles - 1)


def bias_kernel(stride, reach, table_ref, out_ref):
    row = lax.broadcasted_iota(jnp.int32, (tile, tile), 0)
    lane = lax.broadcasted_iota(jnp.int32, (tile, tile), 1)
    heads = out_ref.shape[0]
    for shift in range(-reach, reach + 1):
        for step in range(2 * stride - 1):
            ids = bucket_of(stride * (tile * shift + lane - row) + step - (stride - 1))
            columns = slice((shift + reach) * tile, (shift + reach + 1) * tile)
            for head in range(heads):
                values = jnp.broadcast_to(table_ref[head : head + 1, :], (tile, tile))
                out_ref[head, step, :, columns] = jnp.take_along_axis(values, ids, axis=1)


def bias_tiles(table, stride, tiles):
    heads = table.shape[1]
    reach = near_shift(tiles)
    lanes = jnp.pad(table.astype(float32).T, ((0, 0), (0, tile - table.shape[0])))
    return pl.pallas_call(
        functools.partial(bias_kernel, stride, reach),
        out_shape=jax.ShapeDtypeStruct(
            (heads, 2 * stride - 1, tile, (2 * reach + 1) * tile), float32
        ),
        compiler_params=params(),
        name="bias_tiles",
    )(lanes)


def project_kernel(scale, rows_ref, gain_ref, weight_ref, normed_ref, q_ref, k_ref, v_ref):
    width = rows_ref.shape[1]
    span = q_ref.shape[1]
    depth = weight_ref.shape[1] // 3
    normed = norm_rows(rows_ref[...].astype(float32), gain_ref[...]).astype(bfloat)
    normed_ref[...] = normed
    for idx, out_ref in enumerate((q_ref, k_ref, v_ref)):
        weight = weight_ref[:, idx * depth : (idx + 1) * depth, :].reshape(width, span)
        product = dot_nn(normed, weight).astype(bfloat)
        out_ref[...] = product * bfloat(scale) if idx == 0 else product


def project(rows, gain, packed, scale):
    count, width = rows.shape
    span = packed.shape[2]
    step = min(512, count)
    row_spec = pl.BlockSpec((step, width), lambda i: (i, 0))
    out_spec = pl.BlockSpec((step, span), lambda i: (i, 0))
    return pl.pallas_call(
        functools.partial(project_kernel, scale),
        grid=(count // step,),
        in_specs=[
            row_spec,
            pl.BlockSpec((1, width), lambda i: (0, 0)),
            pl.BlockSpec(packed.shape, lambda i: (0, 0, 0)),
        ],
        out_specs=[row_spec, out_spec, out_spec, out_spec],
        out_shape=[jax.ShapeDtypeStruct((count, width), bfloat)]
        + [jax.ShapeDtypeStruct((count, span), bfloat)] * 3,
        compiler_params=params(),
        cost_estimate=pl.CostEstimate(
            flops=6 * count * width * span, bytes_accessed=4 * count * width, transcendentals=0
        ),
        name="project",
    )(rows, gain, packed)


def segment_of(positions, ends):
    segment = jnp.zeros(positions.shape, jnp.int32)
    for end in ends:
        segment = segment + (positions >= end).astype(jnp.int32)
    return segment


def masked_heads(rows, lane, per, head_dim):
    parts = []
    for sub in range(per):
        inside = (lane >= sub * head_dim) & (lane < (sub + 1) * head_dim)
        parts.append(jnp.where(inside, rows, jnp.zeros_like(rows)))
    return jnp.concatenate(parts, axis=0)


def joined_heads(rows, lane, per, head_dim):
    joined = rows[:tile]
    for sub in range(1, per):
        inside = (lane >= sub * head_dim) & (lane < (sub + 1) * head_dim)
        joined = jnp.where(inside, rows[sub * tile : (sub + 1) * tile], joined)
    return joined


def attend_kernel(
    stride, head_dim, far_ref, ends_ref, q_ref, k_ref, v_ref, bias_ref, probs_ref, out_ref, inv_ref
):
    pair = pl.program_id(0)
    rows_all = q_ref.shape[0]
    rows_part = rows_all // stride
    tiles = rows_part // tile
    reach = near_shift(tiles)
    per = tile // head_dim
    lane = lax.broadcasted_iota(jnp.int32, (tile, tile), 1)
    ends = [ends_ref[idx] for idx in range(ends_ref.shape[0])]
    keys_t = k_ref[...].T
    lane_row = lax.broadcasted_iota(jnp.int32, (1, tile), 1)
    row_column = lax.broadcasted_iota(jnp.int32, (tile, 1), 0)
    key_segments = [
        segment_of(stride * (col * tile + lane_row) + part, ends)
        for part in range(stride)
        for col in range(tiles)
    ]
    for mine in range(stride):
        for block in range(tiles):
            begin = mine * rows_part + block * tile
            rows = slice(begin, begin + tile)
            segment = segment_of(stride * (block * tile + row_column) + mine, ends)
            raw = dot_nn(masked_heads(q_ref[rows, :], lane, per, head_dim), keys_t)
            stacked = []
            inverses = []
            for sub in range(per):
                head = pair * per + sub
                pieces = []
                top = None
                for part in range(stride):
                    for col in range(tiles):
                        start = (part * tiles + col) * tile
                        piece = raw[sub * tile : (sub + 1) * tile, start : start + tile]
                        shift = col - block
                        if shift < -reach:
                            piece = piece + far_ref[0, head]
                        elif shift > reach:
                            piece = piece + far_ref[1, head]
                        else:
                            columns = slice((shift + reach) * tile, (shift + reach + 1) * tile)
                            piece = piece + bias_ref[sub, part - mine + stride - 1, :, columns]
                        same = key_segments[part * tiles + col] == segment
                        piece = jnp.where(same, piece, masked_score)
                        pieces.append(piece)
                        top = piece if top is None else jnp.maximum(top, piece)
                row_max = jnp.max(top, axis=-1, keepdims=True)
                total = None
                for idx, piece in enumerate(pieces):
                    piece = jnp.exp(piece - row_max)
                    total = piece if total is None else total + piece
                    pieces[idx] = piece.astype(bfloat)
                kept = jnp.concatenate(pieces, axis=1)
                probs_ref[sub, rows, :] = kept
                stacked.append(kept)
                inverses.append(1.0 / jnp.sum(total, axis=-1, keepdims=True))
            result = dot_nn(jnp.concatenate(stacked, axis=0), v_ref[...])
            inverse = jnp.broadcast_to(inverses[0], (tile, tile))
            for sub in range(1, per):
                inside = (lane >= sub * head_dim) & (lane < (sub + 1) * head_dim)
                inverse = jnp.where(inside, inverses[sub], inverse)
            out_ref[rows, :] = (joined_heads(result, lane, per, head_dim) * inverse).astype(bfloat)
            inv_ref[rows, :] = inverse


def attend(queries, keys, values, ends, bias, far, head_dim, stride):
    rows_all, span = queries.shape
    per = tile // head_dim
    heads = span // head_dim
    row_spec = pl.BlockSpec((rows_all, tile), lambda i: (0, i))
    return pl.pallas_call(
        functools.partial(attend_kernel, stride, head_dim),
        grid=(span // tile,),
        in_specs=[
            pl.BlockSpec(memory_space=pltpu.SMEM),
            pl.BlockSpec(memory_space=pltpu.SMEM),
            row_spec,
            row_spec,
            row_spec,
            pl.BlockSpec((per,) + bias.shape[1:], lambda i: (i, 0, 0, 0)),
        ],
        out_specs=[
            pl.BlockSpec((per, rows_all, rows_all), lambda i: (i, 0, 0)),
            row_spec,
            row_spec,
        ],
        out_shape=[
            jax.ShapeDtypeStruct((heads, rows_all, rows_all), bfloat),
            jax.ShapeDtypeStruct((rows_all, span), bfloat),
            jax.ShapeDtypeStruct((rows_all, span), float32),
        ],
        compiler_params=params(),
        cost_estimate=pl.CostEstimate(
            flops=16 * rows_all * rows_all * span,
            bytes_accessed=2 * heads * rows_all * rows_all,
            transcendentals=heads * rows_all * rows_all,
        ),
        name="attend",
    )(far, ends, queries, keys, values, bias)


def attend_back_kernel(
    stride,
    head_dim,
    scale,
    probs_ref,
    grad_ref,
    out_ref,
    inv_ref,
    q_ref,
    k_ref,
    v_ref,
    after_ref,
    dq_ref,
    dk_ref,
    dv_ref,
    dbias_ref,
    dfar_ref,
    ds_ref,
    grads_ref,
):
    rows_all = q_ref.shape[0]
    rows_part = rows_all // stride
    tiles = rows_part // tile
    reach = near_shift(tiles)
    per = tile // head_dim
    lane = lax.broadcasted_iota(jnp.int32, (tile, tile), 1)
    queries_t = q_ref[...].T
    values_t = v_ref[...].T
    grads_ref[...] = (grad_ref[...].astype(float32) * inv_ref[...]).astype(bfloat)
    grads_t = grads_ref[...].T
    dbias_ref[...] = jnp.zeros_like(dbias_ref)
    dfar_ref[...] = jnp.zeros_like(dfar_ref)
    for mine in range(stride):
        for block in range(tiles):
            begin = mine * rows_part + block * tile
            rows = slice(begin, begin + tile)
            own = masked_heads(grads_ref[rows, :], lane, per, head_dim)
            outs = out_ref[rows, :].astype(float32)
            raw = dot_nn(own, values_t)
            stacked = []
            for sub in range(per):
                span = slice(sub * tile, (sub + 1) * tile)
                row_dot = jnp.sum(own[span].astype(float32) * outs, axis=-1, keepdims=True)
                pieces = []
                for part in range(stride):
                    for col in range(tiles):
                        start = (part * tiles + col) * tile
                        piece = probs_ref[sub, rows, start : start + tile].astype(float32) * (
                            raw[span, start : start + tile] - row_dot
                        )
                        shift = col - block
                        if shift < -reach:
                            dfar_ref[sub, 0] += piece
                        elif shift > reach:
                            dfar_ref[sub, 1] += piece
                        else:
                            columns = slice((shift + reach) * tile, (shift + reach + 1) * tile)
                            dbias_ref[sub, part - mine + stride - 1, :, columns] += piece
                        pieces.append(piece.astype(bfloat))
                low_grads = jnp.concatenate(pieces, axis=1)
                ds_ref[sub, rows, :] = low_grads
                stacked.append(low_grads)
            result = dot_nn(jnp.concatenate(stacked, axis=0), k_ref[...]) * scale
            dq_ref[rows, :] = joined_heads(result, lane, per, head_dim).astype(bfloat)
    dk_parts = []
    dv_parts = []
    for sub in range(per):
        dims = slice(sub * head_dim, (sub + 1) * head_dim)
        dk_parts.append(dot_nn(queries_t[dims, :], ds_ref[sub]))
        dv_parts.append(dot_nn(grads_t[dims, :], probs_ref[sub]))
    dk_ref[...] = jnp.concatenate(dk_parts, axis=0).T.astype(bfloat)
    dv_ref[...] = jnp.concatenate(dv_parts, axis=0).T.astype(bfloat)


def attend_back(
    probs, grads, outs, inverse, queries, keys, values, after, head_dim, stride, bias_shape
):
    rows_all, span = queries.shape
    per = tile // head_dim
    heads = span // head_dim
    row_spec = pl.BlockSpec((rows_all, tile), lambda i: (0, i))
    return pl.pallas_call(
        functools.partial(attend_back_kernel, stride, head_dim, head_dim ** (-0.5)),
        grid=(span // tile,),
        in_specs=[pl.BlockSpec((per, rows_all, rows_all), lambda i: (i, 0, 0))]
        + [row_spec] * 6
        + [pl.BlockSpec(memory_space=pl.ANY)],
        out_specs=[
            row_spec,
            row_spec,
            row_spec,
            pl.BlockSpec((per,) + bias_shape[1:], lambda i: (i, 0, 0, 0)),
            pl.BlockSpec((per, 2, tile, tile), lambda i: (i, 0, 0, 0)),
        ],
        out_shape=[jax.ShapeDtypeStruct((rows_all, span), bfloat)] * 3
        + [
            jax.ShapeDtypeStruct(bias_shape, float32),
            jax.ShapeDtypeStruct((heads, 2, tile, tile), float32),
        ],
        scratch_shapes=[
            pltpu.VMEM((per, rows_all, rows_all), bfloat),
            pltpu.VMEM((rows_all, tile), bfloat),
        ],
        compiler_params=params(),
        cost_estimate=pl.CostEstimate(
            flops=32 * rows_all * rows_all * span,
            bytes_accessed=2 * heads * rows_all * rows_all,
            transcendentals=0,
        ),
        name="attend_back",
    )(probs, grads, outs, inverse, queries, keys, values, after)


def add_kernel(left_ref, right_ref, after_ref, out_ref):
    out_ref[...] = (left_ref[...].astype(float32) + right_ref[...].astype(float32)).astype(bfloat)


def add_after(left, right, after):
    return pl.pallas_call(
        add_kernel,
        in_specs=[
            pl.BlockSpec(memory_space=pltpu.VMEM),
            pl.BlockSpec(memory_space=pltpu.VMEM),
            pl.BlockSpec(memory_space=pl.ANY),
        ],
        out_specs=pl.BlockSpec(memory_space=pltpu.VMEM),
        out_shape=jax.ShapeDtypeStruct(left.shape, bfloat),
        compiler_params=params(),
        name="add_after",
    )(left, right, after)


def order_kernel(count, place_ref, *refs):
    out_ref = refs[count]
    for place in range(count):
        rows = refs[0][0]
        for step in range(1, count):
            rows = jnp.where(place_ref[0, :, step : step + 1] == place, refs[step][0], rows)
        out_ref[0, place] = rows


def order_rows(parts, offsets):
    batches, rows, width = parts[0].shape
    count = len(parts)
    part_spec = pl.BlockSpec((1, rows, width), lambda i: (i, 0, 0))
    return pl.pallas_call(
        functools.partial(order_kernel, count),
        grid=(batches,),
        in_specs=[pl.BlockSpec((1, rows, count), lambda i: (i, 0, 0))] + [part_spec] * count,
        out_specs=pl.BlockSpec((1, count, rows, width), lambda i: (i, 0, 0, 0)),
        out_shape=jax.ShapeDtypeStruct((batches, count, rows, width), bfloat),
        compiler_params=params(),
        name="order_rows",
    )(offsets, *parts)


def expert_kernel(
    count, slots, width, chunk, inner_ref, outer_ref, *refs
):
    blocks = refs[:count]
    results = refs[count : 2 * count]
    hidden_ref, grad_pre_ref, rows_ref, grads_ref, sum_ref, back_ref = refs[2 * count :]
    turn = pl.program_id(0)

    @pl.when(turn == 0)
    def _():
        for idx in range(count):
            rows = slice(idx * slots, (idx + 1) * slots)
            rows_ref[rows, :] = blocks[idx][:, :width]
            grads_ref[rows, :] = blocks[idx][:, width:]

    inner = inner_ref[...].reshape(width, width)
    outer = outer_ref[...].reshape(width, width)
    rows = rows_ref[...]
    grads = grads_ref[...]
    root = 0.7978845608028654
    for start in range(0, width, chunk):
        columns = slice(start, start + chunk)
        pre = dot_nn(rows, inner[:, columns])
        grad_hidden = dot_nt(grads, outer[columns, :])
        square = pre * pre
        curve = jnp.tanh(root * pre * (1.0 + 0.044715 * square))
        half = 0.5 * (1.0 + curve)
        slope = half + (0.5 * root) * pre * (1.0 - curve * curve) * (1.0 + 0.134145 * square)
        hidden_ref[:, columns] = (pre * half).astype(bfloat)
        grad_pre_ref[:, columns] = (grad_hidden * slope).astype(bfloat)
    product = dot_nn(hidden_ref[...], outer)
    product_back = dot_nt(grad_pre_ref[...], inner)

    @pl.when(turn == 0)
    def _():
        sum_ref[...] = product
        back_ref[...] = product_back

    @pl.when(turn > 0)
    def _():
        sum_ref[...] += product
        back_ref[...] += product_back

    @pl.when(turn == pl.num_programs(0) - 1)
    def _():
        for idx in range(count):
            span = slice(idx * slots, (idx + 1) * slots)
            results[idx][:, :width] = sum_ref[span, :].astype(bfloat)
            results[idx][:, width:] = back_ref[span, :].astype(bfloat)


def run_expert(weights, blocks, width):
    (inner, inner_spec), (outer, outer_spec), turns = weights
    count = len(blocks)
    slots = blocks[0].shape[0]
    total = count * slots
    whole = pl.BlockSpec((slots, 2 * width), lambda i: (0, 0))
    chunk = pl.BlockSpec((total, width), lambda i: (0, i))
    outs = pl.pallas_call(
        functools.partial(expert_kernel, count, slots, width, 256),
        grid=(turns,),
        in_specs=[inner_spec, outer_spec] + [whole] * count,
        out_specs=[whole] * count + [chunk, chunk],
        out_shape=[jax.ShapeDtypeStruct((slots, 2 * width), bfloat)] * count
        + [jax.ShapeDtypeStruct((total, turns * width), bfloat)] * 2,
        scratch_shapes=[
            pltpu.VMEM((total, width), bfloat),
            pltpu.VMEM((total, width), bfloat),
            pltpu.VMEM((total, width), float32),
            pltpu.VMEM((total, width), float32),
        ],
        compiler_params=params(),
        cost_estimate=pl.CostEstimate(
            flops=8 * total * width * width * turns,
            bytes_accessed=4 * width * width * turns,
            transcendentals=total * width * turns,
        ),
        name="run_expert",
    )(inner, outer, *blocks)
    return outs[:count], outs[count], outs[count + 1]


def expert_grad_kernel(batches, count, slots, width, second, *refs):
    groups = [refs[idx * count : (idx + 1) * count] for idx in range(batches)]
    wide = refs[batches * count : batches * count + batches]
    out_ref, rows_ref = refs[-2], refs[-1]
    half = slice(width, 2 * width) if second else slice(0, width)

    @pl.when(pl.program_id(0) == 0)
    def _():
        for batch in range(batches):
            for idx in range(count):
                start = (batch * count + idx) * slots
                rows_ref[start : start + slots, :] = groups[batch][idx][:, half]

    total = None
    span = count * slots
    for batch in range(batches):
        rows = rows_ref[batch * span : (batch + 1) * span, :]
        if second:
            term = dot_tn(wide[batch][...], rows)
        else:
            term = dot_tn(rows, wide[batch][...])
        total = term if total is None else total + term
    out_ref[...] = total.astype(bfloat).reshape(out_ref.shape)


def expert_grad(groups, wide, width, second, out_shape, out_spec, buffer=None):
    batches = len(groups)
    count = len(groups[0])
    slots = groups[0][0].shape[0]
    total = count * slots
    turns = wide[0].shape[1] // width
    kernel = functools.partial(expert_grad_kernel, batches, count, slots, width, second)
    in_specs = [pl.BlockSpec((slots, 2 * width), lambda i: (0, 0))] * (batches * count)
    in_specs = in_specs + [pl.BlockSpec((total, width), lambda i: (0, i))] * batches
    operands = [block for group in groups for block in group] + list(wide)
    aliases = {}
    body = kernel
    if buffer is not None:
        in_specs = [pl.BlockSpec(memory_space=pl.ANY)] + in_specs
        operands = [buffer] + operands
        aliases = {0: 0}

        def body(*refs):
            kernel(*refs[1:])

    return pl.pallas_call(
        body,
        grid=(turns,),
        in_specs=in_specs,
        out_specs=out_spec,
        out_shape=jax.ShapeDtypeStruct(out_shape, bfloat),
        scratch_shapes=[pltpu.VMEM((batches * total, width), bfloat)],
        input_output_aliases=aliases,
        compiler_params=params(),
        cost_estimate=pl.CostEstimate(
            flops=2 * batches * total * width * width * turns,
            bytes_accessed=4 * width * width * turns,
            transcendentals=0,
        ),
        name="expert_grad_outer" if second else "expert_grad_inner",
    )(*operands)


def on_device(
    hidden_in,
    out_grad,
    places,
    lengths,
    routes,
    norm1_gain,
    w_query,
    w_key,
    w_value,
    w_output,
    rel_table,
    norm2_gain,
    w_router,
    w_in,
    w_out,
):
    batches, rows_own, width = hidden_in.shape
    heads = rel_table.shape[1]
    head_dim = width // heads
    scale = head_dim ** (-0.5)
    shards = lax.axis_size("dp")
    members = lax.axis_size("expert")
    me = lax.axis_index("expert")
    experts = w_router.shape[1]
    hidden_width = w_in.shape[2]
    turns = hidden_width // width
    tiles = rows_own // tile
    rows_group = members * rows_own
    depth = width // shards
    depth_out = hidden_width // shards
    table_rows = rel_table.shape[0]
    capacity = max(2, rows_own * 17 // (experts * 16))
    slots = -(-capacity // 16) * 16
    per = tile // head_dim
    heads_own = per * (-(-heads // (per * members)))
    span = heads_own * head_dim
    split = width // span

    def around(step):
        return [(idx, (idx + step) % members) for idx in range(members)]

    def columns_own(weight):
        wide = jnp.pad(weight, ((0, 0), (0, members * span - width)))
        return lax.dynamic_slice_in_dim(wide, me * span, span, axis=1)

    def in_order(parts):
        return jnp.take(jnp.stack(parts), jnp.mod(me - jnp.arange(members), members), axis=0)

    hidden_from = [hidden_in] + [
        lax.ppermute(hidden_in, "expert", around(step)) for step in range(1, members)
    ]

    small = jnp.concatenate(
        [
            norm1_gain.reshape(-1),
            norm2_gain.reshape(-1),
            w_router.reshape(-1),
            rel_table.reshape(-1),
        ]
    )
    small_used = small.shape[0]
    small_pad = -(-small_used // (16 * span)) * 16
    small = jnp.pad(small, (0, small_pad * span - small_used)).reshape(small_pad, span)
    first_own = jnp.concatenate(
        [columns_own(w_query), columns_own(w_key), columns_own(w_value)]
        + [w_output[:, idx * span : (idx + 1) * span] for idx in range(split)]
        + [small],
        axis=0,
    )
    first = lax.all_gather(first_own, "dp", axis=0, tiled=False)
    inner_parts = [w_in[0, :, idx * width : (idx + 1) * width] for idx in range(turns)]
    second_own = jnp.concatenate(inner_parts + [w_out[0]], axis=0)
    second_own, _ = lax.optimization_barrier((second_own, first))
    second = lax.all_gather(second_own, "dp", axis=0, tiled=False)

    small_start = (3 + split) * depth
    small_all = first[:, small_start:].reshape(shards, small_pad * span)
    gain_one = small_all[:, :depth].reshape(1, width).astype(float32)
    gain_two = small_all[:, depth : 2 * depth].reshape(width).astype(float32)
    router_end = 2 * depth + depth * experts
    router_w = small_all[:, 2 * depth : router_end].reshape(width, experts)
    table = small_all[:, router_end:small_used].reshape(shards * table_rows, heads)
    output_w = jnp.concatenate(
        [
            first[:, (3 + idx) * depth : (4 + idx) * depth].reshape(width, span)
            for idx in range(split)
        ],
        axis=1,
    )
    output_wide = jnp.pad(output_w, ((0, members * span - width), (0, 0)))
    output_parts = [
        lax.dynamic_slice_in_dim(output_wide, jnp.mod(me - step, members) * span, span, axis=0)
        for step in range(members)
    ]

    direct = depth % 16 == 0 and turns * depth == depth_out and shards % turns == 0
    if direct:
        group = shards // turns
        packed = first[:, : 3 * depth]
        inner_spec = pl.BlockSpec((shards, depth, width), lambda i: (0, i, 0))
        outer_spec = pl.BlockSpec((group, depth_out, width), lambda i: (i, 1, 0))
        weights = ((second, inner_spec), (second, outer_spec), turns)
    else:
        packed = jnp.concatenate(
            [
                first[:, idx * depth : (idx + 1) * depth].reshape(1, width, span)
                for idx in range(3)
            ],
            axis=1,
        )
        inner_w = second[:, : turns * depth].reshape(shards, turns, depth, width)
        inner_w = jnp.transpose(inner_w, (1, 0, 2, 3)).reshape(turns, width, width)
        outer_w = second[:, turns * depth : turns * depth + depth_out].reshape(
            turns, width, width
        )
        plain = pl.BlockSpec((1, width, width), lambda i: (i, 0, 0))
        weights = ((inner_w, plain), (outer_w, plain), turns)
    query_w, key_w, value_w = (
        first[:, idx * depth : (idx + 1) * depth].reshape(width, span) for idx in range(3)
    )

    places_in = places[:, 0].reshape(batches, members, rows_own)
    offsets = places_in - members * jnp.arange(rows_own, dtype=jnp.int32)[None, None]
    offset_from = [
        jnp.take(offsets, jnp.mod(me - step, members), axis=1) for step in range(members)
    ]
    ends = jnp.cumsum(lengths[:, 0], axis=-1)[:, :-1]

    def of_member(ordered, batch, step):
        rows = ordered[:rows_own]
        for place in range(1, members):
            rows = jnp.where(
                (offset_from[step][batch] == place)[:, None],
                ordered[place * rows_own : (place + 1) * rows_own],
                rows,
            )
        return rows

    def by_place(parts, batch):
        ordered = []
        for place in range(members):
            rows = parts[0]
            for step in range(1, members):
                rows = jnp.where((offset_from[step][batch] == place)[:, None], parts[step], rows)
            ordered.append(rows)
        return jnp.concatenate(ordered, axis=0)

    chosen = routes[:, :, 0]
    picked = chosen[:, :, None] == jnp.arange(experts, dtype=jnp.int32)
    counts = picked.astype(jnp.int32)
    slot = jnp.sum((jnp.cumsum(counts, axis=1) - counts) * counts, axis=2)
    target = jnp.mod(chosen - me, members) * slots + slot
    dispatch = (
        jnp.arange(members * slots, dtype=jnp.int32)[None, :, None] == target[:, None, :]
    ).astype(bfloat)

    ordered_in = order_rows(hidden_from, jnp.stack(offset_from, axis=-1))
    flat_in = ordered_in.reshape(batches * rows_group, width)
    flat_normed, flat_q, flat_k, flat_v = project(flat_in, gain_one, packed, scale)
    queries = flat_q.reshape(batches, rows_group, span)
    keys = flat_k.reshape(batches, rows_group, span)
    values = flat_v.reshape(batches, rows_group, span)
    own_f = hidden_in.astype(float32)
    table_wide = jnp.pad(table, ((0, 0), (0, members * heads_own - heads)))
    table_own = lax.dynamic_slice_in_dim(table_wide, me * heads_own, heads_own, axis=1)
    bias = bias_tiles(table_own, members, tiles)
    table_f = table_own.astype(float32)
    far = jnp.stack([table_f[levels_all - 1], table_f[2 * levels_all - 1]])

    probs = []
    outs = []
    inverses = []
    attended = []
    resid_mid = []
    normed_two = []
    gate_all = []
    gate = []
    blocks = []
    for batch in range(batches):
        kept, joined, inverse = attend(
            queries[batch], keys[batch], values[batch], ends[batch], bias, far, head_dim, members
        )
        probs.append(kept)
        outs.append(joined)
        inverses.append(inverse)
        head_parts = [of_member(joined, batch, 0)]
        for step in range(1, members):
            head_parts.append(
                lax.ppermute(
                    of_member(joined, batch, members - step), "expert", around(step)
                )
            )
        attended.append(head_parts)
        mid = own_f[batch]
        for part, weight in zip(head_parts, output_parts):
            mid = mid + dot_nn(part, weight)
        normed = norm_rows(mid, gain_two).astype(bfloat)
        logits = dot_nn(normed, router_w)
        shifted = jnp.exp(logits - jnp.max(logits, axis=-1, keepdims=True))
        router_probs = shifted / jnp.sum(shifted, axis=-1, keepdims=True)
        gate_own = jnp.sum(jnp.where(picked[batch], router_probs, 0.0), axis=1, keepdims=True)
        grad_expert = (gate_own * out_grad[batch].astype(float32)).astype(bfloat)
        outgoing = dot_nn(
            dispatch[batch], jnp.concatenate([normed, grad_expert], axis=1)
        ).astype(bfloat)
        received = [outgoing[:slots]]
        for step in range(1, members):
            received.append(
                lax.ppermute(
                    outgoing[step * slots : (step + 1) * slots], "expert", around(step)
                )
            )
        resid_mid.append(mid)
        normed_two.append(normed)
        gate_all.append(router_probs)
        gate.append(gate_own)
        blocks.append(received)

    returned = []
    hidden = []
    grad_pre = []
    for batch in range(batches):
        results, hidden_rows, grad_rows = run_expert(weights, blocks[batch], width)
        hidden.append(hidden_rows)
        grad_pre.append(grad_rows)
        back = [results[0]]
        for step in range(1, members):
            back.append(lax.ppermute(results[step], "expert", around(-step)))
        returned.append(jnp.concatenate(back, axis=0))

    if direct:
        buffer_shape = (shards, turns * depth + depth_out, width)
        buffer = expert_grad(
            blocks,
            grad_pre,
            width,
            False,
            buffer_shape,
            pl.BlockSpec((shards, depth, width), lambda i: (0, i, 0)),
        )
        buffer = expert_grad(
            blocks,
            hidden,
            width,
            True,
            buffer_shape,
            pl.BlockSpec((group, depth_out, width), lambda i: (i, 1, 0)),
            buffer,
        )
    else:
        plain_shape = (turns, width, width)
        inner_g = expert_grad(blocks, grad_pre, width, False, plain_shape, plain)
        outer_g = expert_grad(blocks, hidden, width, True, plain_shape, plain)
        inner_g = jnp.transpose(inner_g.reshape(turns, shards, depth, width), (1, 0, 2, 3))
        buffer = jnp.concatenate(
            [
                inner_g.reshape(shards, turns * depth, width),
                outer_g.reshape(shards, depth_out, width),
            ],
            axis=1,
        )
    expert_sum = lax.psum_scatter(buffer, "dp", scatter_dimension=0, tiled=False)

    layer_rows = []
    grad_mid_rows = []
    grad_attn_rows = []
    grad_head_rows = []
    grad_gain_two = 0.0
    grad_router = 0.0
    router_f = router_w.astype(float32)
    for batch in range(batches):
        home = dot_tn(dispatch[batch], returned[batch])
        expert_back = home[:, :width]
        grad_output = out_grad[batch].astype(float32)
        layer_rows.append((resid_mid[batch] + gate[batch] * expert_back).astype(bfloat))
        grad_gate = jnp.sum(grad_output * expert_back, axis=1, keepdims=True)
        grad_logits = (grad_gate * gate[batch]) * (
            jnp.where(picked[batch], 1.0, 0.0) - gate_all[batch]
        )
        grad_normed = home[:, width:] + lax.dot_general(
            grad_logits, router_f, (((1,), (1,)), ((), ())), precision=precise
        )
        grad_router = grad_router + lax.dot_general(
            normed_two[batch].astype(float32),
            grad_logits,
            (((0,), (0,)), ((), ())),
            precision=precise,
        )
        grad_resid, gain_terms = norm_back(resid_mid[batch], gain_two, grad_normed)
        grad_gain_two = grad_gain_two + jnp.sum(gain_terms, axis=0)
        grad_mid = grad_output + grad_resid
        grad_mid_rows.append(grad_mid)
        grad_attn = grad_mid.astype(bfloat)
        grad_attn_rows.append(grad_attn)
        parts = [dot_nt(grad_attn, weight).astype(bfloat) for weight in output_parts]
        from_members = [parts[0]]
        for step in range(1, members):
            from_members.append(lax.ppermute(parts[members - step], "expert", around(step)))
        grad_head_rows.append(by_place(from_members, batch))

    input_rows = []
    grad_q_rows = []
    grad_k_rows = []
    grad_v_rows = []
    grad_gain_one = 0.0
    grad_bias = 0.0
    grad_far = 0.0
    for batch in range(batches):
        grad_q, grad_k, grad_v, bias_terms, far_terms = attend_back(
            probs[batch],
            grad_head_rows[batch],
            outs[batch],
            inverses[batch],
            queries[batch],
            keys[batch],
            values[batch],
            buffer,
            head_dim,
            members,
            bias.shape,
        )
        grad_q_rows.append(grad_q)
        grad_k_rows.append(grad_k)
        grad_v_rows.append(grad_v)
        grad_bias = grad_bias + bias_terms
        grad_far = grad_far + far_terms
        grad_ordered = dot_nt(grad_q, query_w) + dot_nt(grad_k, key_w) + dot_nt(grad_v, value_w)
        home_rows = of_member(grad_ordered, batch, 0)
        for step in range(1, members):
            sent = of_member(grad_ordered, batch, step).astype(bfloat)
            home_rows = home_rows + lax.ppermute(sent, "expert", around(-step)).astype(float32)
        grad_tokens, _ = norm_back(own_f[batch], gain_one, home_rows)
        input_rows.append(grad_mid_rows[batch] + grad_tokens)
        rows = slice(batch * rows_group, (batch + 1) * rows_group)
        _, terms = norm_back(flat_in[rows].astype(float32), gain_one, grad_ordered)
        grad_gain_one = grad_gain_one + jnp.sum(terms, axis=0)

    def flat(rows):
        return jnp.concatenate(rows, axis=0)

    grad_out_parts = [
        dot_tn(flat([parts[step] for parts in attended]), flat(grad_attn_rows)).astype(bfloat)
        for step in range(members)
    ]
    grad_wo = in_order(grad_out_parts).reshape(members * span, width)[:width]
    grad_wq = dot_tn(flat_normed, flat(grad_q_rows))
    grad_wk = dot_tn(flat_normed, flat(grad_k_rows))
    grad_wv = dot_tn(flat_normed, flat(grad_v_rows))

    steps = 2 * members - 1
    reach = near_shift(tiles)
    shape = (steps, tile, (2 * reach + 1) * tile)
    delta = (
        members
        * (
            lax.broadcasted_iota(jnp.int32, shape, 2)
            - reach * tile
            - lax.broadcasted_iota(jnp.int32, shape, 1)
        )
        + lax.broadcasted_iota(jnp.int32, shape, 0)
        - (members - 1)
    )
    buckets = shards * table_rows
    onehot = (
        bucket_of(delta)[None] == jnp.arange(buckets, dtype=jnp.int32)[:, None, None, None]
    ).astype(bfloat)
    grad_table = jnp.einsum(
        "hsab,ksab->kh", grad_bias.astype(bfloat), onehot, preferred_element_type=float32
    )
    far_sum = jnp.sum(grad_far, axis=(2, 3))
    grad_table = grad_table.at[levels_all - 1].add(far_sum[:, 0])
    grad_table = grad_table.at[2 * levels_all - 1].add(far_sum[:, 1])
    grad_table = lax.dynamic_update_slice_in_dim(
        jnp.zeros((buckets, members * heads_own), float32), grad_table, me * heads_own, axis=1
    )[:, :heads]

    small_grad = jnp.concatenate(
        [
            grad_gain_one.reshape(shards, depth),
            grad_gain_two.reshape(shards, depth),
            grad_router.reshape(shards, depth * experts),
            grad_table.reshape(shards, table_rows * heads),
        ],
        axis=1,
    )
    small_grad = jnp.pad(small_grad, ((0, 0), (0, small_pad * span - small_used)))
    dense = jnp.concatenate(
        [
            grad_wq.astype(bfloat).reshape(shards, depth, span),
            grad_wk.astype(bfloat).reshape(shards, depth, span),
            grad_wv.astype(bfloat).reshape(shards, depth, span),
        ]
        + [
            grad_wo[:, idx * span : (idx + 1) * span].reshape(shards, depth, span)
            for idx in range(split)
        ]
        + [small_grad.astype(bfloat).reshape(shards, small_pad, span)],
        axis=1,
    )

    line = shards // 4
    my_shard = lax.axis_index("dp")
    rows_dense = dense.shape[1]
    dense = dense.reshape(line, 2, 2, rows_dense, span)
    odd = my_shard % 2 == 1
    sent = jnp.where(odd, dense[:, :, 0], dense[:, :, 1])
    held = jnp.where(odd, dense[:, :, 1], dense[:, :, 0])
    got = lax.ppermute(sent, "dp", [(idx, idx ^ 1) for idx in range(shards)])
    dense = (held.astype(float32) + got.astype(float32)).astype(bfloat)
    odd = (my_shard // 2) % 2 == 1
    sent = jnp.where(odd, dense[:, 0], dense[:, 1])
    held = jnp.where(odd, dense[:, 1], dense[:, 0])
    got = lax.ppermute(sent, "dp", [(idx, idx ^ 2) for idx in range(shards)])
    dense = add_after(held, got, expert_sum)
    dense_part = lax.psum_scatter(
        dense,
        "dp",
        scatter_dimension=0,
        tiled=False,
        axis_index_groups=[[rest + 4 * idx for idx in range(line)] for rest in range(4)],
    )
    parts = [dense_part] + [
        lax.ppermute(dense_part, "expert", around(step)) for step in range(1, members)
    ]
    qkv_parts = in_order([part[: 3 * depth] for part in parts]).astype(float32)
    qkv_grads = [
        jnp.concatenate(
            [qkv_parts[idx, kind * depth : (kind + 1) * depth] for idx in range(members)], axis=1
        )[:, :width]
        for kind in range(3)
    ]
    rest_sum = sum(part[3 * depth :].astype(float32) for part in parts)
    out_grad_sum = jnp.concatenate(
        [rest_sum[idx * depth : (idx + 1) * depth] for idx in range(split)], axis=1
    )
    small_sum = rest_sum[split * depth :].reshape(-1)

    expert_f = expert_sum.astype(float32)
    inner_sum = jnp.concatenate(
        [expert_f[idx * depth : (idx + 1) * depth] for idx in range(turns)], axis=1
    )[None]
    outer_sum = expert_f[turns * depth :][None]
    return (
        jnp.stack(layer_rows),
        jnp.stack(input_rows),
        small_sum[:depth],
        qkv_grads[0],
        qkv_grads[1],
        qkv_grads[2],
        out_grad_sum,
        small_sum[router_end:small_used].reshape(table_rows, heads),
        small_sum[depth : 2 * depth],
        small_sum[2 * depth : router_end].reshape(depth, experts),
        inner_sum,
        outer_sum,
    )


def solution(mesh):
    return jax.shard_map(
        on_device,
        mesh=mesh,
        in_specs=(
            P(None, ("dp", "expert"), None),
            P(None, ("dp", "expert"), None),
            P(None, "dp", None),
            P(None, "dp", None),
            P(None, ("dp", "expert"), None),
            P("dp"),
            P("dp", None),
            P("dp", None),
            P("dp", None),
            P("dp", None),
            P("dp", None),
            P("dp"),
            P("dp", None),
            P("expert", "dp", None),
            P("expert", "dp", None),
        ),
        out_specs=(
            P(None, ("dp", "expert"), None),
            P(None, ("dp", "expert"), None),
            P("dp"),
            P("dp", None),
            P("dp", None),
            P("dp", None),
            P("dp", None),
            P("dp", None),
            P("dp"),
            P("dp", None),
            P("expert", "dp", None),
            P("expert", "dp", None),
        ),
        check_vma=False,
    )
```

```python
import functools

import jax
import jax.numpy as jnp
from jax import lax
from jax.experimental import pallas as pl
from jax.experimental.pallas import tpu as pltpu
from jax.sharding import PartitionSpec as P

bucket_edges = (1, 2, 3, 4, 5, 6, 7, 8, 12, 16, 23, 32, 46, 64, 91)
levels_all = len(bucket_edges) + 1
epsilon = 1e-06
masked_score = -1000000000.0
precise = lax.Precision.HIGHEST
float32 = jnp.float32
bfloat = jnp.bfloat16
tile = 128
vmem_bytes = 56 * 1024 * 1024


def params():
    return pltpu.CompilerParams(vmem_limit_bytes=vmem_bytes)


def dot_nn(left, right):
    return lax.dot_general(left, right, (((1,), (0,)), ((), ())), preferred_element_type=float32)


def dot_nt(left, right):
    return lax.dot_general(left, right, (((1,), (1,)), ((), ())), preferred_element_type=float32)


def dot_tn(left, right):
    return lax.dot_general(left, right, (((0,), (0,)), ((), ())), preferred_element_type=float32)


def norm_rows(rows, gain):
    mean_square = jnp.mean(rows * rows, axis=-1, keepdims=True)
    return rows * lax.rsqrt(mean_square + epsilon) * gain


def norm_back(rows, gain, grad):
    scale = lax.rsqrt(jnp.mean(rows * rows, axis=-1, keepdims=True) + epsilon)
    unit = rows * scale
    weighted = grad * gain
    inner = jnp.mean(weighted * unit, axis=-1, keepdims=True)
    return scale * (weighted - unit * inner), grad * unit


def bucket_of(offset):
    distance = jnp.abs(offset)
    levels = jnp.zeros(offset.shape, jnp.int32)
    for edge_value in bucket_edges:
        levels = levels + (distance >= edge_value).astype(jnp.int32)
    return levels + levels_all * (offset > 0).astype(jnp.int32)


def near_shift(tiles):
    return min(1, tiles - 1)


def bias_kernel(stride, reach, table_ref, out_ref):
    row = lax.broadcasted_iota(jnp.int32, (tile, tile), 0)
    lane = lax.broadcasted_iota(jnp.int32, (tile, tile), 1)
    heads = out_ref.shape[0]
    for shift in range(-reach, reach + 1):
        for step in range(2 * stride - 1):
            ids = bucket_of(stride * (tile * shift + lane - row) + step - (stride - 1))
            columns = slice((shift + reach) * tile, (shift + reach + 1) * tile)
            for head in range(heads):
                values = jnp.broadcast_to(table_ref[head : head + 1, :], (tile, tile))
                out_ref[head, step, :, columns] = jnp.take_along_axis(values, ids, axis=1)


def bias_tiles(table, stride, tiles):
    heads = table.shape[1]
    reach = near_shift(tiles)
    lanes = jnp.pad(table.astype(float32).T, ((0, 0), (0, tile - table.shape[0])))
    return pl.pallas_call(
        functools.partial(bias_kernel, stride, reach),
        out_shape=jax.ShapeDtypeStruct(
            (heads, 2 * stride - 1, tile, (2 * reach + 1) * tile), float32
        ),
        compiler_params=params(),
        name="bias_tiles",
    )(lanes)


def project_kernel(pairs, scale, rows_ref, gain_ref, weight_ref, normed_ref, out_ref):
    width = rows_ref.shape[2]
    depth = weight_ref.shape[1] // pairs
    lanes = weight_ref.shape[2]
    normed = norm_rows(rows_ref[0].astype(float32), gain_ref[...]).astype(bfloat)
    normed_ref[...] = normed
    for pair in range(pairs):
        weight = weight_ref[:, pair * depth : (pair + 1) * depth, :].reshape(width, lanes)
        product = dot_nn(normed, weight).astype(bfloat)
        start = pair * lanes
        out_ref[:, start : start + tile] = product[:, :tile] * bfloat(scale)
        out_ref[:, start + tile : start + lanes] = product[:, tile:]


def project(batch, rows, gain, packed, pairs, scale):
    _, count, width = rows.shape
    lanes = packed.shape[2]
    weight_shape = (packed.shape[0], pairs * width // packed.shape[0], lanes)
    step = min(512, count)
    return pl.pallas_call(
        functools.partial(project_kernel, pairs, scale),
        grid=(count // step,),
        in_specs=[
            pl.BlockSpec((1, step, width), lambda i: (batch, i, 0)),
            pl.BlockSpec((1, width), lambda i: (0, 0)),
            pl.BlockSpec(weight_shape, lambda i: (0, 0, 0)),
        ],
        out_specs=[
            pl.BlockSpec((step, width), lambda i: (i, 0)),
            pl.BlockSpec((step, pairs * lanes), lambda i: (i, 0)),
        ],
        out_shape=[
            jax.ShapeDtypeStruct((count, width), bfloat),
            jax.ShapeDtypeStruct((count, pairs * lanes), bfloat),
        ],
        compiler_params=params(),
        cost_estimate=pl.CostEstimate(
            flops=2 * count * width * lanes * pairs,
            bytes_accessed=6 * count * width,
            transcendentals=0,
        ),
        name="project",
    )(rows, gain, packed)


def count_earlier(picked, first_axis):
    size = picked.shape[1 - first_axis]
    row = lax.broadcasted_iota(jnp.int32, (size, size), 0)
    column = lax.broadcasted_iota(jnp.int32, (size, size), 1)
    if first_axis == 0:
        return dot_nn(picked, (row < column).astype(float32).astype(bfloat))
    return dot_nn((column < row).astype(float32).astype(bfloat), picked)


def tables_kernel(
    members,
    slots,
    me_ref,
    row_ref,
    column_ref,
    place_ref,
    after_ref,
    carried_ref,
    send_ref,
    back_ref,
    offset_ref,
    handed_ref,
):
    me = me_ref[0]
    batches, rows = column_ref.shape[0], column_ref.shape[1]
    names = 128
    for batch in range(batches):
        route = row_ref[batch]
        picked = lax.broadcasted_iota(jnp.int32, (names, rows), 0) == route
        earlier = count_earlier(picked.astype(float32).astype(bfloat), 0)
        slot = jnp.sum(jnp.where(picked, earlier, 0.0), axis=0, keepdims=True).astype(jnp.int32)
        target = jnp.where(route >= me, route - me, route - me + members) * slots + slot
        index = lax.broadcasted_iota(jnp.int32, (members * slots, rows), 0)
        send_ref[batch] = (index == target).astype(float32).astype(bfloat)

        route = column_ref[batch]
        picked = lax.broadcasted_iota(jnp.int32, (rows, names), 1) == route
        earlier = count_earlier(picked.astype(float32).astype(bfloat), 1)
        slot = jnp.sum(jnp.where(picked, earlier, 0.0), axis=1, keepdims=True).astype(jnp.int32)
        target = jnp.where(route >= me, route - me, route - me + members) * slots + slot
        index = lax.broadcasted_iota(jnp.int32, (rows, members * slots), 1)
        back_ref[batch] = (index == target).astype(float32).astype(bfloat)

        offsets = place_ref[batch] - members * lax.broadcasted_iota(
            jnp.int32, (rows, members), 0
        )
        lane = lax.broadcasted_iota(jnp.int32, (rows, members), 1)
        for step in range(members):
            owner = jnp.where(me >= step, me - step, me - step + members)
            chosen = jnp.sum(jnp.where(lane == owner, offsets, 0), axis=1, keepdims=True)
            offset_ref[batch, :, step : step + 1] = chosen


def row_tables(me, routes, places, after, carried, members, slots):
    batches, rows, _ = routes.shape
    vmem = pl.BlockSpec(memory_space=pltpu.VMEM)
    return pl.pallas_call(
        functools.partial(tables_kernel, members, slots),
        in_specs=[pl.BlockSpec(memory_space=pltpu.SMEM), vmem, vmem, vmem]
        + [pl.BlockSpec(memory_space=pl.ANY)] * 2,
        out_specs=[vmem, vmem, vmem, pl.BlockSpec(memory_space=pl.ANY)],
        out_shape=[
            jax.ShapeDtypeStruct((batches, members * slots, rows), bfloat),
            jax.ShapeDtypeStruct((batches, rows, members * slots), bfloat),
            jax.ShapeDtypeStruct((batches, rows, members), jnp.int32),
            jax.ShapeDtypeStruct(carried.shape, carried.dtype),
        ],
        input_output_aliases={5: 3},
        compiler_params=params(),
        name="row_tables",
    )(
        me,
        routes.reshape(batches, 1, rows),
        routes,
        jnp.transpose(places, (0, 2, 1)),
        after,
        carried,
    )


def member_rows(ordered, offset_ref, step, members):
    count = ordered.shape[0] // members
    rows = ordered[:count]
    for place in range(1, members):
        rows = jnp.where(
            offset_ref[0, :, step : step + 1] == place,
            ordered[place * count : (place + 1) * count],
            rows,
        )
    return rows


def middle_kernel(
    members,
    experts,
    me_ref,
    joined_ref,
    offset_ref,
    weight_ref,
    rows_ref,
    grad_ref,
    gain_ref,
    router_ref,
    route_ref,
    send_ref,
    after_ref,
    *refs,
):
    received = refs[: members - 1]
    mid_ref, normed_ref, probs_ref = refs[members - 1 : members + 2]
    out_refs = refs[members + 2 :]
    me = me_ref[0]
    span = joined_ref.shape[1]
    width = rows_ref.shape[2]
    slots = out_refs[0].shape[0]
    mid = rows_ref[0].astype(float32)
    for step in range(members):
        owner = jnp.where(me >= step, me - step, me - step + members)
        part = (
            member_rows(joined_ref[...], offset_ref, 0, members)
            if step == 0
            else received[step - 1][...]
        )
        mid = mid + dot_nn(part, weight_ref[pl.ds(pl.multiple_of(owner * span, span), span), :])
    mid_ref[...] = mid
    normed = norm_rows(mid, gain_ref[...]).astype(bfloat)
    normed_ref[...] = normed
    logits = dot_nn(normed, router_ref[...])
    lane = lax.broadcasted_iota(jnp.int32, logits.shape, 1)
    logits = jnp.where(lane < experts, logits, -jnp.inf)
    shifted = jnp.exp(logits - jnp.max(logits, axis=-1, keepdims=True))
    probs = shifted / jnp.sum(shifted, axis=-1, keepdims=True)
    probs_ref[...] = probs
    gate = jnp.sum(jnp.where(lane == route_ref[0], probs, 0.0), axis=1, keepdims=True)
    grad_expert = (gate * grad_ref[0].astype(float32)).astype(bfloat)
    tokens = dot_nn(send_ref[0], normed).astype(bfloat)
    grads = dot_nn(send_ref[0], grad_expert).astype(bfloat)
    for step in range(members):
        rows = slice(step * slots, (step + 1) * slots)
        out_refs[step][:, :width] = tokens[rows]
        out_refs[step][:, width:] = grads[rows]


def middle(
    batch, me, joined, received, offsets, weight, rows, grads, gain, router, routes, send, after
):
    members = offsets.shape[2]
    experts = members
    _, count, width = rows.shape
    slots = send.shape[1] // members
    row_spec = pl.BlockSpec((1, count, width), lambda i: (batch, 0, 0))

    def full(array):
        return pl.BlockSpec(array.shape, lambda i: (0,) * array.ndim)

    def own(array):
        return pl.BlockSpec((1,) + array.shape[1:], lambda i: (batch, 0, 0))

    out_shape = [
        jax.ShapeDtypeStruct((count, width), float32),
        jax.ShapeDtypeStruct((count, width), bfloat),
        jax.ShapeDtypeStruct((count, tile), float32),
    ] + [jax.ShapeDtypeStruct((slots, 2 * width), bfloat)] * members
    outs = pl.pallas_call(
        functools.partial(middle_kernel, members, experts),
        grid=(1,),
        in_specs=[
            pl.BlockSpec(memory_space=pltpu.SMEM),
            full(joined),
            own(offsets),
            full(weight),
            row_spec,
            row_spec,
            full(gain),
            full(router),
            own(routes),
            own(send),
            pl.BlockSpec(memory_space=pl.ANY),
        ]
        + [full(part) for part in received],
        out_specs=[full(shape) for shape in out_shape],
        out_shape=out_shape,
        compiler_params=params(),
        cost_estimate=pl.CostEstimate(
            flops=6 * count * width * width, bytes_accessed=12 * count * width, transcendentals=0
        ),
        name="middle",
    )(me, joined, offsets, weight, rows, grads, gain, router, routes, send, after, *received)
    return outs[0], outs[1], outs[2], list(outs[3:])


def second_kernel(
    members,
    experts,
    aliased,
    me_ref,
    back_ref,
    mid_ref,
    normed_ref,
    probs_ref,
    grad_ref,
    route_ref,
    gain_ref,
    router_ref,
    weight_ref,
    *refs,
):
    returned = refs[:members]
    outs = refs[members + aliased :]
    layer_ref, grad_mid_ref, grad_attn_ref, gain_out_ref, router_out_ref = outs[:5]
    part_refs = outs[5:]
    me = me_ref[0]
    width = mid_ref.shape[1]
    span = part_refs[0].shape[1]
    blocks = jnp.concatenate([ref[...] for ref in returned], axis=0)
    home = dot_nn(back_ref[0], blocks)
    expert_back = home[:, :width]
    mid = mid_ref[...]
    gain = gain_ref[...]
    grads = grad_ref[0].astype(float32)
    probs = probs_ref[...]
    lane = lax.broadcasted_iota(jnp.int32, probs.shape, 1)
    picked = lane == route_ref[0]
    gate = jnp.sum(jnp.where(picked, probs, 0.0), axis=1, keepdims=True)
    layer_ref[0] = (mid + gate * expert_back).astype(bfloat)
    grad_gate = jnp.sum(grads * expert_back, axis=1, keepdims=True)
    grad_logits = (grad_gate * gate) * (jnp.where(picked, 1.0, 0.0) - probs)
    grad_logits = jnp.where(lane < experts, grad_logits, 0.0)
    grad_normed = home[:, width:]
    for name in range(experts):
        grad_normed = grad_normed + grad_logits[:, name : name + 1] * router_ref[name : name + 1, :]
    upper = grad_logits.astype(bfloat)
    lower = (grad_logits - upper.astype(float32)).astype(bfloat)
    normed = normed_ref[...]
    router_out_ref[...] = dot_tn(upper, normed) + dot_tn(lower, normed)
    grad_resid, terms = norm_back(mid, gain, grad_normed)
    gain_out_ref[...] = jnp.sum(terms, axis=0, keepdims=True)
    grad_mid = grads + grad_resid
    grad_mid_ref[...] = grad_mid
    grad_attn = grad_mid.astype(bfloat)
    grad_attn_ref[...] = grad_attn
    for step in range(members):
        owner = jnp.where(me >= step, me - step, me - step + members)
        rows = weight_ref[pl.ds(pl.multiple_of(owner * span, span), span), :]
        part_refs[step][...] = dot_nt(grad_attn, rows).astype(bfloat)


def second_back(
    batch,
    batches,
    me,
    returned,
    back,
    mid,
    normed,
    probs,
    grads,
    routes,
    gain,
    router,
    weight,
    members,
    span,
    layer,
):
    count, width = mid.shape
    grad_spec = pl.BlockSpec((1, count, width), lambda i: (batch, 0, 0))

    def full(array):
        return pl.BlockSpec(array.shape, lambda i: (0,) * array.ndim)

    def own(array):
        return pl.BlockSpec((1,) + array.shape[1:], lambda i: (batch, 0, 0))

    rest = [
        jax.ShapeDtypeStruct((count, width), float32),
        jax.ShapeDtypeStruct((count, width), bfloat),
        jax.ShapeDtypeStruct((1, width), float32),
        jax.ShapeDtypeStruct((tile, width), float32),
    ] + [jax.ShapeDtypeStruct((count, span), bfloat)] * members
    aliased = 0 if layer is None else 1
    outs = pl.pallas_call(
        functools.partial(second_kernel, members, members, aliased),
        grid=(1,),
        in_specs=[
            pl.BlockSpec(memory_space=pltpu.SMEM),
            own(back),
            full(mid),
            full(normed),
            full(probs),
            grad_spec,
            own(routes),
            full(gain),
            full(router),
            full(weight),
        ]
        + [full(part) for part in returned]
        + [pl.BlockSpec(memory_space=pl.ANY)] * aliased,
        out_specs=[grad_spec] + [full(shape) for shape in rest],
        out_shape=[jax.ShapeDtypeStruct((batches, count, width), bfloat)] + rest,
        input_output_aliases={10 + members: 0} if aliased else {},
        compiler_params=params(),
        cost_estimate=pl.CostEstimate(
            flops=6 * count * width * width, bytes_accessed=12 * count * width, transcendentals=0
        ),
        name="second_back",
    )(
        me,
        back,
        mid,
        normed,
        probs,
        grads,
        routes,
        gain,
        router,
        weight,
        *returned,
        *([] if layer is None else [layer]),
    )
    return outs[0], outs[1], outs[2], outs[3], outs[4], list(outs[5:])


def first_kernel(
    members, pairs, grads_ref, weight_ref, rows_ref, gain_ref, offset_ref, gain_out_ref, *out_refs
):
    width = rows_ref.shape[2]
    depth = weight_ref.shape[1] // pairs
    lanes = weight_ref.shape[2]
    total = None
    for pair in range(pairs):
        weight = weight_ref[:, pair * depth : (pair + 1) * depth, :].reshape(width, lanes)
        term = dot_nt(grads_ref[:, pair * lanes : (pair + 1) * lanes], weight)
        total = term if total is None else total + term
    rows = rows_ref[0].astype(float32)
    scale = lax.rsqrt(jnp.mean(rows * rows, axis=-1, keepdims=True) + epsilon)
    gain_out_ref[...] = jnp.sum(total * rows * scale, axis=0, keepdims=True)
    for step in range(members):
        out_refs[step][...] = member_rows(total, offset_ref, step, members).astype(
            out_refs[step].dtype
        )


def first_back(batch, grads, packed, pairs, rows, gain, offsets):
    members = offsets.shape[2]
    _, count, width = rows.shape
    lanes = packed.shape[2]
    weight_shape = (packed.shape[0], pairs * width // packed.shape[0], lanes)
    own = jax.ShapeDtypeStruct((count // members, width), float32)
    sent = jax.ShapeDtypeStruct((count // members, width), bfloat)
    out_shape = [jax.ShapeDtypeStruct((1, width), float32), own] + [sent] * (members - 1)

    def full(array):
        return pl.BlockSpec(array.shape, lambda i: (0,) * len(array.shape))

    outs = pl.pallas_call(
        functools.partial(first_kernel, members, pairs),
        grid=(1,),
        in_specs=[
            full(grads),
            pl.BlockSpec(weight_shape, lambda i: (0, 0, 0)),
            pl.BlockSpec((1, count, width), lambda i: (batch, 0, 0)),
            full(gain),
            pl.BlockSpec((1,) + offsets.shape[1:], lambda i: (batch, 0, 0)),
        ],
        out_specs=[full(shape) for shape in out_shape],
        out_shape=out_shape,
        compiler_params=params(),
        cost_estimate=pl.CostEstimate(
            flops=2 * count * width * lanes * pairs,
            bytes_accessed=8 * count * width,
            transcendentals=0,
        ),
        name="first_back",
    )(grads, packed, rows, gain, offsets)
    return outs[0], outs[1], list(outs[2:])


def finish_kernel(received, own_ref, rows_ref, gain_ref, mid_ref, *refs):
    total = own_ref[...]
    for ref in refs[:received]:
        total = total + ref[...].astype(float32)
    grad, _ = norm_back(rows_ref[0].astype(float32), gain_ref[...], total)
    refs[-1][0] = mid_ref[...] + grad


def finish(batch, own, received, rows, gain, mid, buffer):
    batches, count, width = rows.shape
    row_spec = pl.BlockSpec((1, count, width), lambda i: (batch, 0, 0))

    def full(array):
        return pl.BlockSpec(array.shape, lambda i: (0,) * array.ndim)

    operands = [own, rows, gain, mid] + received
    in_specs = [full(own), row_spec, full(gain), full(mid)] + [full(part) for part in received]
    aliases = {}
    if buffer is not None:
        aliases = {len(operands): 0}
        operands.append(buffer)
        in_specs.append(pl.BlockSpec(memory_space=pl.ANY))
    return pl.pallas_call(
        functools.partial(finish_kernel, len(received)),
        grid=(1,),
        in_specs=in_specs,
        out_specs=row_spec,
        out_shape=jax.ShapeDtypeStruct((batches, count, width), float32),
        input_output_aliases=aliases,
        compiler_params=params(),
        name="finish",
    )(*operands)


def dense_kernel(batches, *refs):
    out_ref = refs[-1]
    total = None
    for batch in range(batches):
        term = dot_tn(refs[batch][...], refs[batches + batch][...])
        total = term if total is None else total + term
    out_ref[...] = total.astype(bfloat).reshape(out_ref.shape)


def dense_grad(left, right, lanes, shards, direct):
    batches = len(left)
    count, width = left[0].shape
    blocks = right[0].shape[1] // lanes
    depth = width // shards
    if direct:
        out_shape = (shards, blocks * depth, lanes)
        out_spec = pl.BlockSpec((shards, depth, lanes), lambda i: (0, i, 0))
    else:
        out_shape = (blocks, width, lanes)
        out_spec = pl.BlockSpec((1, width, lanes), lambda i: (i, 0, 0))
    out = pl.pallas_call(
        functools.partial(dense_kernel, batches),
        grid=(blocks,),
        in_specs=[pl.BlockSpec((count, width), lambda i: (0, 0))] * batches
        + [pl.BlockSpec((count, lanes), lambda i: (0, i))] * batches,
        out_specs=out_spec,
        out_shape=jax.ShapeDtypeStruct(out_shape, bfloat),
        compiler_params=params(),
        cost_estimate=pl.CostEstimate(
            flops=2 * batches * count * width * lanes * blocks,
            bytes_accessed=2 * batches * count * width,
            transcendentals=0,
        ),
        name="dense_grad",
    )(*left, *right)
    if not direct:
        out = jnp.transpose(out.reshape(blocks, shards, depth, lanes), (1, 0, 2, 3))
        out = out.reshape(shards, blocks * depth, lanes)
    return out


def segment_of(positions, ends):
    segment = jnp.zeros(positions.shape, jnp.int32)
    for end in ends:
        segment = segment + (positions >= end).astype(jnp.int32)
    return segment


def masked_heads(rows, lane, per, head_dim):
    parts = []
    for sub in range(per):
        inside = (lane >= sub * head_dim) & (lane < (sub + 1) * head_dim)
        parts.append(jnp.where(inside, rows, jnp.zeros_like(rows)))
    return jnp.concatenate(parts, axis=0)


def joined_heads(rows, lane, per, head_dim):
    joined = rows[:tile]
    for sub in range(1, per):
        inside = (lane >= sub * head_dim) & (lane < (sub + 1) * head_dim)
        joined = jnp.where(inside, rows[sub * tile : (sub + 1) * tile], joined)
    return joined


def attend_kernel(
    stride,
    head_dim,
    far_ref,
    ends_ref,
    q_ref,
    k_ref,
    v_ref,
    bias_ref,
    after_ref,
    probs_ref,
    out_ref,
    inv_ref,
):
    pair = pl.program_id(0)
    rows_all = q_ref.shape[0]
    rows_part = rows_all // stride
    tiles = rows_part // tile
    reach = near_shift(tiles)
    per = tile // head_dim
    lane = lax.broadcasted_iota(jnp.int32, (tile, tile), 1)
    ends = [ends_ref[idx] for idx in range(ends_ref.shape[0])]
    keys_t = k_ref[...].T
    lane_row = lax.broadcasted_iota(jnp.int32, (1, tile), 1)
    row_column = lax.broadcasted_iota(jnp.int32, (tile, 1), 0)
    key_segments = [
        segment_of(stride * (col * tile + lane_row) + part, ends)
        for part in range(stride)
        for col in range(tiles)
    ]
    for mine in range(stride):
        for block in range(tiles):
            begin = mine * rows_part + block * tile
            rows = slice(begin, begin + tile)
            segment = segment_of(stride * (block * tile + row_column) + mine, ends)
            raw = dot_nn(masked_heads(q_ref[rows, :], lane, per, head_dim), keys_t)
            stacked = []
            inverses = []
            for sub in range(per):
                head = pair * per + sub
                pieces = []
                top = None
                for part in range(stride):
                    for col in range(tiles):
                        start = (part * tiles + col) * tile
                        piece = raw[sub * tile : (sub + 1) * tile, start : start + tile]
                        shift = col - block
                        if shift < -reach:
                            piece = piece + far_ref[0, head]
                        elif shift > reach:
                            piece = piece + far_ref[1, head]
                        else:
                            columns = slice((shift + reach) * tile, (shift + reach + 1) * tile)
                            piece = piece + bias_ref[sub, part - mine + stride - 1, :, columns]
                        same = key_segments[part * tiles + col] == segment
                        piece = jnp.where(same, piece, masked_score)
                        pieces.append(piece)
                        top = piece if top is None else jnp.maximum(top, piece)
                row_max = jnp.max(top, axis=-1, keepdims=True)
                total = None
                for idx, piece in enumerate(pieces):
                    piece = jnp.exp(piece - row_max)
                    total = piece if total is None else total + piece
                    pieces[idx] = piece.astype(bfloat)
                kept = jnp.concatenate(pieces, axis=1)
                probs_ref[sub, rows, :] = kept
                stacked.append(kept)
                inverses.append(1.0 / jnp.sum(total, axis=-1, keepdims=True))
            result = dot_nn(jnp.concatenate(stacked, axis=0), v_ref[...])
            inverse = jnp.broadcast_to(inverses[0], (tile, tile))
            for sub in range(1, per):
                inside = (lane >= sub * head_dim) & (lane < (sub + 1) * head_dim)
                inverse = jnp.where(inside, inverses[sub], inverse)
            out_ref[rows, :] = (joined_heads(result, lane, per, head_dim) * inverse).astype(bfloat)
            inv_ref[rows, :] = inverse


def kind_specs(rows_all):
    return [
        pl.BlockSpec((rows_all, tile), lambda i, kind=kind: (0, 3 * i + kind)) for kind in range(3)
    ]


def attend(qkv, ends, bias, far, after, head_dim, stride):
    rows_all, span = qkv.shape[0], qkv.shape[1] // 3
    per = tile // head_dim
    heads = span // head_dim
    row_spec = pl.BlockSpec((rows_all, tile), lambda i: (0, i))
    return pl.pallas_call(
        functools.partial(attend_kernel, stride, head_dim),
        grid=(span // tile,),
        in_specs=[
            pl.BlockSpec(memory_space=pltpu.SMEM),
            pl.BlockSpec(memory_space=pltpu.SMEM),
            *kind_specs(rows_all),
            pl.BlockSpec((per,) + bias.shape[1:], lambda i: (i, 0, 0, 0)),
            pl.BlockSpec(memory_space=pl.ANY),
        ],
        out_specs=[
            pl.BlockSpec((per, rows_all, rows_all), lambda i: (i, 0, 0)),
            row_spec,
            row_spec,
        ],
        out_shape=[
            jax.ShapeDtypeStruct((heads, rows_all, rows_all), bfloat),
            jax.ShapeDtypeStruct((rows_all, span), bfloat),
            jax.ShapeDtypeStruct((rows_all, span), float32),
        ],
        compiler_params=params(),
        cost_estimate=pl.CostEstimate(
            flops=16 * rows_all * rows_all * span,
            bytes_accessed=2 * heads * rows_all * rows_all,
            transcendentals=heads * rows_all * rows_all,
        ),
        name="attend",
    )(far, ends, qkv, qkv, qkv, bias, after)


def attend_back_kernel(
    stride,
    head_dim,
    scale,
    probs_ref,
    grad_ref,
    out_ref,
    inv_ref,
    q_ref,
    k_ref,
    v_ref,
    after_ref,
    dqkv_ref,
    dbias_ref,
    dfar_ref,
    ds_ref,
    grads_ref,
):
    rows_all = q_ref.shape[0]
    rows_part = rows_all // stride
    tiles = rows_part // tile
    reach = near_shift(tiles)
    per = tile // head_dim
    lane = lax.broadcasted_iota(jnp.int32, (tile, tile), 1)
    queries_t = q_ref[...].T
    values_t = v_ref[...].T
    grads_ref[...] = (grad_ref[...].astype(float32) * inv_ref[...]).astype(bfloat)
    grads_t = grads_ref[...].T
    dbias_ref[...] = jnp.zeros_like(dbias_ref)
    dfar_ref[...] = jnp.zeros_like(dfar_ref)
    for mine in range(stride):
        for block in range(tiles):
            begin = mine * rows_part + block * tile
            rows = slice(begin, begin + tile)
            own = masked_heads(grads_ref[rows, :], lane, per, head_dim)
            outs = out_ref[rows, :].astype(float32)
            raw = dot_nn(own, values_t)
            stacked = []
            for sub in range(per):
                span = slice(sub * tile, (sub + 1) * tile)
                row_dot = jnp.sum(own[span].astype(float32) * outs, axis=-1, keepdims=True)
                pieces = []
                for part in range(stride):
                    for col in range(tiles):
                        start = (part * tiles + col) * tile
                        piece = probs_ref[sub, rows, start : start + tile].astype(float32) * (
                            raw[span, start : start + tile] - row_dot
                        )
                        shift = col - block
                        if shift < -reach:
                            dfar_ref[sub, 0] += piece
                        elif shift > reach:
                            dfar_ref[sub, 1] += piece
                        else:
                            columns = slice((shift + reach) * tile, (shift + reach + 1) * tile)
                            dbias_ref[sub, part - mine + stride - 1, :, columns] += piece
                        pieces.append(piece.astype(bfloat))
                low_grads = jnp.concatenate(pieces, axis=1)
                ds_ref[sub, rows, :] = low_grads
                stacked.append(low_grads)
            result = dot_nn(jnp.concatenate(stacked, axis=0), k_ref[...]) * scale
            dqkv_ref[rows, :tile] = joined_heads(result, lane, per, head_dim).astype(bfloat)
    dk_parts = []
    dv_parts = []
    for sub in range(per):
        dims = slice(sub * head_dim, (sub + 1) * head_dim)
        dk_parts.append(dot_nn(queries_t[dims, :], ds_ref[sub]))
        dv_parts.append(dot_nn(grads_t[dims, :], probs_ref[sub]))
    dqkv_ref[:, tile : 2 * tile] = jnp.concatenate(dk_parts, axis=0).T.astype(bfloat)
    dqkv_ref[:, 2 * tile :] = jnp.concatenate(dv_parts, axis=0).T.astype(bfloat)


def attend_back(probs, grads, outs, inverse, qkv, after, head_dim, stride, bias_shape):
    rows_all, span = outs.shape
    per = tile // head_dim
    heads = span // head_dim
    row_spec = pl.BlockSpec((rows_all, tile), lambda i: (0, i))
    return pl.pallas_call(
        functools.partial(attend_back_kernel, stride, head_dim, head_dim ** (-0.5)),
        grid=(span // tile,),
        in_specs=[pl.BlockSpec((per, rows_all, rows_all), lambda i: (i, 0, 0))]
        + [row_spec] * 3
        + kind_specs(rows_all)
        + [pl.BlockSpec(memory_space=pl.ANY)],
        out_specs=[
            pl.BlockSpec((rows_all, 3 * tile), lambda i: (0, i)),
            pl.BlockSpec((per,) + bias_shape[1:], lambda i: (i, 0, 0, 0)),
            pl.BlockSpec((per, 2, tile, tile), lambda i: (i, 0, 0, 0)),
        ],
        out_shape=[
            jax.ShapeDtypeStruct((rows_all, 3 * span), bfloat),
            jax.ShapeDtypeStruct(bias_shape, float32),
            jax.ShapeDtypeStruct((heads, 2, tile, tile), float32),
        ],
        scratch_shapes=[
            pltpu.VMEM((per, rows_all, rows_all), bfloat),
            pltpu.VMEM((rows_all, tile), bfloat),
        ],
        compiler_params=params(),
        cost_estimate=pl.CostEstimate(
            flops=32 * rows_all * rows_all * span,
            bytes_accessed=2 * heads * rows_all * rows_all,
            transcendentals=0,
        ),
        name="attend_back",
    )(probs, grads, outs, inverse, qkv, qkv, qkv, after)


def add_kernel(after_ref, *refs):
    out_ref = refs[-1]
    start = 0
    for left_ref, right_ref in zip(refs[:-1:2], refs[1:-1:2]):
        rows = left_ref.shape[1]
        out_ref[:, start : start + rows] = (
            left_ref[...].astype(float32) + right_ref[...].astype(float32)
        ).astype(bfloat)
        start += rows


def add_after(after, *operands):
    vmem = pl.BlockSpec(memory_space=pltpu.VMEM)
    outer, _, lanes = operands[0].shape
    rows = sum(operand.shape[1] for operand in operands[::2])
    return pl.pallas_call(
        add_kernel,
        in_specs=[pl.BlockSpec(memory_space=pl.ANY)] + [vmem] * len(operands),
        out_specs=vmem,
        out_shape=jax.ShapeDtypeStruct((outer, rows, lanes), bfloat),
        compiler_params=params(),
        name="add_after",
    )(after, *operands)


def order_kernel(count, place_ref, *refs):
    out_ref = refs[count + 1]
    for place in range(count):
        rows = refs[0][0]
        for step in range(1, count):
            rows = jnp.where(place_ref[0, :, step : step + 1] == place, refs[step][0], rows)
        out_ref[0, place] = rows


def order_rows(parts, offsets, carried):
    batches, rows, width = parts[0].shape
    count = len(parts)
    part_spec = pl.BlockSpec((1, rows, width), lambda i: (i, 0, 0))
    return pl.pallas_call(
        functools.partial(order_kernel, count),
        grid=(batches,),
        in_specs=[pl.BlockSpec((1, rows, count), lambda i: (i, 0, 0))]
        + [part_spec] * count
        + [pl.BlockSpec(memory_space=pl.ANY)],
        out_specs=[
            pl.BlockSpec((1, count, rows, width), lambda i: (i, 0, 0, 0)),
            pl.BlockSpec(memory_space=pl.ANY),
        ],
        out_shape=[
            jax.ShapeDtypeStruct((batches, count, rows, width), bfloat),
            jax.ShapeDtypeStruct(carried.shape, carried.dtype),
        ],
        input_output_aliases={count + 1: 1},
        compiler_params=params(),
        name="order_rows",
    )(offsets, *parts, carried)


def expert_kernel(
    count, slots, width, chunk, inner_ref, outer_ref, after_ref, *refs
):
    blocks = refs[:count]
    results = refs[count : 2 * count]
    hidden_ref, grad_pre_ref, rows_ref, grads_ref, sum_ref, back_ref = refs[2 * count :]
    turn = pl.program_id(0)

    @pl.when(turn == 0)
    def _():
        for idx in range(count):
            rows = slice(idx * slots, (idx + 1) * slots)
            rows_ref[rows, :] = blocks[idx][:, :width]
            grads_ref[rows, :] = blocks[idx][:, width:]

    inner = inner_ref[...].reshape(width, width)
    outer = outer_ref[...].reshape(width, width)
    rows = rows_ref[...]
    grads = grads_ref[...]
    root = 0.7978845608028654
    for start in range(0, width, chunk):
        columns = slice(start, start + chunk)
        pre = dot_nn(rows, inner[:, columns])
        grad_hidden = dot_nt(grads, outer[columns, :])
        square = pre * pre
        curve = jnp.tanh(root * pre * (1.0 + 0.044715 * square))
        half = 0.5 * (1.0 + curve)
        slope = half + (0.5 * root) * pre * (1.0 - curve * curve) * (1.0 + 0.134145 * square)
        hidden_ref[:, columns] = (pre * half).astype(bfloat)
        grad_pre_ref[:, columns] = (grad_hidden * slope).astype(bfloat)
    product = dot_nn(hidden_ref[...], outer)
    product_back = dot_nt(grad_pre_ref[...], inner)

    @pl.when(turn == 0)
    def _():
        sum_ref[...] = product
        back_ref[...] = product_back

    @pl.when(turn > 0)
    def _():
        sum_ref[...] += product
        back_ref[...] += product_back

    @pl.when(turn == pl.num_programs(0) - 1)
    def _():
        for idx in range(count):
            span = slice(idx * slots, (idx + 1) * slots)
            results[idx][:, :width] = sum_ref[span, :].astype(bfloat)
            results[idx][:, width:] = back_ref[span, :].astype(bfloat)


def run_expert(weights, blocks, width, after):
    (inner, inner_spec), (outer, outer_spec), turns = weights
    count = len(blocks)
    slots = blocks[0].shape[0]
    total = count * slots
    whole = pl.BlockSpec((slots, 2 * width), lambda i: (0, 0))
    chunk = pl.BlockSpec((total, width), lambda i: (0, i))
    outs = pl.pallas_call(
        functools.partial(expert_kernel, count, slots, width, 256),
        grid=(turns,),
        in_specs=[inner_spec, outer_spec, pl.BlockSpec(memory_space=pl.ANY)] + [whole] * count,
        out_specs=[whole] * count + [chunk, chunk],
        out_shape=[jax.ShapeDtypeStruct((slots, 2 * width), bfloat)] * count
        + [jax.ShapeDtypeStruct((total, turns * width), bfloat)] * 2,
        scratch_shapes=[
            pltpu.VMEM((total, width), bfloat),
            pltpu.VMEM((total, width), bfloat),
            pltpu.VMEM((total, width), float32),
            pltpu.VMEM((total, width), float32),
        ],
        compiler_params=params(),
        cost_estimate=pl.CostEstimate(
            flops=8 * total * width * width * turns,
            bytes_accessed=4 * width * width * turns,
            transcendentals=total * width * turns,
        ),
        name="run_expert",
    )(inner, outer, after, *blocks)
    return outs[:count], outs[count], outs[count + 1]


def expert_grad_kernel(batches, count, slots, width, second, *refs):
    groups = [refs[idx * count : (idx + 1) * count] for idx in range(batches)]
    wide = refs[batches * count : batches * count + batches]
    out_ref, rows_ref = refs[-2], refs[-1]
    half = slice(width, 2 * width) if second else slice(0, width)

    @pl.when(pl.program_id(0) == 0)
    def _():
        for batch in range(batches):
            for idx in range(count):
                start = (batch * count + idx) * slots
                rows_ref[start : start + slots, :] = groups[batch][idx][:, half]

    total = None
    span = count * slots
    for batch in range(batches):
        rows = rows_ref[batch * span : (batch + 1) * span, :]
        if second:
            term = dot_tn(wide[batch][...], rows)
        else:
            term = dot_tn(rows, wide[batch][...])
        total = term if total is None else total + term
    out_ref[...] = total.astype(bfloat).reshape(out_ref.shape)


def expert_grad(groups, wide, width, second, out_shape, out_spec, buffer=None):
    batches = len(groups)
    count = len(groups[0])
    slots = groups[0][0].shape[0]
    total = count * slots
    turns = wide[0].shape[1] // width
    kernel = functools.partial(expert_grad_kernel, batches, count, slots, width, second)
    in_specs = [pl.BlockSpec((slots, 2 * width), lambda i: (0, 0))] * (batches * count)
    in_specs = in_specs + [pl.BlockSpec((total, width), lambda i: (0, i))] * batches
    operands = [block for group in groups for block in group] + list(wide)
    aliases = {}
    body = kernel
    if buffer is not None:
        in_specs = [pl.BlockSpec(memory_space=pl.ANY)] + in_specs
        operands = [buffer] + operands
        aliases = {0: 0}

        def body(*refs):
            kernel(*refs[1:])

    return pl.pallas_call(
        body,
        grid=(turns,),
        in_specs=in_specs,
        out_specs=out_spec,
        out_shape=jax.ShapeDtypeStruct(out_shape, bfloat),
        scratch_shapes=[pltpu.VMEM((batches * total, width), bfloat)],
        input_output_aliases=aliases,
        compiler_params=params(),
        cost_estimate=pl.CostEstimate(
            flops=2 * batches * total * width * width * turns,
            bytes_accessed=4 * width * width * turns,
            transcendentals=0,
        ),
        name="expert_grad_outer" if second else "expert_grad_inner",
    )(*operands)


def on_device(
    hidden_in,
    out_grad,
    places,
    lengths,
    routes,
    norm1_gain,
    w_query,
    w_key,
    w_value,
    w_output,
    rel_table,
    norm2_gain,
    w_router,
    w_in,
    w_out,
):
    batches, rows_own, width = hidden_in.shape
    heads = rel_table.shape[1]
    head_dim = width // heads
    scale = head_dim ** (-0.5)
    shards = lax.axis_size("dp")
    members = lax.axis_size("expert")
    me = lax.axis_index("expert")
    experts = w_router.shape[1]
    hidden_width = w_in.shape[2]
    turns = hidden_width // width
    tiles = rows_own // tile
    rows_group = members * rows_own
    depth = width // shards
    depth_out = hidden_width // shards
    table_rows = rel_table.shape[0]
    capacity = max(2, rows_own * 17 // (experts * 16))
    slots = -(-capacity // 16) * 16
    per = tile // head_dim
    heads_own = per * (-(-heads // (per * members)))
    span = heads_own * head_dim
    pairs = span // tile
    lanes = 3 * tile
    split = width // lanes
    me_row = me.reshape(1)

    def around(step):
        return [(idx, (idx + step) % members) for idx in range(members)]

    def columns_own(weight):
        wide = jnp.pad(weight, ((0, 0), (0, members * span - width)))
        return lax.dynamic_slice_in_dim(wide, me * span, span, axis=1)

    def in_order(parts):
        if members == 2:
            return [
                jnp.where(me == 0, parts[0], parts[1]),
                jnp.where(me == 0, parts[1], parts[0]),
            ]
        stacked = jnp.stack(parts)
        return [stacked[jnp.mod(me - idx, members)] for idx in range(members)]

    hidden_from = [hidden_in] + [
        lax.ppermute(hidden_in, "expert", around(step)) for step in range(1, members)
    ]

    small = jnp.concatenate(
        [
            norm1_gain.reshape(-1),
            norm2_gain.reshape(-1),
            w_router.reshape(-1),
            rel_table.reshape(-1),
        ]
    )
    small_used = small.shape[0]
    small_pad = -(-small_used // (16 * lanes)) * 16
    small = jnp.pad(small, (0, small_pad * lanes - small_used)).reshape(small_pad, lanes)
    kinds = [columns_own(weight) for weight in (w_query, w_key, w_value)]
    first_own = jnp.concatenate(
        [
            jnp.concatenate([kind[:, idx * tile : (idx + 1) * tile] for kind in kinds], axis=1)
            for idx in range(pairs)
        ]
        + [w_output[:, idx * lanes : (idx + 1) * lanes] for idx in range(split)]
        + [small],
        axis=0,
    )
    first = lax.all_gather(first_own, "dp", axis=0, tiled=False)
    inner_parts = [w_in[0, :, idx * width : (idx + 1) * width] for idx in range(turns)]
    second_own = jnp.concatenate(inner_parts + [w_out[0]], axis=0)
    places_in = places[:, 0].reshape(batches, members, rows_own)
    dispatch, collect, offsets, second_own = row_tables(
        me_row, routes, places_in, hidden_from[-1], second_own, members, slots
    )
    second = lax.all_gather(second_own, "dp", axis=0, tiled=False)
    ends = jnp.cumsum(lengths[:, 0], axis=-1)[:, :-1]
    ordered_in, first = order_rows(hidden_from, offsets, first)
    ordered_in = ordered_in.reshape(batches, rows_group, width)

    small_start = (pairs + split) * depth
    small_all = first[:, small_start:].reshape(shards, small_pad * lanes)
    gain_one = small_all[:, :depth].reshape(1, width).astype(float32)
    gain_two = small_all[:, depth : 2 * depth].reshape(1, width).astype(float32)
    router_end = 2 * depth + depth * experts
    router_w = small_all[:, 2 * depth : router_end].reshape(width, experts)
    table = small_all[:, router_end:small_used].reshape(shards * table_rows, heads)
    router_wide = jnp.pad(router_w, ((0, 0), (0, tile - experts)))
    router_t = router_w.astype(float32).T
    output_w = jnp.concatenate(
        [
            first[:, (pairs + idx) * depth : (pairs + idx + 1) * depth].reshape(width, lanes)
            for idx in range(split)
        ],
        axis=1,
    )
    output_w = jnp.pad(output_w, ((0, members * span - width), (0, 0)))

    direct = depth % 16 == 0 and turns * depth == depth_out and shards % turns == 0
    if direct:
        group = shards // turns
        packed = first
        inner_spec = pl.BlockSpec((shards, depth, width), lambda i: (0, i, 0))
        outer_spec = pl.BlockSpec((group, depth_out, width), lambda i: (i, 1, 0))
        weights = ((second, inner_spec), (second, outer_spec), turns)
    else:
        packed = jnp.concatenate(
            [
                first[:, idx * depth : (idx + 1) * depth].reshape(1, width, lanes)
                for idx in range(pairs)
            ],
            axis=1,
        )
        inner_w = second[:, : turns * depth].reshape(shards, turns, depth, width)
        inner_w = jnp.transpose(inner_w, (1, 0, 2, 3)).reshape(turns, width, width)
        outer_w = second[:, turns * depth : turns * depth + depth_out].reshape(
            turns, width, width
        )
        plain = pl.BlockSpec((1, width, width), lambda i: (i, 0, 0))
        weights = ((inner_w, plain), (outer_w, plain), turns)

    table_wide = jnp.pad(table, ((0, 0), (0, members * heads_own - heads)))
    table_own = lax.dynamic_slice_in_dim(table_wide, me * heads_own, heads_own, axis=1)
    bias = bias_tiles(table_own, members, tiles)
    table_f = table_own.astype(float32)
    far = jnp.stack([table_f[levels_all - 1], table_f[2 * levels_all - 1]])

    def send_rows(batch, ordered):
        arrived = []
        for step in range(1, members):
            rows = ordered[:rows_own]
            for place in range(1, members):
                rows = jnp.where(
                    offsets[batch, :, members - step : members - step + 1] == place,
                    ordered[place * rows_own : (place + 1) * rows_own],
                    rows,
                )
            arrived.append(lax.ppermute(rows, "expert", around(step)))
        return arrived

    normed_one = []
    qkv = []
    probs = []
    outs = []
    inverses = []
    arrived_heads = []
    resid_mid = []
    normed_two = []
    router_probs = []
    blocks = []
    after = table
    for batch in range(batches):
        normed, packed_rows = project(batch, ordered_in, gain_one, packed, pairs, scale)
        normed_one.append(normed)
        qkv.append(packed_rows)
        kept, joined, inverse = attend(
            packed_rows, ends[batch], bias, far, after, head_dim, members
        )
        probs.append(kept)
        outs.append(joined)
        inverses.append(inverse)
        heads_in = send_rows(batch, joined)
        arrived_heads.append(heads_in)
        mid, normed, chances, outgoing = middle(
            batch,
            me_row,
            joined,
            heads_in,
            offsets,
            output_w,
            hidden_in,
            out_grad,
            gain_two,
            router_wide,
            routes,
            dispatch,
            blocks[-1][-1] if blocks else table,
        )
        after = outgoing[-1]
        blocks.append(
            [outgoing[0]]
            + [
                lax.ppermute(outgoing[step], "expert", around(step))
                for step in range(1, members)
            ]
        )
        resid_mid.append(mid)
        normed_two.append(normed)
        router_probs.append(chances)

    returned = []
    hidden = []
    grad_pre = []
    for batch in range(batches):
        results, hidden_rows, grad_rows = run_expert(
            weights, blocks[batch], width, hidden[-1] if hidden else table
        )
        hidden.append(hidden_rows)
        grad_pre.append(grad_rows)
        returned.append(
            [results[0]]
            + [
                lax.ppermute(results[step], "expert", around(-step))
                for step in range(1, members)
            ]
        )

    if direct:
        buffer_shape = (shards, turns * depth + depth_out, width)
        buffer = expert_grad(
            blocks,
            grad_pre,
            width,
            False,
            buffer_shape,
            pl.BlockSpec((shards, depth, width), lambda i: (0, i, 0)),
        )
        buffer = expert_grad(
            blocks,
            hidden,
            width,
            True,
            buffer_shape,
            pl.BlockSpec((group, depth_out, width), lambda i: (i, 1, 0)),
            buffer,
        )
    else:
        plain_shape = (turns, width, width)
        inner_g = expert_grad(blocks, grad_pre, width, False, plain_shape, plain)
        outer_g = expert_grad(blocks, hidden, width, True, plain_shape, plain)
        inner_g = jnp.transpose(inner_g.reshape(turns, shards, depth, width), (1, 0, 2, 3))
        buffer = jnp.concatenate(
            [
                inner_g.reshape(shards, turns * depth, width),
                outer_g.reshape(shards, depth_out, width),
            ],
            axis=1,
        )
    expert_sum = lax.psum_scatter(buffer, "dp", scatter_dimension=0, tiled=False)

    line = shards // 4
    my_shard = lax.axis_index("dp")

    def by_core_and_y(dense):
        dense = dense.reshape((line, 2, 2) + dense.shape[1:])
        odd = my_shard % 2 == 1
        sent = jnp.where(odd, dense[:, :, 0], dense[:, :, 1])
        held = jnp.where(odd, dense[:, :, 1], dense[:, :, 0])
        got = lax.ppermute(sent, "dp", [(idx, idx ^ 1) for idx in range(shards)])
        dense = (held.astype(float32) + got.astype(float32)).astype(bfloat)
        odd = (my_shard // 2) % 2 == 1
        sent = jnp.where(odd, dense[:, 0], dense[:, 1])
        held = jnp.where(odd, dense[:, 1], dense[:, 0])
        return held, lax.ppermute(sent, "dp", [(idx, idx ^ 2) for idx in range(shards)])

    layer = None
    grad_mid = []
    grad_attn = []
    grad_heads = []
    grad_gain_two = 0.0
    grad_router = 0.0
    for batch in range(batches):
        layer, mid, attn, gain_terms, router_terms, parts = second_back(
            batch,
            batches,
            me_row,
            returned[batch],
            collect,
            resid_mid[batch],
            normed_two[batch],
            router_probs[batch],
            out_grad,
            routes,
            gain_two,
            router_t,
            output_w,
            members,
            span,
            layer,
        )
        grad_mid.append(mid)
        grad_attn.append(attn)
        grad_gain_two = grad_gain_two + gain_terms
        grad_router = grad_router + router_terms[:experts]
        from_members = [parts[0]] + [
            lax.ppermute(parts[members - step], "expert", around(step))
            for step in range(1, members)
        ]
        ordered = []
        for place in range(members):
            rows = from_members[0]
            for step in range(1, members):
                rows = jnp.where(
                    offsets[batch, :, step : step + 1] == place, from_members[step], rows
                )
            ordered.append(rows)
        grad_heads.append(jnp.concatenate(ordered, axis=0))

    grad_qkv = []
    grad_gain_one = 0.0
    grad_bias = 0.0
    grad_far = 0.0
    in_grad = None
    for batch in range(batches):
        grads, bias_terms, far_terms = attend_back(
            probs[batch],
            grad_heads[batch],
            outs[batch],
            inverses[batch],
            qkv[batch],
            buffer,
            head_dim,
            members,
            bias.shape,
        )
        grad_qkv.append(grads)
        grad_bias = grad_bias + bias_terms
        grad_far = grad_far + far_terms
        gain_terms, own_rows, sent = first_back(
            batch, grads, packed, pairs, ordered_in, gain_one, offsets
        )
        grad_gain_one = grad_gain_one + gain_terms
        received = [
            lax.ppermute(rows, "expert", around(-step)) for step, rows in enumerate(sent, 1)
        ]
        in_grad = finish(
            batch, own_rows, received, hidden_in, gain_one, grad_mid[batch], in_grad
        )

    def own_rows_of(batch):
        joined = outs[batch]
        rows = joined[:rows_own]
        for place in range(1, members):
            rows = jnp.where(
                offsets[batch, :, 0:1] == place,
                joined[place * rows_own : (place + 1) * rows_own],
                rows,
            )
        return rows

    attended = [
        jnp.concatenate(in_order([own_rows_of(batch)] + arrived_heads[batch]), axis=1)[:, :width]
        for batch in range(batches)
    ]
    early = by_core_and_y(dense_grad(attended, grad_attn, lanes, shards, direct))
    grad_dense = dense_grad(normed_one, grad_qkv, lanes, shards, direct)

    steps = 2 * members - 1
    reach = near_shift(tiles)
    shape = (steps, tile, (2 * reach + 1) * tile)
    delta = (
        members
        * (
            lax.broadcasted_iota(jnp.int32, shape, 2)
            - reach * tile
            - lax.broadcasted_iota(jnp.int32, shape, 1)
        )
        + lax.broadcasted_iota(jnp.int32, shape, 0)
        - (members - 1)
    )
    buckets = shards * table_rows
    onehot = (
        bucket_of(delta)[None] == jnp.arange(buckets, dtype=jnp.int32)[:, None, None, None]
    ).astype(bfloat)
    grad_table = jnp.einsum(
        "hsab,ksab->kh", grad_bias.astype(bfloat), onehot, preferred_element_type=float32
    )
    far_sum = jnp.sum(grad_far, axis=(2, 3))
    grad_table = grad_table.at[levels_all - 1].add(far_sum[:, 0])
    grad_table = grad_table.at[2 * levels_all - 1].add(far_sum[:, 1])
    grad_table = lax.dynamic_update_slice_in_dim(
        jnp.zeros((buckets, members * heads_own), float32), grad_table, me * heads_own, axis=1
    )[:, :heads]

    small_grad = jnp.concatenate(
        [
            grad_gain_one.reshape(shards, depth),
            grad_gain_two.reshape(shards, depth),
            grad_router.T.reshape(shards, depth * experts),
            grad_table.reshape(shards, table_rows * heads),
        ],
        axis=1,
    )
    small_grad = jnp.pad(small_grad, ((0, 0), (0, small_pad * lanes - small_used)))
    small_grad = small_grad.astype(bfloat).reshape(shards, small_pad, lanes)
    late = by_core_and_y(jnp.concatenate([grad_dense, small_grad], axis=1))
    dense_part = lax.psum_scatter(
        add_after(expert_sum, *late, *early),
        "dp",
        scatter_dimension=0,
        tiled=False,
        axis_index_groups=[[rest + 4 * idx for idx in range(line)] for rest in range(4)],
    )
    parts = [dense_part] + [
        lax.ppermute(dense_part, "expert", around(step)) for step in range(1, members)
    ]
    qkv_parts = [
        part.astype(float32) for part in in_order([part[: pairs * depth] for part in parts])
    ]
    qkv_grads = [
        jnp.concatenate(
            [
                part[pair * depth : (pair + 1) * depth, kind * tile : (kind + 1) * tile]
                for part in qkv_parts
                for pair in range(pairs)
            ],
            axis=1,
        )[:, :width]
        for kind in range(3)
    ]
    rest_sum = sum(part[pairs * depth :].astype(float32) for part in parts)
    out_grad_sum = jnp.concatenate(
        [
            rest_sum[small_pad + idx * depth : small_pad + (idx + 1) * depth]
            for idx in range(split)
        ],
        axis=1,
    )
    small_sum = rest_sum[:small_pad].reshape(-1)

    expert_f = expert_sum.astype(float32)
    inner_sum = jnp.concatenate(
        [expert_f[idx * depth : (idx + 1) * depth] for idx in range(turns)], axis=1
    )[None]
    outer_sum = expert_f[turns * depth :][None]
    return (
        layer,
        in_grad,
        small_sum[:depth],
        qkv_grads[0],
        qkv_grads[1],
        qkv_grads[2],
        out_grad_sum,
        small_sum[router_end:small_used].reshape(table_rows, heads),
        small_sum[depth : 2 * depth],
        small_sum[2 * depth : router_end].reshape(depth, experts),
        inner_sum,
        outer_sum,
    )


def solution(mesh):
    return jax.shard_map(
        on_device,
        mesh=mesh,
        in_specs=(
            P(None, ("dp", "expert"), None),
            P(None, ("dp", "expert"), None),
            P(None, "dp", None),
            P(None, "dp", None),
            P(None, ("dp", "expert"), None),
            P("dp"),
            P("dp", None),
            P("dp", None),
            P("dp", None),
            P("dp", None),
            P("dp", None),
            P("dp"),
            P("dp", None),
            P("expert", "dp", None),
            P("expert", "dp", None),
        ),
        out_specs=(
            P(None, ("dp", "expert"), None),
            P(None, ("dp", "expert"), None),
            P("dp"),
            P("dp", None),
            P("dp", None),
            P("dp", None),
            P("dp", None),
            P("dp", None),
            P("dp"),
            P("dp", None),
            P("expert", "dp", None),
            P("expert", "dp", None),
        ),
        check_vma=False,
    )
```

```python
import functools

import jax
import jax.numpy as jnp
from jax import lax
from jax.experimental import pallas as pl
from jax.experimental.pallas import tpu as pltpu
from jax.sharding import PartitionSpec as P

bucket_edges = (1, 2, 3, 4, 5, 6, 7, 8, 12, 16, 23, 32, 46, 64, 91)
levels_all = len(bucket_edges) + 1
epsilon = 1e-06
masked_score = -1000000000.0
precise = lax.Precision.HIGHEST
float32 = jnp.float32
bfloat = jnp.bfloat16
tile = 128
vmem_bytes = 56 * 1024 * 1024


def params():
    return pltpu.CompilerParams(vmem_limit_bytes=vmem_bytes)


def dot_nn(left, right):
    return lax.dot_general(left, right, (((1,), (0,)), ((), ())), preferred_element_type=float32)


def dot_nt(left, right):
    return lax.dot_general(left, right, (((1,), (1,)), ((), ())), preferred_element_type=float32)


def dot_tn(left, right):
    return lax.dot_general(left, right, (((0,), (0,)), ((), ())), preferred_element_type=float32)


def norm_rows(rows, gain):
    mean_square = jnp.mean(rows * rows, axis=-1, keepdims=True)
    return rows * lax.rsqrt(mean_square + epsilon) * gain


def norm_back(rows, gain, grad):
    scale = lax.rsqrt(jnp.mean(rows * rows, axis=-1, keepdims=True) + epsilon)
    unit = rows * scale
    weighted = grad * gain
    inner = jnp.mean(weighted * unit, axis=-1, keepdims=True)
    return scale * (weighted - unit * inner), grad * unit


def bucket_of(offset):
    distance = jnp.abs(offset)
    levels = jnp.zeros(offset.shape, jnp.int32)
    for edge_value in bucket_edges:
        levels = levels + (distance >= edge_value).astype(jnp.int32)
    return levels + levels_all * (offset > 0).astype(jnp.int32)


def near_shift(tiles):
    return min(1, tiles - 1)


def bias_kernel(stride, reach, table_ref, out_ref):
    row = lax.broadcasted_iota(jnp.int32, (tile, tile), 0)
    lane = lax.broadcasted_iota(jnp.int32, (tile, tile), 1)
    heads = out_ref.shape[0]
    for shift in range(-reach, reach + 1):
        for step in range(2 * stride - 1):
            ids = bucket_of(stride * (tile * shift + lane - row) + step - (stride - 1))
            columns = slice((shift + reach) * tile, (shift + reach + 1) * tile)
            for head in range(heads):
                values = jnp.broadcast_to(table_ref[head : head + 1, :], (tile, tile))
                out_ref[head, step, :, columns] = jnp.take_along_axis(values, ids, axis=1)


def bias_tiles(table, stride, tiles):
    heads = table.shape[1]
    reach = near_shift(tiles)
    lanes = jnp.pad(table.astype(float32).T, ((0, 0), (0, tile - table.shape[0])))
    return pl.pallas_call(
        functools.partial(bias_kernel, stride, reach),
        out_shape=jax.ShapeDtypeStruct(
            (heads, 2 * stride - 1, tile, (2 * reach + 1) * tile), float32
        ),
        compiler_params=params(),
        name="bias_tiles",
    )(lanes)


def project_kernel(pairs, scale, rows_ref, gain_ref, weight_ref, normed_ref, out_ref):
    width = rows_ref.shape[2]
    depth = weight_ref.shape[1] // pairs
    lanes = weight_ref.shape[2]
    normed = norm_rows(rows_ref[0].astype(float32), gain_ref[...]).astype(bfloat)
    normed_ref[...] = normed
    for pair in range(pairs):
        weight = weight_ref[:, pair * depth : (pair + 1) * depth, :].reshape(width, lanes)
        product = dot_nn(normed, weight).astype(bfloat)
        start = pair * lanes
        out_ref[:, start : start + tile] = product[:, :tile] * bfloat(scale)
        out_ref[:, start + tile : start + lanes] = product[:, tile:]


def project(batch, rows, gain, packed, pairs, scale):
    _, count, width = rows.shape
    lanes = packed.shape[2]
    weight_shape = (packed.shape[0], pairs * width // packed.shape[0], lanes)
    step = min(512, count)
    return pl.pallas_call(
        functools.partial(project_kernel, pairs, scale),
        grid=(count // step,),
        in_specs=[
            pl.BlockSpec((1, step, width), lambda i: (batch, i, 0)),
            pl.BlockSpec((1, width), lambda i: (0, 0)),
            pl.BlockSpec(weight_shape, lambda i: (0, 0, 0)),
        ],
        out_specs=[
            pl.BlockSpec((step, width), lambda i: (i, 0)),
            pl.BlockSpec((step, pairs * lanes), lambda i: (i, 0)),
        ],
        out_shape=[
            jax.ShapeDtypeStruct((count, width), bfloat),
            jax.ShapeDtypeStruct((count, pairs * lanes), bfloat),
        ],
        compiler_params=params(),
        cost_estimate=pl.CostEstimate(
            flops=2 * count * width * lanes * pairs,
            bytes_accessed=6 * count * width,
            transcendentals=0,
        ),
        name="project",
    )(rows, gain, packed)


def count_earlier(picked, first_axis):
    size = picked.shape[1 - first_axis]
    row = lax.broadcasted_iota(jnp.int32, (size, size), 0)
    column = lax.broadcasted_iota(jnp.int32, (size, size), 1)
    if first_axis == 0:
        return dot_nn(picked, (row < column).astype(float32).astype(bfloat))
    return dot_nn((column < row).astype(float32).astype(bfloat), picked)


def tables_kernel(
    members,
    slots,
    me_ref,
    row_ref,
    column_ref,
    place_ref,
    after_ref,
    carried_ref,
    send_ref,
    back_ref,
    offset_ref,
    handed_ref,
):
    me = me_ref[0]
    batches, rows = column_ref.shape[0], column_ref.shape[1]
    names = 128
    for batch in range(batches):
        route = row_ref[batch]
        picked = lax.broadcasted_iota(jnp.int32, (names, rows), 0) == route
        earlier = count_earlier(picked.astype(float32).astype(bfloat), 0)
        slot = jnp.sum(jnp.where(picked, earlier, 0.0), axis=0, keepdims=True).astype(jnp.int32)
        target = jnp.where(route >= me, route - me, route - me + members) * slots + slot
        index = lax.broadcasted_iota(jnp.int32, (members * slots, rows), 0)
        send_ref[batch] = (index == target).astype(float32).astype(bfloat)

        route = column_ref[batch]
        picked = lax.broadcasted_iota(jnp.int32, (rows, names), 1) == route
        earlier = count_earlier(picked.astype(float32).astype(bfloat), 1)
        slot = jnp.sum(jnp.where(picked, earlier, 0.0), axis=1, keepdims=True).astype(jnp.int32)
        target = jnp.where(route >= me, route - me, route - me + members) * slots + slot
        index = lax.broadcasted_iota(jnp.int32, (rows, members * slots), 1)
        back_ref[batch] = (index == target).astype(float32).astype(bfloat)

        offsets = place_ref[batch] - members * lax.broadcasted_iota(
            jnp.int32, (rows, members), 0
        )
        lane = lax.broadcasted_iota(jnp.int32, (rows, members), 1)
        for step in range(members):
            owner = jnp.where(me >= step, me - step, me - step + members)
            chosen = jnp.sum(jnp.where(lane == owner, offsets, 0), axis=1, keepdims=True)
            offset_ref[batch, :, step : step + 1] = chosen


def row_tables(me, routes, places, after, carried, members, slots):
    batches, rows, _ = routes.shape
    vmem = pl.BlockSpec(memory_space=pltpu.VMEM)
    return pl.pallas_call(
        functools.partial(tables_kernel, members, slots),
        in_specs=[pl.BlockSpec(memory_space=pltpu.SMEM), vmem, vmem, vmem]
        + [pl.BlockSpec(memory_space=pl.ANY)] * 2,
        out_specs=[vmem, vmem, vmem, pl.BlockSpec(memory_space=pl.ANY)],
        out_shape=[
            jax.ShapeDtypeStruct((batches, members * slots, rows), bfloat),
            jax.ShapeDtypeStruct((batches, rows, members * slots), bfloat),
            jax.ShapeDtypeStruct((batches, rows, members), jnp.int32),
            jax.ShapeDtypeStruct(carried.shape, carried.dtype),
        ],
        input_output_aliases={5: 3},
        compiler_params=params(),
        name="row_tables",
    )(
        me,
        routes.reshape(batches, 1, rows),
        routes,
        jnp.transpose(places, (0, 2, 1)),
        after,
        carried,
    )


def member_rows(ordered, offset_ref, step, members):
    count = ordered.shape[0] // members
    rows = ordered[:count]
    for place in range(1, members):
        rows = jnp.where(
            offset_ref[0, :, step : step + 1] == place,
            ordered[place * count : (place + 1) * count],
            rows,
        )
    return rows


def middle_kernel(
    members,
    experts,
    me_ref,
    joined_ref,
    offset_ref,
    weight_ref,
    rows_ref,
    grad_ref,
    gain_ref,
    router_ref,
    route_ref,
    send_ref,
    after_ref,
    *refs,
):
    received = refs[: members - 1]
    mid_ref, normed_ref, probs_ref = refs[members - 1 : members + 2]
    out_refs = refs[members + 2 :]
    me = me_ref[0]
    span = joined_ref.shape[1]
    width = rows_ref.shape[2]
    slots = out_refs[0].shape[0]
    mid = rows_ref[0].astype(float32)
    for step in range(members):
        owner = jnp.where(me >= step, me - step, me - step + members)
        part = (
            member_rows(joined_ref[...], offset_ref, 0, members)
            if step == 0
            else received[step - 1][...]
        )
        mid = mid + dot_nn(part, weight_ref[pl.ds(pl.multiple_of(owner * span, span), span), :])
    mid_ref[...] = mid
    normed = norm_rows(mid, gain_ref[...]).astype(bfloat)
    normed_ref[...] = normed
    logits = dot_nn(normed, router_ref[...])
    lane = lax.broadcasted_iota(jnp.int32, logits.shape, 1)
    logits = jnp.where(lane < experts, logits, -jnp.inf)
    shifted = jnp.exp(logits - jnp.max(logits, axis=-1, keepdims=True))
    probs = shifted / jnp.sum(shifted, axis=-1, keepdims=True)
    probs_ref[...] = probs
    gate = jnp.sum(jnp.where(lane == route_ref[0], probs, 0.0), axis=1, keepdims=True)
    grad_expert = (gate * grad_ref[0].astype(float32)).astype(bfloat)
    tokens = dot_nn(send_ref[0], normed).astype(bfloat)
    grads = dot_nn(send_ref[0], grad_expert).astype(bfloat)
    for step in range(members):
        rows = slice(step * slots, (step + 1) * slots)
        out_refs[step][:, :width] = tokens[rows]
        out_refs[step][:, width:] = grads[rows]


def middle(
    batch, me, joined, received, offsets, weight, rows, grads, gain, router, routes, send, after
):
    members = offsets.shape[2]
    experts = members
    _, count, width = rows.shape
    slots = send.shape[1] // members
    row_spec = pl.BlockSpec((1, count, width), lambda i: (batch, 0, 0))

    def full(array):
        return pl.BlockSpec(array.shape, lambda i: (0,) * array.ndim)

    def own(array):
        return pl.BlockSpec((1,) + array.shape[1:], lambda i: (batch, 0, 0))

    out_shape = [
        jax.ShapeDtypeStruct((count, width), float32),
        jax.ShapeDtypeStruct((count, width), bfloat),
        jax.ShapeDtypeStruct((count, tile), float32),
    ] + [jax.ShapeDtypeStruct((slots, 2 * width), bfloat)] * members
    outs = pl.pallas_call(
        functools.partial(middle_kernel, members, experts),
        grid=(1,),
        in_specs=[
            pl.BlockSpec(memory_space=pltpu.SMEM),
            full(joined),
            own(offsets),
            full(weight),
            row_spec,
            row_spec,
            full(gain),
            full(router),
            own(routes),
            own(send),
            pl.BlockSpec(memory_space=pl.ANY),
        ]
        + [full(part) for part in received],
        out_specs=[full(shape) for shape in out_shape],
        out_shape=out_shape,
        compiler_params=params(),
        cost_estimate=pl.CostEstimate(
            flops=6 * count * width * width, bytes_accessed=12 * count * width, transcendentals=0
        ),
        name="middle",
    )(me, joined, offsets, weight, rows, grads, gain, router, routes, send, after, *received)
    return outs[0], outs[1], outs[2], list(outs[3:])


def second_kernel(
    members,
    experts,
    aliased,
    me_ref,
    back_ref,
    mid_ref,
    normed_ref,
    probs_ref,
    grad_ref,
    route_ref,
    gain_ref,
    router_ref,
    weight_ref,
    after_ref,
    *refs,
):
    returned = refs[:members]
    outs = refs[members + aliased :]
    layer_ref, grad_mid_ref, grad_attn_ref, gain_out_ref, router_out_ref = outs[:5]
    part_refs = outs[5:]
    me = me_ref[0]
    width = mid_ref.shape[1]
    span = part_refs[0].shape[1]
    blocks = jnp.concatenate([ref[...] for ref in returned], axis=0)
    home = dot_nn(back_ref[0], blocks)
    expert_back = home[:, :width]
    mid = mid_ref[...]
    gain = gain_ref[...]
    grads = grad_ref[0].astype(float32)
    probs = probs_ref[...]
    lane = lax.broadcasted_iota(jnp.int32, probs.shape, 1)
    picked = lane == route_ref[0]
    gate = jnp.sum(jnp.where(picked, probs, 0.0), axis=1, keepdims=True)
    layer_ref[0] = (mid + gate * expert_back).astype(bfloat)
    grad_gate = jnp.sum(grads * expert_back, axis=1, keepdims=True)
    grad_logits = (grad_gate * gate) * (jnp.where(picked, 1.0, 0.0) - probs)
    grad_logits = jnp.where(lane < experts, grad_logits, 0.0)
    grad_normed = home[:, width:]
    for name in range(experts):
        grad_normed = grad_normed + grad_logits[:, name : name + 1] * router_ref[name : name + 1, :]
    upper = grad_logits.astype(bfloat)
    lower = (grad_logits - upper.astype(float32)).astype(bfloat)
    normed = normed_ref[...]
    router_out_ref[...] = dot_tn(upper, normed) + dot_tn(lower, normed)
    grad_resid, terms = norm_back(mid, gain, grad_normed)
    gain_out_ref[...] = jnp.sum(terms, axis=0, keepdims=True)
    grad_mid = grads + grad_resid
    grad_mid_ref[...] = grad_mid
    grad_attn = grad_mid.astype(bfloat)
    grad_attn_ref[...] = grad_attn
    for step in range(members):
        owner = jnp.where(me >= step, me - step, me - step + members)
        rows = weight_ref[pl.ds(pl.multiple_of(owner * span, span), span), :]
        part_refs[step][...] = dot_nt(grad_attn, rows).astype(bfloat)


def second_back(
    batch,
    batches,
    me,
    returned,
    back,
    mid,
    normed,
    probs,
    grads,
    routes,
    gain,
    router,
    weight,
    members,
    span,
    after,
    layer,
):
    count, width = mid.shape
    grad_spec = pl.BlockSpec((1, count, width), lambda i: (batch, 0, 0))

    def full(array):
        return pl.BlockSpec(array.shape, lambda i: (0,) * array.ndim)

    def own(array):
        return pl.BlockSpec((1,) + array.shape[1:], lambda i: (batch, 0, 0))

    rest = [
        jax.ShapeDtypeStruct((count, width), float32),
        jax.ShapeDtypeStruct((count, width), bfloat),
        jax.ShapeDtypeStruct((1, width), float32),
        jax.ShapeDtypeStruct((tile, width), float32),
    ] + [jax.ShapeDtypeStruct((count, span), bfloat)] * members
    aliased = 0 if layer is None else 1
    outs = pl.pallas_call(
        functools.partial(second_kernel, members, members, aliased),
        grid=(1,),
        in_specs=[
            pl.BlockSpec(memory_space=pltpu.SMEM),
            own(back),
            full(mid),
            full(normed),
            full(probs),
            grad_spec,
            own(routes),
            full(gain),
            full(router),
            full(weight),
            pl.BlockSpec(memory_space=pl.ANY),
        ]
        + [full(part) for part in returned]
        + [pl.BlockSpec(memory_space=pl.ANY)] * aliased,
        out_specs=[grad_spec] + [full(shape) for shape in rest],
        out_shape=[jax.ShapeDtypeStruct((batches, count, width), bfloat)] + rest,
        input_output_aliases={11 + members: 0} if aliased else {},
        compiler_params=params(),
        cost_estimate=pl.CostEstimate(
            flops=6 * count * width * width, bytes_accessed=12 * count * width, transcendentals=0
        ),
        name="second_back",
    )(
        me,
        back,
        mid,
        normed,
        probs,
        grads,
        routes,
        gain,
        router,
        weight,
        after,
        *returned,
        *([] if layer is None else [layer]),
    )
    return outs[0], outs[1], outs[2], outs[3], outs[4], list(outs[5:])


def first_kernel(
    members,
    pairs,
    grads_ref,
    weight_ref,
    offset_ref,
    after_ref,
    *out_refs,
):
    width = out_refs[0].shape[1]
    depth = weight_ref.shape[1] // pairs
    lanes = weight_ref.shape[2]
    total = None
    for pair in range(pairs):
        weight = weight_ref[:, pair * depth : (pair + 1) * depth, :].reshape(width, lanes)
        term = dot_nt(grads_ref[:, pair * lanes : (pair + 1) * lanes], weight)
        total = term if total is None else total + term
    for step in range(members):
        out_refs[step][...] = member_rows(total, offset_ref, step, members).astype(
            out_refs[step].dtype
        )


def first_back(batch, grads, packed, pairs, width, offsets, after):
    members = offsets.shape[2]
    count = grads.shape[0]
    lanes = packed.shape[2]
    weight_shape = (packed.shape[0], pairs * width // packed.shape[0], lanes)
    own = jax.ShapeDtypeStruct((count // members, width), float32)
    sent = jax.ShapeDtypeStruct((count // members, width), bfloat)
    out_shape = [own] + [sent] * (members - 1)

    def full(array):
        return pl.BlockSpec(array.shape, lambda i: (0,) * len(array.shape))

    outs = pl.pallas_call(
        functools.partial(first_kernel, members, pairs),
        grid=(1,),
        in_specs=[
            full(grads),
            pl.BlockSpec(weight_shape, lambda i: (0, 0, 0)),
            pl.BlockSpec((1,) + offsets.shape[1:], lambda i: (batch, 0, 0)),
            pl.BlockSpec(memory_space=pl.ANY),
        ],
        out_specs=[full(shape) for shape in out_shape],
        out_shape=out_shape,
        compiler_params=params(),
        cost_estimate=pl.CostEstimate(
            flops=2 * count * width * lanes * pairs,
            bytes_accessed=8 * count * width,
            transcendentals=0,
        ),
        name="first_back",
    )(grads, packed, offsets, after)
    return outs[0], list(outs[1:])


def finish_kernel(received, own_ref, rows_ref, gain_ref, mid_ref, *refs):
    total = own_ref[...]
    for ref in refs[:received]:
        total = total + ref[...].astype(float32)
    grad, _ = norm_back(rows_ref[0].astype(float32), gain_ref[...], total)
    refs[-1][0] = mid_ref[...] + grad


def finish(batch, own, received, rows, gain, mid, buffer):
    batches, count, width = rows.shape
    row_spec = pl.BlockSpec((1, count, width), lambda i: (batch, 0, 0))

    def full(array):
        return pl.BlockSpec(array.shape, lambda i: (0,) * array.ndim)

    operands = [own, rows, gain, mid] + received
    in_specs = [full(own), row_spec, full(gain), full(mid)] + [full(part) for part in received]
    aliases = {}
    if buffer is not None:
        aliases = {len(operands): 0}
        operands.append(buffer)
        in_specs.append(pl.BlockSpec(memory_space=pl.ANY))
    return pl.pallas_call(
        functools.partial(finish_kernel, len(received)),
        grid=(1,),
        in_specs=in_specs,
        out_specs=row_spec,
        out_shape=jax.ShapeDtypeStruct((batches, count, width), float32),
        input_output_aliases=aliases,
        compiler_params=params(),
        name="finish",
    )(*operands)


def dense_kernel(batches, weighted, after_ref, *refs):
    out_ref = refs[2 * batches + weighted]
    total = None
    for batch in range(batches):
        term = dot_tn(refs[batch][...], refs[batches + batch][...])
        total = term if total is None else total + term
    out_ref[...] = total.astype(bfloat).reshape(out_ref.shape)
    if weighted:
        sum_ref = refs[-1]
        weight = refs[2 * batches][...].reshape(total.shape).astype(float32)
        term = jnp.sum(total * weight, axis=1, keepdims=True)

        @pl.when(pl.program_id(0) == 0)
        def _():
            sum_ref[...] = term

        @pl.when(pl.program_id(0) > 0)
        def _():
            sum_ref[...] += term


def dense_grad(left, right, lanes, shards, direct, after, packed=None):
    batches = len(left)
    count, width = left[0].shape
    blocks = right[0].shape[1] // lanes
    depth = width // shards
    if direct:
        out_shape = (shards, blocks * depth, lanes)
        out_spec = pl.BlockSpec((shards, depth, lanes), lambda i: (0, i, 0))
    else:
        out_shape = (blocks, width, lanes)
        out_spec = pl.BlockSpec((1, width, lanes), lambda i: (i, 0, 0))
    weighted = 0 if packed is None else 1
    outs = pl.pallas_call(
        functools.partial(dense_kernel, batches, weighted),
        grid=(blocks,),
        in_specs=[pl.BlockSpec(memory_space=pl.ANY)]
        + [pl.BlockSpec((count, width), lambda i: (0, 0))] * batches
        + [pl.BlockSpec((count, lanes), lambda i: (0, i))] * batches
        + (
            [pl.BlockSpec((packed.shape[0], width // packed.shape[0], lanes), lambda i: (0, i, 0))]
            if weighted
            else []
        ),
        out_specs=[out_spec] + [pl.BlockSpec((width, 1), lambda i: (0, 0))] * weighted,
        out_shape=[jax.ShapeDtypeStruct(out_shape, bfloat)]
        + [jax.ShapeDtypeStruct((width, 1), float32)] * weighted,
        compiler_params=params(),
        cost_estimate=pl.CostEstimate(
            flops=2 * batches * count * width * lanes * blocks,
            bytes_accessed=2 * batches * count * width,
            transcendentals=0,
        ),
        name="dense_grad",
    )(after, *left, *right, *([packed] if weighted else []))
    out = outs[0]
    if not direct:
        out = jnp.transpose(out.reshape(blocks, shards, depth, lanes), (1, 0, 2, 3))
        out = out.reshape(shards, blocks * depth, lanes)
    return (out, outs[1]) if weighted else out


def segment_of(positions, ends):
    segment = jnp.zeros(positions.shape, jnp.int32)
    for end in ends:
        segment = segment + (positions >= end).astype(jnp.int32)
    return segment


def masked_heads(rows, lane, per, head_dim):
    parts = []
    for sub in range(per):
        inside = (lane >= sub * head_dim) & (lane < (sub + 1) * head_dim)
        parts.append(jnp.where(inside, rows, jnp.zeros_like(rows)))
    return jnp.concatenate(parts, axis=0)


def joined_heads(rows, lane, per, head_dim):
    joined = rows[:tile]
    for sub in range(1, per):
        inside = (lane >= sub * head_dim) & (lane < (sub + 1) * head_dim)
        joined = jnp.where(inside, rows[sub * tile : (sub + 1) * tile], joined)
    return joined


def attend_kernel(
    stride,
    head_dim,
    far_ref,
    ends_ref,
    q_ref,
    k_ref,
    v_ref,
    bias_ref,
    after_ref,
    probs_ref,
    out_ref,
    inv_ref,
):
    pair = pl.program_id(0)
    rows_all = q_ref.shape[0]
    rows_part = rows_all // stride
    tiles = rows_part // tile
    reach = near_shift(tiles)
    per = tile // head_dim
    lane = lax.broadcasted_iota(jnp.int32, (tile, tile), 1)
    ends = [ends_ref[idx] for idx in range(ends_ref.shape[0])]
    keys_t = k_ref[...].T
    lane_row = lax.broadcasted_iota(jnp.int32, (1, tile), 1)
    row_column = lax.broadcasted_iota(jnp.int32, (tile, 1), 0)
    key_segments = [
        segment_of(stride * (col * tile + lane_row) + part, ends)
        for part in range(stride)
        for col in range(tiles)
    ]
    for mine in range(stride):
        for block in range(tiles):
            begin = mine * rows_part + block * tile
            rows = slice(begin, begin + tile)
            segment = segment_of(stride * (block * tile + row_column) + mine, ends)
            raw = dot_nn(masked_heads(q_ref[rows, :], lane, per, head_dim), keys_t)
            stacked = []
            inverses = []
            for sub in range(per):
                head = pair * per + sub
                pieces = []
                top = None
                for part in range(stride):
                    for col in range(tiles):
                        start = (part * tiles + col) * tile
                        piece = raw[sub * tile : (sub + 1) * tile, start : start + tile]
                        shift = col - block
                        if shift < -reach:
                            piece = piece + far_ref[0, head]
                        elif shift > reach:
                            piece = piece + far_ref[1, head]
                        else:
                            columns = slice((shift + reach) * tile, (shift + reach + 1) * tile)
                            piece = piece + bias_ref[sub, part - mine + stride - 1, :, columns]
                        same = key_segments[part * tiles + col] == segment
                        piece = jnp.where(same, piece, masked_score)
                        pieces.append(piece)
                        top = piece if top is None else jnp.maximum(top, piece)
                row_max = jnp.max(top, axis=-1, keepdims=True)
                total = None
                for idx, piece in enumerate(pieces):
                    piece = jnp.exp(piece - row_max)
                    total = piece if total is None else total + piece
                    pieces[idx] = piece.astype(bfloat)
                kept = jnp.concatenate(pieces, axis=1)
                probs_ref[sub, rows, :] = kept
                stacked.append(kept)
                inverses.append(1.0 / jnp.sum(total, axis=-1, keepdims=True))
            result = dot_nn(jnp.concatenate(stacked, axis=0), v_ref[...])
            inverse = jnp.broadcast_to(inverses[0], (tile, tile))
            for sub in range(1, per):
                inside = (lane >= sub * head_dim) & (lane < (sub + 1) * head_dim)
                inverse = jnp.where(inside, inverses[sub], inverse)
            out_ref[rows, :] = (joined_heads(result, lane, per, head_dim) * inverse).astype(bfloat)
            inv_ref[rows, :] = inverse


def kind_specs(rows_all):
    return [
        pl.BlockSpec((rows_all, tile), lambda i, kind=kind: (0, 3 * i + kind)) for kind in range(3)
    ]


def attend(qkv, ends, bias, far, after, head_dim, stride):
    rows_all, span = qkv.shape[0], qkv.shape[1] // 3
    per = tile // head_dim
    heads = span // head_dim
    row_spec = pl.BlockSpec((rows_all, tile), lambda i: (0, i))
    return pl.pallas_call(
        functools.partial(attend_kernel, stride, head_dim),
        grid=(span // tile,),
        in_specs=[
            pl.BlockSpec(memory_space=pltpu.SMEM),
            pl.BlockSpec(memory_space=pltpu.SMEM),
            *kind_specs(rows_all),
            pl.BlockSpec((per,) + bias.shape[1:], lambda i: (i, 0, 0, 0)),
            pl.BlockSpec(memory_space=pl.ANY),
        ],
        out_specs=[
            pl.BlockSpec((per, rows_all, rows_all), lambda i: (i, 0, 0)),
            row_spec,
            row_spec,
        ],
        out_shape=[
            jax.ShapeDtypeStruct((heads, rows_all, rows_all), bfloat),
            jax.ShapeDtypeStruct((rows_all, span), bfloat),
            jax.ShapeDtypeStruct((rows_all, span), float32),
        ],
        compiler_params=params(),
        cost_estimate=pl.CostEstimate(
            flops=16 * rows_all * rows_all * span,
            bytes_accessed=2 * heads * rows_all * rows_all,
            transcendentals=heads * rows_all * rows_all,
        ),
        name="attend",
    )(far, ends, qkv, qkv, qkv, bias, after)


def attend_back_kernel(
    stride,
    head_dim,
    scale,
    carried,
    probs_ref,
    out_ref,
    inv_ref,
    q_ref,
    k_ref,
    v_ref,
    offset_ref,
    after_ref,
    *refs,
):
    grad_refs = refs[:stride]
    dqkv_ref, dbias_ref, dfar_ref, ds_ref, grads_ref = refs[-5:]
    rows_all = q_ref.shape[0]
    rows_part = rows_all // stride
    tiles = rows_part // tile
    reach = near_shift(tiles)
    per = tile // head_dim
    lane = lax.broadcasted_iota(jnp.int32, (tile, tile), 1)
    queries_t = q_ref[...].T
    values_t = v_ref[...].T
    for place in range(stride):
        span = slice(place * rows_part, (place + 1) * rows_part)
        rows = grad_refs[0][...]
        for step in range(1, stride):
            rows = jnp.where(offset_ref[0, :, step : step + 1] == place, grad_refs[step][...], rows)
        grads_ref[span, :] = (rows.astype(float32) * inv_ref[span, :]).astype(bfloat)
    grads_t = grads_ref[...].T
    if carried:
        dbias_ref[...] = refs[stride][...]
        dfar_ref[...] = refs[stride + 1][...]
    else:
        dbias_ref[...] = jnp.zeros_like(dbias_ref)
        dfar_ref[...] = jnp.zeros_like(dfar_ref)
    for mine in range(stride):
        for block in range(tiles):
            begin = mine * rows_part + block * tile
            rows = slice(begin, begin + tile)
            own = masked_heads(grads_ref[rows, :], lane, per, head_dim)
            outs = out_ref[rows, :].astype(float32)
            raw = dot_nn(own, values_t)
            stacked = []
            for sub in range(per):
                span = slice(sub * tile, (sub + 1) * tile)
                row_dot = jnp.sum(own[span].astype(float32) * outs, axis=-1, keepdims=True)
                pieces = []
                for part in range(stride):
                    for col in range(tiles):
                        start = (part * tiles + col) * tile
                        piece = probs_ref[sub, rows, start : start + tile].astype(float32) * (
                            raw[span, start : start + tile] - row_dot
                        )
                        shift = col - block
                        if shift < -reach:
                            dfar_ref[sub, 0] += piece
                        elif shift > reach:
                            dfar_ref[sub, 1] += piece
                        else:
                            columns = slice((shift + reach) * tile, (shift + reach + 1) * tile)
                            dbias_ref[sub, part - mine + stride - 1, :, columns] += piece
                        pieces.append(piece.astype(bfloat))
                low_grads = jnp.concatenate(pieces, axis=1)
                ds_ref[sub, rows, :] = low_grads
                stacked.append(low_grads)
            result = dot_nn(jnp.concatenate(stacked, axis=0), k_ref[...]) * scale
            dqkv_ref[rows, :tile] = joined_heads(result, lane, per, head_dim).astype(bfloat)
    dk_parts = []
    dv_parts = []
    for sub in range(per):
        dims = slice(sub * head_dim, (sub + 1) * head_dim)
        dk_parts.append(dot_nn(queries_t[dims, :], ds_ref[sub]))
        dv_parts.append(dot_nn(grads_t[dims, :], probs_ref[sub]))
    dqkv_ref[:, tile : 2 * tile] = jnp.concatenate(dk_parts, axis=0).T.astype(bfloat)
    dqkv_ref[:, 2 * tile :] = jnp.concatenate(dv_parts, axis=0).T.astype(bfloat)


def attend_back(
    batch, probs, grads, outs, inverse, qkv, offsets, after, sums, head_dim, stride, bias_shape
):
    rows_all, span = outs.shape
    per = tile // head_dim
    heads = span // head_dim
    row_spec = pl.BlockSpec((rows_all, tile), lambda i: (0, i))
    part_spec = pl.BlockSpec((rows_all // stride, tile), lambda i: (0, i))
    sum_specs = [
        pl.BlockSpec((per,) + bias_shape[1:], lambda i: (i, 0, 0, 0)),
        pl.BlockSpec((per, 2, tile, tile), lambda i: (i, 0, 0, 0)),
    ]
    carried = len(sums) > 0
    first = 8 + stride
    return pl.pallas_call(
        functools.partial(attend_back_kernel, stride, head_dim, head_dim ** (-0.5), carried),
        grid=(span // tile,),
        in_specs=[pl.BlockSpec((per, rows_all, rows_all), lambda i: (i, 0, 0))]
        + [row_spec] * 2
        + kind_specs(rows_all)
        + [pl.BlockSpec((1,) + offsets.shape[1:], lambda i: (batch, 0, 0))]
        + [pl.BlockSpec(memory_space=pl.ANY)]
        + [part_spec] * stride
        + (sum_specs if carried else []),
        out_specs=[pl.BlockSpec((rows_all, 3 * tile), lambda i: (0, i))] + sum_specs,
        out_shape=[
            jax.ShapeDtypeStruct((rows_all, 3 * span), bfloat),
            jax.ShapeDtypeStruct(bias_shape, float32),
            jax.ShapeDtypeStruct((heads, 2, tile, tile), float32),
        ],
        scratch_shapes=[
            pltpu.VMEM((per, rows_all, rows_all), bfloat),
            pltpu.VMEM((rows_all, tile), bfloat),
        ],
        input_output_aliases={first: 1, first + 1: 2} if carried else {},
        compiler_params=params(),
        cost_estimate=pl.CostEstimate(
            flops=32 * rows_all * rows_all * span,
            bytes_accessed=2 * heads * rows_all * rows_all,
            transcendentals=0,
        ),
        name="attend_back",
    )(probs, outs, inverse, qkv, qkv, qkv, offsets, after, *grads, *sums)


def add_kernel(after_ref, *refs):
    out_ref = refs[-1]
    start = 0
    for left_ref, right_ref in zip(refs[:-1:2], refs[1:-1:2]):
        rows = left_ref.shape[1]
        out_ref[:, start : start + rows] = (
            left_ref[...].astype(float32) + right_ref[...].astype(float32)
        ).astype(bfloat)
        start += rows


def add_after(after, *operands):
    vmem = pl.BlockSpec(memory_space=pltpu.VMEM)
    outer, _, lanes = operands[0].shape
    rows = sum(operand.shape[1] for operand in operands[::2])
    return pl.pallas_call(
        add_kernel,
        in_specs=[pl.BlockSpec(memory_space=pl.ANY)] + [vmem] * len(operands),
        out_specs=vmem,
        out_shape=jax.ShapeDtypeStruct((outer, rows, lanes), bfloat),
        compiler_params=params(),
        name="add_after",
    )(after, *operands)


def order_kernel(count, place_ref, *refs):
    out_ref = refs[count + 1]
    for place in range(count):
        rows = refs[0][0]
        for step in range(1, count):
            rows = jnp.where(place_ref[0, :, step : step + 1] == place, refs[step][0], rows)
        out_ref[0, place] = rows


def order_rows(parts, offsets, carried):
    batches, rows, width = parts[0].shape
    count = len(parts)
    part_spec = pl.BlockSpec((1, rows, width), lambda i: (i, 0, 0))
    return pl.pallas_call(
        functools.partial(order_kernel, count),
        grid=(batches,),
        in_specs=[pl.BlockSpec((1, rows, count), lambda i: (i, 0, 0))]
        + [part_spec] * count
        + [pl.BlockSpec(memory_space=pl.ANY)],
        out_specs=[
            pl.BlockSpec((1, count, rows, width), lambda i: (i, 0, 0, 0)),
            pl.BlockSpec(memory_space=pl.ANY),
        ],
        out_shape=[
            jax.ShapeDtypeStruct((batches, count, rows, width), bfloat),
            jax.ShapeDtypeStruct(carried.shape, carried.dtype),
        ],
        input_output_aliases={count + 1: 1},
        compiler_params=params(),
        name="order_rows",
    )(offsets, *parts, carried)


def expert_kernel(
    count, slots, width, chunk, inner_ref, outer_ref, after_ref, *refs
):
    blocks = refs[:count]
    results = refs[count : 2 * count]
    hidden_ref, grad_pre_ref, rows_ref, grads_ref, sum_ref, back_ref = refs[2 * count :]
    turn = pl.program_id(0)

    @pl.when(turn == 0)
    def _():
        for idx in range(count):
            rows = slice(idx * slots, (idx + 1) * slots)
            rows_ref[rows, :] = blocks[idx][:, :width]
            grads_ref[rows, :] = blocks[idx][:, width:]

    inner = inner_ref[...].reshape(width, width)
    outer = outer_ref[...].reshape(width, width)
    rows = rows_ref[...]
    grads = grads_ref[...]
    root = 0.7978845608028654
    for start in range(0, width, chunk):
        columns = slice(start, start + chunk)
        pre = dot_nn(rows, inner[:, columns])
        grad_hidden = dot_nt(grads, outer[columns, :])
        square = pre * pre
        curve = jnp.tanh(root * pre * (1.0 + 0.044715 * square))
        half = 0.5 * (1.0 + curve)
        slope = half + (0.5 * root) * pre * (1.0 - curve * curve) * (1.0 + 0.134145 * square)
        hidden_ref[:, columns] = (pre * half).astype(bfloat)
        grad_pre_ref[:, columns] = (grad_hidden * slope).astype(bfloat)
    product = dot_nn(hidden_ref[...], outer)
    product_back = dot_nt(grad_pre_ref[...], inner)

    @pl.when(turn == 0)
    def _():
        sum_ref[...] = product
        back_ref[...] = product_back

    @pl.when(turn > 0)
    def _():
        sum_ref[...] += product
        back_ref[...] += product_back

    @pl.when(turn == pl.num_programs(0) - 1)
    def _():
        for idx in range(count):
            span = slice(idx * slots, (idx + 1) * slots)
            results[idx][:, :width] = sum_ref[span, :].astype(bfloat)
            results[idx][:, width:] = back_ref[span, :].astype(bfloat)


def run_expert(weights, blocks, width, after):
    (inner, inner_spec), (outer, outer_spec), turns = weights
    count = len(blocks)
    slots = blocks[0].shape[0]
    total = count * slots
    whole = pl.BlockSpec((slots, 2 * width), lambda i: (0, 0))
    chunk = pl.BlockSpec((total, width), lambda i: (0, i))
    outs = pl.pallas_call(
        functools.partial(expert_kernel, count, slots, width, 256),
        grid=(turns,),
        in_specs=[inner_spec, outer_spec, pl.BlockSpec(memory_space=pl.ANY)] + [whole] * count,
        out_specs=[whole] * count + [chunk, chunk],
        out_shape=[jax.ShapeDtypeStruct((slots, 2 * width), bfloat)] * count
        + [jax.ShapeDtypeStruct((total, turns * width), bfloat)] * 2,
        scratch_shapes=[
            pltpu.VMEM((total, width), bfloat),
            pltpu.VMEM((total, width), bfloat),
            pltpu.VMEM((total, width), float32),
            pltpu.VMEM((total, width), float32),
        ],
        compiler_params=params(),
        cost_estimate=pl.CostEstimate(
            flops=8 * total * width * width * turns,
            bytes_accessed=4 * width * width * turns,
            transcendentals=total * width * turns,
        ),
        name="run_expert",
    )(inner, outer, after, *blocks)
    return outs[:count], outs[count], outs[count + 1]


def expert_grad_kernel(batches, count, slots, width, second, *refs):
    groups = [refs[idx * count : (idx + 1) * count] for idx in range(batches)]
    wide = refs[batches * count : batches * count + batches]
    out_ref, rows_ref = refs[-2], refs[-1]
    half = slice(width, 2 * width) if second else slice(0, width)

    @pl.when(pl.program_id(0) == 0)
    def _():
        for batch in range(batches):
            for idx in range(count):
                start = (batch * count + idx) * slots
                rows_ref[start : start + slots, :] = groups[batch][idx][:, half]

    total = None
    span = count * slots
    for batch in range(batches):
        rows = rows_ref[batch * span : (batch + 1) * span, :]
        if second:
            term = dot_tn(wide[batch][...], rows)
        else:
            term = dot_tn(rows, wide[batch][...])
        total = term if total is None else total + term
    out_ref[...] = total.astype(bfloat).reshape(out_ref.shape)


def expert_grad(groups, wide, width, second, out_shape, out_spec, after, buffer=None):
    batches = len(groups)
    count = len(groups[0])
    slots = groups[0][0].shape[0]
    total = count * slots
    turns = wide[0].shape[1] // width
    kernel = functools.partial(expert_grad_kernel, batches, count, slots, width, second)
    in_specs = [pl.BlockSpec((slots, 2 * width), lambda i: (0, 0))] * (batches * count)
    in_specs = in_specs + [pl.BlockSpec((total, width), lambda i: (0, i))] * batches
    operands = [block for group in groups for block in group] + list(wide)
    aliases = {}
    carried = [after]
    if buffer is not None:
        carried = [buffer, after]
        aliases = {0: 0}
    skipped = len(carried)
    in_specs = [pl.BlockSpec(memory_space=pl.ANY)] * skipped + in_specs
    operands = carried + operands

    def body(*refs):
        kernel(*refs[skipped:])

    return pl.pallas_call(
        body,
        grid=(turns,),
        in_specs=in_specs,
        out_specs=out_spec,
        out_shape=jax.ShapeDtypeStruct(out_shape, bfloat),
        scratch_shapes=[pltpu.VMEM((batches * total, width), bfloat)],
        input_output_aliases=aliases,
        compiler_params=params(),
        cost_estimate=pl.CostEstimate(
            flops=2 * batches * total * width * width * turns,
            bytes_accessed=4 * width * width * turns,
            transcendentals=0,
        ),
        name="expert_grad_outer" if second else "expert_grad_inner",
    )(*operands)


def on_device(
    hidden_in,
    out_grad,
    places,
    lengths,
    routes,
    norm1_gain,
    w_query,
    w_key,
    w_value,
    w_output,
    rel_table,
    norm2_gain,
    w_router,
    w_in,
    w_out,
):
    batches, rows_own, width = hidden_in.shape
    heads = rel_table.shape[1]
    head_dim = width // heads
    scale = head_dim ** (-0.5)
    shards = lax.axis_size("dp")
    members = lax.axis_size("expert")
    me = lax.axis_index("expert")
    experts = w_router.shape[1]
    hidden_width = w_in.shape[2]
    turns = hidden_width // width
    tiles = rows_own // tile
    rows_group = members * rows_own
    depth = width // shards
    depth_out = hidden_width // shards
    table_rows = rel_table.shape[0]
    capacity = max(2, rows_own * 17 // (experts * 16))
    slots = -(-capacity // 16) * 16
    per = tile // head_dim
    heads_own = per * (-(-heads // (per * members)))
    span = heads_own * head_dim
    pairs = span // tile
    lanes = 3 * tile
    split = width // lanes
    me_row = me.reshape(1)

    def around(step):
        return [(idx, (idx + step) % members) for idx in range(members)]

    def columns_own(weight):
        wide = jnp.pad(weight, ((0, 0), (0, members * span - width)))
        return lax.dynamic_slice_in_dim(wide, me * span, span, axis=1)

    def in_order(parts):
        if members == 2:
            return [
                jnp.where(me == 0, parts[0], parts[1]),
                jnp.where(me == 0, parts[1], parts[0]),
            ]
        stacked = jnp.stack(parts)
        return [stacked[jnp.mod(me - idx, members)] for idx in range(members)]

    hidden_from = [hidden_in] + [
        lax.ppermute(hidden_in, "expert", around(step)) for step in range(1, members)
    ]

    small = jnp.concatenate(
        [
            norm1_gain.reshape(-1),
            norm2_gain.reshape(-1),
            w_router.reshape(-1),
            rel_table.reshape(-1),
        ]
    )
    small_used = small.shape[0]
    small_pad = -(-small_used // (16 * lanes)) * 16
    small = jnp.pad(small, (0, small_pad * lanes - small_used)).reshape(small_pad, lanes)
    kinds = [columns_own(weight) for weight in (w_query, w_key, w_value)]
    first_own = jnp.concatenate(
        [
            jnp.concatenate([kind[:, idx * tile : (idx + 1) * tile] for kind in kinds], axis=1)
            for idx in range(pairs)
        ]
        + [w_output[:, idx * lanes : (idx + 1) * lanes] for idx in range(split)]
        + [small],
        axis=0,
    )
    first = lax.all_gather(first_own, "dp", axis=0, tiled=False)
    inner_parts = [w_in[0, :, idx * width : (idx + 1) * width] for idx in range(turns)]
    second_own = jnp.concatenate(inner_parts + [w_out[0]], axis=0)
    places_in = places[:, 0].reshape(batches, members, rows_own)
    dispatch, collect, offsets, second_own = row_tables(
        me_row, routes, places_in, hidden_from[-1], second_own, members, slots
    )
    second = lax.all_gather(second_own, "dp", axis=0, tiled=False)
    ends = jnp.cumsum(lengths[:, 0], axis=-1)[:, :-1]
    ordered_in, first = order_rows(hidden_from, offsets, first)
    ordered_in = ordered_in.reshape(batches, rows_group, width)

    small_start = (pairs + split) * depth
    small_all = first[:, small_start:].reshape(shards, small_pad * lanes)
    gain_one = small_all[:, :depth].reshape(1, width).astype(float32)
    gain_two = small_all[:, depth : 2 * depth].reshape(1, width).astype(float32)
    router_end = 2 * depth + depth * experts
    router_w = small_all[:, 2 * depth : router_end].reshape(width, experts)
    table = small_all[:, router_end:small_used].reshape(shards * table_rows, heads)
    router_wide = jnp.pad(router_w, ((0, 0), (0, tile - experts)))
    router_t = router_w.astype(float32).T
    output_w = jnp.concatenate(
        [
            first[:, (pairs + idx) * depth : (pairs + idx + 1) * depth].reshape(width, lanes)
            for idx in range(split)
        ],
        axis=1,
    )
    output_w = jnp.pad(output_w, ((0, members * span - width), (0, 0)))

    direct = depth % 16 == 0 and turns * depth == depth_out and shards % turns == 0
    if direct:
        group = shards // turns
        packed = first
        inner_spec = pl.BlockSpec((shards, depth, width), lambda i: (0, i, 0))
        outer_spec = pl.BlockSpec((group, depth_out, width), lambda i: (i, 1, 0))
        weights = ((second, inner_spec), (second, outer_spec), turns)
    else:
        packed = jnp.concatenate(
            [
                first[:, idx * depth : (idx + 1) * depth].reshape(1, width, lanes)
                for idx in range(pairs)
            ],
            axis=1,
        )
        inner_w = second[:, : turns * depth].reshape(shards, turns, depth, width)
        inner_w = jnp.transpose(inner_w, (1, 0, 2, 3)).reshape(turns, width, width)
        outer_w = second[:, turns * depth : turns * depth + depth_out].reshape(
            turns, width, width
        )
        plain = pl.BlockSpec((1, width, width), lambda i: (i, 0, 0))
        weights = ((inner_w, plain), (outer_w, plain), turns)

    table_wide = jnp.pad(table, ((0, 0), (0, members * heads_own - heads)))
    table_own = lax.dynamic_slice_in_dim(table_wide, me * heads_own, heads_own, axis=1)
    bias = bias_tiles(table_own, members, tiles)
    table_f = table_own.astype(float32)
    far = jnp.stack([table_f[levels_all - 1], table_f[2 * levels_all - 1]])

    def send_rows(batch, ordered):
        arrived = []
        for step in range(1, members):
            rows = ordered[:rows_own]
            for place in range(1, members):
                rows = jnp.where(
                    offsets[batch, :, members - step : members - step + 1] == place,
                    ordered[place * rows_own : (place + 1) * rows_own],
                    rows,
                )
            arrived.append(lax.ppermute(rows, "expert", around(step)))
        return arrived

    normed_one = []
    qkv = []
    probs = []
    outs = []
    inverses = []
    arrived_heads = []
    resid_mid = []
    normed_two = []
    router_probs = []
    blocks = []
    after = table
    for batch in range(batches):
        normed, packed_rows = project(batch, ordered_in, gain_one, packed, pairs, scale)
        normed_one.append(normed)
        qkv.append(packed_rows)
        kept, joined, inverse = attend(
            packed_rows, ends[batch], bias, far, after, head_dim, members
        )
        probs.append(kept)
        outs.append(joined)
        inverses.append(inverse)
        heads_in = send_rows(batch, joined)
        arrived_heads.append(heads_in)
        mid, normed, chances, outgoing = middle(
            batch,
            me_row,
            joined,
            heads_in,
            offsets,
            output_w,
            hidden_in,
            out_grad,
            gain_two,
            router_wide,
            routes,
            dispatch,
            blocks[-1][-1] if blocks else table,
        )
        after = outgoing[-1]
        blocks.append(
            [outgoing[0]]
            + [
                lax.ppermute(outgoing[step], "expert", around(step))
                for step in range(1, members)
            ]
        )
        resid_mid.append(mid)
        normed_two.append(normed)
        router_probs.append(chances)

    returned = []
    hidden = []
    grad_pre = []
    for batch in range(batches):
        results, hidden_rows, grad_rows = run_expert(
            weights, blocks[batch], width, hidden[-1] if hidden else table
        )
        hidden.append(hidden_rows)
        grad_pre.append(grad_rows)
        returned.append(
            [results[0]]
            + [
                lax.ppermute(results[step], "expert", around(-step))
                for step in range(1, members)
            ]
        )

    if direct:
        buffer_shape = (shards, turns * depth + depth_out, width)
        buffer = expert_grad(
            blocks,
            grad_pre,
            width,
            False,
            buffer_shape,
            pl.BlockSpec((shards, depth, width), lambda i: (0, i, 0)),
            returned[0][-1],
        )
        buffer = expert_grad(
            blocks,
            hidden,
            width,
            True,
            buffer_shape,
            pl.BlockSpec((group, depth_out, width), lambda i: (i, 1, 0)),
            returned[0][-1],
            buffer,
        )
    else:
        plain_shape = (turns, width, width)
        inner_g = expert_grad(
            blocks, grad_pre, width, False, plain_shape, plain, returned[0][-1]
        )
        outer_g = expert_grad(
            blocks, hidden, width, True, plain_shape, plain, returned[0][-1]
        )
        inner_g = jnp.transpose(inner_g.reshape(turns, shards, depth, width), (1, 0, 2, 3))
        buffer = jnp.concatenate(
            [
                inner_g.reshape(shards, turns * depth, width),
                outer_g.reshape(shards, depth_out, width),
            ],
            axis=1,
        )
    expert_sum = lax.psum_scatter(buffer, "dp", scatter_dimension=0, tiled=False)

    line = shards // 4
    my_shard = lax.axis_index("dp")

    def by_core(dense):
        dense = dense.reshape((line, 2, 2) + dense.shape[1:])
        odd = my_shard % 2 == 1
        sent = jnp.where(odd, dense[:, :, 0], dense[:, :, 1])
        held = jnp.where(odd, dense[:, :, 1], dense[:, :, 0])
        return held, lax.ppermute(sent, "dp", [(idx, idx ^ 1) for idx in range(shards)])

    def by_y(core_parts):
        held, got = core_parts
        odd = (my_shard // 2) % 2 == 1

        def half(idx):
            return held[:, idx].astype(float32) + got[:, idx].astype(float32)

        sent = jnp.where(odd, half(0), half(1)).astype(bfloat)
        kept = jnp.where(odd, half(1), half(0)).astype(bfloat)
        return kept, lax.ppermute(sent, "dp", [(idx, idx ^ 2) for idx in range(shards)])

    layer = None
    grad_mid = []
    grad_attn = []
    grad_heads = []
    grad_gain_two = 0.0
    grad_router = 0.0
    for batch in range(batches):
        layer, mid, attn, gain_terms, router_terms, parts = second_back(
            batch,
            batches,
            me_row,
            returned[batch],
            collect,
            resid_mid[batch],
            normed_two[batch],
            router_probs[batch],
            out_grad,
            routes,
            gain_two,
            router_t,
            output_w,
            members,
            span,
            returned[-1][-1] if batch == 0 else buffer,
            layer,
        )
        grad_mid.append(mid)
        grad_attn.append(attn)
        grad_gain_two = grad_gain_two + gain_terms
        grad_router = grad_router + router_terms[:experts]
        from_members = [parts[0]] + [
            lax.ppermute(parts[members - step], "expert", around(step))
            for step in range(1, members)
        ]
        grad_heads.append(from_members)

    def own_rows_of(batch):
        joined = outs[batch]
        rows = joined[:rows_own]
        for place in range(1, members):
            rows = jnp.where(
                offsets[batch, :, 0:1] == place,
                joined[place * rows_own : (place + 1) * rows_own],
                rows,
            )
        return rows

    attended = [
        jnp.concatenate(in_order([own_rows_of(batch)] + arrived_heads[batch]), axis=1)[:, :width]
        for batch in range(batches)
    ]
    early_core = by_core(
        dense_grad(attended, grad_attn, lanes, shards, direct, grad_heads[0][-1])
    )
    early = by_y(early_core)
    grad_qkv = []
    sums = []
    for batch in range(batches):
        grads, *sums = attend_back(
            batch,
            probs[batch],
            grad_heads[batch],
            outs[batch],
            inverses[batch],
            qkv[batch],
            offsets,
            buffer if batch == 0 else early_core[1],
            sums,
            head_dim,
            members,
            bias.shape,
        )
        grad_qkv.append(grads)
    grad_bias, grad_far = sums
    grad_dense, weighted = dense_grad(
        normed_one, grad_qkv, lanes, shards, direct, early[1], packed
    )
    grad_gain_one = weighted[:, 0] / gain_one[0]
    late_core = by_core(grad_dense)
    late = by_y(late_core)

    in_grad = None
    for batch in range(batches):
        own_rows, sent = first_back(
            batch,
            grad_qkv[batch],
            packed,
            pairs,
            width,
            offsets,
            late_core[1] if batch == 0 else late[1],
        )
        received = [
            lax.ppermute(rows, "expert", around(-step)) for step, rows in enumerate(sent, 1)
        ]
        in_grad = finish(
            batch, own_rows, received, hidden_in, gain_one, grad_mid[batch], in_grad
        )

    steps = 2 * members - 1
    reach = near_shift(tiles)
    shape = (steps, tile, (2 * reach + 1) * tile)
    delta = (
        members
        * (
            lax.broadcasted_iota(jnp.int32, shape, 2)
            - reach * tile
            - lax.broadcasted_iota(jnp.int32, shape, 1)
        )
        + lax.broadcasted_iota(jnp.int32, shape, 0)
        - (members - 1)
    )
    buckets = shards * table_rows
    onehot = (
        bucket_of(delta)[None] == jnp.arange(buckets, dtype=jnp.int32)[:, None, None, None]
    ).astype(bfloat)
    grad_table = jnp.einsum(
        "hsab,ksab->kh", grad_bias.astype(bfloat), onehot, preferred_element_type=float32
    )
    far_sum = jnp.sum(grad_far, axis=(2, 3))
    grad_table = grad_table.at[levels_all - 1].add(far_sum[:, 0])
    grad_table = grad_table.at[2 * levels_all - 1].add(far_sum[:, 1])
    grad_table = lax.dynamic_update_slice_in_dim(
        jnp.zeros((buckets, members * heads_own), float32), grad_table, me * heads_own, axis=1
    )[:, :heads]

    small_grad = jnp.concatenate(
        [
            grad_gain_one.reshape(shards, depth),
            grad_gain_two.reshape(shards, depth),
            grad_router.T.reshape(shards, depth * experts),
            grad_table.reshape(shards, table_rows * heads),
        ],
        axis=1,
    )
    small_grad = jnp.pad(small_grad, ((0, 0), (0, small_pad * lanes - small_used)))
    small_grad = small_grad.astype(bfloat).reshape(shards, small_pad, lanes)
    little = by_y(by_core(small_grad))
    dense_part = lax.psum_scatter(
        add_after(expert_sum, *late, *little, *early),
        "dp",
        scatter_dimension=0,
        tiled=False,
        axis_index_groups=[[rest + 4 * idx for idx in range(line)] for rest in range(4)],
    )
    parts = [dense_part] + [
        lax.ppermute(dense_part, "expert", around(step)) for step in range(1, members)
    ]
    qkv_parts = [
        part.astype(float32) for part in in_order([part[: pairs * depth] for part in parts])
    ]
    qkv_grads = [
        jnp.concatenate(
            [
                part[pair * depth : (pair + 1) * depth, kind * tile : (kind + 1) * tile]
                for part in qkv_parts
                for pair in range(pairs)
            ],
            axis=1,
        )[:, :width]
        for kind in range(3)
    ]
    rest_sum = sum(part[pairs * depth :].astype(float32) for part in parts)
    out_grad_sum = jnp.concatenate(
        [
            rest_sum[small_pad + idx * depth : small_pad + (idx + 1) * depth]
            for idx in range(split)
        ],
        axis=1,
    )
    small_sum = rest_sum[:small_pad].reshape(-1)

    expert_f = expert_sum.astype(float32)
    inner_sum = jnp.concatenate(
        [expert_f[idx * depth : (idx + 1) * depth] for idx in range(turns)], axis=1
    )[None]
    outer_sum = expert_f[turns * depth :][None]
    return (
        layer,
        in_grad,
        small_sum[:depth],
        qkv_grads[0],
        qkv_grads[1],
        qkv_grads[2],
        out_grad_sum,
        small_sum[router_end:small_used].reshape(table_rows, heads),
        small_sum[depth : 2 * depth],
        small_sum[2 * depth : router_end].reshape(depth, experts),
        inner_sum,
        outer_sum,
    )


def solution(mesh):
    return jax.shard_map(
        on_device,
        mesh=mesh,
        in_specs=(
            P(None, ("dp", "expert"), None),
            P(None, ("dp", "expert"), None),
            P(None, "dp", None),
            P(None, "dp", None),
            P(None, ("dp", "expert"), None),
            P("dp"),
            P("dp", None),
            P("dp", None),
            P("dp", None),
            P("dp", None),
            P("dp", None),
            P("dp"),
            P("dp", None),
            P("expert", "dp", None),
            P("expert", "dp", None),
        ),
        out_specs=(
            P(None, ("dp", "expert"), None),
            P(None, ("dp", "expert"), None),
            P("dp"),
            P("dp", None),
            P("dp", None),
            P("dp", None),
            P("dp", None),
            P("dp", None),
            P("dp"),
            P("dp", None),
            P("expert", "dp", None),
            P("expert", "dp", None),
        ),
        check_vma=False,
    )
```

```python
import functools

import jax
import jax.numpy as jnp
from jax import lax
from jax.experimental import pallas as pl
from jax.experimental.pallas import tpu as pltpu
from jax.sharding import PartitionSpec as P

bucket_edges = (1, 2, 3, 4, 5, 6, 7, 8, 12, 16, 23, 32, 46, 64, 91)
levels_all = len(bucket_edges) + 1
epsilon = 1e-06
masked_score = -1000000000.0
precise = lax.Precision.HIGHEST
float32 = jnp.float32
bfloat = jnp.bfloat16
tile = 128
vmem_bytes = 56 * 1024 * 1024


def params():
    return pltpu.CompilerParams(vmem_limit_bytes=vmem_bytes)


def dot_nn(left, right):
    return lax.dot_general(left, right, (((1,), (0,)), ((), ())), preferred_element_type=float32)


def dot_nt(left, right):
    return lax.dot_general(left, right, (((1,), (1,)), ((), ())), preferred_element_type=float32)


def dot_tn(left, right):
    return lax.dot_general(left, right, (((0,), (0,)), ((), ())), preferred_element_type=float32)


def norm_rows(rows, gain):
    mean_square = jnp.mean(rows * rows, axis=-1, keepdims=True)
    return rows * lax.rsqrt(mean_square + epsilon) * gain


def norm_back(rows, gain, grad):
    scale = lax.rsqrt(jnp.mean(rows * rows, axis=-1, keepdims=True) + epsilon)
    unit = rows * scale
    weighted = grad * gain
    inner = jnp.mean(weighted * unit, axis=-1, keepdims=True)
    return scale * (weighted - unit * inner), grad * unit


def bucket_of(offset):
    distance = jnp.abs(offset)
    levels = jnp.zeros(offset.shape, jnp.int32)
    for edge_value in bucket_edges:
        levels = levels + (distance >= edge_value).astype(jnp.int32)
    return levels + levels_all * (offset > 0).astype(jnp.int32)


def near_shift(tiles):
    return min(1, tiles - 1)


def bias_kernel(stride, reach, table_ref, out_ref):
    row = lax.broadcasted_iota(jnp.int32, (tile, tile), 0)
    lane = lax.broadcasted_iota(jnp.int32, (tile, tile), 1)
    heads = out_ref.shape[0]
    for shift in range(-reach, reach + 1):
        for step in range(2 * stride - 1):
            ids = bucket_of(stride * (tile * shift + lane - row) + step - (stride - 1))
            columns = slice((shift + reach) * tile, (shift + reach + 1) * tile)
            for head in range(heads):
                values = jnp.broadcast_to(table_ref[head : head + 1, :], (tile, tile))
                out_ref[head, step, :, columns] = jnp.take_along_axis(values, ids, axis=1)


def bias_tiles(table, stride, tiles):
    heads = table.shape[1]
    reach = near_shift(tiles)
    lanes = jnp.pad(table.astype(float32).T, ((0, 0), (0, tile - table.shape[0])))
    return pl.pallas_call(
        functools.partial(bias_kernel, stride, reach),
        out_shape=jax.ShapeDtypeStruct(
            (heads, 2 * stride - 1, tile, (2 * reach + 1) * tile), float32
        ),
        compiler_params=params(),
        name="bias_tiles",
    )(lanes)


def project_kernel(pairs, scale, rows_ref, gain_ref, weight_ref, normed_ref, out_ref):
    width = rows_ref.shape[2]
    depth = weight_ref.shape[1] // pairs
    lanes = weight_ref.shape[2]
    normed = norm_rows(rows_ref[0].astype(float32), gain_ref[...]).astype(bfloat)
    normed_ref[...] = normed
    for pair in range(pairs):
        weight = weight_ref[:, pair * depth : (pair + 1) * depth, :].reshape(width, lanes)
        product = dot_nn(normed, weight).astype(bfloat)
        start = pair * lanes
        out_ref[:, start : start + tile] = product[:, :tile] * bfloat(scale)
        out_ref[:, start + tile : start + lanes] = product[:, tile:]


def project(batch, rows, gain, packed, pairs, scale):
    _, count, width = rows.shape
    lanes = packed.shape[2]
    weight_shape = (packed.shape[0], pairs * width // packed.shape[0], lanes)
    step = min(512, count)
    return pl.pallas_call(
        functools.partial(project_kernel, pairs, scale),
        grid=(count // step,),
        in_specs=[
            pl.BlockSpec((1, step, width), lambda i: (batch, i, 0)),
            pl.BlockSpec((1, width), lambda i: (0, 0)),
            pl.BlockSpec(weight_shape, lambda i: (0, 0, 0)),
        ],
        out_specs=[
            pl.BlockSpec((step, width), lambda i: (i, 0)),
            pl.BlockSpec((step, pairs * lanes), lambda i: (i, 0)),
        ],
        out_shape=[
            jax.ShapeDtypeStruct((count, width), bfloat),
            jax.ShapeDtypeStruct((count, pairs * lanes), bfloat),
        ],
        compiler_params=params(),
        cost_estimate=pl.CostEstimate(
            flops=2 * count * width * lanes * pairs,
            bytes_accessed=6 * count * width,
            transcendentals=0,
        ),
        name="project",
    )(rows, gain, packed)


def count_earlier(picked, first_axis):
    size = picked.shape[1 - first_axis]
    row = lax.broadcasted_iota(jnp.int32, (size, size), 0)
    column = lax.broadcasted_iota(jnp.int32, (size, size), 1)
    if first_axis == 0:
        return dot_nn(picked, (row < column).astype(float32).astype(bfloat))
    return dot_nn((column < row).astype(float32).astype(bfloat), picked)


def tables_kernel(
    members,
    slots,
    me_ref,
    row_ref,
    column_ref,
    place_ref,
    after_ref,
    carried_ref,
    send_ref,
    back_ref,
    offset_ref,
    handed_ref,
):
    me = me_ref[0]
    batches, rows = column_ref.shape[0], column_ref.shape[1]
    names = 128
    for batch in range(batches):
        route = row_ref[batch]
        picked = lax.broadcasted_iota(jnp.int32, (names, rows), 0) == route
        earlier = count_earlier(picked.astype(float32).astype(bfloat), 0)
        slot = jnp.sum(jnp.where(picked, earlier, 0.0), axis=0, keepdims=True).astype(jnp.int32)
        target = jnp.where(route >= me, route - me, route - me + members) * slots + slot
        index = lax.broadcasted_iota(jnp.int32, (members * slots, rows), 0)
        send_ref[batch] = (index == target).astype(float32).astype(bfloat)

        route = column_ref[batch]
        picked = lax.broadcasted_iota(jnp.int32, (rows, names), 1) == route
        earlier = count_earlier(picked.astype(float32).astype(bfloat), 1)
        slot = jnp.sum(jnp.where(picked, earlier, 0.0), axis=1, keepdims=True).astype(jnp.int32)
        target = jnp.where(route >= me, route - me, route - me + members) * slots + slot
        index = lax.broadcasted_iota(jnp.int32, (rows, members * slots), 1)
        back_ref[batch] = (index == target).astype(float32).astype(bfloat)

        offsets = place_ref[batch] - members * lax.broadcasted_iota(
            jnp.int32, (rows, members), 0
        )
        lane = lax.broadcasted_iota(jnp.int32, (rows, members), 1)
        for step in range(members):
            owner = jnp.where(me >= step, me - step, me - step + members)
            chosen = jnp.sum(jnp.where(lane == owner, offsets, 0), axis=1, keepdims=True)
            offset_ref[batch, :, step : step + 1] = chosen


def row_tables(me, routes, places, after, carried, members, slots):
    batches, rows, _ = routes.shape
    vmem = pl.BlockSpec(memory_space=pltpu.VMEM)
    return pl.pallas_call(
        functools.partial(tables_kernel, members, slots),
        in_specs=[pl.BlockSpec(memory_space=pltpu.SMEM), vmem, vmem, vmem]
        + [pl.BlockSpec(memory_space=pl.ANY)] * 2,
        out_specs=[vmem, vmem, vmem, pl.BlockSpec(memory_space=pl.ANY)],
        out_shape=[
            jax.ShapeDtypeStruct((batches, members * slots, rows), bfloat),
            jax.ShapeDtypeStruct((batches, rows, members * slots), bfloat),
            jax.ShapeDtypeStruct((batches, rows, members), jnp.int32),
            jax.ShapeDtypeStruct(carried.shape, carried.dtype),
        ],
        input_output_aliases={5: 3},
        compiler_params=params(),
        name="row_tables",
    )(
        me,
        routes.reshape(batches, 1, rows),
        routes,
        jnp.transpose(places, (0, 2, 1)),
        after,
        carried,
    )


def member_rows(ordered, offset_ref, step, members):
    count = ordered.shape[0] // members
    rows = ordered[:count]
    for place in range(1, members):
        rows = jnp.where(
            offset_ref[0, :, step : step + 1] == place,
            ordered[place * count : (place + 1) * count],
            rows,
        )
    return rows


def middle_kernel(
    members,
    experts,
    me_ref,
    joined_ref,
    offset_ref,
    weight_ref,
    rows_ref,
    grad_ref,
    gain_ref,
    router_ref,
    route_ref,
    send_ref,
    after_ref,
    *refs,
):
    received = refs[: members - 1]
    mid_ref, normed_ref, probs_ref = refs[members - 1 : members + 2]
    out_refs = refs[members + 2 :]
    me = me_ref[0]
    span = joined_ref.shape[1]
    width = rows_ref.shape[2]
    slots = out_refs[0].shape[0]
    mid = rows_ref[0].astype(float32)
    for step in range(members):
        owner = jnp.where(me >= step, me - step, me - step + members)
        part = (
            member_rows(joined_ref[...], offset_ref, 0, members)
            if step == 0
            else received[step - 1][...]
        )
        mid = mid + dot_nn(part, weight_ref[pl.ds(pl.multiple_of(owner * span, span), span), :])
    mid_ref[...] = mid
    normed = norm_rows(mid, gain_ref[...]).astype(bfloat)
    normed_ref[...] = normed
    logits = dot_nn(normed, router_ref[...])
    lane = lax.broadcasted_iota(jnp.int32, logits.shape, 1)
    logits = jnp.where(lane < experts, logits, -jnp.inf)
    shifted = jnp.exp(logits - jnp.max(logits, axis=-1, keepdims=True))
    probs = shifted / jnp.sum(shifted, axis=-1, keepdims=True)
    probs_ref[...] = probs
    gate = jnp.sum(jnp.where(lane == route_ref[0], probs, 0.0), axis=1, keepdims=True)
    grad_expert = (gate * grad_ref[0].astype(float32)).astype(bfloat)
    tokens = dot_nn(send_ref[0], normed).astype(bfloat)
    grads = dot_nn(send_ref[0], grad_expert).astype(bfloat)
    for step in range(members):
        rows = slice(step * slots, (step + 1) * slots)
        out_refs[step][:, :width] = tokens[rows]
        out_refs[step][:, width:] = grads[rows]


def middle(
    batch, me, joined, received, offsets, weight, rows, grads, gain, router, routes, send, after
):
    members = offsets.shape[2]
    experts = members
    _, count, width = rows.shape
    slots = send.shape[1] // members
    row_spec = pl.BlockSpec((1, count, width), lambda i: (batch, 0, 0))

    def full(array):
        return pl.BlockSpec(array.shape, lambda i: (0,) * array.ndim)

    def own(array):
        return pl.BlockSpec((1,) + array.shape[1:], lambda i: (batch, 0, 0))

    out_shape = [
        jax.ShapeDtypeStruct((count, width), float32),
        jax.ShapeDtypeStruct((count, width), bfloat),
        jax.ShapeDtypeStruct((count, tile), float32),
    ] + [jax.ShapeDtypeStruct((slots, 2 * width), bfloat)] * members
    outs = pl.pallas_call(
        functools.partial(middle_kernel, members, experts),
        grid=(1,),
        in_specs=[
            pl.BlockSpec(memory_space=pltpu.SMEM),
            full(joined),
            own(offsets),
            full(weight),
            row_spec,
            row_spec,
            full(gain),
            full(router),
            own(routes),
            own(send),
            pl.BlockSpec(memory_space=pl.ANY),
        ]
        + [full(part) for part in received],
        out_specs=[full(shape) for shape in out_shape],
        out_shape=out_shape,
        compiler_params=params(),
        cost_estimate=pl.CostEstimate(
            flops=48 * count * width * width, bytes_accessed=12 * count * width, transcendentals=0
        ),
        name="middle",
    )(me, joined, offsets, weight, rows, grads, gain, router, routes, send, after, *received)
    return outs[0], outs[1], outs[2], list(outs[3:])


def second_kernel(
    members,
    experts,
    aliased,
    me_ref,
    back_ref,
    mid_ref,
    normed_ref,
    probs_ref,
    grad_ref,
    route_ref,
    gain_ref,
    router_ref,
    weight_ref,
    after_ref,
    *refs,
):
    returned = refs[:members]
    outs = refs[members + aliased :]
    layer_ref, grad_mid_ref, grad_attn_ref, gain_out_ref, router_out_ref = outs[:5]
    part_refs = outs[5:]
    me = me_ref[0]
    width = mid_ref.shape[1]
    span = part_refs[0].shape[1]
    blocks = jnp.concatenate([ref[...] for ref in returned], axis=0)
    home = dot_nn(back_ref[0], blocks)
    expert_back = home[:, :width]
    mid = mid_ref[...]
    gain = gain_ref[...]
    grads = grad_ref[0].astype(float32)
    probs = probs_ref[...]
    lane = lax.broadcasted_iota(jnp.int32, probs.shape, 1)
    picked = lane == route_ref[0]
    gate = jnp.sum(jnp.where(picked, probs, 0.0), axis=1, keepdims=True)
    layer_ref[0] = (mid + gate * expert_back).astype(bfloat)
    grad_gate = jnp.sum(grads * expert_back, axis=1, keepdims=True)
    grad_logits = (grad_gate * gate) * (jnp.where(picked, 1.0, 0.0) - probs)
    grad_logits = jnp.where(lane < experts, grad_logits, 0.0)
    grad_normed = home[:, width:]
    for name in range(experts):
        grad_normed = grad_normed + grad_logits[:, name : name + 1] * router_ref[name : name + 1, :]
    upper = grad_logits.astype(bfloat)
    lower = (grad_logits - upper.astype(float32)).astype(bfloat)
    normed = normed_ref[...]
    router_out_ref[...] = dot_tn(upper, normed) + dot_tn(lower, normed)
    grad_resid, terms = norm_back(mid, gain, grad_normed)
    gain_out_ref[...] = jnp.sum(terms, axis=0, keepdims=True)
    grad_mid = grads + grad_resid
    grad_mid_ref[...] = grad_mid
    grad_attn = grad_mid.astype(bfloat)
    grad_attn_ref[...] = grad_attn
    for step in range(members):
        owner = jnp.where(me >= step, me - step, me - step + members)
        rows = weight_ref[pl.ds(pl.multiple_of(owner * span, span), span), :]
        part_refs[step][...] = dot_nt(grad_attn, rows).astype(bfloat)


def second_back(
    batch,
    batches,
    me,
    returned,
    back,
    mid,
    normed,
    probs,
    grads,
    routes,
    gain,
    router,
    weight,
    members,
    span,
    after,
    layer,
):
    count, width = mid.shape
    grad_spec = pl.BlockSpec((1, count, width), lambda i: (batch, 0, 0))

    def full(array):
        return pl.BlockSpec(array.shape, lambda i: (0,) * array.ndim)

    def own(array):
        return pl.BlockSpec((1,) + array.shape[1:], lambda i: (batch, 0, 0))

    rest = [
        jax.ShapeDtypeStruct((count, width), float32),
        jax.ShapeDtypeStruct((count, width), bfloat),
        jax.ShapeDtypeStruct((1, width), float32),
        jax.ShapeDtypeStruct((tile, width), float32),
    ] + [jax.ShapeDtypeStruct((count, span), bfloat)] * members
    aliased = 0 if layer is None else 1
    outs = pl.pallas_call(
        functools.partial(second_kernel, members, members, aliased),
        grid=(1,),
        in_specs=[
            pl.BlockSpec(memory_space=pltpu.SMEM),
            own(back),
            full(mid),
            full(normed),
            full(probs),
            grad_spec,
            own(routes),
            full(gain),
            full(router),
            full(weight),
            pl.BlockSpec(memory_space=pl.ANY),
        ]
        + [full(part) for part in returned]
        + [pl.BlockSpec(memory_space=pl.ANY)] * aliased,
        out_specs=[grad_spec] + [full(shape) for shape in rest],
        out_shape=[jax.ShapeDtypeStruct((batches, count, width), bfloat)] + rest,
        input_output_aliases={11 + members: 0} if aliased else {},
        compiler_params=params(),
        cost_estimate=pl.CostEstimate(
            flops=6 * count * width * width, bytes_accessed=12 * count * width, transcendentals=0
        ),
        name="second_back",
    )(
        me,
        back,
        mid,
        normed,
        probs,
        grads,
        routes,
        gain,
        router,
        weight,
        after,
        *returned,
        *([] if layer is None else [layer]),
    )
    return outs[0], outs[1], outs[2], outs[3], outs[4], list(outs[5:])


def first_kernel(
    members,
    pairs,
    grads_ref,
    weight_ref,
    offset_ref,
    after_ref,
    *out_refs,
):
    width = out_refs[0].shape[1]
    depth = weight_ref.shape[1] // pairs
    lanes = weight_ref.shape[2]
    total = None
    for pair in range(pairs):
        weight = weight_ref[:, pair * depth : (pair + 1) * depth, :].reshape(width, lanes)
        term = dot_nt(grads_ref[:, pair * lanes : (pair + 1) * lanes], weight)
        total = term if total is None else total + term
    for step in range(members):
        out_refs[step][...] = member_rows(total, offset_ref, step, members).astype(
            out_refs[step].dtype
        )


def first_back(batch, grads, packed, pairs, width, offsets, after):
    members = offsets.shape[2]
    count = grads.shape[0]
    lanes = packed.shape[2]
    weight_shape = (packed.shape[0], pairs * width // packed.shape[0], lanes)
    own = jax.ShapeDtypeStruct((count // members, width), float32)
    sent = jax.ShapeDtypeStruct((count // members, width), bfloat)
    out_shape = [own] + [sent] * (members - 1)

    def full(array):
        return pl.BlockSpec(array.shape, lambda i: (0,) * len(array.shape))

    outs = pl.pallas_call(
        functools.partial(first_kernel, members, pairs),
        grid=(1,),
        in_specs=[
            full(grads),
            pl.BlockSpec(weight_shape, lambda i: (0, 0, 0)),
            pl.BlockSpec((1,) + offsets.shape[1:], lambda i: (batch, 0, 0)),
            pl.BlockSpec(memory_space=pl.ANY),
        ],
        out_specs=[full(shape) for shape in out_shape],
        out_shape=out_shape,
        compiler_params=params(),
        cost_estimate=pl.CostEstimate(
            flops=2 * count * width * lanes * pairs,
            bytes_accessed=8 * count * width,
            transcendentals=0,
        ),
        name="first_back",
    )(grads, packed, offsets, after)
    return outs[0], list(outs[1:])


def finish_kernel(received, own_ref, rows_ref, gain_ref, mid_ref, *refs):
    total = own_ref[...]
    for ref in refs[:received]:
        total = total + ref[...].astype(float32)
    grad, _ = norm_back(rows_ref[0].astype(float32), gain_ref[...], total)
    refs[-1][0] = mid_ref[...] + grad


def finish(batch, own, received, rows, gain, mid, buffer):
    batches, count, width = rows.shape
    row_spec = pl.BlockSpec((1, count, width), lambda i: (batch, 0, 0))

    def full(array):
        return pl.BlockSpec(array.shape, lambda i: (0,) * array.ndim)

    operands = [own, rows, gain, mid] + received
    in_specs = [full(own), row_spec, full(gain), full(mid)] + [full(part) for part in received]
    aliases = {}
    if buffer is not None:
        aliases = {len(operands): 0}
        operands.append(buffer)
        in_specs.append(pl.BlockSpec(memory_space=pl.ANY))
    return pl.pallas_call(
        functools.partial(finish_kernel, len(received)),
        grid=(1,),
        in_specs=in_specs,
        out_specs=row_spec,
        out_shape=jax.ShapeDtypeStruct((batches, count, width), float32),
        input_output_aliases=aliases,
        compiler_params=params(),
        name="finish",
    )(*operands)


def dense_kernel(batches, weighted, blocks, after_ref, *refs):
    out_ref = refs[2 * batches + weighted]
    left = jnp.concatenate([ref[...] for ref in refs[:batches]], axis=0)
    right = jnp.concatenate([ref[...] for ref in refs[batches : 2 * batches]], axis=0)
    total = dot_tn(left, right)
    depth = out_ref.shape[1] // blocks
    lanes = out_ref.shape[2]
    term = None
    for block in range(blocks):
        part = total[:, block * lanes : (block + 1) * lanes]
        rows = slice(block * depth, (block + 1) * depth)
        out_ref[:, rows, :] = part.astype(bfloat).reshape(out_ref.shape[0], depth, lanes)
        if weighted:
            weight = refs[2 * batches][:, rows, :].reshape(part.shape).astype(float32)
            term = part * weight if term is None else term + part * weight
    if weighted:
        refs[-1][...] = jnp.sum(term, axis=1, keepdims=True)


def dense_grad(left, right, lanes, shards, direct, after, packed=None):
    batches = len(left)
    count, width = left[0].shape
    columns = right[0].shape[1]
    blocks = columns // lanes
    depth = width // shards
    steps = 2 if direct and width % (2 * tile) == 0 and shards % 2 == 0 else 1
    outer = shards // steps if direct else 1
    inner = depth if direct else width
    weighted = 0 if packed is None else 1
    outs = pl.pallas_call(
        functools.partial(dense_kernel, batches, weighted, blocks),
        grid=(steps,),
        in_specs=[pl.BlockSpec(memory_space=pl.ANY)]
        + [pl.BlockSpec((count, width // steps), lambda i: (0, i))] * batches
        + [pl.BlockSpec((count, columns), lambda i: (0, 0))] * batches
        + [pl.BlockSpec((outer, blocks * inner, lanes), lambda i: (i, 0, 0))] * weighted,
        out_specs=[pl.BlockSpec((outer, blocks * inner, lanes), lambda i: (i, 0, 0))]
        + [pl.BlockSpec((width // steps, 1), lambda i: (i, 0))] * weighted,
        out_shape=[jax.ShapeDtypeStruct((outer * steps, blocks * inner, lanes), bfloat)]
        + [jax.ShapeDtypeStruct((width, 1), float32)] * weighted,
        compiler_params=params(),
        cost_estimate=pl.CostEstimate(
            flops=2 * batches * count * width * columns,
            bytes_accessed=2 * batches * count * width,
            transcendentals=0,
        ),
        name="dense_grad",
    )(after, *left, *right, *([packed] if weighted else []))
    out = outs[0]
    if not direct:
        out = jnp.transpose(out.reshape(blocks, shards, depth, lanes), (1, 0, 2, 3))
        out = out.reshape(shards, blocks * depth, lanes)
    return (out, outs[1]) if weighted else out


def segment_of(positions, ends):
    segment = jnp.zeros(positions.shape, jnp.int32)
    for end in ends:
        segment = segment + (positions >= end).astype(jnp.int32)
    return segment


def masked_heads(rows, lane, per, head_dim):
    parts = []
    for sub in range(per):
        inside = (lane >= sub * head_dim) & (lane < (sub + 1) * head_dim)
        parts.append(jnp.where(inside, rows, jnp.zeros_like(rows)))
    return jnp.concatenate(parts, axis=0)


def joined_heads(rows, lane, per, head_dim):
    joined = rows[:tile]
    for sub in range(1, per):
        inside = (lane >= sub * head_dim) & (lane < (sub + 1) * head_dim)
        joined = jnp.where(inside, rows[sub * tile : (sub + 1) * tile], joined)
    return joined


def attend_kernel(
    stride,
    head_dim,
    far_ref,
    ends_ref,
    q_ref,
    k_ref,
    v_ref,
    bias_ref,
    after_ref,
    probs_ref,
    out_ref,
    inv_ref,
):
    pair = pl.program_id(0)
    rows_all = q_ref.shape[0]
    rows_part = rows_all // stride
    tiles = rows_part // tile
    reach = near_shift(tiles)
    per = tile // head_dim
    lane = lax.broadcasted_iota(jnp.int32, (tile, tile), 1)
    ends = [ends_ref[idx] for idx in range(ends_ref.shape[0])]
    keys_t = k_ref[...].T
    lane_row = lax.broadcasted_iota(jnp.int32, (1, tile), 1)
    row_column = lax.broadcasted_iota(jnp.int32, (tile, 1), 0)
    key_segments = [
        segment_of(stride * (col * tile + lane_row) + part, ends)
        for part in range(stride)
        for col in range(tiles)
    ]
    for mine in range(stride):
        for block in range(tiles):
            begin = mine * rows_part + block * tile
            rows = slice(begin, begin + tile)
            segment = segment_of(stride * (block * tile + row_column) + mine, ends)
            raw = dot_nn(masked_heads(q_ref[rows, :], lane, per, head_dim), keys_t)
            stacked = []
            inverses = []
            for sub in range(per):
                head = pair * per + sub
                pieces = []
                top = None
                for part in range(stride):
                    for col in range(tiles):
                        start = (part * tiles + col) * tile
                        piece = raw[sub * tile : (sub + 1) * tile, start : start + tile]
                        shift = col - block
                        if shift < -reach:
                            piece = piece + far_ref[0, head]
                        elif shift > reach:
                            piece = piece + far_ref[1, head]
                        else:
                            columns = slice((shift + reach) * tile, (shift + reach + 1) * tile)
                            piece = piece + bias_ref[sub, part - mine + stride - 1, :, columns]
                        same = key_segments[part * tiles + col] == segment
                        piece = jnp.where(same, piece, masked_score)
                        pieces.append(piece)
                        top = piece if top is None else jnp.maximum(top, piece)
                row_max = jnp.max(top, axis=-1, keepdims=True)
                total = None
                for idx, piece in enumerate(pieces):
                    piece = jnp.exp(piece - row_max)
                    total = piece if total is None else total + piece
                    pieces[idx] = piece.astype(bfloat)
                kept = jnp.concatenate(pieces, axis=1)
                probs_ref[sub, rows, :] = kept
                stacked.append(kept)
                inverses.append(1.0 / jnp.sum(total, axis=-1, keepdims=True))
            result = dot_nn(jnp.concatenate(stacked, axis=0), v_ref[...])
            inverse = jnp.broadcast_to(inverses[0], (tile, tile))
            for sub in range(1, per):
                inside = (lane >= sub * head_dim) & (lane < (sub + 1) * head_dim)
                inverse = jnp.where(inside, inverses[sub], inverse)
            out_ref[rows, :] = (joined_heads(result, lane, per, head_dim) * inverse).astype(bfloat)
            inv_ref[rows, :] = inverse


def kind_specs(rows_all):
    return [
        pl.BlockSpec((rows_all, tile), lambda i, kind=kind: (0, 3 * i + kind)) for kind in range(3)
    ]


def attend(qkv, ends, bias, far, after, head_dim, stride):
    rows_all, span = qkv.shape[0], qkv.shape[1] // 3
    per = tile // head_dim
    heads = span // head_dim
    row_spec = pl.BlockSpec((rows_all, tile), lambda i: (0, i))
    return pl.pallas_call(
        functools.partial(attend_kernel, stride, head_dim),
        grid=(span // tile,),
        in_specs=[
            pl.BlockSpec(memory_space=pltpu.SMEM),
            pl.BlockSpec(memory_space=pltpu.SMEM),
            *kind_specs(rows_all),
            pl.BlockSpec((per,) + bias.shape[1:], lambda i: (i, 0, 0, 0)),
            pl.BlockSpec(memory_space=pl.ANY),
        ],
        out_specs=[
            pl.BlockSpec((per, rows_all, rows_all), lambda i: (i, 0, 0)),
            row_spec,
            row_spec,
        ],
        out_shape=[
            jax.ShapeDtypeStruct((heads, rows_all, rows_all), bfloat),
            jax.ShapeDtypeStruct((rows_all, span), bfloat),
            jax.ShapeDtypeStruct((rows_all, span), float32),
        ],
        compiler_params=params(),
        cost_estimate=pl.CostEstimate(
            flops=16 * rows_all * rows_all * span,
            bytes_accessed=2 * heads * rows_all * rows_all,
            transcendentals=heads * rows_all * rows_all,
        ),
        name="attend",
    )(far, ends, qkv, qkv, qkv, bias, after)


def attend_back_kernel(
    stride,
    head_dim,
    scale,
    carried,
    probs_ref,
    out_ref,
    inv_ref,
    q_ref,
    k_ref,
    v_ref,
    offset_ref,
    after_ref,
    *refs,
):
    grad_refs = refs[:stride]
    dqkv_ref, dbias_ref, dfar_ref, ds_ref, grads_ref = refs[-5:]
    rows_all = q_ref.shape[0]
    rows_part = rows_all // stride
    tiles = rows_part // tile
    reach = near_shift(tiles)
    per = tile // head_dim
    lane = lax.broadcasted_iota(jnp.int32, (tile, tile), 1)
    queries_t = q_ref[...].T
    values_t = v_ref[...].T
    for place in range(stride):
        span = slice(place * rows_part, (place + 1) * rows_part)
        rows = grad_refs[0][...]
        for step in range(1, stride):
            rows = jnp.where(offset_ref[0, :, step : step + 1] == place, grad_refs[step][...], rows)
        grads_ref[span, :] = (rows.astype(float32) * inv_ref[span, :]).astype(bfloat)
    grads_t = grads_ref[...].T
    if carried:
        dbias_ref[...] = refs[stride][...]
        dfar_ref[...] = refs[stride + 1][...]
    else:
        dbias_ref[...] = jnp.zeros_like(dbias_ref)
        dfar_ref[...] = jnp.zeros_like(dfar_ref)
    for mine in range(stride):
        for block in range(tiles):
            begin = mine * rows_part + block * tile
            rows = slice(begin, begin + tile)
            own = masked_heads(grads_ref[rows, :], lane, per, head_dim)
            outs = out_ref[rows, :].astype(float32)
            raw = dot_nn(own, values_t)
            stacked = []
            for sub in range(per):
                span = slice(sub * tile, (sub + 1) * tile)
                row_dot = jnp.sum(own[span].astype(float32) * outs, axis=-1, keepdims=True)
                pieces = []
                for part in range(stride):
                    for col in range(tiles):
                        start = (part * tiles + col) * tile
                        piece = probs_ref[sub, rows, start : start + tile].astype(float32) * (
                            raw[span, start : start + tile] - row_dot
                        )
                        shift = col - block
                        if shift < -reach:
                            dfar_ref[sub, 0] += piece
                        elif shift > reach:
                            dfar_ref[sub, 1] += piece
                        else:
                            columns = slice((shift + reach) * tile, (shift + reach + 1) * tile)
                            dbias_ref[sub, part - mine + stride - 1, :, columns] += piece
                        pieces.append(piece.astype(bfloat))
                low_grads = jnp.concatenate(pieces, axis=1)
                ds_ref[sub, rows, :] = low_grads
                stacked.append(low_grads)
            result = dot_nn(jnp.concatenate(stacked, axis=0), k_ref[...]) * scale
            dqkv_ref[rows, :tile] = joined_heads(result, lane, per, head_dim).astype(bfloat)
    dk_parts = []
    dv_parts = []
    for sub in range(per):
        dims = slice(sub * head_dim, (sub + 1) * head_dim)
        dk_parts.append(dot_nn(queries_t[dims, :], ds_ref[sub]))
        dv_parts.append(dot_nn(grads_t[dims, :], probs_ref[sub]))
    dqkv_ref[:, tile : 2 * tile] = jnp.concatenate(dk_parts, axis=0).T.astype(bfloat)
    dqkv_ref[:, 2 * tile :] = jnp.concatenate(dv_parts, axis=0).T.astype(bfloat)


def attend_back(
    batch, probs, grads, outs, inverse, qkv, offsets, after, sums, head_dim, stride, bias_shape
):
    rows_all, span = outs.shape
    per = tile // head_dim
    heads = span // head_dim
    row_spec = pl.BlockSpec((rows_all, tile), lambda i: (0, i))
    part_spec = pl.BlockSpec((rows_all // stride, tile), lambda i: (0, i))
    sum_specs = [
        pl.BlockSpec((per,) + bias_shape[1:], lambda i: (i, 0, 0, 0)),
        pl.BlockSpec((per, 2, tile, tile), lambda i: (i, 0, 0, 0)),
    ]
    carried = len(sums) > 0
    first = 8 + stride
    return pl.pallas_call(
        functools.partial(attend_back_kernel, stride, head_dim, head_dim ** (-0.5), carried),
        grid=(span // tile,),
        in_specs=[pl.BlockSpec((per, rows_all, rows_all), lambda i: (i, 0, 0))]
        + [row_spec] * 2
        + kind_specs(rows_all)
        + [pl.BlockSpec((1,) + offsets.shape[1:], lambda i: (batch, 0, 0))]
        + [pl.BlockSpec(memory_space=pl.ANY)]
        + [part_spec] * stride
        + (sum_specs if carried else []),
        out_specs=[pl.BlockSpec((rows_all, 3 * tile), lambda i: (0, i))] + sum_specs,
        out_shape=[
            jax.ShapeDtypeStruct((rows_all, 3 * span), bfloat),
            jax.ShapeDtypeStruct(bias_shape, float32),
            jax.ShapeDtypeStruct((heads, 2, tile, tile), float32),
        ],
        scratch_shapes=[
            pltpu.VMEM((per, rows_all, rows_all), bfloat),
            pltpu.VMEM((rows_all, tile), bfloat),
        ],
        input_output_aliases={first: 1, first + 1: 2} if carried else {},
        compiler_params=params(),
        cost_estimate=pl.CostEstimate(
            flops=32 * rows_all * rows_all * span,
            bytes_accessed=2 * heads * rows_all * rows_all,
            transcendentals=0,
        ),
        name="attend_back",
    )(probs, outs, inverse, qkv, qkv, qkv, offsets, after, *grads, *sums)


def add_kernel(after_ref, *refs):
    out_ref = refs[-1]
    start = 0
    for left_ref, right_ref in zip(refs[:-1:2], refs[1:-1:2]):
        rows = left_ref.shape[1]
        out_ref[:, start : start + rows] = (
            left_ref[...].astype(float32) + right_ref[...].astype(float32)
        ).astype(bfloat)
        start += rows


def add_after(after, *operands):
    vmem = pl.BlockSpec(memory_space=pltpu.VMEM)
    outer, _, lanes = operands[0].shape
    rows = sum(operand.shape[1] for operand in operands[::2])
    return pl.pallas_call(
        add_kernel,
        in_specs=[pl.BlockSpec(memory_space=pl.ANY)] + [vmem] * len(operands),
        out_specs=vmem,
        out_shape=jax.ShapeDtypeStruct((outer, rows, lanes), bfloat),
        compiler_params=params(),
        name="add_after",
    )(after, *operands)


def order_kernel(count, place_ref, *refs):
    out_ref = refs[count + 1]
    for place in range(count):
        rows = refs[0][0]
        for step in range(1, count):
            rows = jnp.where(place_ref[0, :, step : step + 1] == place, refs[step][0], rows)
        out_ref[0, place] = rows


def order_rows(parts, offsets, carried):
    batches, rows, width = parts[0].shape
    count = len(parts)
    part_spec = pl.BlockSpec((1, rows, width), lambda i: (i, 0, 0))
    return pl.pallas_call(
        functools.partial(order_kernel, count),
        grid=(batches,),
        in_specs=[pl.BlockSpec((1, rows, count), lambda i: (i, 0, 0))]
        + [part_spec] * count
        + [pl.BlockSpec(memory_space=pl.ANY)],
        out_specs=[
            pl.BlockSpec((1, count, rows, width), lambda i: (i, 0, 0, 0)),
            pl.BlockSpec(memory_space=pl.ANY),
        ],
        out_shape=[
            jax.ShapeDtypeStruct((batches, count, rows, width), bfloat),
            jax.ShapeDtypeStruct(carried.shape, carried.dtype),
        ],
        input_output_aliases={count + 1: 1},
        compiler_params=params(),
        name="order_rows",
    )(offsets, *parts, carried)


def expert_kernel(
    count, slots, width, inner_ref, outer_ref, after_ref, *refs
):
    blocks = refs[:count]
    results = refs[count : 2 * count]
    hidden_ref, grad_pre_ref, rows_ref, grads_ref, sum_ref, back_ref = refs[2 * count :]
    turn = pl.program_id(0)

    @pl.when(turn == 0)
    def _():
        for idx in range(count):
            rows = slice(idx * slots, (idx + 1) * slots)
            rows_ref[rows, :] = blocks[idx][:, :width]
            grads_ref[rows, :] = blocks[idx][:, width:]

    inner = inner_ref[...].reshape(width, width)
    outer = outer_ref[...].reshape(width, width)
    rows = rows_ref[...]
    grads = grads_ref[...]
    root = 0.7978845608028654
    pre = dot_nn(rows, inner)
    grad_hidden = dot_nt(grads, outer)
    square = pre * pre
    curve = jnp.tanh(root * pre * (1.0 + 0.044715 * square))
    half = 0.5 * (1.0 + curve)
    slope = half + (0.5 * root) * pre * (1.0 - curve * curve) * (1.0 + 0.134145 * square)
    hidden_ref[...] = (pre * half).astype(bfloat)
    grad_pre_ref[...] = (grad_hidden * slope).astype(bfloat)
    product = dot_nn(hidden_ref[...], outer)
    product_back = dot_nt(grad_pre_ref[...], inner)

    @pl.when(turn == 0)
    def _():
        sum_ref[...] = product
        back_ref[...] = product_back

    @pl.when(turn > 0)
    def _():
        sum_ref[...] += product
        back_ref[...] += product_back

    @pl.when(turn == pl.num_programs(0) - 1)
    def _():
        for idx in range(count):
            span = slice(idx * slots, (idx + 1) * slots)
            results[idx][:, :width] = sum_ref[span, :].astype(bfloat)
            results[idx][:, width:] = back_ref[span, :].astype(bfloat)


def run_expert(weights, blocks, width, after):
    (inner, inner_spec), (outer, outer_spec), turns = weights
    count = len(blocks)
    slots = blocks[0].shape[0]
    total = count * slots
    whole = pl.BlockSpec((slots, 2 * width), lambda i: (0, 0))
    chunk = pl.BlockSpec((total, width), lambda i: (0, i))
    outs = pl.pallas_call(
        functools.partial(expert_kernel, count, slots, width),
        grid=(turns,),
        in_specs=[inner_spec, outer_spec, pl.BlockSpec(memory_space=pl.ANY)] + [whole] * count,
        out_specs=[whole] * count + [chunk, chunk],
        out_shape=[jax.ShapeDtypeStruct((slots, 2 * width), bfloat)] * count
        + [jax.ShapeDtypeStruct((total, turns * width), bfloat)] * 2,
        scratch_shapes=[
            pltpu.VMEM((total, width), bfloat),
            pltpu.VMEM((total, width), bfloat),
            pltpu.VMEM((total, width), float32),
            pltpu.VMEM((total, width), float32),
        ],
        compiler_params=params(),
        cost_estimate=pl.CostEstimate(
            flops=8 * total * width * width * turns,
            bytes_accessed=4 * width * width * turns,
            transcendentals=total * width * turns,
        ),
        name="run_expert",
    )(inner, outer, after, *blocks)
    return outs[:count], outs[count], outs[count + 1]


def expert_grad_kernel(batches, count, slots, width, second, *refs):
    groups = [refs[idx * count : (idx + 1) * count] for idx in range(batches)]
    wide = refs[batches * count : batches * count + batches]
    out_ref, rows_ref = refs[-2], refs[-1]
    half = slice(width, 2 * width) if second else slice(0, width)

    @pl.when(pl.program_id(0) == 0)
    def _():
        for batch in range(batches):
            for idx in range(count):
                start = (batch * count + idx) * slots
                rows_ref[start : start + slots, :] = groups[batch][idx][:, half]

    rows = rows_ref[...]
    columns = jnp.concatenate([ref[...] for ref in wide], axis=0)
    total = dot_tn(columns, rows) if second else dot_tn(rows, columns)
    out_ref[...] = total.astype(bfloat).reshape(out_ref.shape)


def expert_grad(groups, wide, width, second, out_shape, out_spec, after, buffer=None):
    batches = len(groups)
    count = len(groups[0])
    slots = groups[0][0].shape[0]
    total = count * slots
    turns = wide[0].shape[1] // width
    kernel = functools.partial(expert_grad_kernel, batches, count, slots, width, second)
    in_specs = [pl.BlockSpec((slots, 2 * width), lambda i: (0, 0))] * (batches * count)
    in_specs = in_specs + [pl.BlockSpec((total, width), lambda i: (0, i))] * batches
    operands = [block for group in groups for block in group] + list(wide)
    aliases = {}
    carried = [after]
    if buffer is not None:
        carried = [buffer, after]
        aliases = {0: 0}
    skipped = len(carried)
    in_specs = [pl.BlockSpec(memory_space=pl.ANY)] * skipped + in_specs
    operands = carried + operands

    def body(*refs):
        kernel(*refs[skipped:])

    return pl.pallas_call(
        body,
        grid=(turns,),
        in_specs=in_specs,
        out_specs=out_spec,
        out_shape=jax.ShapeDtypeStruct(out_shape, bfloat),
        scratch_shapes=[pltpu.VMEM((batches * total, width), bfloat)],
        input_output_aliases=aliases,
        compiler_params=params(),
        cost_estimate=pl.CostEstimate(
            flops=2 * batches * total * width * width * turns,
            bytes_accessed=4 * width * width * turns,
            transcendentals=0,
        ),
        name="expert_grad_outer" if second else "expert_grad_inner",
    )(*operands)


def on_device(
    hidden_in,
    out_grad,
    places,
    lengths,
    routes,
    norm1_gain,
    w_query,
    w_key,
    w_value,
    w_output,
    rel_table,
    norm2_gain,
    w_router,
    w_in,
    w_out,
):
    batches, rows_own, width = hidden_in.shape
    heads = rel_table.shape[1]
    head_dim = width // heads
    scale = head_dim ** (-0.5)
    shards = lax.axis_size("dp")
    members = lax.axis_size("expert")
    me = lax.axis_index("expert")
    experts = w_router.shape[1]
    hidden_width = w_in.shape[2]
    turns = hidden_width // width
    tiles = rows_own // tile
    rows_group = members * rows_own
    depth = width // shards
    depth_out = hidden_width // shards
    table_rows = rel_table.shape[0]
    capacity = max(2, rows_own * 17 // (experts * 16))
    slots = -(-capacity // 16) * 16
    per = tile // head_dim
    heads_own = per * (-(-heads // (per * members)))
    span = heads_own * head_dim
    pairs = span // tile
    lanes = 3 * tile
    split = width // lanes
    me_row = me.reshape(1)

    def around(step):
        return [(idx, (idx + step) % members) for idx in range(members)]

    def columns_own(weight):
        wide = jnp.pad(weight, ((0, 0), (0, members * span - width)))
        return lax.dynamic_slice_in_dim(wide, me * span, span, axis=1)

    def in_order(parts):
        if members == 2:
            return [
                jnp.where(me == 0, parts[0], parts[1]),
                jnp.where(me == 0, parts[1], parts[0]),
            ]
        stacked = jnp.stack(parts)
        return [stacked[jnp.mod(me - idx, members)] for idx in range(members)]

    hidden_from = [hidden_in] + [
        lax.ppermute(hidden_in, "expert", around(step)) for step in range(1, members)
    ]

    small = jnp.concatenate(
        [
            norm1_gain.reshape(-1),
            norm2_gain.reshape(-1),
            w_router.reshape(-1),
            rel_table.reshape(-1),
        ]
    )
    small_used = small.shape[0]
    small_pad = -(-small_used // (16 * lanes)) * 16
    small = jnp.pad(small, (0, small_pad * lanes - small_used)).reshape(small_pad, lanes)
    kinds = [columns_own(weight) for weight in (w_query, w_key, w_value)]
    first_own = jnp.concatenate(
        [
            jnp.concatenate([kind[:, idx * tile : (idx + 1) * tile] for kind in kinds], axis=1)
            for idx in range(pairs)
        ]
        + [w_output[:, idx * lanes : (idx + 1) * lanes] for idx in range(split)]
        + [small],
        axis=0,
    )
    first = lax.all_gather(first_own, "dp", axis=0, tiled=False)
    inner_parts = [w_in[0, :, idx * width : (idx + 1) * width] for idx in range(turns)]
    second_own = jnp.concatenate(inner_parts + [w_out[0]], axis=0)
    places_in = places[:, 0].reshape(batches, members, rows_own)
    dispatch, collect, offsets, second_own = row_tables(
        me_row, routes, places_in, hidden_from[-1], second_own, members, slots
    )
    second = lax.all_gather(second_own, "dp", axis=0, tiled=False)
    ends = jnp.cumsum(lengths[:, 0], axis=-1)[:, :-1]
    ordered_in, first = order_rows(hidden_from, offsets, first)
    ordered_in = ordered_in.reshape(batches, rows_group, width)

    small_start = (pairs + split) * depth
    small_all = first[:, small_start:].reshape(shards, small_pad * lanes)
    gain_one = small_all[:, :depth].reshape(1, width).astype(float32)
    gain_two = small_all[:, depth : 2 * depth].reshape(1, width).astype(float32)
    router_end = 2 * depth + depth * experts
    router_w = small_all[:, 2 * depth : router_end].reshape(width, experts)
    table = small_all[:, router_end:small_used].reshape(shards * table_rows, heads)
    router_wide = jnp.pad(router_w, ((0, 0), (0, tile - experts)))
    router_t = router_w.astype(float32).T
    output_w = jnp.concatenate(
        [
            first[:, (pairs + idx) * depth : (pairs + idx + 1) * depth].reshape(width, lanes)
            for idx in range(split)
        ],
        axis=1,
    )
    output_w = jnp.pad(output_w, ((0, members * span - width), (0, 0)))

    direct = depth % 16 == 0 and turns * depth == depth_out and shards % turns == 0
    if direct:
        group = shards // turns
        packed = first
        inner_spec = pl.BlockSpec((shards, depth, width), lambda i: (0, i, 0))
        outer_spec = pl.BlockSpec((group, depth_out, width), lambda i: (i, 1, 0))
        weights = ((second, inner_spec), (second, outer_spec), turns)
    else:
        packed = jnp.concatenate(
            [
                first[:, idx * depth : (idx + 1) * depth].reshape(1, width, lanes)
                for idx in range(pairs)
            ],
            axis=1,
        )
        inner_w = second[:, : turns * depth].reshape(shards, turns, depth, width)
        inner_w = jnp.transpose(inner_w, (1, 0, 2, 3)).reshape(turns, width, width)
        outer_w = second[:, turns * depth : turns * depth + depth_out].reshape(
            turns, width, width
        )
        plain = pl.BlockSpec((1, width, width), lambda i: (i, 0, 0))
        weights = ((inner_w, plain), (outer_w, plain), turns)

    table_wide = jnp.pad(table, ((0, 0), (0, members * heads_own - heads)))
    table_own = lax.dynamic_slice_in_dim(table_wide, me * heads_own, heads_own, axis=1)
    bias = bias_tiles(table_own, members, tiles)
    table_f = table_own.astype(float32)
    far = jnp.stack([table_f[levels_all - 1], table_f[2 * levels_all - 1]])

    def send_rows(batch, ordered):
        arrived = []
        for step in range(1, members):
            rows = ordered[:rows_own]
            for place in range(1, members):
                rows = jnp.where(
                    offsets[batch, :, members - step : members - step + 1] == place,
                    ordered[place * rows_own : (place + 1) * rows_own],
                    rows,
                )
            arrived.append(lax.ppermute(rows, "expert", around(step)))
        return arrived

    normed_one = []
    qkv = []
    probs = []
    outs = []
    inverses = []
    arrived_heads = []
    resid_mid = []
    normed_two = []
    router_probs = []
    blocks = []
    for batch in range(batches):
        normed, packed_rows = project(batch, ordered_in, gain_one, packed, pairs, scale)
        normed_one.append(normed)
        qkv.append(packed_rows)
        kept, joined, inverse = attend(
            packed_rows,
            ends[batch],
            bias,
            far,
            arrived_heads[-1][-1] if arrived_heads else table,
            head_dim,
            members,
        )
        probs.append(kept)
        outs.append(joined)
        inverses.append(inverse)
        arrived_heads.append(send_rows(batch, joined))
    for batch in range(batches):
        mid, normed, chances, outgoing = middle(
            batch,
            me_row,
            outs[batch],
            arrived_heads[batch],
            offsets,
            output_w,
            hidden_in,
            out_grad,
            gain_two,
            router_wide,
            routes,
            dispatch,
            outs[-1],
        )
        blocks.append(
            [outgoing[0]]
            + [
                lax.ppermute(outgoing[step], "expert", around(step))
                for step in range(1, members)
            ]
        )
        resid_mid.append(mid)
        normed_two.append(normed)
        router_probs.append(chances)

    returned = []
    hidden = []
    grad_pre = []
    for batch in range(batches):
        results, hidden_rows, grad_rows = run_expert(
            weights, blocks[batch], width, hidden[-1] if hidden else table
        )
        hidden.append(hidden_rows)
        grad_pre.append(grad_rows)
        returned.append(
            [results[0]]
            + [
                lax.ppermute(results[step], "expert", around(-step))
                for step in range(1, members)
            ]
        )

    if direct:
        buffer_shape = (shards, turns * depth + depth_out, width)
        buffer = expert_grad(
            blocks,
            grad_pre,
            width,
            False,
            buffer_shape,
            pl.BlockSpec((shards, depth, width), lambda i: (0, i, 0)),
            returned[0][-1],
        )
        buffer = expert_grad(
            blocks,
            hidden,
            width,
            True,
            buffer_shape,
            pl.BlockSpec((group, depth_out, width), lambda i: (i, 1, 0)),
            returned[-1][-1],
            buffer,
        )
    else:
        plain_shape = (turns, width, width)
        inner_g = expert_grad(
            blocks, grad_pre, width, False, plain_shape, plain, returned[0][-1]
        )
        outer_g = expert_grad(
            blocks, hidden, width, True, plain_shape, plain, returned[0][-1]
        )
        inner_g = jnp.transpose(inner_g.reshape(turns, shards, depth, width), (1, 0, 2, 3))
        buffer = jnp.concatenate(
            [
                inner_g.reshape(shards, turns * depth, width),
                outer_g.reshape(shards, depth_out, width),
            ],
            axis=1,
        )
    expert_sum = lax.psum_scatter(buffer, "dp", scatter_dimension=0, tiled=False)

    line = shards // 4
    my_shard = lax.axis_index("dp")

    def by_core(dense):
        dense = dense.reshape((line, 2, 2) + dense.shape[1:])
        odd = my_shard % 2 == 1
        sent = jnp.where(odd, dense[:, :, 0], dense[:, :, 1])
        held = jnp.where(odd, dense[:, :, 1], dense[:, :, 0])
        return held, lax.ppermute(sent, "dp", [(idx, idx ^ 1) for idx in range(shards)])

    def by_y(core_parts):
        held, got = core_parts
        odd = (my_shard // 2) % 2 == 1

        def half(idx):
            return held[:, idx].astype(float32) + got[:, idx].astype(float32)

        sent = jnp.where(odd, half(0), half(1)).astype(bfloat)
        kept = jnp.where(odd, half(1), half(0)).astype(bfloat)
        return kept, lax.ppermute(sent, "dp", [(idx, idx ^ 2) for idx in range(shards)])

    layer = None
    grad_mid = []
    grad_attn = []
    grad_heads = []
    grad_gain_two = 0.0
    grad_router = 0.0
    for batch in range(batches):
        layer, mid, attn, gain_terms, router_terms, parts = second_back(
            batch,
            batches,
            me_row,
            returned[batch],
            collect,
            resid_mid[batch],
            normed_two[batch],
            router_probs[batch],
            out_grad,
            routes,
            gain_two,
            router_t,
            output_w,
            members,
            span,
            buffer,
            layer,
        )
        grad_mid.append(mid)
        grad_attn.append(attn)
        grad_gain_two = grad_gain_two + gain_terms
        grad_router = grad_router + router_terms[:experts]
        from_members = [parts[0]] + [
            lax.ppermute(parts[members - step], "expert", around(step))
            for step in range(1, members)
        ]
        grad_heads.append(from_members)

    def own_rows_of(batch):
        joined = outs[batch]
        rows = joined[:rows_own]
        for place in range(1, members):
            rows = jnp.where(
                offsets[batch, :, 0:1] == place,
                joined[place * rows_own : (place + 1) * rows_own],
                rows,
            )
        return rows

    attended = [
        jnp.concatenate(in_order([own_rows_of(batch)] + arrived_heads[batch]), axis=1)[:, :width]
        for batch in range(batches)
    ]
    early_core = by_core(
        dense_grad(attended, grad_attn, lanes, shards, direct, grad_heads[0][-1])
    )
    early = by_y(early_core)
    grad_qkv = []
    sums = []
    for batch in range(batches):
        grads, *sums = attend_back(
            batch,
            probs[batch],
            grad_heads[batch],
            outs[batch],
            inverses[batch],
            qkv[batch],
            offsets,
            buffer if batch == 0 else early_core[1],
            sums,
            head_dim,
            members,
            bias.shape,
        )
        grad_qkv.append(grads)
    grad_bias, grad_far = sums
    grad_dense, weighted = dense_grad(
        normed_one, grad_qkv, lanes, shards, direct, early[1], packed
    )
    grad_gain_one = weighted[:, 0] / gain_one[0]
    late_core = by_core(grad_dense)
    late = by_y(late_core)

    in_grad = None
    for batch in range(batches):
        own_rows, sent = first_back(
            batch,
            grad_qkv[batch],
            packed,
            pairs,
            width,
            offsets,
            late_core[1] if batch == 0 else late[1],
        )
        received = [
            lax.ppermute(rows, "expert", around(-step)) for step, rows in enumerate(sent, 1)
        ]
        in_grad = finish(
            batch, own_rows, received, hidden_in, gain_one, grad_mid[batch], in_grad
        )

    steps = 2 * members - 1
    reach = near_shift(tiles)
    shape = (steps, tile, (2 * reach + 1) * tile)
    delta = (
        members
        * (
            lax.broadcasted_iota(jnp.int32, shape, 2)
            - reach * tile
            - lax.broadcasted_iota(jnp.int32, shape, 1)
        )
        + lax.broadcasted_iota(jnp.int32, shape, 0)
        - (members - 1)
    )
    buckets = shards * table_rows
    onehot = (
        bucket_of(delta)[None] == jnp.arange(buckets, dtype=jnp.int32)[:, None, None, None]
    ).astype(bfloat)
    grad_table = jnp.einsum(
        "hsab,ksab->kh", grad_bias.astype(bfloat), onehot, preferred_element_type=float32
    )
    far_sum = jnp.sum(grad_far, axis=(2, 3))
    grad_table = grad_table.at[levels_all - 1].add(far_sum[:, 0])
    grad_table = grad_table.at[2 * levels_all - 1].add(far_sum[:, 1])
    grad_table = lax.dynamic_update_slice_in_dim(
        jnp.zeros((buckets, members * heads_own), float32), grad_table, me * heads_own, axis=1
    )[:, :heads]

    small_grad = jnp.concatenate(
        [
            grad_gain_one.reshape(shards, depth),
            grad_gain_two.reshape(shards, depth),
            grad_router.T.reshape(shards, depth * experts),
            grad_table.reshape(shards, table_rows * heads),
        ],
        axis=1,
    )
    small_grad = jnp.pad(small_grad, ((0, 0), (0, small_pad * lanes - small_used)))
    small_grad = small_grad.astype(bfloat).reshape(shards, small_pad, lanes)
    little = by_y(by_core(small_grad))
    dense_part = lax.psum_scatter(
        add_after(expert_sum, *late, *little, *early),
        "dp",
        scatter_dimension=0,
        tiled=False,
        axis_index_groups=[[rest + 4 * idx for idx in range(line)] for rest in range(4)],
    )
    parts = [dense_part] + [
        lax.ppermute(dense_part, "expert", around(step)) for step in range(1, members)
    ]
    qkv_parts = [
        part.astype(float32) for part in in_order([part[: pairs * depth] for part in parts])
    ]
    qkv_grads = [
        jnp.concatenate(
            [
                part[pair * depth : (pair + 1) * depth, kind * tile : (kind + 1) * tile]
                for part in qkv_parts
                for pair in range(pairs)
            ],
            axis=1,
        )[:, :width]
        for kind in range(3)
    ]
    rest_sum = sum(part[pairs * depth :].astype(float32) for part in parts)
    out_grad_sum = jnp.concatenate(
        [
            rest_sum[small_pad + idx * depth : small_pad + (idx + 1) * depth]
            for idx in range(split)
        ],
        axis=1,
    )
    small_sum = rest_sum[:small_pad].reshape(-1)

    expert_f = expert_sum.astype(float32)
    inner_sum = jnp.concatenate(
        [expert_f[idx * depth : (idx + 1) * depth] for idx in range(turns)], axis=1
    )[None]
    outer_sum = expert_f[turns * depth :][None]
    return (
        layer,
        in_grad,
        small_sum[:depth],
        qkv_grads[0],
        qkv_grads[1],
        qkv_grads[2],
        out_grad_sum,
        small_sum[router_end:small_used].reshape(table_rows, heads),
        small_sum[depth : 2 * depth],
        small_sum[2 * depth : router_end].reshape(depth, experts),
        inner_sum,
        outer_sum,
    )


def solution(mesh):
    return jax.shard_map(
        on_device,
        mesh=mesh,
        in_specs=(
            P(None, ("dp", "expert"), None),
            P(None, ("dp", "expert"), None),
            P(None, "dp", None),
            P(None, "dp", None),
            P(None, ("dp", "expert"), None),
            P("dp"),
            P("dp", None),
            P("dp", None),
            P("dp", None),
            P("dp", None),
            P("dp", None),
            P("dp"),
            P("dp", None),
            P("expert", "dp", None),
            P("expert", "dp", None),
        ),
        out_specs=(
            P(None, ("dp", "expert"), None),
            P(None, ("dp", "expert"), None),
            P("dp"),
            P("dp", None),
            P("dp", None),
            P("dp", None),
            P("dp", None),
            P("dp", None),
            P("dp"),
            P("dp", None),
            P("expert", "dp", None),
            P("expert", "dp", None),
        ),
        check_vma=False,
    )
```

```python
import functools

import jax
import jax.numpy as jnp
from jax import lax
from jax.experimental import pallas as pl
from jax.experimental.pallas import tpu as pltpu
from jax.sharding import PartitionSpec as P

bucket_edges = (1, 2, 3, 4, 5, 6, 7, 8, 12, 16, 23, 32, 46, 64, 91)
levels_all = len(bucket_edges) + 1
epsilon = 1e-06
masked_score = -1000000000.0
precise = lax.Precision.HIGHEST
float32 = jnp.float32
bfloat = jnp.bfloat16
tile = 128
vmem_bytes = 56 * 1024 * 1024


def params():
    return pltpu.CompilerParams(vmem_limit_bytes=vmem_bytes)


def dot_nn(left, right):
    return lax.dot_general(left, right, (((1,), (0,)), ((), ())), preferred_element_type=float32)


def dot_nt(left, right):
    return lax.dot_general(left, right, (((1,), (1,)), ((), ())), preferred_element_type=float32)


def dot_tn(left, right):
    return lax.dot_general(left, right, (((0,), (0,)), ((), ())), preferred_element_type=float32)


def norm_rows(rows, gain):
    mean_square = jnp.mean(rows * rows, axis=-1, keepdims=True)
    return rows * lax.rsqrt(mean_square + epsilon) * gain


def norm_back(rows, gain, grad):
    scale = lax.rsqrt(jnp.mean(rows * rows, axis=-1, keepdims=True) + epsilon)
    unit = rows * scale
    weighted = grad * gain
    inner = jnp.mean(weighted * unit, axis=-1, keepdims=True)
    return scale * (weighted - unit * inner), grad * unit


def bucket_of(offset):
    distance = jnp.abs(offset)
    levels = jnp.zeros(offset.shape, jnp.int32)
    for edge_value in bucket_edges:
        levels = levels + (distance >= edge_value).astype(jnp.int32)
    return levels + levels_all * (offset > 0).astype(jnp.int32)


def near_shift(tiles):
    return min(1, tiles - 1)


def bias_kernel(stride, reach, table_ref, out_ref):
    row = lax.broadcasted_iota(jnp.int32, (tile, tile), 0)
    lane = lax.broadcasted_iota(jnp.int32, (tile, tile), 1)
    heads = out_ref.shape[0]
    for shift in range(-reach, reach + 1):
        for step in range(2 * stride - 1):
            ids = bucket_of(stride * (tile * shift + lane - row) + step - (stride - 1))
            columns = slice((shift + reach) * tile, (shift + reach + 1) * tile)
            for head in range(heads):
                values = jnp.broadcast_to(table_ref[head : head + 1, :], (tile, tile))
                out_ref[head, step, :, columns] = jnp.take_along_axis(values, ids, axis=1)


def bias_tiles(table, stride, tiles):
    heads = table.shape[1]
    reach = near_shift(tiles)
    lanes = jnp.pad(table.astype(float32).T, ((0, 0), (0, tile - table.shape[0])))
    return pl.pallas_call(
        functools.partial(bias_kernel, stride, reach),
        out_shape=jax.ShapeDtypeStruct(
            (heads, 2 * stride - 1, tile, (2 * reach + 1) * tile), float32
        ),
        compiler_params=params(),
        name="bias_tiles",
    )(lanes)


def project_kernel(pairs, scale, rows_ref, gain_ref, weight_ref, normed_ref, out_ref):
    width = rows_ref.shape[2]
    depth = weight_ref.shape[1] // pairs
    lanes = weight_ref.shape[2]
    normed = norm_rows(rows_ref[0].astype(float32), gain_ref[...]).astype(bfloat)
    normed_ref[...] = normed
    for pair in range(pairs):
        weight = weight_ref[:, pair * depth : (pair + 1) * depth, :].reshape(width, lanes)
        product = dot_nn(normed, weight).astype(bfloat)
        start = pair * lanes
        out_ref[:, start : start + tile] = product[:, :tile] * bfloat(scale)
        out_ref[:, start + tile : start + lanes] = product[:, tile:]


def project(batch, rows, gain, packed, pairs, scale):
    _, count, width = rows.shape
    lanes = packed.shape[2]
    weight_shape = (packed.shape[0], pairs * width // packed.shape[0], lanes)
    step = min(512, count)
    return pl.pallas_call(
        functools.partial(project_kernel, pairs, scale),
        grid=(count // step,),
        in_specs=[
            pl.BlockSpec((1, step, width), lambda i: (batch, i, 0)),
            pl.BlockSpec((1, width), lambda i: (0, 0)),
            pl.BlockSpec(weight_shape, lambda i: (0, 0, 0)),
        ],
        out_specs=[
            pl.BlockSpec((step, width), lambda i: (i, 0)),
            pl.BlockSpec((step, pairs * lanes), lambda i: (i, 0)),
        ],
        out_shape=[
            jax.ShapeDtypeStruct((count, width), bfloat),
            jax.ShapeDtypeStruct((count, pairs * lanes), bfloat),
        ],
        compiler_params=params(),
        cost_estimate=pl.CostEstimate(
            flops=2 * count * width * lanes * pairs,
            bytes_accessed=6 * count * width,
            transcendentals=0,
        ),
        name="project",
    )(rows, gain, packed)


def count_earlier(picked, first_axis):
    size = picked.shape[1 - first_axis]
    row = lax.broadcasted_iota(jnp.int32, (size, size), 0)
    column = lax.broadcasted_iota(jnp.int32, (size, size), 1)
    if first_axis == 0:
        return dot_nn(picked, (row < column).astype(float32).astype(bfloat))
    return dot_nn((column < row).astype(float32).astype(bfloat), picked)


def tables_kernel(
    members,
    slots,
    me_ref,
    row_ref,
    column_ref,
    place_ref,
    after_ref,
    carried_ref,
    send_ref,
    back_ref,
    offset_ref,
    handed_ref,
):
    me = me_ref[0]
    batches, rows = column_ref.shape[0], column_ref.shape[1]
    names = 128
    for batch in range(batches):
        route = row_ref[batch]
        picked = lax.broadcasted_iota(jnp.int32, (names, rows), 0) == route
        earlier = count_earlier(picked.astype(float32).astype(bfloat), 0)
        slot = jnp.sum(jnp.where(picked, earlier, 0.0), axis=0, keepdims=True).astype(jnp.int32)
        target = jnp.where(route >= me, route - me, route - me + members) * slots + slot
        index = lax.broadcasted_iota(jnp.int32, (members * slots, rows), 0)
        send_ref[batch] = (index == target).astype(float32).astype(bfloat)

        route = column_ref[batch]
        picked = lax.broadcasted_iota(jnp.int32, (rows, names), 1) == route
        earlier = count_earlier(picked.astype(float32).astype(bfloat), 1)
        slot = jnp.sum(jnp.where(picked, earlier, 0.0), axis=1, keepdims=True).astype(jnp.int32)
        target = jnp.where(route >= me, route - me, route - me + members) * slots + slot
        index = lax.broadcasted_iota(jnp.int32, (rows, members * slots), 1)
        back_ref[batch] = (index == target).astype(float32).astype(bfloat)

        offsets = place_ref[batch] - members * lax.broadcasted_iota(
            jnp.int32, (rows, members), 0
        )
        lane = lax.broadcasted_iota(jnp.int32, (rows, members), 1)
        for step in range(members):
            owner = jnp.where(me >= step, me - step, me - step + members)
            chosen = jnp.sum(jnp.where(lane == owner, offsets, 0), axis=1, keepdims=True)
            offset_ref[batch, :, step : step + 1] = chosen


def row_tables(me, routes, places, after, carried, members, slots):
    batches, rows, _ = routes.shape
    vmem = pl.BlockSpec(memory_space=pltpu.VMEM)
    return pl.pallas_call(
        functools.partial(tables_kernel, members, slots),
        in_specs=[pl.BlockSpec(memory_space=pltpu.SMEM), vmem, vmem, vmem]
        + [pl.BlockSpec(memory_space=pl.ANY)] * 2,
        out_specs=[vmem, vmem, vmem, pl.BlockSpec(memory_space=pl.ANY)],
        out_shape=[
            jax.ShapeDtypeStruct((batches, members * slots, rows), bfloat),
            jax.ShapeDtypeStruct((batches, rows, members * slots), bfloat),
            jax.ShapeDtypeStruct((batches, rows, members), jnp.int32),
            jax.ShapeDtypeStruct(carried.shape, carried.dtype),
        ],
        input_output_aliases={5: 3},
        compiler_params=params(),
        name="row_tables",
    )(
        me,
        routes.reshape(batches, 1, rows),
        routes,
        jnp.transpose(places, (0, 2, 1)),
        after,
        carried,
    )


def member_rows(ordered, offset_ref, step, members):
    count = ordered.shape[0] // members
    rows = ordered[:count]
    for place in range(1, members):
        rows = jnp.where(
            offset_ref[0, :, step : step + 1] == place,
            ordered[place * count : (place + 1) * count],
            rows,
        )
    return rows


def middle_kernel(
    members,
    experts,
    me_ref,
    joined_ref,
    offset_ref,
    weight_ref,
    rows_ref,
    grad_ref,
    gain_ref,
    router_ref,
    route_ref,
    send_ref,
    after_ref,
    *refs,
):
    received = refs[: members - 1]
    mid_ref, normed_ref, probs_ref = refs[members - 1 : members + 2]
    out_refs = refs[members + 2 :]
    me = me_ref[0]
    span = joined_ref.shape[1]
    width = rows_ref.shape[2]
    slots = out_refs[0].shape[0]
    mid = rows_ref[0].astype(float32)
    for step in range(members):
        owner = jnp.where(me >= step, me - step, me - step + members)
        part = (
            member_rows(joined_ref[...], offset_ref, 0, members)
            if step == 0
            else received[step - 1][...]
        )
        mid = mid + dot_nn(part, weight_ref[pl.ds(pl.multiple_of(owner * span, span), span), :])
    mid_ref[...] = mid
    normed = norm_rows(mid, gain_ref[...]).astype(bfloat)
    normed_ref[...] = normed
    logits = dot_nn(normed, router_ref[...])
    lane = lax.broadcasted_iota(jnp.int32, logits.shape, 1)
    logits = jnp.where(lane < experts, logits, -jnp.inf)
    shifted = jnp.exp(logits - jnp.max(logits, axis=-1, keepdims=True))
    probs = shifted / jnp.sum(shifted, axis=-1, keepdims=True)
    probs_ref[...] = probs
    gate = jnp.sum(jnp.where(lane == route_ref[0], probs, 0.0), axis=1, keepdims=True)
    grad_expert = (gate * grad_ref[0].astype(float32)).astype(bfloat)
    tokens = dot_nn(send_ref[0], normed).astype(bfloat)
    grads = dot_nn(send_ref[0], grad_expert).astype(bfloat)
    for step in range(members):
        rows = slice(step * slots, (step + 1) * slots)
        out_refs[step][:, :width] = tokens[rows]
        out_refs[step][:, width:] = grads[rows]


def middle(
    batch, me, joined, received, offsets, weight, rows, grads, gain, router, routes, send, after
):
    members = offsets.shape[2]
    experts = members
    _, count, width = rows.shape
    slots = send.shape[1] // members
    row_spec = pl.BlockSpec((1, count, width), lambda i: (batch, 0, 0))

    def full(array):
        return pl.BlockSpec(array.shape, lambda i: (0,) * array.ndim)

    def own(array):
        return pl.BlockSpec((1,) + array.shape[1:], lambda i: (batch, 0, 0))

    out_shape = [
        jax.ShapeDtypeStruct((count, width), float32),
        jax.ShapeDtypeStruct((count, width), bfloat),
        jax.ShapeDtypeStruct((count, tile), float32),
    ] + [jax.ShapeDtypeStruct((slots, 2 * width), bfloat)] * members
    outs = pl.pallas_call(
        functools.partial(middle_kernel, members, experts),
        grid=(1,),
        in_specs=[
            pl.BlockSpec(memory_space=pltpu.SMEM),
            full(joined),
            own(offsets),
            full(weight),
            row_spec,
            row_spec,
            full(gain),
            full(router),
            own(routes),
            own(send),
            pl.BlockSpec(memory_space=pl.ANY),
        ]
        + [full(part) for part in received],
        out_specs=[full(shape) for shape in out_shape],
        out_shape=out_shape,
        compiler_params=params(),
        cost_estimate=pl.CostEstimate(
            flops=48 * count * width * width, bytes_accessed=12 * count * width, transcendentals=0
        ),
        name="middle",
    )(me, joined, offsets, weight, rows, grads, gain, router, routes, send, after, *received)
    return outs[0], outs[1], outs[2], list(outs[3:])


def second_kernel(
    members,
    experts,
    aliased,
    me_ref,
    back_ref,
    mid_ref,
    normed_ref,
    probs_ref,
    grad_ref,
    route_ref,
    gain_ref,
    router_ref,
    weight_ref,
    after_ref,
    *refs,
):
    returned = refs[:members]
    outs = refs[members + aliased :]
    layer_ref, grad_mid_ref, grad_attn_ref, gain_out_ref, router_out_ref = outs[:5]
    part_refs = outs[5:]
    me = me_ref[0]
    width = mid_ref.shape[1]
    span = part_refs[0].shape[1]
    blocks = jnp.concatenate([ref[...] for ref in returned], axis=0)
    home = dot_nn(back_ref[0], blocks)
    expert_back = home[:, :width]
    mid = mid_ref[...]
    gain = gain_ref[...]
    grads = grad_ref[0].astype(float32)
    probs = probs_ref[...]
    lane = lax.broadcasted_iota(jnp.int32, probs.shape, 1)
    picked = lane == route_ref[0]
    gate = jnp.sum(jnp.where(picked, probs, 0.0), axis=1, keepdims=True)
    layer_ref[0] = (mid + gate * expert_back).astype(bfloat)
    grad_gate = jnp.sum(grads * expert_back, axis=1, keepdims=True)
    grad_logits = (grad_gate * gate) * (jnp.where(picked, 1.0, 0.0) - probs)
    grad_logits = jnp.where(lane < experts, grad_logits, 0.0)
    grad_normed = home[:, width:]
    for name in range(experts):
        grad_normed = grad_normed + grad_logits[:, name : name + 1] * router_ref[name : name + 1, :]
    upper = grad_logits.astype(bfloat)
    lower = (grad_logits - upper.astype(float32)).astype(bfloat)
    normed = normed_ref[...]
    router_out_ref[...] = dot_tn(upper, normed) + dot_tn(lower, normed)
    grad_resid, terms = norm_back(mid, gain, grad_normed)
    gain_out_ref[...] = jnp.sum(terms, axis=0, keepdims=True)
    grad_mid = grads + grad_resid
    grad_mid_ref[...] = grad_mid
    grad_attn = grad_mid.astype(bfloat)
    grad_attn_ref[...] = grad_attn
    for step in range(members):
        owner = jnp.where(me >= step, me - step, me - step + members)
        rows = weight_ref[pl.ds(pl.multiple_of(owner * span, span), span), :]
        part_refs[step][...] = dot_nt(grad_attn, rows).astype(bfloat)


def second_back(
    batch,
    batches,
    me,
    returned,
    back,
    mid,
    normed,
    probs,
    grads,
    routes,
    gain,
    router,
    weight,
    members,
    span,
    after,
    layer,
):
    count, width = mid.shape
    grad_spec = pl.BlockSpec((1, count, width), lambda i: (batch, 0, 0))

    def full(array):
        return pl.BlockSpec(array.shape, lambda i: (0,) * array.ndim)

    def own(array):
        return pl.BlockSpec((1,) + array.shape[1:], lambda i: (batch, 0, 0))

    rest = [
        jax.ShapeDtypeStruct((count, width), float32),
        jax.ShapeDtypeStruct((count, width), bfloat),
        jax.ShapeDtypeStruct((1, width), float32),
        jax.ShapeDtypeStruct((tile, width), float32),
    ] + [jax.ShapeDtypeStruct((count, span), bfloat)] * members
    aliased = 0 if layer is None else 1
    outs = pl.pallas_call(
        functools.partial(second_kernel, members, members, aliased),
        grid=(1,),
        in_specs=[
            pl.BlockSpec(memory_space=pltpu.SMEM),
            own(back),
            full(mid),
            full(normed),
            full(probs),
            grad_spec,
            own(routes),
            full(gain),
            full(router),
            full(weight),
            pl.BlockSpec(memory_space=pl.ANY),
        ]
        + [full(part) for part in returned]
        + [pl.BlockSpec(memory_space=pl.ANY)] * aliased,
        out_specs=[grad_spec] + [full(shape) for shape in rest],
        out_shape=[jax.ShapeDtypeStruct((batches, count, width), bfloat)] + rest,
        input_output_aliases={11 + members: 0} if aliased else {},
        compiler_params=params(),
        cost_estimate=pl.CostEstimate(
            flops=6 * count * width * width, bytes_accessed=12 * count * width, transcendentals=0
        ),
        name="second_back",
    )(
        me,
        back,
        mid,
        normed,
        probs,
        grads,
        routes,
        gain,
        router,
        weight,
        after,
        *returned,
        *([] if layer is None else [layer]),
    )
    return outs[0], outs[1], outs[2], outs[3], outs[4], list(outs[5:])


def first_kernel(
    members,
    pairs,
    grads_ref,
    weight_ref,
    offset_ref,
    after_ref,
    *out_refs,
):
    width = out_refs[0].shape[1]
    depth = weight_ref.shape[1] // pairs
    lanes = weight_ref.shape[2]
    total = None
    for pair in range(pairs):
        weight = weight_ref[:, pair * depth : (pair + 1) * depth, :].reshape(width, lanes)
        term = dot_nt(grads_ref[:, pair * lanes : (pair + 1) * lanes], weight)
        total = term if total is None else total + term
    for step in range(members):
        out_refs[step][...] = member_rows(total, offset_ref, step, members).astype(
            out_refs[step].dtype
        )


def first_back(batch, grads, packed, pairs, width, offsets, after):
    members = offsets.shape[2]
    count = grads.shape[0]
    lanes = packed.shape[2]
    weight_shape = (packed.shape[0], pairs * width // packed.shape[0], lanes)
    own = jax.ShapeDtypeStruct((count // members, width), float32)
    sent = jax.ShapeDtypeStruct((count // members, width), bfloat)
    out_shape = [own] + [sent] * (members - 1)

    def full(array):
        return pl.BlockSpec(array.shape, lambda i: (0,) * len(array.shape))

    outs = pl.pallas_call(
        functools.partial(first_kernel, members, pairs),
        grid=(1,),
        in_specs=[
            full(grads),
            pl.BlockSpec(weight_shape, lambda i: (0, 0, 0)),
            pl.BlockSpec((1,) + offsets.shape[1:], lambda i: (batch, 0, 0)),
            pl.BlockSpec(memory_space=pl.ANY),
        ],
        out_specs=[full(shape) for shape in out_shape],
        out_shape=out_shape,
        compiler_params=params(),
        cost_estimate=pl.CostEstimate(
            flops=2 * count * width * lanes * pairs,
            bytes_accessed=8 * count * width,
            transcendentals=0,
        ),
        name="first_back",
    )(grads, packed, offsets, after)
    return outs[0], list(outs[1:])


def finish_kernel(received, own_ref, rows_ref, gain_ref, mid_ref, after_ref, *refs):
    total = own_ref[...]
    for ref in refs[:received]:
        total = total + ref[...].astype(float32)
    grad, _ = norm_back(rows_ref[0].astype(float32), gain_ref[...], total)
    refs[-1][0] = mid_ref[...] + grad


def finish(batch, own, received, rows, gain, mid, buffer, after):
    batches, count, width = rows.shape
    row_spec = pl.BlockSpec((1, count, width), lambda i: (batch, 0, 0))

    def full(array):
        return pl.BlockSpec(array.shape, lambda i: (0,) * array.ndim)

    operands = [own, rows, gain, mid, after] + received
    in_specs = [full(own), row_spec, full(gain), full(mid), pl.BlockSpec(memory_space=pl.ANY)]
    in_specs = in_specs + [full(part) for part in received]
    aliases = {}
    if buffer is not None:
        aliases = {len(operands): 0}
        operands.append(buffer)
        in_specs.append(pl.BlockSpec(memory_space=pl.ANY))
    return pl.pallas_call(
        functools.partial(finish_kernel, len(received)),
        grid=(1,),
        in_specs=in_specs,
        out_specs=row_spec,
        out_shape=jax.ShapeDtypeStruct((batches, count, width), float32),
        input_output_aliases=aliases,
        compiler_params=params(),
        name="finish",
    )(*operands)


def dense_kernel(skipped, batches, weighted, blocks, *refs):
    refs = refs[skipped:]
    out_ref = refs[2 * batches + weighted]
    left = jnp.concatenate([ref[...] for ref in refs[:batches]], axis=0)
    right = jnp.concatenate([ref[...] for ref in refs[batches : 2 * batches]], axis=0)
    total = dot_tn(left, right)
    depth = out_ref.shape[1] // blocks
    lanes = out_ref.shape[2]
    term = None
    for block in range(blocks):
        part = total[:, block * lanes : (block + 1) * lanes]
        rows = slice(block * depth, (block + 1) * depth)
        out_ref[:, rows, :] = part.astype(bfloat).reshape(out_ref.shape[0], depth, lanes)
        if weighted:
            weight = refs[2 * batches][:, rows, :].reshape(part.shape).astype(float32)
            term = part * weight if term is None else term + part * weight
    if weighted:
        refs[-1][...] = jnp.sum(term, axis=1, keepdims=True)


def dense_grad(left, right, lanes, shards, direct, afters, packed=None):
    batches = len(left)
    count, width = left[0].shape
    columns = right[0].shape[1]
    blocks = columns // lanes
    depth = width // shards
    steps = 2 if direct and width % (2 * tile) == 0 and shards % 2 == 0 else 1
    outer = shards // steps if direct else 1
    inner = depth if direct else width
    weighted = 0 if packed is None else 1
    outs = pl.pallas_call(
        functools.partial(dense_kernel, len(afters), batches, weighted, blocks),
        grid=(steps,),
        in_specs=[pl.BlockSpec(memory_space=pl.ANY)] * len(afters)
        + [pl.BlockSpec((count, width // steps), lambda i: (0, i))] * batches
        + [pl.BlockSpec((count, columns), lambda i: (0, 0))] * batches
        + [pl.BlockSpec((outer, blocks * inner, lanes), lambda i: (i, 0, 0))] * weighted,
        out_specs=[pl.BlockSpec((outer, blocks * inner, lanes), lambda i: (i, 0, 0))]
        + [pl.BlockSpec((width // steps, 1), lambda i: (i, 0))] * weighted,
        out_shape=[jax.ShapeDtypeStruct((outer * steps, blocks * inner, lanes), bfloat)]
        + [jax.ShapeDtypeStruct((width, 1), float32)] * weighted,
        compiler_params=params(),
        cost_estimate=pl.CostEstimate(
            flops=2 * batches * count * width * columns,
            bytes_accessed=2 * batches * count * width,
            transcendentals=0,
        ),
        name="dense_grad",
    )(*afters, *left, *right, *([packed] if weighted else []))
    out = outs[0]
    if not direct:
        out = jnp.transpose(out.reshape(blocks, shards, depth, lanes), (1, 0, 2, 3))
        out = out.reshape(shards, blocks * depth, lanes)
    return (out, outs[1]) if weighted else out


def segment_of(positions, ends):
    segment = jnp.zeros(positions.shape, jnp.int32)
    for end in ends:
        segment = segment + (positions >= end).astype(jnp.int32)
    return segment


def masked_heads(rows, lane, per, head_dim):
    parts = []
    for sub in range(per):
        inside = (lane >= sub * head_dim) & (lane < (sub + 1) * head_dim)
        parts.append(jnp.where(inside, rows, jnp.zeros_like(rows)))
    return jnp.concatenate(parts, axis=0)


def joined_heads(rows, lane, per, head_dim):
    joined = rows[:tile]
    for sub in range(1, per):
        inside = (lane >= sub * head_dim) & (lane < (sub + 1) * head_dim)
        joined = jnp.where(inside, rows[sub * tile : (sub + 1) * tile], joined)
    return joined


def attend_kernel(
    stride,
    head_dim,
    far_ref,
    ends_ref,
    q_ref,
    k_ref,
    v_ref,
    bias_ref,
    after_ref,
    probs_ref,
    out_ref,
    inv_ref,
):
    pair = pl.program_id(0)
    rows_all = q_ref.shape[0]
    rows_part = rows_all // stride
    tiles = rows_part // tile
    reach = near_shift(tiles)
    per = tile // head_dim
    lane = lax.broadcasted_iota(jnp.int32, (tile, tile), 1)
    ends = [ends_ref[idx] for idx in range(ends_ref.shape[0])]
    keys_t = k_ref[...].T
    lane_row = lax.broadcasted_iota(jnp.int32, (1, tile), 1)
    row_column = lax.broadcasted_iota(jnp.int32, (tile, 1), 0)
    key_segments = [
        segment_of(stride * (col * tile + lane_row) + part, ends)
        for part in range(stride)
        for col in range(tiles)
    ]
    for mine in range(stride):
        for block in range(tiles):
            begin = mine * rows_part + block * tile
            rows = slice(begin, begin + tile)
            segment = segment_of(stride * (block * tile + row_column) + mine, ends)
            raw = dot_nn(masked_heads(q_ref[rows, :], lane, per, head_dim), keys_t)
            stacked = []
            inverses = []
            for sub in range(per):
                head = pair * per + sub
                pieces = []
                top = None
                for part in range(stride):
                    for col in range(tiles):
                        start = (part * tiles + col) * tile
                        piece = raw[sub * tile : (sub + 1) * tile, start : start + tile]
                        shift = col - block
                        if shift < -reach:
                            piece = piece + far_ref[0, head]
                        elif shift > reach:
                            piece = piece + far_ref[1, head]
                        else:
                            columns = slice((shift + reach) * tile, (shift + reach + 1) * tile)
                            piece = piece + bias_ref[sub, part - mine + stride - 1, :, columns]
                        same = key_segments[part * tiles + col] == segment
                        piece = jnp.where(same, piece, masked_score)
                        pieces.append(piece)
                        top = piece if top is None else jnp.maximum(top, piece)
                row_max = jnp.max(top, axis=-1, keepdims=True)
                total = None
                for idx, piece in enumerate(pieces):
                    piece = jnp.exp(piece - row_max)
                    total = piece if total is None else total + piece
                    pieces[idx] = piece.astype(bfloat)
                kept = jnp.concatenate(pieces, axis=1)
                probs_ref[sub, rows, :] = kept
                stacked.append(kept)
                inverses.append(1.0 / jnp.sum(total, axis=-1, keepdims=True))
            result = dot_nn(jnp.concatenate(stacked, axis=0), v_ref[...])
            inverse = jnp.broadcast_to(inverses[0], (tile, tile))
            for sub in range(1, per):
                inside = (lane >= sub * head_dim) & (lane < (sub + 1) * head_dim)
                inverse = jnp.where(inside, inverses[sub], inverse)
            out_ref[rows, :] = (joined_heads(result, lane, per, head_dim) * inverse).astype(bfloat)
            inv_ref[rows, :] = inverse


def kind_specs(rows_all):
    return [
        pl.BlockSpec((rows_all, tile), lambda i, kind=kind: (0, 3 * i + kind)) for kind in range(3)
    ]


def attend(qkv, ends, bias, far, after, head_dim, stride):
    rows_all, span = qkv.shape[0], qkv.shape[1] // 3
    per = tile // head_dim
    heads = span // head_dim
    row_spec = pl.BlockSpec((rows_all, tile), lambda i: (0, i))
    return pl.pallas_call(
        functools.partial(attend_kernel, stride, head_dim),
        grid=(span // tile,),
        in_specs=[
            pl.BlockSpec(memory_space=pltpu.SMEM),
            pl.BlockSpec(memory_space=pltpu.SMEM),
            *kind_specs(rows_all),
            pl.BlockSpec((per,) + bias.shape[1:], lambda i: (i, 0, 0, 0)),
            pl.BlockSpec(memory_space=pl.ANY),
        ],
        out_specs=[
            pl.BlockSpec((per, rows_all, rows_all), lambda i: (i, 0, 0)),
            row_spec,
            row_spec,
        ],
        out_shape=[
            jax.ShapeDtypeStruct((heads, rows_all, rows_all), bfloat),
            jax.ShapeDtypeStruct((rows_all, span), bfloat),
            jax.ShapeDtypeStruct((rows_all, span), float32),
        ],
        compiler_params=params(),
        cost_estimate=pl.CostEstimate(
            flops=16 * rows_all * rows_all * span,
            bytes_accessed=2 * heads * rows_all * rows_all,
            transcendentals=heads * rows_all * rows_all,
        ),
        name="attend",
    )(far, ends, qkv, qkv, qkv, bias, after)


def attend_back_kernel(
    stride,
    head_dim,
    scale,
    carried,
    probs_ref,
    out_ref,
    inv_ref,
    q_ref,
    k_ref,
    v_ref,
    offset_ref,
    after_ref,
    *refs,
):
    grad_refs = refs[:stride]
    dqkv_ref, dbias_ref, dfar_ref, ds_ref, grads_ref = refs[-5:]
    rows_all = q_ref.shape[0]
    rows_part = rows_all // stride
    tiles = rows_part // tile
    reach = near_shift(tiles)
    per = tile // head_dim
    lane = lax.broadcasted_iota(jnp.int32, (tile, tile), 1)
    queries_t = q_ref[...].T
    values_t = v_ref[...].T
    for place in range(stride):
        span = slice(place * rows_part, (place + 1) * rows_part)
        rows = grad_refs[0][...]
        for step in range(1, stride):
            rows = jnp.where(offset_ref[0, :, step : step + 1] == place, grad_refs[step][...], rows)
        grads_ref[span, :] = (rows.astype(float32) * inv_ref[span, :]).astype(bfloat)
    grads_t = grads_ref[...].T
    if carried:
        dbias_ref[...] = refs[stride][...]
        dfar_ref[...] = refs[stride + 1][...]
    else:
        dbias_ref[...] = jnp.zeros_like(dbias_ref)
        dfar_ref[...] = jnp.zeros_like(dfar_ref)
    for mine in range(stride):
        for block in range(tiles):
            begin = mine * rows_part + block * tile
            rows = slice(begin, begin + tile)
            own = masked_heads(grads_ref[rows, :], lane, per, head_dim)
            outs = out_ref[rows, :].astype(float32)
            raw = dot_nn(own, values_t)
            stacked = []
            for sub in range(per):
                span = slice(sub * tile, (sub + 1) * tile)
                row_dot = jnp.sum(own[span].astype(float32) * outs, axis=-1, keepdims=True)
                pieces = []
                for part in range(stride):
                    for col in range(tiles):
                        start = (part * tiles + col) * tile
                        piece = probs_ref[sub, rows, start : start + tile].astype(float32) * (
                            raw[span, start : start + tile] - row_dot
                        )
                        shift = col - block
                        if shift < -reach:
                            dfar_ref[sub, 0] += piece
                        elif shift > reach:
                            dfar_ref[sub, 1] += piece
                        else:
                            columns = slice((shift + reach) * tile, (shift + reach + 1) * tile)
                            dbias_ref[sub, part - mine + stride - 1, :, columns] += piece
                        pieces.append(piece.astype(bfloat))
                low_grads = jnp.concatenate(pieces, axis=1)
                ds_ref[sub, rows, :] = low_grads
                stacked.append(low_grads)
            result = dot_nn(jnp.concatenate(stacked, axis=0), k_ref[...]) * scale
            dqkv_ref[rows, :tile] = joined_heads(result, lane, per, head_dim).astype(bfloat)
    dk_parts = []
    dv_parts = []
    for sub in range(per):
        dims = slice(sub * head_dim, (sub + 1) * head_dim)
        dk_parts.append(dot_nn(queries_t[dims, :], ds_ref[sub]))
        dv_parts.append(dot_nn(grads_t[dims, :], probs_ref[sub]))
    dqkv_ref[:, tile : 2 * tile] = jnp.concatenate(dk_parts, axis=0).T.astype(bfloat)
    dqkv_ref[:, 2 * tile :] = jnp.concatenate(dv_parts, axis=0).T.astype(bfloat)


def attend_back(
    batch, probs, grads, outs, inverse, qkv, offsets, after, sums, head_dim, stride, bias_shape
):
    rows_all, span = outs.shape
    per = tile // head_dim
    heads = span // head_dim
    row_spec = pl.BlockSpec((rows_all, tile), lambda i: (0, i))
    part_spec = pl.BlockSpec((rows_all // stride, tile), lambda i: (0, i))
    sum_specs = [
        pl.BlockSpec((per,) + bias_shape[1:], lambda i: (i, 0, 0, 0)),
        pl.BlockSpec((per, 2, tile, tile), lambda i: (i, 0, 0, 0)),
    ]
    carried = len(sums) > 0
    first = 8 + stride
    return pl.pallas_call(
        functools.partial(attend_back_kernel, stride, head_dim, head_dim ** (-0.5), carried),
        grid=(span // tile,),
        in_specs=[pl.BlockSpec((per, rows_all, rows_all), lambda i: (i, 0, 0))]
        + [row_spec] * 2
        + kind_specs(rows_all)
        + [pl.BlockSpec((1,) + offsets.shape[1:], lambda i: (batch, 0, 0))]
        + [pl.BlockSpec(memory_space=pl.ANY)]
        + [part_spec] * stride
        + (sum_specs if carried else []),
        out_specs=[pl.BlockSpec((rows_all, 3 * tile), lambda i: (0, i))] + sum_specs,
        out_shape=[
            jax.ShapeDtypeStruct((rows_all, 3 * span), bfloat),
            jax.ShapeDtypeStruct(bias_shape, float32),
            jax.ShapeDtypeStruct((heads, 2, tile, tile), float32),
        ],
        scratch_shapes=[
            pltpu.VMEM((per, rows_all, rows_all), bfloat),
            pltpu.VMEM((rows_all, tile), bfloat),
        ],
        input_output_aliases={first: 1, first + 1: 2} if carried else {},
        compiler_params=params(),
        cost_estimate=pl.CostEstimate(
            flops=32 * rows_all * rows_all * span,
            bytes_accessed=2 * heads * rows_all * rows_all,
            transcendentals=0,
        ),
        name="attend_back",
    )(probs, outs, inverse, qkv, qkv, qkv, offsets, after, *grads, *sums)


def add_kernel(skipped, *refs):
    refs = refs[skipped:]
    out_ref = refs[-1]
    start = 0
    for left_ref, right_ref in zip(refs[:-1:2], refs[1:-1:2]):
        rows = left_ref.shape[1]
        out_ref[:, start : start + rows] = (
            left_ref[...].astype(float32) + right_ref[...].astype(float32)
        ).astype(bfloat)
        start += rows


def add_after(afters, *operands):
    vmem = pl.BlockSpec(memory_space=pltpu.VMEM)
    outer, _, lanes = operands[0].shape
    rows = sum(operand.shape[1] for operand in operands[::2])
    return pl.pallas_call(
        functools.partial(add_kernel, len(afters)),
        in_specs=[pl.BlockSpec(memory_space=pl.ANY)] * len(afters) + [vmem] * len(operands),
        out_specs=vmem,
        out_shape=jax.ShapeDtypeStruct((outer, rows, lanes), bfloat),
        compiler_params=params(),
        name="add_after",
    )(*afters, *operands)


def order_kernel(count, place_ref, *refs):
    out_ref = refs[count + 1]
    for place in range(count):
        rows = refs[0][0]
        for step in range(1, count):
            rows = jnp.where(place_ref[0, :, step : step + 1] == place, refs[step][0], rows)
        out_ref[0, place] = rows


def order_rows(parts, offsets, carried):
    batches, rows, width = parts[0].shape
    count = len(parts)
    part_spec = pl.BlockSpec((1, rows, width), lambda i: (i, 0, 0))
    return pl.pallas_call(
        functools.partial(order_kernel, count),
        grid=(batches,),
        in_specs=[pl.BlockSpec((1, rows, count), lambda i: (i, 0, 0))]
        + [part_spec] * count
        + [pl.BlockSpec(memory_space=pl.ANY)],
        out_specs=[
            pl.BlockSpec((1, count, rows, width), lambda i: (i, 0, 0, 0)),
            pl.BlockSpec(memory_space=pl.ANY),
        ],
        out_shape=[
            jax.ShapeDtypeStruct((batches, count, rows, width), bfloat),
            jax.ShapeDtypeStruct(carried.shape, carried.dtype),
        ],
        input_output_aliases={count + 1: 1},
        compiler_params=params(),
        name="order_rows",
    )(offsets, *parts, carried)


def expert_kernel(
    count, slots, width, inner_ref, outer_ref, after_ref, *refs
):
    blocks = refs[:count]
    results = refs[count : 2 * count]
    hidden_ref, grad_pre_ref, rows_ref, grads_ref, sum_ref, back_ref = refs[2 * count :]
    turn = pl.program_id(0)

    @pl.when(turn == 0)
    def _():
        for idx in range(count):
            rows = slice(idx * slots, (idx + 1) * slots)
            rows_ref[rows, :] = blocks[idx][:, :width]
            grads_ref[rows, :] = blocks[idx][:, width:]

    inner = inner_ref[...].reshape(width, width)
    outer = outer_ref[...].reshape(width, width)
    rows = rows_ref[...]
    grads = grads_ref[...]
    root = 0.7978845608028654
    pre = dot_nn(rows, inner)
    grad_hidden = dot_nt(grads, outer)
    square = pre * pre
    curve = jnp.tanh(root * pre * (1.0 + 0.044715 * square))
    half = 0.5 * (1.0 + curve)
    slope = half + (0.5 * root) * pre * (1.0 - curve * curve) * (1.0 + 0.134145 * square)
    hidden_ref[...] = (pre * half).astype(bfloat)
    grad_pre_ref[...] = (grad_hidden * slope).astype(bfloat)
    product = dot_nn(hidden_ref[...], outer)
    product_back = dot_nt(grad_pre_ref[...], inner)

    @pl.when(turn == 0)
    def _():
        sum_ref[...] = product
        back_ref[...] = product_back

    @pl.when(turn > 0)
    def _():
        sum_ref[...] += product
        back_ref[...] += product_back

    @pl.when(turn == pl.num_programs(0) - 1)
    def _():
        for idx in range(count):
            span = slice(idx * slots, (idx + 1) * slots)
            results[idx][:, :width] = sum_ref[span, :].astype(bfloat)
            results[idx][:, width:] = back_ref[span, :].astype(bfloat)


def run_expert(weights, blocks, width, after):
    (inner, inner_spec), (outer, outer_spec), turns = weights
    count = len(blocks)
    slots = blocks[0].shape[0]
    total = count * slots
    whole = pl.BlockSpec((slots, 2 * width), lambda i: (0, 0))
    chunk = pl.BlockSpec((total, width), lambda i: (0, i))
    outs = pl.pallas_call(
        functools.partial(expert_kernel, count, slots, width),
        grid=(turns,),
        in_specs=[inner_spec, outer_spec, pl.BlockSpec(memory_space=pl.ANY)] + [whole] * count,
        out_specs=[whole] * count + [chunk, chunk],
        out_shape=[jax.ShapeDtypeStruct((slots, 2 * width), bfloat)] * count
        + [jax.ShapeDtypeStruct((total, turns * width), bfloat)] * 2,
        scratch_shapes=[
            pltpu.VMEM((total, width), bfloat),
            pltpu.VMEM((total, width), bfloat),
            pltpu.VMEM((total, width), float32),
            pltpu.VMEM((total, width), float32),
        ],
        compiler_params=params(),
        cost_estimate=pl.CostEstimate(
            flops=8 * total * width * width * turns,
            bytes_accessed=4 * width * width * turns,
            transcendentals=total * width * turns,
        ),
        name="run_expert",
    )(inner, outer, after, *blocks)
    return outs[:count], outs[count], outs[count + 1]


def expert_grad_kernel(batches, count, slots, width, second, *refs):
    groups = [refs[idx * count : (idx + 1) * count] for idx in range(batches)]
    wide = refs[batches * count : batches * count + batches]
    out_ref, rows_ref = refs[-2], refs[-1]
    half = slice(width, 2 * width) if second else slice(0, width)

    @pl.when(pl.program_id(0) == 0)
    def _():
        for batch in range(batches):
            for idx in range(count):
                start = (batch * count + idx) * slots
                rows_ref[start : start + slots, :] = groups[batch][idx][:, half]

    rows = rows_ref[...]
    columns = jnp.concatenate([ref[...] for ref in wide], axis=0)
    total = dot_tn(columns, rows) if second else dot_tn(rows, columns)
    out_ref[...] = total.astype(bfloat).reshape(out_ref.shape)


def expert_grad(groups, wide, width, second, out_shape, out_spec, after, buffer=None):
    batches = len(groups)
    count = len(groups[0])
    slots = groups[0][0].shape[0]
    total = count * slots
    turns = wide[0].shape[1] // width
    kernel = functools.partial(expert_grad_kernel, batches, count, slots, width, second)
    in_specs = [pl.BlockSpec((slots, 2 * width), lambda i: (0, 0))] * (batches * count)
    in_specs = in_specs + [pl.BlockSpec((total, width), lambda i: (0, i))] * batches
    operands = [block for group in groups for block in group] + list(wide)
    aliases = {}
    carried = [after]
    if buffer is not None:
        carried = [buffer, after]
        aliases = {0: 0}
    skipped = len(carried)
    in_specs = [pl.BlockSpec(memory_space=pl.ANY)] * skipped + in_specs
    operands = carried + operands

    def body(*refs):
        kernel(*refs[skipped:])

    return pl.pallas_call(
        body,
        grid=(turns,),
        in_specs=in_specs,
        out_specs=out_spec,
        out_shape=jax.ShapeDtypeStruct(out_shape, bfloat),
        scratch_shapes=[pltpu.VMEM((batches * total, width), bfloat)],
        input_output_aliases=aliases,
        compiler_params=params(),
        cost_estimate=pl.CostEstimate(
            flops=2 * batches * total * width * width * turns,
            bytes_accessed=4 * width * width * turns,
            transcendentals=0,
        ),
        name="expert_grad_outer" if second else "expert_grad_inner",
    )(*operands)


def on_device(
    hidden_in,
    out_grad,
    places,
    lengths,
    routes,
    norm1_gain,
    w_query,
    w_key,
    w_value,
    w_output,
    rel_table,
    norm2_gain,
    w_router,
    w_in,
    w_out,
):
    batches, rows_own, width = hidden_in.shape
    heads = rel_table.shape[1]
    head_dim = width // heads
    scale = head_dim ** (-0.5)
    shards = lax.axis_size("dp")
    members = lax.axis_size("expert")
    me = lax.axis_index("expert")
    experts = w_router.shape[1]
    hidden_width = w_in.shape[2]
    turns = hidden_width // width
    tiles = rows_own // tile
    rows_group = members * rows_own
    depth = width // shards
    depth_out = hidden_width // shards
    table_rows = rel_table.shape[0]
    capacity = max(2, rows_own * 17 // (experts * 16))
    slots = -(-capacity // 16) * 16
    per = tile // head_dim
    heads_own = per * (-(-heads // (per * members)))
    span = heads_own * head_dim
    pairs = span // tile
    lanes = 3 * tile
    split = width // lanes
    me_row = me.reshape(1)

    def around(step):
        return [(idx, (idx + step) % members) for idx in range(members)]

    def columns_own(weight):
        wide = jnp.pad(weight, ((0, 0), (0, members * span - width)))
        return lax.dynamic_slice_in_dim(wide, me * span, span, axis=1)

    def in_order(parts):
        if members == 2:
            return [
                jnp.where(me == 0, parts[0], parts[1]),
                jnp.where(me == 0, parts[1], parts[0]),
            ]
        stacked = jnp.stack(parts)
        return [stacked[jnp.mod(me - idx, members)] for idx in range(members)]

    hidden_from = [hidden_in] + [
        lax.ppermute(hidden_in, "expert", around(step)) for step in range(1, members)
    ]

    small = jnp.concatenate(
        [
            norm1_gain.reshape(-1),
            norm2_gain.reshape(-1),
            w_router.reshape(-1),
            rel_table.reshape(-1),
        ]
    )
    small_used = small.shape[0]
    small_pad = -(-small_used // (16 * lanes)) * 16
    small = jnp.pad(small, (0, small_pad * lanes - small_used)).reshape(small_pad, lanes)
    kinds = [columns_own(weight) for weight in (w_query, w_key, w_value)]
    first_own = jnp.concatenate(
        [
            jnp.concatenate([kind[:, idx * tile : (idx + 1) * tile] for kind in kinds], axis=1)
            for idx in range(pairs)
        ]
        + [w_output[:, idx * lanes : (idx + 1) * lanes] for idx in range(split)]
        + [small],
        axis=0,
    )
    first = lax.all_gather(first_own, "dp", axis=0, tiled=False)
    inner_parts = [w_in[0, :, idx * width : (idx + 1) * width] for idx in range(turns)]
    second_own = jnp.concatenate(inner_parts + [w_out[0]], axis=0)
    places_in = places[:, 0].reshape(batches, members, rows_own)
    dispatch, collect, offsets, second_own = row_tables(
        me_row, routes, places_in, hidden_from[-1], second_own, members, slots
    )
    second = lax.all_gather(second_own, "dp", axis=0, tiled=False)
    ends = jnp.cumsum(lengths[:, 0], axis=-1)[:, :-1]
    ordered_in, first = order_rows(hidden_from, offsets, first)
    ordered_in = ordered_in.reshape(batches, rows_group, width)

    small_start = (pairs + split) * depth
    small_all = first[:, small_start:].reshape(shards, small_pad * lanes)
    gain_one = small_all[:, :depth].reshape(1, width).astype(float32)
    gain_two = small_all[:, depth : 2 * depth].reshape(1, width).astype(float32)
    router_end = 2 * depth + depth * experts
    router_w = small_all[:, 2 * depth : router_end].reshape(width, experts)
    table = small_all[:, router_end:small_used].reshape(shards * table_rows, heads)
    router_wide = jnp.pad(router_w, ((0, 0), (0, tile - experts)))
    router_t = router_w.astype(float32).T
    output_w = jnp.concatenate(
        [
            first[:, (pairs + idx) * depth : (pairs + idx + 1) * depth].reshape(width, lanes)
            for idx in range(split)
        ],
        axis=1,
    )
    output_w = jnp.pad(output_w, ((0, members * span - width), (0, 0)))

    direct = depth % 16 == 0 and turns * depth == depth_out and shards % turns == 0
    if direct:
        group = shards // turns
        packed = first
        inner_spec = pl.BlockSpec((shards, depth, width), lambda i: (0, i, 0))
        outer_spec = pl.BlockSpec((group, depth_out, width), lambda i: (i, 1, 0))
        weights = ((second, inner_spec), (second, outer_spec), turns)
    else:
        packed = jnp.concatenate(
            [
                first[:, idx * depth : (idx + 1) * depth].reshape(1, width, lanes)
                for idx in range(pairs)
            ],
            axis=1,
        )
        inner_w = second[:, : turns * depth].reshape(shards, turns, depth, width)
        inner_w = jnp.transpose(inner_w, (1, 0, 2, 3)).reshape(turns, width, width)
        outer_w = second[:, turns * depth : turns * depth + depth_out].reshape(
            turns, width, width
        )
        plain = pl.BlockSpec((1, width, width), lambda i: (i, 0, 0))
        weights = ((inner_w, plain), (outer_w, plain), turns)

    table_wide = jnp.pad(table, ((0, 0), (0, members * heads_own - heads)))
    table_own = lax.dynamic_slice_in_dim(table_wide, me * heads_own, heads_own, axis=1)
    bias = bias_tiles(table_own, members, tiles)
    table_f = table_own.astype(float32)
    far = jnp.stack([table_f[levels_all - 1], table_f[2 * levels_all - 1]])

    def send_rows(batch, ordered):
        arrived = []
        for step in range(1, members):
            rows = ordered[:rows_own]
            for place in range(1, members):
                rows = jnp.where(
                    offsets[batch, :, members - step : members - step + 1] == place,
                    ordered[place * rows_own : (place + 1) * rows_own],
                    rows,
                )
            arrived.append(lax.ppermute(rows, "expert", around(step)))
        return arrived

    normed_one = []
    qkv = []
    probs = []
    outs = []
    inverses = []
    arrived_heads = []
    resid_mid = []
    normed_two = []
    router_probs = []
    blocks = []
    after = table
    for batch in range(batches):
        normed, packed_rows = project(batch, ordered_in, gain_one, packed, pairs, scale)
        normed_one.append(normed)
        qkv.append(packed_rows)
        kept, joined, inverse = attend(
            packed_rows,
            ends[batch],
            bias,
            far,
            after,
            head_dim,
            members,
        )
        probs.append(kept)
        outs.append(joined)
        inverses.append(inverse)
        arrived_heads.append(send_rows(batch, joined))
        mid, normed, chances, outgoing = middle(
            batch,
            me_row,
            joined,
            arrived_heads[batch],
            offsets,
            output_w,
            hidden_in,
            out_grad,
            gain_two,
            router_wide,
            routes,
            dispatch,
            blocks[-1][-1] if blocks else table,
        )
        after = outgoing[-1]
        blocks.append(
            [outgoing[0]]
            + [
                lax.ppermute(outgoing[step], "expert", around(step))
                for step in range(1, members)
            ]
        )
        resid_mid.append(mid)
        normed_two.append(normed)
        router_probs.append(chances)

    returned = []
    hidden = []
    grad_pre = []
    for batch in range(batches):
        results, hidden_rows, grad_rows = run_expert(
            weights, blocks[batch], width, hidden[-1] if hidden else table
        )
        hidden.append(hidden_rows)
        grad_pre.append(grad_rows)
        returned.append(
            [results[0]]
            + [
                lax.ppermute(results[step], "expert", around(-step))
                for step in range(1, members)
            ]
        )

    if direct:
        buffer_shape = (shards, turns * depth + depth_out, width)
        buffer = expert_grad(
            blocks,
            grad_pre,
            width,
            False,
            buffer_shape,
            pl.BlockSpec((shards, depth, width), lambda i: (0, i, 0)),
            returned[0][-1],
        )
        buffer = expert_grad(
            blocks,
            hidden,
            width,
            True,
            buffer_shape,
            pl.BlockSpec((group, depth_out, width), lambda i: (i, 1, 0)),
            returned[0][-1],
            buffer,
        )
    else:
        plain_shape = (turns, width, width)
        inner_g = expert_grad(
            blocks, grad_pre, width, False, plain_shape, plain, returned[0][-1]
        )
        outer_g = expert_grad(
            blocks, hidden, width, True, plain_shape, plain, returned[0][-1]
        )
        inner_g = jnp.transpose(inner_g.reshape(turns, shards, depth, width), (1, 0, 2, 3))
        buffer = jnp.concatenate(
            [
                inner_g.reshape(shards, turns * depth, width),
                outer_g.reshape(shards, depth_out, width),
            ],
            axis=1,
        )
    expert_sum = lax.psum_scatter(buffer, "dp", scatter_dimension=0, tiled=False)

    line = shards // 4
    my_shard = lax.axis_index("dp")

    def by_core(dense):
        dense = dense.reshape((line, 2, 2) + dense.shape[1:])
        odd = my_shard % 2 == 1
        sent = jnp.where(odd, dense[:, :, 0], dense[:, :, 1])
        held = jnp.where(odd, dense[:, :, 1], dense[:, :, 0])
        return held, lax.ppermute(sent, "dp", [(idx, idx ^ 1) for idx in range(shards)])

    def by_y(core_parts):
        held, got = core_parts
        odd = (my_shard // 2) % 2 == 1

        def half(idx):
            return held[:, idx].astype(float32) + got[:, idx].astype(float32)

        sent = jnp.where(odd, half(0), half(1)).astype(bfloat)
        kept = jnp.where(odd, half(1), half(0)).astype(bfloat)
        return kept, lax.ppermute(sent, "dp", [(idx, idx ^ 2) for idx in range(shards)])

    layer = None
    grad_mid = []
    grad_attn = []
    grad_heads = []
    grad_gain_two = 0.0
    grad_router = 0.0
    for batch in range(batches):
        layer, mid, attn, gain_terms, router_terms, parts = second_back(
            batch,
            batches,
            me_row,
            returned[batch],
            collect,
            resid_mid[batch],
            normed_two[batch],
            router_probs[batch],
            out_grad,
            routes,
            gain_two,
            router_t,
            output_w,
            members,
            span,
            buffer,
            layer,
        )
        grad_mid.append(mid)
        grad_attn.append(attn)
        grad_gain_two = grad_gain_two + gain_terms
        grad_router = grad_router + router_terms[:experts]
        from_members = [parts[0]] + [
            lax.ppermute(parts[members - step], "expert", around(step))
            for step in range(1, members)
        ]
        grad_heads.append(from_members)

    def own_rows_of(batch):
        joined = outs[batch]
        rows = joined[:rows_own]
        for place in range(1, members):
            rows = jnp.where(
                offsets[batch, :, 0:1] == place,
                joined[place * rows_own : (place + 1) * rows_own],
                rows,
            )
        return rows

    attended = [
        jnp.concatenate(in_order([own_rows_of(batch)] + arrived_heads[batch]), axis=1)[:, :width]
        for batch in range(batches)
    ]
    early_core = by_core(
        dense_grad(attended, grad_attn, lanes, shards, direct, [grad_heads[0][-1]])
    )
    early = by_y(early_core)
    grad_qkv = []
    sums = []
    own_rows = []
    received_rows = []
    sent_last = buffer

    def first_part(batch, after):
        own, sent = first_back(batch, grad_qkv[batch], packed, pairs, width, offsets, after)
        own_rows.append(own)
        received_rows.append(
            [lax.ppermute(rows, "expert", around(-step)) for step, rows in enumerate(sent, 1)]
        )
        return sent[-1]

    for batch in range(batches):
        if batch > 0:
            sent_last = first_part(batch - 1, buffer)
        grads, *sums = attend_back(
            batch,
            probs[batch],
            grad_heads[batch],
            outs[batch],
            inverses[batch],
            qkv[batch],
            offsets,
            sent_last,
            sums,
            head_dim,
            members,
            bias.shape,
        )
        grad_qkv.append(grads)
    grad_bias, grad_far = sums
    grad_dense, weighted = dense_grad(
        normed_one,
        grad_qkv,
        lanes,
        shards,
        direct,
        [early[1]] + [rows[-1] for rows in received_rows],
        packed,
    )
    grad_gain_one = weighted[:, 0] / gain_one[0]
    late_core = by_core(grad_dense)
    late = by_y(late_core)
    sent_last = first_part(batches - 1, late_core[1])

    steps = 2 * members - 1
    reach = near_shift(tiles)
    shape = (steps, tile, (2 * reach + 1) * tile)
    delta = (
        members
        * (
            lax.broadcasted_iota(jnp.int32, shape, 2)
            - reach * tile
            - lax.broadcasted_iota(jnp.int32, shape, 1)
        )
        + lax.broadcasted_iota(jnp.int32, shape, 0)
        - (members - 1)
    )
    buckets = shards * table_rows
    onehot = (
        bucket_of(delta)[None] == jnp.arange(buckets, dtype=jnp.int32)[:, None, None, None]
    ).astype(bfloat)
    grad_table = jnp.einsum(
        "hsab,ksab->kh", grad_bias.astype(bfloat), onehot, preferred_element_type=float32
    )
    far_sum = jnp.sum(grad_far, axis=(2, 3))
    grad_table = grad_table.at[levels_all - 1].add(far_sum[:, 0])
    grad_table = grad_table.at[2 * levels_all - 1].add(far_sum[:, 1])
    grad_table = lax.dynamic_update_slice_in_dim(
        jnp.zeros((buckets, members * heads_own), float32), grad_table, me * heads_own, axis=1
    )[:, :heads]

    small_grad = jnp.concatenate(
        [
            grad_gain_one.reshape(shards, depth),
            grad_gain_two.reshape(shards, depth),
            grad_router.T.reshape(shards, depth * experts),
            grad_table.reshape(shards, table_rows * heads),
        ],
        axis=1,
    )
    small_grad = jnp.pad(small_grad, ((0, 0), (0, small_pad * lanes - small_used)))
    small_grad = small_grad.astype(bfloat).reshape(shards, small_pad, lanes)
    little = by_y(by_core(small_grad))
    dense_added = add_after([expert_sum, sent_last], *late, *little, *early)
    in_grad = None
    for batch in range(batches):
        in_grad = finish(
            batch,
            own_rows[batch],
            received_rows[batch],
            hidden_in,
            gain_one,
            grad_mid[batch],
            in_grad,
            buffer if batch < batches - 1 else dense_added,
        )
    dense_part = lax.psum_scatter(
        dense_added,
        "dp",
        scatter_dimension=0,
        tiled=False,
        axis_index_groups=[[rest + 4 * idx for idx in range(line)] for rest in range(4)],
    )
    parts = [dense_part] + [
        lax.ppermute(dense_part, "expert", around(step)) for step in range(1, members)
    ]
    qkv_parts = [
        part.astype(float32) for part in in_order([part[: pairs * depth] for part in parts])
    ]
    qkv_grads = [
        jnp.concatenate(
            [
                part[pair * depth : (pair + 1) * depth, kind * tile : (kind + 1) * tile]
                for part in qkv_parts
                for pair in range(pairs)
            ],
            axis=1,
        )[:, :width]
        for kind in range(3)
    ]
    rest_sum = sum(part[pairs * depth :].astype(float32) for part in parts)
    out_grad_sum = jnp.concatenate(
        [
            rest_sum[small_pad + idx * depth : small_pad + (idx + 1) * depth]
            for idx in range(split)
        ],
        axis=1,
    )
    small_sum = rest_sum[:small_pad].reshape(-1)

    expert_f = expert_sum.astype(float32)
    inner_sum = jnp.concatenate(
        [expert_f[idx * depth : (idx + 1) * depth] for idx in range(turns)], axis=1
    )[None]
    outer_sum = expert_f[turns * depth :][None]
    return (
        layer,
        in_grad,
        small_sum[:depth],
        qkv_grads[0],
        qkv_grads[1],
        qkv_grads[2],
        out_grad_sum,
        small_sum[router_end:small_used].reshape(table_rows, heads),
        small_sum[depth : 2 * depth],
        small_sum[2 * depth : router_end].reshape(depth, experts),
        inner_sum,
        outer_sum,
    )


def solution(mesh):
    return jax.shard_map(
        on_device,
        mesh=mesh,
        in_specs=(
            P(None, ("dp", "expert"), None),
            P(None, ("dp", "expert"), None),
            P(None, "dp", None),
            P(None, "dp", None),
            P(None, ("dp", "expert"), None),
            P("dp"),
            P("dp", None),
            P("dp", None),
            P("dp", None),
            P("dp", None),
            P("dp", None),
            P("dp"),
            P("dp", None),
            P("expert", "dp", None),
            P("expert", "dp", None),
        ),
        out_specs=(
            P(None, ("dp", "expert"), None),
            P(None, ("dp", "expert"), None),
            P("dp"),
            P("dp", None),
            P("dp", None),
            P("dp", None),
            P("dp", None),
            P("dp", None),
            P("dp"),
            P("dp", None),
            P("expert", "dp", None),
            P("expert", "dp", None),
        ),
        check_vma=False,
    )
```

```python
import functools

import jax
import jax.numpy as jnp
from jax import lax
from jax.experimental import pallas as pl
from jax.experimental.pallas import tpu as pltpu
from jax.sharding import PartitionSpec as P

bucket_edges = (1, 2, 3, 4, 5, 6, 7, 8, 12, 16, 23, 32, 46, 64, 91)
levels_all = len(bucket_edges) + 1
epsilon = 1e-06
masked_score = -1000000000.0
precise = lax.Precision.HIGHEST
float32 = jnp.float32
bfloat = jnp.bfloat16
tile = 128
vmem_bytes = 56 * 1024 * 1024


def params():
    return pltpu.CompilerParams(vmem_limit_bytes=vmem_bytes)


def dot_nn(left, right):
    return lax.dot_general(left, right, (((1,), (0,)), ((), ())), preferred_element_type=float32)


def dot_nt(left, right):
    return lax.dot_general(left, right, (((1,), (1,)), ((), ())), preferred_element_type=float32)


def dot_tn(left, right):
    return lax.dot_general(left, right, (((0,), (0,)), ((), ())), preferred_element_type=float32)


def norm_rows(rows, gain):
    mean_square = jnp.mean(rows * rows, axis=-1, keepdims=True)
    return rows * lax.rsqrt(mean_square + epsilon) * gain


def norm_back(rows, gain, grad):
    scale = lax.rsqrt(jnp.mean(rows * rows, axis=-1, keepdims=True) + epsilon)
    unit = rows * scale
    weighted = grad * gain
    inner = jnp.mean(weighted * unit, axis=-1, keepdims=True)
    return scale * (weighted - unit * inner), grad * unit


def bucket_of(offset):
    distance = jnp.abs(offset)
    levels = jnp.zeros(offset.shape, jnp.int32)
    for edge_value in bucket_edges:
        levels = levels + (distance >= edge_value).astype(jnp.int32)
    return levels + levels_all * (offset > 0).astype(jnp.int32)


def near_shift(tiles):
    return min(1, tiles - 1)


def bias_kernel(stride, reach, table_ref, out_ref):
    row = lax.broadcasted_iota(jnp.int32, (tile, tile), 0)
    lane = lax.broadcasted_iota(jnp.int32, (tile, tile), 1)
    heads = out_ref.shape[0]
    for shift in range(-reach, reach + 1):
        for step in range(2 * stride - 1):
            ids = bucket_of(stride * (tile * shift + lane - row) + step - (stride - 1))
            columns = slice((shift + reach) * tile, (shift + reach + 1) * tile)
            for head in range(heads):
                values = jnp.broadcast_to(table_ref[head : head + 1, :], (tile, tile))
                out_ref[head, step, :, columns] = jnp.take_along_axis(values, ids, axis=1)


def bias_tiles(table, stride, tiles):
    heads = table.shape[1]
    reach = near_shift(tiles)
    lanes = jnp.pad(table.astype(float32).T, ((0, 0), (0, tile - table.shape[0])))
    return pl.pallas_call(
        functools.partial(bias_kernel, stride, reach),
        out_shape=jax.ShapeDtypeStruct(
            (heads, 2 * stride - 1, tile, (2 * reach + 1) * tile), float32
        ),
        compiler_params=params(),
        name="bias_tiles",
    )(lanes)


def project_kernel(pairs, scale, rows_ref, gain_ref, weight_ref, normed_ref, out_ref):
    width = rows_ref.shape[2]
    depth = weight_ref.shape[1] // pairs
    lanes = weight_ref.shape[2]
    normed = norm_rows(rows_ref[0].astype(float32), gain_ref[...]).astype(bfloat)
    normed_ref[...] = normed
    for pair in range(pairs):
        weight = weight_ref[:, pair * depth : (pair + 1) * depth, :].reshape(width, lanes)
        product = dot_nn(normed, weight).astype(bfloat)
        start = pair * lanes
        out_ref[:, start : start + tile] = product[:, :tile] * bfloat(scale)
        out_ref[:, start + tile : start + lanes] = product[:, tile:]


def project(batch, rows, gain, packed, pairs, scale):
    _, count, width = rows.shape
    lanes = packed.shape[2]
    weight_shape = (packed.shape[0], pairs * width // packed.shape[0], lanes)
    step = min(512, count)
    return pl.pallas_call(
        functools.partial(project_kernel, pairs, scale),
        grid=(count // step,),
        in_specs=[
            pl.BlockSpec((1, step, width), lambda i: (batch, i, 0)),
            pl.BlockSpec((1, width), lambda i: (0, 0)),
            pl.BlockSpec(weight_shape, lambda i: (0, 0, 0)),
        ],
        out_specs=[
            pl.BlockSpec((step, width), lambda i: (i, 0)),
            pl.BlockSpec((step, pairs * lanes), lambda i: (i, 0)),
        ],
        out_shape=[
            jax.ShapeDtypeStruct((count, width), bfloat),
            jax.ShapeDtypeStruct((count, pairs * lanes), bfloat),
        ],
        compiler_params=params(),
        cost_estimate=pl.CostEstimate(
            flops=2 * count * width * lanes * pairs,
            bytes_accessed=6 * count * width,
            transcendentals=0,
        ),
        name="project",
    )(rows, gain, packed)


def count_earlier(picked, first_axis):
    size = picked.shape[1 - first_axis]
    row = lax.broadcasted_iota(jnp.int32, (size, size), 0)
    column = lax.broadcasted_iota(jnp.int32, (size, size), 1)
    if first_axis == 0:
        return dot_nn(picked, (row < column).astype(float32).astype(bfloat))
    return dot_nn((column < row).astype(float32).astype(bfloat), picked)


def tables_kernel(
    members,
    slots,
    me_ref,
    row_ref,
    column_ref,
    place_ref,
    after_ref,
    carried_ref,
    send_ref,
    back_ref,
    offset_ref,
    handed_ref,
):
    me = me_ref[0]
    batches, rows = column_ref.shape[0], column_ref.shape[1]
    names = 128
    for batch in range(batches):
        route = row_ref[batch]
        picked = lax.broadcasted_iota(jnp.int32, (names, rows), 0) == route
        earlier = count_earlier(picked.astype(float32).astype(bfloat), 0)
        slot = jnp.sum(jnp.where(picked, earlier, 0.0), axis=0, keepdims=True).astype(jnp.int32)
        target = jnp.where(route >= me, route - me, route - me + members) * slots + slot
        index = lax.broadcasted_iota(jnp.int32, (members * slots, rows), 0)
        send_ref[batch] = (index == target).astype(float32).astype(bfloat)

        route = column_ref[batch]
        picked = lax.broadcasted_iota(jnp.int32, (rows, names), 1) == route
        earlier = count_earlier(picked.astype(float32).astype(bfloat), 1)
        slot = jnp.sum(jnp.where(picked, earlier, 0.0), axis=1, keepdims=True).astype(jnp.int32)
        target = jnp.where(route >= me, route - me, route - me + members) * slots + slot
        index = lax.broadcasted_iota(jnp.int32, (rows, members * slots), 1)
        back_ref[batch] = (index == target).astype(float32).astype(bfloat)

        offsets = place_ref[batch] - members * lax.broadcasted_iota(
            jnp.int32, (rows, members), 0
        )
        lane = lax.broadcasted_iota(jnp.int32, (rows, members), 1)
        for step in range(members):
            owner = jnp.where(me >= step, me - step, me - step + members)
            chosen = jnp.sum(jnp.where(lane == owner, offsets, 0), axis=1, keepdims=True)
            offset_ref[batch, :, step : step + 1] = chosen


def row_tables(me, routes, places, after, carried, members, slots):
    batches, rows, _ = routes.shape
    vmem = pl.BlockSpec(memory_space=pltpu.VMEM)
    return pl.pallas_call(
        functools.partial(tables_kernel, members, slots),
        in_specs=[pl.BlockSpec(memory_space=pltpu.SMEM), vmem, vmem, vmem]
        + [pl.BlockSpec(memory_space=pl.ANY)] * 2,
        out_specs=[vmem, vmem, vmem, pl.BlockSpec(memory_space=pl.ANY)],
        out_shape=[
            jax.ShapeDtypeStruct((batches, members * slots, rows), bfloat),
            jax.ShapeDtypeStruct((batches, rows, members * slots), bfloat),
            jax.ShapeDtypeStruct((batches, rows, members), jnp.int32),
            jax.ShapeDtypeStruct(carried.shape, carried.dtype),
        ],
        input_output_aliases={5: 3},
        compiler_params=params(),
        name="row_tables",
    )(
        me,
        routes.reshape(batches, 1, rows),
        routes,
        jnp.transpose(places, (0, 2, 1)),
        after,
        carried,
    )


def member_rows(ordered, offset_ref, step, members):
    count = ordered.shape[0] // members
    rows = ordered[:count]
    for place in range(1, members):
        rows = jnp.where(
            offset_ref[0, :, step : step + 1] == place,
            ordered[place * count : (place + 1) * count],
            rows,
        )
    return rows


def middle_kernel(
    members,
    experts,
    me_ref,
    joined_ref,
    offset_ref,
    weight_ref,
    rows_ref,
    grad_ref,
    gain_ref,
    router_ref,
    route_ref,
    send_ref,
    after_ref,
    *refs,
):
    received = refs[: members - 1]
    mid_ref, normed_ref, probs_ref = refs[members - 1 : members + 2]
    out_refs = refs[members + 2 :]
    me = me_ref[0]
    span = joined_ref.shape[1]
    width = rows_ref.shape[2]
    slots = out_refs[0].shape[0]
    mid = rows_ref[0].astype(float32)
    for step in range(members):
        owner = jnp.where(me >= step, me - step, me - step + members)
        part = (
            member_rows(joined_ref[...], offset_ref, 0, members)
            if step == 0
            else received[step - 1][...]
        )
        mid = mid + dot_nn(part, weight_ref[pl.ds(pl.multiple_of(owner * span, span), span), :])
    mid_ref[...] = mid
    normed = norm_rows(mid, gain_ref[...]).astype(bfloat)
    normed_ref[...] = normed
    logits = dot_nn(normed, router_ref[...])
    lane = lax.broadcasted_iota(jnp.int32, logits.shape, 1)
    logits = jnp.where(lane < experts, logits, -jnp.inf)
    shifted = jnp.exp(logits - jnp.max(logits, axis=-1, keepdims=True))
    probs = shifted / jnp.sum(shifted, axis=-1, keepdims=True)
    probs_ref[...] = probs
    gate = jnp.sum(jnp.where(lane == route_ref[0], probs, 0.0), axis=1, keepdims=True)
    grad_expert = (gate * grad_ref[0].astype(float32)).astype(bfloat)
    tokens = dot_nn(send_ref[0], normed).astype(bfloat)
    grads = dot_nn(send_ref[0], grad_expert).astype(bfloat)
    for step in range(members):
        rows = slice(step * slots, (step + 1) * slots)
        out_refs[step][:, :width] = tokens[rows]
        out_refs[step][:, width:] = grads[rows]


def middle(
    batch, me, joined, received, offsets, weight, rows, grads, gain, router, routes, send, after
):
    members = offsets.shape[2]
    experts = members
    _, count, width = rows.shape
    slots = send.shape[1] // members
    row_spec = pl.BlockSpec((1, count, width), lambda i: (batch, 0, 0))

    def full(array):
        return pl.BlockSpec(array.shape, lambda i: (0,) * array.ndim)

    def own(array):
        return pl.BlockSpec((1,) + array.shape[1:], lambda i: (batch, 0, 0))

    out_shape = [
        jax.ShapeDtypeStruct((count, width), float32),
        jax.ShapeDtypeStruct((count, width), bfloat),
        jax.ShapeDtypeStruct((count, tile), float32),
    ] + [jax.ShapeDtypeStruct((slots, 2 * width), bfloat)] * members
    outs = pl.pallas_call(
        functools.partial(middle_kernel, members, experts),
        grid=(1,),
        in_specs=[
            pl.BlockSpec(memory_space=pltpu.SMEM),
            full(joined),
            own(offsets),
            full(weight),
            row_spec,
            row_spec,
            full(gain),
            full(router),
            own(routes),
            own(send),
            pl.BlockSpec(memory_space=pl.ANY),
        ]
        + [full(part) for part in received],
        out_specs=[full(shape) for shape in out_shape],
        out_shape=out_shape,
        compiler_params=params(),
        cost_estimate=pl.CostEstimate(
            flops=48 * count * width * width, bytes_accessed=12 * count * width, transcendentals=0
        ),
        name="middle",
    )(me, joined, offsets, weight, rows, grads, gain, router, routes, send, after, *received)
    return outs[0], outs[1], outs[2], list(outs[3:])


def second_kernel(
    members,
    experts,
    aliased,
    me_ref,
    back_ref,
    mid_ref,
    normed_ref,
    probs_ref,
    grad_ref,
    route_ref,
    gain_ref,
    router_ref,
    weight_ref,
    after_ref,
    *refs,
):
    returned = refs[:members]
    outs = refs[members + aliased :]
    layer_ref, grad_mid_ref, grad_attn_ref, gain_out_ref, router_out_ref = outs[:5]
    part_refs = outs[5:]
    me = me_ref[0]
    width = mid_ref.shape[1]
    span = part_refs[0].shape[1]
    blocks = jnp.concatenate([ref[...] for ref in returned], axis=0)
    home = dot_nn(back_ref[0], blocks)
    expert_back = home[:, :width]
    mid = mid_ref[...]
    gain = gain_ref[...]
    grads = grad_ref[0].astype(float32)
    probs = probs_ref[...]
    lane = lax.broadcasted_iota(jnp.int32, probs.shape, 1)
    picked = lane == route_ref[0]
    gate = jnp.sum(jnp.where(picked, probs, 0.0), axis=1, keepdims=True)
    layer_ref[0] = (mid + gate * expert_back).astype(bfloat)
    grad_gate = jnp.sum(grads * expert_back, axis=1, keepdims=True)
    grad_logits = (grad_gate * gate) * (jnp.where(picked, 1.0, 0.0) - probs)
    grad_logits = jnp.where(lane < experts, grad_logits, 0.0)
    grad_normed = home[:, width:]
    for name in range(experts):
        grad_normed = grad_normed + grad_logits[:, name : name + 1] * router_ref[name : name + 1, :]
    upper = grad_logits.astype(bfloat)
    lower = (grad_logits - upper.astype(float32)).astype(bfloat)
    normed = normed_ref[...]
    router_out_ref[...] = dot_tn(upper, normed) + dot_tn(lower, normed)
    grad_resid, terms = norm_back(mid, gain, grad_normed)
    gain_out_ref[...] = jnp.sum(terms, axis=0, keepdims=True)
    grad_mid = grads + grad_resid
    grad_mid_ref[...] = grad_mid
    grad_attn = grad_mid.astype(bfloat)
    grad_attn_ref[...] = grad_attn
    for step in range(members):
        owner = jnp.where(me >= step, me - step, me - step + members)
        rows = weight_ref[pl.ds(pl.multiple_of(owner * span, span), span), :]
        part_refs[step][...] = dot_nt(grad_attn, rows).astype(bfloat)


def second_back(
    batch,
    batches,
    me,
    returned,
    back,
    mid,
    normed,
    probs,
    grads,
    routes,
    gain,
    router,
    weight,
    members,
    span,
    after,
    layer,
):
    count, width = mid.shape
    grad_spec = pl.BlockSpec((1, count, width), lambda i: (batch, 0, 0))

    def full(array):
        return pl.BlockSpec(array.shape, lambda i: (0,) * array.ndim)

    def own(array):
        return pl.BlockSpec((1,) + array.shape[1:], lambda i: (batch, 0, 0))

    rest = [
        jax.ShapeDtypeStruct((count, width), float32),
        jax.ShapeDtypeStruct((count, width), bfloat),
        jax.ShapeDtypeStruct((1, width), float32),
        jax.ShapeDtypeStruct((tile, width), float32),
    ] + [jax.ShapeDtypeStruct((count, span), bfloat)] * members
    aliased = 0 if layer is None else 1
    outs = pl.pallas_call(
        functools.partial(second_kernel, members, members, aliased),
        grid=(1,),
        in_specs=[
            pl.BlockSpec(memory_space=pltpu.SMEM),
            own(back),
            full(mid),
            full(normed),
            full(probs),
            grad_spec,
            own(routes),
            full(gain),
            full(router),
            full(weight),
            pl.BlockSpec(memory_space=pl.ANY),
        ]
        + [full(part) for part in returned]
        + [pl.BlockSpec(memory_space=pl.ANY)] * aliased,
        out_specs=[grad_spec] + [full(shape) for shape in rest],
        out_shape=[jax.ShapeDtypeStruct((batches, count, width), bfloat)] + rest,
        input_output_aliases={11 + members: 0} if aliased else {},
        compiler_params=params(),
        cost_estimate=pl.CostEstimate(
            flops=6 * count * width * width, bytes_accessed=12 * count * width, transcendentals=0
        ),
        name="second_back",
    )(
        me,
        back,
        mid,
        normed,
        probs,
        grads,
        routes,
        gain,
        router,
        weight,
        after,
        *returned,
        *([] if layer is None else [layer]),
    )
    return outs[0], outs[1], outs[2], outs[3], outs[4], list(outs[5:])


def first_kernel(
    members,
    pairs,
    grads_ref,
    weight_ref,
    offset_ref,
    after_ref,
    *out_refs,
):
    width = out_refs[0].shape[1]
    depth = weight_ref.shape[1] // pairs
    lanes = weight_ref.shape[2]
    total = None
    for pair in range(pairs):
        weight = weight_ref[:, pair * depth : (pair + 1) * depth, :].reshape(width, lanes)
        term = dot_nt(grads_ref[:, pair * lanes : (pair + 1) * lanes], weight)
        total = term if total is None else total + term
    for step in range(members):
        out_refs[step][...] = member_rows(total, offset_ref, step, members).astype(
            out_refs[step].dtype
        )


def first_back(batch, grads, packed, pairs, width, offsets, after):
    members = offsets.shape[2]
    count = grads.shape[0]
    lanes = packed.shape[2]
    weight_shape = (packed.shape[0], pairs * width // packed.shape[0], lanes)
    own = jax.ShapeDtypeStruct((count // members, width), float32)
    sent = jax.ShapeDtypeStruct((count // members, width), bfloat)
    out_shape = [own] + [sent] * (members - 1)

    def full(array):
        return pl.BlockSpec(array.shape, lambda i: (0,) * len(array.shape))

    outs = pl.pallas_call(
        functools.partial(first_kernel, members, pairs),
        grid=(1,),
        in_specs=[
            full(grads),
            pl.BlockSpec(weight_shape, lambda i: (0, 0, 0)),
            pl.BlockSpec((1,) + offsets.shape[1:], lambda i: (batch, 0, 0)),
            pl.BlockSpec(memory_space=pl.ANY),
        ],
        out_specs=[full(shape) for shape in out_shape],
        out_shape=out_shape,
        compiler_params=params(),
        cost_estimate=pl.CostEstimate(
            flops=2 * count * width * lanes * pairs,
            bytes_accessed=8 * count * width,
            transcendentals=0,
        ),
        name="first_back",
    )(grads, packed, offsets, after)
    return outs[0], list(outs[1:])


def finish_kernel(received, own_ref, rows_ref, gain_ref, mid_ref, after_ref, *refs):
    total = own_ref[...]
    for ref in refs[:received]:
        total = total + ref[...].astype(float32)
    grad, _ = norm_back(rows_ref[0].astype(float32), gain_ref[...], total)
    refs[-1][0] = mid_ref[...] + grad


def finish(batch, own, received, rows, gain, mid, buffer, after):
    batches, count, width = rows.shape
    row_spec = pl.BlockSpec((1, count, width), lambda i: (batch, 0, 0))

    def full(array):
        return pl.BlockSpec(array.shape, lambda i: (0,) * array.ndim)

    operands = [own, rows, gain, mid, after] + received
    in_specs = [full(own), row_spec, full(gain), full(mid), pl.BlockSpec(memory_space=pl.ANY)]
    in_specs = in_specs + [full(part) for part in received]
    aliases = {}
    if buffer is not None:
        aliases = {len(operands): 0}
        operands.append(buffer)
        in_specs.append(pl.BlockSpec(memory_space=pl.ANY))
    return pl.pallas_call(
        functools.partial(finish_kernel, len(received)),
        grid=(1,),
        in_specs=in_specs,
        out_specs=row_spec,
        out_shape=jax.ShapeDtypeStruct((batches, count, width), float32),
        input_output_aliases=aliases,
        compiler_params=params(),
        name="finish",
    )(*operands)


def dense_kernel(skipped, handed, batches, weighted, blocks, *refs):
    refs = refs[skipped : len(refs) - handed]
    out_ref = refs[2 * batches + weighted]
    left = jnp.concatenate([ref[...] for ref in refs[:batches]], axis=0)
    right = jnp.concatenate([ref[...] for ref in refs[batches : 2 * batches]], axis=0)
    total = dot_tn(left, right)
    depth = out_ref.shape[1] // blocks
    lanes = out_ref.shape[2]
    term = None
    for block in range(blocks):
        part = total[:, block * lanes : (block + 1) * lanes]
        rows = slice(block * depth, (block + 1) * depth)
        out_ref[:, rows, :] = part.astype(bfloat).reshape(out_ref.shape[0], depth, lanes)
        if weighted:
            weight = refs[2 * batches][:, rows, :].reshape(part.shape).astype(float32)
            term = part * weight if term is None else term + part * weight
    if weighted:
        refs[-1][...] = jnp.sum(term, axis=1, keepdims=True)


def dense_grad(left, right, lanes, shards, direct, afters, packed=None, handed=()):
    afters = list(handed) + list(afters)
    batches = len(left)
    count, width = left[0].shape
    columns = right[0].shape[1]
    blocks = columns // lanes
    depth = width // shards
    steps = 2 if direct and width % (2 * tile) == 0 and shards % 2 == 0 else 1
    outer = shards // steps if direct else 1
    inner = depth if direct else width
    weighted = 0 if packed is None else 1
    outs = pl.pallas_call(
        functools.partial(dense_kernel, len(afters), len(handed), batches, weighted, blocks),
        grid=(steps,),
        in_specs=[pl.BlockSpec(memory_space=pl.ANY)] * len(afters)
        + [pl.BlockSpec((count, width // steps), lambda i: (0, i))] * batches
        + [pl.BlockSpec((count, columns), lambda i: (0, 0))] * batches
        + [pl.BlockSpec((outer, blocks * inner, lanes), lambda i: (i, 0, 0))] * weighted,
        out_specs=[pl.BlockSpec((outer, blocks * inner, lanes), lambda i: (i, 0, 0))]
        + [pl.BlockSpec((width // steps, 1), lambda i: (i, 0))] * weighted
        + [pl.BlockSpec(memory_space=pl.ANY)] * len(handed),
        out_shape=[jax.ShapeDtypeStruct((outer * steps, blocks * inner, lanes), bfloat)]
        + [jax.ShapeDtypeStruct((width, 1), float32)] * weighted
        + [jax.ShapeDtypeStruct(array.shape, array.dtype) for array in handed],
        input_output_aliases={idx: 1 + weighted + idx for idx in range(len(handed))},
        compiler_params=params(),
        cost_estimate=pl.CostEstimate(
            flops=2 * batches * count * width * columns,
            bytes_accessed=2 * batches * count * width,
            transcendentals=0,
        ),
        name="dense_grad",
    )(*afters, *left, *right, *([packed] if weighted else []))
    out = outs[0]
    if not direct:
        out = jnp.transpose(out.reshape(blocks, shards, depth, lanes), (1, 0, 2, 3))
        out = out.reshape(shards, blocks * depth, lanes)
    return (out,) + tuple(outs[1:])


def segment_of(positions, ends):
    segment = jnp.zeros(positions.shape, jnp.int32)
    for end in ends:
        segment = segment + (positions >= end).astype(jnp.int32)
    return segment


def masked_heads(rows, lane, per, head_dim):
    parts = []
    for sub in range(per):
        inside = (lane >= sub * head_dim) & (lane < (sub + 1) * head_dim)
        parts.append(jnp.where(inside, rows, jnp.zeros_like(rows)))
    return jnp.concatenate(parts, axis=0)


def joined_heads(rows, lane, per, head_dim):
    joined = rows[:tile]
    for sub in range(1, per):
        inside = (lane >= sub * head_dim) & (lane < (sub + 1) * head_dim)
        joined = jnp.where(inside, rows[sub * tile : (sub + 1) * tile], joined)
    return joined


def attend_kernel(
    stride,
    head_dim,
    far_ref,
    ends_ref,
    q_ref,
    k_ref,
    v_ref,
    bias_ref,
    after_ref,
    probs_ref,
    out_ref,
    inv_ref,
):
    pair = pl.program_id(0)
    rows_all = q_ref.shape[0]
    rows_part = rows_all // stride
    tiles = rows_part // tile
    reach = near_shift(tiles)
    per = tile // head_dim
    lane = lax.broadcasted_iota(jnp.int32, (tile, tile), 1)
    ends = [ends_ref[idx] for idx in range(ends_ref.shape[0])]
    keys_t = k_ref[...].T
    lane_row = lax.broadcasted_iota(jnp.int32, (1, tile), 1)
    row_column = lax.broadcasted_iota(jnp.int32, (tile, 1), 0)
    key_segments = [
        segment_of(stride * (col * tile + lane_row) + part, ends)
        for part in range(stride)
        for col in range(tiles)
    ]
    for mine in range(stride):
        for block in range(tiles):
            begin = mine * rows_part + block * tile
            rows = slice(begin, begin + tile)
            segment = segment_of(stride * (block * tile + row_column) + mine, ends)
            raw = dot_nn(masked_heads(q_ref[rows, :], lane, per, head_dim), keys_t)
            stacked = []
            inverses = []
            for sub in range(per):
                head = pair * per + sub
                pieces = []
                top = None
                for part in range(stride):
                    for col in range(tiles):
                        start = (part * tiles + col) * tile
                        piece = raw[sub * tile : (sub + 1) * tile, start : start + tile]
                        shift = col - block
                        if shift < -reach:
                            piece = piece + far_ref[0, head]
                        elif shift > reach:
                            piece = piece + far_ref[1, head]
                        else:
                            columns = slice((shift + reach) * tile, (shift + reach + 1) * tile)
                            piece = piece + bias_ref[sub, part - mine + stride - 1, :, columns]
                        same = key_segments[part * tiles + col] == segment
                        piece = jnp.where(same, piece, masked_score)
                        pieces.append(piece)
                        top = piece if top is None else jnp.maximum(top, piece)
                row_max = jnp.max(top, axis=-1, keepdims=True)
                total = None
                for idx, piece in enumerate(pieces):
                    piece = jnp.exp(piece - row_max)
                    total = piece if total is None else total + piece
                    pieces[idx] = piece.astype(bfloat)
                kept = jnp.concatenate(pieces, axis=1)
                probs_ref[sub, rows, :] = kept
                stacked.append(kept)
                inverses.append(1.0 / jnp.sum(total, axis=-1, keepdims=True))
            result = dot_nn(jnp.concatenate(stacked, axis=0), v_ref[...])
            inverse = jnp.broadcast_to(inverses[0], (tile, tile))
            for sub in range(1, per):
                inside = (lane >= sub * head_dim) & (lane < (sub + 1) * head_dim)
                inverse = jnp.where(inside, inverses[sub], inverse)
            out_ref[rows, :] = (joined_heads(result, lane, per, head_dim) * inverse).astype(bfloat)
            inv_ref[rows, :] = inverse


def kind_specs(rows_all):
    return [
        pl.BlockSpec((rows_all, tile), lambda i, kind=kind: (0, 3 * i + kind)) for kind in range(3)
    ]


def attend(qkv, ends, bias, far, after, head_dim, stride):
    rows_all, span = qkv.shape[0], qkv.shape[1] // 3
    per = tile // head_dim
    heads = span // head_dim
    row_spec = pl.BlockSpec((rows_all, tile), lambda i: (0, i))
    return pl.pallas_call(
        functools.partial(attend_kernel, stride, head_dim),
        grid=(span // tile,),
        in_specs=[
            pl.BlockSpec(memory_space=pltpu.SMEM),
            pl.BlockSpec(memory_space=pltpu.SMEM),
            *kind_specs(rows_all),
            pl.BlockSpec((per,) + bias.shape[1:], lambda i: (i, 0, 0, 0)),
            pl.BlockSpec(memory_space=pl.ANY),
        ],
        out_specs=[
            pl.BlockSpec((per, rows_all, rows_all), lambda i: (i, 0, 0)),
            row_spec,
            row_spec,
        ],
        out_shape=[
            jax.ShapeDtypeStruct((heads, rows_all, rows_all), bfloat),
            jax.ShapeDtypeStruct((rows_all, span), bfloat),
            jax.ShapeDtypeStruct((rows_all, span), float32),
        ],
        compiler_params=params(),
        cost_estimate=pl.CostEstimate(
            flops=16 * rows_all * rows_all * span,
            bytes_accessed=2 * heads * rows_all * rows_all,
            transcendentals=heads * rows_all * rows_all,
        ),
        name="attend",
    )(far, ends, qkv, qkv, qkv, bias, after)


def attend_back_kernel(
    stride,
    head_dim,
    scale,
    carried,
    skipped,
    probs_ref,
    out_ref,
    inv_ref,
    q_ref,
    k_ref,
    v_ref,
    offset_ref,
    *refs,
):
    refs = refs[skipped:]
    grad_refs = refs[:stride]
    dqkv_ref, dbias_ref, dfar_ref, ds_ref, grads_ref = refs[-5:]
    rows_all = q_ref.shape[0]
    rows_part = rows_all // stride
    tiles = rows_part // tile
    reach = near_shift(tiles)
    per = tile // head_dim
    lane = lax.broadcasted_iota(jnp.int32, (tile, tile), 1)
    queries_t = q_ref[...].T
    values_t = v_ref[...].T
    for place in range(stride):
        span = slice(place * rows_part, (place + 1) * rows_part)
        rows = grad_refs[0][...]
        for step in range(1, stride):
            rows = jnp.where(offset_ref[0, :, step : step + 1] == place, grad_refs[step][...], rows)
        grads_ref[span, :] = (rows.astype(float32) * inv_ref[span, :]).astype(bfloat)
    grads_t = grads_ref[...].T
    if carried:
        dbias_ref[...] = refs[stride][...]
        dfar_ref[...] = refs[stride + 1][...]
    else:
        dbias_ref[...] = jnp.zeros_like(dbias_ref)
        dfar_ref[...] = jnp.zeros_like(dfar_ref)
    for mine in range(stride):
        for block in range(tiles):
            begin = mine * rows_part + block * tile
            rows = slice(begin, begin + tile)
            own = masked_heads(grads_ref[rows, :], lane, per, head_dim)
            outs = out_ref[rows, :].astype(float32)
            raw = dot_nn(own, values_t)
            stacked = []
            for sub in range(per):
                span = slice(sub * tile, (sub + 1) * tile)
                row_dot = jnp.sum(own[span].astype(float32) * outs, axis=-1, keepdims=True)
                pieces = []
                for part in range(stride):
                    for col in range(tiles):
                        start = (part * tiles + col) * tile
                        piece = probs_ref[sub, rows, start : start + tile].astype(float32) * (
                            raw[span, start : start + tile] - row_dot
                        )
                        shift = col - block
                        if shift < -reach:
                            dfar_ref[sub, 0] += piece
                        elif shift > reach:
                            dfar_ref[sub, 1] += piece
                        else:
                            columns = slice((shift + reach) * tile, (shift + reach + 1) * tile)
                            dbias_ref[sub, part - mine + stride - 1, :, columns] += piece
                        pieces.append(piece.astype(bfloat))
                low_grads = jnp.concatenate(pieces, axis=1)
                ds_ref[sub, rows, :] = low_grads
                stacked.append(low_grads)
            result = dot_nn(jnp.concatenate(stacked, axis=0), k_ref[...]) * scale
            dqkv_ref[rows, :tile] = joined_heads(result, lane, per, head_dim).astype(bfloat)
    dk_parts = []
    dv_parts = []
    for sub in range(per):
        dims = slice(sub * head_dim, (sub + 1) * head_dim)
        dk_parts.append(dot_nn(queries_t[dims, :], ds_ref[sub]))
        dv_parts.append(dot_nn(grads_t[dims, :], probs_ref[sub]))
    dqkv_ref[:, tile : 2 * tile] = jnp.concatenate(dk_parts, axis=0).T.astype(bfloat)
    dqkv_ref[:, 2 * tile :] = jnp.concatenate(dv_parts, axis=0).T.astype(bfloat)


def attend_back(
    batch, probs, grads, outs, inverse, qkv, offsets, afters, sums, head_dim, stride, bias_shape
):
    rows_all, span = outs.shape
    per = tile // head_dim
    heads = span // head_dim
    row_spec = pl.BlockSpec((rows_all, tile), lambda i: (0, i))
    part_spec = pl.BlockSpec((rows_all // stride, tile), lambda i: (0, i))
    sum_specs = [
        pl.BlockSpec((per,) + bias_shape[1:], lambda i: (i, 0, 0, 0)),
        pl.BlockSpec((per, 2, tile, tile), lambda i: (i, 0, 0, 0)),
    ]
    carried = len(sums) > 0
    first = 7 + len(afters) + stride
    return pl.pallas_call(
        functools.partial(
            attend_back_kernel, stride, head_dim, head_dim ** (-0.5), carried, len(afters)
        ),
        grid=(span // tile,),
        in_specs=[pl.BlockSpec((per, rows_all, rows_all), lambda i: (i, 0, 0))]
        + [row_spec] * 2
        + kind_specs(rows_all)
        + [pl.BlockSpec((1,) + offsets.shape[1:], lambda i: (batch, 0, 0))]
        + [pl.BlockSpec(memory_space=pl.ANY)] * len(afters)
        + [part_spec] * stride
        + (sum_specs if carried else []),
        out_specs=[pl.BlockSpec((rows_all, 3 * tile), lambda i: (0, i))] + sum_specs,
        out_shape=[
            jax.ShapeDtypeStruct((rows_all, 3 * span), bfloat),
            jax.ShapeDtypeStruct(bias_shape, float32),
            jax.ShapeDtypeStruct((heads, 2, tile, tile), float32),
        ],
        scratch_shapes=[
            pltpu.VMEM((per, rows_all, rows_all), bfloat),
            pltpu.VMEM((rows_all, tile), bfloat),
        ],
        input_output_aliases={first: 1, first + 1: 2} if carried else {},
        compiler_params=params(),
        cost_estimate=pl.CostEstimate(
            flops=32 * rows_all * rows_all * span,
            bytes_accessed=2 * heads * rows_all * rows_all,
            transcendentals=0,
        ),
        name="attend_back",
    )(probs, outs, inverse, qkv, qkv, qkv, offsets, *afters, *grads, *sums)


def add_kernel(skipped, *refs):
    refs = refs[skipped:]
    out_ref = refs[-1]
    start = 0
    for left_ref, right_ref in zip(refs[:-1:2], refs[1:-1:2]):
        rows = left_ref.shape[1]
        out_ref[:, start : start + rows] = (
            left_ref[...].astype(float32) + right_ref[...].astype(float32)
        ).astype(bfloat)
        start += rows


def add_after(afters, *operands):
    vmem = pl.BlockSpec(memory_space=pltpu.VMEM)
    outer, _, lanes = operands[0].shape
    rows = sum(operand.shape[1] for operand in operands[::2])
    return pl.pallas_call(
        functools.partial(add_kernel, len(afters)),
        in_specs=[pl.BlockSpec(memory_space=pl.ANY)] * len(afters) + [vmem] * len(operands),
        out_specs=vmem,
        out_shape=jax.ShapeDtypeStruct((outer, rows, lanes), bfloat),
        compiler_params=params(),
        name="add_after",
    )(*afters, *operands)


def order_kernel(count, place_ref, *refs):
    out_ref = refs[count + 1]
    for place in range(count):
        rows = refs[0][0]
        for step in range(1, count):
            rows = jnp.where(place_ref[0, :, step : step + 1] == place, refs[step][0], rows)
        out_ref[0, place] = rows


def order_rows(parts, offsets, carried):
    batches, rows, width = parts[0].shape
    count = len(parts)
    part_spec = pl.BlockSpec((1, rows, width), lambda i: (i, 0, 0))
    return pl.pallas_call(
        functools.partial(order_kernel, count),
        grid=(batches,),
        in_specs=[pl.BlockSpec((1, rows, count), lambda i: (i, 0, 0))]
        + [part_spec] * count
        + [pl.BlockSpec(memory_space=pl.ANY)],
        out_specs=[
            pl.BlockSpec((1, count, rows, width), lambda i: (i, 0, 0, 0)),
            pl.BlockSpec(memory_space=pl.ANY),
        ],
        out_shape=[
            jax.ShapeDtypeStruct((batches, count, rows, width), bfloat),
            jax.ShapeDtypeStruct(carried.shape, carried.dtype),
        ],
        input_output_aliases={count + 1: 1},
        compiler_params=params(),
        name="order_rows",
    )(offsets, *parts, carried)


def expert_kernel(
    count, slots, width, inner_ref, outer_ref, after_ref, *refs
):
    blocks = refs[:count]
    results = refs[count : 2 * count]
    hidden_ref, grad_pre_ref, rows_ref, grads_ref, sum_ref, back_ref = refs[2 * count :]
    turn = pl.program_id(0)

    @pl.when(turn == 0)
    def _():
        for idx in range(count):
            rows = slice(idx * slots, (idx + 1) * slots)
            rows_ref[rows, :] = blocks[idx][:, :width]
            grads_ref[rows, :] = blocks[idx][:, width:]

    inner = inner_ref[...].reshape(width, width)
    outer = outer_ref[...].reshape(width, width)
    rows = rows_ref[...]
    grads = grads_ref[...]
    root = 0.7978845608028654
    pre = dot_nn(rows, inner)
    grad_hidden = dot_nt(grads, outer)
    square = pre * pre
    curve = jnp.tanh(root * pre * (1.0 + 0.044715 * square))
    half = 0.5 * (1.0 + curve)
    slope = half + (0.5 * root) * pre * (1.0 - curve * curve) * (1.0 + 0.134145 * square)
    hidden_ref[...] = (pre * half).astype(bfloat)
    grad_pre_ref[...] = (grad_hidden * slope).astype(bfloat)
    product = dot_nn(hidden_ref[...], outer)
    product_back = dot_nt(grad_pre_ref[...], inner)

    @pl.when(turn == 0)
    def _():
        sum_ref[...] = product
        back_ref[...] = product_back

    @pl.when(turn > 0)
    def _():
        sum_ref[...] += product
        back_ref[...] += product_back

    @pl.when(turn == pl.num_programs(0) - 1)
    def _():
        for idx in range(count):
            span = slice(idx * slots, (idx + 1) * slots)
            results[idx][:, :width] = sum_ref[span, :].astype(bfloat)
            results[idx][:, width:] = back_ref[span, :].astype(bfloat)


def run_expert(weights, blocks, width, after):
    (inner, inner_spec), (outer, outer_spec), turns = weights
    count = len(blocks)
    slots = blocks[0].shape[0]
    total = count * slots
    whole = pl.BlockSpec((slots, 2 * width), lambda i: (0, 0))
    chunk = pl.BlockSpec((total, width), lambda i: (0, i))
    outs = pl.pallas_call(
        functools.partial(expert_kernel, count, slots, width),
        grid=(turns,),
        in_specs=[inner_spec, outer_spec, pl.BlockSpec(memory_space=pl.ANY)] + [whole] * count,
        out_specs=[whole] * count + [chunk, chunk],
        out_shape=[jax.ShapeDtypeStruct((slots, 2 * width), bfloat)] * count
        + [jax.ShapeDtypeStruct((total, turns * width), bfloat)] * 2,
        scratch_shapes=[
            pltpu.VMEM((total, width), bfloat),
            pltpu.VMEM((total, width), bfloat),
            pltpu.VMEM((total, width), float32),
            pltpu.VMEM((total, width), float32),
        ],
        compiler_params=params(),
        cost_estimate=pl.CostEstimate(
            flops=8 * total * width * width * turns,
            bytes_accessed=4 * width * width * turns,
            transcendentals=total * width * turns,
        ),
        name="run_expert",
    )(inner, outer, after, *blocks)
    return outs[:count], outs[count], outs[count + 1]


def expert_grad_kernel(batches, count, slots, width, second, *refs):
    groups = [refs[idx * count : (idx + 1) * count] for idx in range(batches)]
    wide = refs[batches * count : batches * count + batches]
    out_ref, rows_ref = refs[-2], refs[-1]
    half = slice(width, 2 * width) if second else slice(0, width)

    @pl.when(pl.program_id(0) == 0)
    def _():
        for batch in range(batches):
            for idx in range(count):
                start = (batch * count + idx) * slots
                rows_ref[start : start + slots, :] = groups[batch][idx][:, half]

    rows = rows_ref[...]
    columns = jnp.concatenate([ref[...] for ref in wide], axis=0)
    total = dot_tn(columns, rows) if second else dot_tn(rows, columns)
    out_ref[...] = total.astype(bfloat).reshape(out_ref.shape)


def expert_grad(groups, wide, width, second, out_shape, out_spec, afters, buffer=None):
    batches = len(groups)
    count = len(groups[0])
    slots = groups[0][0].shape[0]
    total = count * slots
    turns = wide[0].shape[1] // width
    kernel = functools.partial(expert_grad_kernel, batches, count, slots, width, second)
    in_specs = [pl.BlockSpec((slots, 2 * width), lambda i: (0, 0))] * (batches * count)
    in_specs = in_specs + [pl.BlockSpec((total, width), lambda i: (0, i))] * batches
    operands = [block for group in groups for block in group] + list(wide)
    aliases = {}
    carried = list(afters)
    if buffer is not None:
        carried = [buffer] + carried
        aliases = {0: 0}
    skipped = len(carried)
    in_specs = [pl.BlockSpec(memory_space=pl.ANY)] * skipped + in_specs
    operands = carried + operands

    def body(*refs):
        kernel(*refs[skipped:])

    return pl.pallas_call(
        body,
        grid=(turns,),
        in_specs=in_specs,
        out_specs=out_spec,
        out_shape=jax.ShapeDtypeStruct(out_shape, bfloat),
        scratch_shapes=[pltpu.VMEM((batches * total, width), bfloat)],
        input_output_aliases=aliases,
        compiler_params=params(),
        cost_estimate=pl.CostEstimate(
            flops=2 * batches * total * width * width * turns,
            bytes_accessed=4 * width * width * turns,
            transcendentals=0,
        ),
        name="expert_grad_outer" if second else "expert_grad_inner",
    )(*operands)


def on_device(
    hidden_in,
    out_grad,
    places,
    lengths,
    routes,
    norm1_gain,
    w_query,
    w_key,
    w_value,
    w_output,
    rel_table,
    norm2_gain,
    w_router,
    w_in,
    w_out,
):
    batches, rows_own, width = hidden_in.shape
    heads = rel_table.shape[1]
    head_dim = width // heads
    scale = head_dim ** (-0.5)
    shards = lax.axis_size("dp")
    members = lax.axis_size("expert")
    me = lax.axis_index("expert")
    experts = w_router.shape[1]
    hidden_width = w_in.shape[2]
    turns = hidden_width // width
    tiles = rows_own // tile
    rows_group = members * rows_own
    depth = width // shards
    depth_out = hidden_width // shards
    table_rows = rel_table.shape[0]
    capacity = max(2, rows_own * 17 // (experts * 16))
    slots = -(-capacity // 16) * 16
    per = tile // head_dim
    heads_own = per * (-(-heads // (per * members)))
    span = heads_own * head_dim
    pairs = span // tile
    lanes = 3 * tile
    split = width // lanes
    me_row = me.reshape(1)

    def around(step):
        return [(idx, (idx + step) % members) for idx in range(members)]

    def columns_own(weight):
        wide = jnp.pad(weight, ((0, 0), (0, members * span - width)))
        return lax.dynamic_slice_in_dim(wide, me * span, span, axis=1)

    def in_order(parts):
        if members == 2:
            return [
                jnp.where(me == 0, parts[0], parts[1]),
                jnp.where(me == 0, parts[1], parts[0]),
            ]
        stacked = jnp.stack(parts)
        return [stacked[jnp.mod(me - idx, members)] for idx in range(members)]

    hidden_from = [hidden_in] + [
        lax.ppermute(hidden_in, "expert", around(step)) for step in range(1, members)
    ]

    small = jnp.concatenate(
        [
            norm1_gain.reshape(-1),
            norm2_gain.reshape(-1),
            w_router.reshape(-1),
            rel_table.reshape(-1),
        ]
    )
    small_used = small.shape[0]
    small_pad = -(-small_used // (16 * lanes)) * 16
    small = jnp.pad(small, (0, small_pad * lanes - small_used)).reshape(small_pad, lanes)
    kinds = [columns_own(weight) for weight in (w_query, w_key, w_value)]
    first_own = jnp.concatenate(
        [
            jnp.concatenate([kind[:, idx * tile : (idx + 1) * tile] for kind in kinds], axis=1)
            for idx in range(pairs)
        ]
        + [w_output[:, idx * lanes : (idx + 1) * lanes] for idx in range(split)]
        + [small],
        axis=0,
    )
    first = lax.all_gather(first_own, "dp", axis=0, tiled=False)
    inner_parts = [w_in[0, :, idx * width : (idx + 1) * width] for idx in range(turns)]
    second_own = jnp.concatenate(inner_parts + [w_out[0]], axis=0)
    places_in = places[:, 0].reshape(batches, members, rows_own)
    dispatch, collect, offsets, second_own = row_tables(
        me_row, routes, places_in, hidden_from[-1], second_own, members, slots
    )
    second = lax.all_gather(second_own, "dp", axis=0, tiled=False)
    ends = jnp.cumsum(lengths[:, 0], axis=-1)[:, :-1]
    ordered_in, first = order_rows(hidden_from, offsets, first)
    ordered_in = ordered_in.reshape(batches, rows_group, width)

    small_start = (pairs + split) * depth
    small_all = first[:, small_start:].reshape(shards, small_pad * lanes)
    gain_one = small_all[:, :depth].reshape(1, width).astype(float32)
    gain_two = small_all[:, depth : 2 * depth].reshape(1, width).astype(float32)
    router_end = 2 * depth + depth * experts
    router_w = small_all[:, 2 * depth : router_end].reshape(width, experts)
    table = small_all[:, router_end:small_used].reshape(shards * table_rows, heads)
    router_wide = jnp.pad(router_w, ((0, 0), (0, tile - experts)))
    router_t = router_w.astype(float32).T
    output_w = jnp.concatenate(
        [
            first[:, (pairs + idx) * depth : (pairs + idx + 1) * depth].reshape(width, lanes)
            for idx in range(split)
        ],
        axis=1,
    )
    output_w = jnp.pad(output_w, ((0, members * span - width), (0, 0)))

    direct = depth % 16 == 0 and turns * depth == depth_out and shards % turns == 0
    if direct:
        group = shards // turns
        packed = first
        inner_spec = pl.BlockSpec((shards, depth, width), lambda i: (0, i, 0))
        outer_spec = pl.BlockSpec((group, depth_out, width), lambda i: (i, 1, 0))
        weights = ((second, inner_spec), (second, outer_spec), turns)
    else:
        packed = jnp.concatenate(
            [
                first[:, idx * depth : (idx + 1) * depth].reshape(1, width, lanes)
                for idx in range(pairs)
            ],
            axis=1,
        )
        inner_w = second[:, : turns * depth].reshape(shards, turns, depth, width)
        inner_w = jnp.transpose(inner_w, (1, 0, 2, 3)).reshape(turns, width, width)
        outer_w = second[:, turns * depth : turns * depth + depth_out].reshape(
            turns, width, width
        )
        plain = pl.BlockSpec((1, width, width), lambda i: (i, 0, 0))
        weights = ((inner_w, plain), (outer_w, plain), turns)

    table_wide = jnp.pad(table, ((0, 0), (0, members * heads_own - heads)))
    table_own = lax.dynamic_slice_in_dim(table_wide, me * heads_own, heads_own, axis=1)
    bias = bias_tiles(table_own, members, tiles)
    table_f = table_own.astype(float32)
    far = jnp.stack([table_f[levels_all - 1], table_f[2 * levels_all - 1]])

    def send_rows(batch, ordered):
        arrived = []
        for step in range(1, members):
            rows = ordered[:rows_own]
            for place in range(1, members):
                rows = jnp.where(
                    offsets[batch, :, members - step : members - step + 1] == place,
                    ordered[place * rows_own : (place + 1) * rows_own],
                    rows,
                )
            arrived.append(lax.ppermute(rows, "expert", around(step)))
        return arrived

    normed_one = []
    qkv = []
    probs = []
    outs = []
    inverses = []
    arrived_heads = []
    resid_mid = []
    normed_two = []
    router_probs = []
    blocks = []
    after = table
    for batch in range(batches):
        normed, packed_rows = project(batch, ordered_in, gain_one, packed, pairs, scale)
        normed_one.append(normed)
        qkv.append(packed_rows)
        kept, joined, inverse = attend(
            packed_rows,
            ends[batch],
            bias,
            far,
            after,
            head_dim,
            members,
        )
        probs.append(kept)
        outs.append(joined)
        inverses.append(inverse)
        arrived_heads.append(send_rows(batch, joined))
        mid, normed, chances, outgoing = middle(
            batch,
            me_row,
            joined,
            arrived_heads[batch],
            offsets,
            output_w,
            hidden_in,
            out_grad,
            gain_two,
            router_wide,
            routes,
            dispatch,
            blocks[-1][-1] if blocks else table,
        )
        after = outgoing[-1]
        blocks.append(
            [outgoing[0]]
            + [
                lax.ppermute(outgoing[step], "expert", around(step))
                for step in range(1, members)
            ]
        )
        resid_mid.append(mid)
        normed_two.append(normed)
        router_probs.append(chances)

    returned = []
    hidden = []
    grad_pre = []
    for batch in range(batches):
        results, hidden_rows, grad_rows = run_expert(
            weights, blocks[batch], width, hidden[-1] if hidden else table
        )
        hidden.append(hidden_rows)
        grad_pre.append(grad_rows)
        returned.append(
            [results[0]]
            + [
                lax.ppermute(results[step], "expert", around(-step))
                for step in range(1, members)
            ]
        )

    layer_rows = [None]
    grad_mid = []
    grad_attn = []
    grad_heads = []
    gain_two_terms = []
    router_terms_all = []

    def norm_part(batch, after):
        layer, mid, attn, gain_terms, router_terms, parts = second_back(
            batch,
            batches,
            me_row,
            returned[batch],
            collect,
            resid_mid[batch],
            normed_two[batch],
            router_probs[batch],
            out_grad,
            routes,
            gain_two,
            router_t,
            output_w,
            members,
            span,
            after,
            layer_rows[-1],
        )
        grad_mid.append(mid)
        grad_attn.append(attn)
        layer_rows.append(layer)
        gain_two_terms.append(gain_terms)
        router_terms_all.append(router_terms[:experts])
        from_members = [parts[0]] + [
            lax.ppermute(parts[members - step], "expert", around(step))
            for step in range(1, members)
        ]
        grad_heads.append(from_members)

    if direct:
        buffer_shape = (shards, turns * depth + depth_out, width)
        buffer = expert_grad(
            blocks,
            grad_pre,
            width,
            False,
            buffer_shape,
            pl.BlockSpec((shards, depth, width), lambda i: (0, i, 0)),
            [returned[0][-1]],
        )
        norm_part(0, table)
        buffer = expert_grad(
            blocks,
            hidden,
            width,
            True,
            buffer_shape,
            pl.BlockSpec((group, depth_out, width), lambda i: (i, 1, 0)),
            [returned[-1][-1], grad_attn[0]],
            buffer,
        )
    else:
        plain_shape = (turns, width, width)
        inner_g = expert_grad(
            blocks, grad_pre, width, False, plain_shape, plain, [returned[0][-1]]
        )
        norm_part(0, table)
        outer_g = expert_grad(
            blocks, hidden, width, True, plain_shape, plain, [returned[-1][-1]]
        )
        inner_g = jnp.transpose(inner_g.reshape(turns, shards, depth, width), (1, 0, 2, 3))
        buffer = jnp.concatenate(
            [
                inner_g.reshape(shards, turns * depth, width),
                outer_g.reshape(shards, depth_out, width),
            ],
            axis=1,
        )
    expert_sum = lax.psum_scatter(buffer, "dp", scatter_dimension=0, tiled=False)
    for batch in range(1, batches):
        norm_part(batch, buffer)
    layer = layer_rows[-1]
    grad_gain_two = sum(gain_two_terms)
    grad_router = sum(router_terms_all)

    line = shards // 4
    my_shard = lax.axis_index("dp")

    def by_core(dense):
        dense = dense.reshape((line, 2, 2) + dense.shape[1:])
        odd = my_shard % 2 == 1
        sent = jnp.where(odd, dense[:, :, 0], dense[:, :, 1])
        held = jnp.where(odd, dense[:, :, 1], dense[:, :, 0])
        return held, lax.ppermute(sent, "dp", [(idx, idx ^ 1) for idx in range(shards)])

    def by_y(core_parts):
        held, got = core_parts
        odd = (my_shard // 2) % 2 == 1

        def half(idx):
            return held[:, idx].astype(float32) + got[:, idx].astype(float32)

        sent = jnp.where(odd, half(0), half(1)).astype(bfloat)
        kept = jnp.where(odd, half(1), half(0)).astype(bfloat)
        return kept, lax.ppermute(sent, "dp", [(idx, idx ^ 2) for idx in range(shards)])

    def own_rows_of(batch):
        joined = outs[batch]
        rows = joined[:rows_own]
        for place in range(1, members):
            rows = jnp.where(
                offsets[batch, :, 0:1] == place,
                joined[place * rows_own : (place + 1) * rows_own],
                rows,
            )
        return rows

    attended = [
        jnp.concatenate(in_order([own_rows_of(batch)] + arrived_heads[batch]), axis=1)[:, :width]
        for batch in range(batches)
    ]
    early_core = by_core(
        dense_grad(attended, grad_attn, lanes, shards, direct, [grad_heads[0][-1]])[0]
    )
    early = by_y(early_core)
    grad_qkv = []
    sums = []
    own_rows = []
    received_rows = []
    sent_last = buffer

    def first_part(batch, after):
        own, sent = first_back(batch, grad_qkv[batch], packed, pairs, width, offsets, after)
        own_rows.append(own)
        received_rows.append(
            [lax.ppermute(rows, "expert", around(-step)) for step, rows in enumerate(sent, 1)]
        )
        return sent[-1]

    for batch in range(batches):
        if batch > 0:
            sent_last = first_part(batch - 1, buffer)
        grads, *sums = attend_back(
            batch,
            probs[batch],
            grad_heads[batch],
            outs[batch],
            inverses[batch],
            qkv[batch],
            offsets,
            [buffer] if batch == 0 else [sent_last, early_core[1]],
            sums,
            head_dim,
            members,
            bias.shape,
        )
        grad_qkv.append(grads)
    grad_dense, weighted, grad_bias, grad_far = dense_grad(
        normed_one,
        grad_qkv,
        lanes,
        shards,
        direct,
        [early[1]] + [rows[-1] for rows in received_rows],
        packed,
        sums,
    )
    grad_gain_one = weighted[:, 0] / gain_one[0]
    late_core = by_core(grad_dense)
    late = by_y(late_core)
    sent_last = first_part(batches - 1, late_core[1])

    steps = 2 * members - 1
    reach = near_shift(tiles)
    shape = (steps, tile, (2 * reach + 1) * tile)
    delta = (
        members
        * (
            lax.broadcasted_iota(jnp.int32, shape, 2)
            - reach * tile
            - lax.broadcasted_iota(jnp.int32, shape, 1)
        )
        + lax.broadcasted_iota(jnp.int32, shape, 0)
        - (members - 1)
    )
    buckets = shards * table_rows
    onehot = (
        bucket_of(delta)[None] == jnp.arange(buckets, dtype=jnp.int32)[:, None, None, None]
    ).astype(bfloat)
    grad_table = jnp.einsum(
        "hsab,ksab->kh", grad_bias.astype(bfloat), onehot, preferred_element_type=float32
    )
    far_sum = jnp.sum(grad_far, axis=(2, 3))
    grad_table = grad_table.at[levels_all - 1].add(far_sum[:, 0])
    grad_table = grad_table.at[2 * levels_all - 1].add(far_sum[:, 1])
    grad_table = lax.dynamic_update_slice_in_dim(
        jnp.zeros((buckets, members * heads_own), float32), grad_table, me * heads_own, axis=1
    )[:, :heads]

    small_grad = jnp.concatenate(
        [
            grad_gain_one.reshape(shards, depth),
            grad_gain_two.reshape(shards, depth),
            grad_router.T.reshape(shards, depth * experts),
            grad_table.reshape(shards, table_rows * heads),
        ],
        axis=1,
    )
    small_grad = jnp.pad(small_grad, ((0, 0), (0, small_pad * lanes - small_used)))
    small_grad = small_grad.astype(bfloat).reshape(shards, small_pad, lanes)
    little = by_y(by_core(small_grad))
    dense_added = add_after([expert_sum, sent_last], *late, *little, *early)
    in_grad = None
    for batch in range(batches):
        in_grad = finish(
            batch,
            own_rows[batch],
            received_rows[batch],
            hidden_in,
            gain_one,
            grad_mid[batch],
            in_grad,
            buffer if batch < batches - 1 else dense_added,
        )
    dense_part = lax.psum_scatter(
        dense_added,
        "dp",
        scatter_dimension=0,
        tiled=False,
        axis_index_groups=[[rest + 4 * idx for idx in range(line)] for rest in range(4)],
    )
    parts = [dense_part] + [
        lax.ppermute(dense_part, "expert", around(step)) for step in range(1, members)
    ]
    qkv_parts = [
        part.astype(float32) for part in in_order([part[: pairs * depth] for part in parts])
    ]
    qkv_grads = [
        jnp.concatenate(
            [
                part[pair * depth : (pair + 1) * depth, kind * tile : (kind + 1) * tile]
                for part in qkv_parts
                for pair in range(pairs)
            ],
            axis=1,
        )[:, :width]
        for kind in range(3)
    ]
    rest_sum = sum(part[pairs * depth :].astype(float32) for part in parts)
    out_grad_sum = jnp.concatenate(
        [
            rest_sum[small_pad + idx * depth : small_pad + (idx + 1) * depth]
            for idx in range(split)
        ],
        axis=1,
    )
    small_sum = rest_sum[:small_pad].reshape(-1)

    expert_f = expert_sum.astype(float32)
    inner_sum = jnp.concatenate(
        [expert_f[idx * depth : (idx + 1) * depth] for idx in range(turns)], axis=1
    )[None]
    outer_sum = expert_f[turns * depth :][None]
    return (
        layer,
        in_grad,
        small_sum[:depth],
        qkv_grads[0],
        qkv_grads[1],
        qkv_grads[2],
        out_grad_sum,
        small_sum[router_end:small_used].reshape(table_rows, heads),
        small_sum[depth : 2 * depth],
        small_sum[2 * depth : router_end].reshape(depth, experts),
        inner_sum,
        outer_sum,
    )


def solution(mesh):
    return jax.shard_map(
        on_device,
        mesh=mesh,
        in_specs=(
            P(None, ("dp", "expert"), None),
            P(None, ("dp", "expert"), None),
            P(None, "dp", None),
            P(None, "dp", None),
            P(None, ("dp", "expert"), None),
            P("dp"),
            P("dp", None),
            P("dp", None),
            P("dp", None),
            P("dp", None),
            P("dp", None),
            P("dp"),
            P("dp", None),
            P("expert", "dp", None),
            P("expert", "dp", None),
        ),
        out_specs=(
            P(None, ("dp", "expert"), None),
            P(None, ("dp", "expert"), None),
            P("dp"),
            P("dp", None),
            P("dp", None),
            P("dp", None),
            P("dp", None),
            P("dp", None),
            P("dp"),
            P("dp", None),
            P("expert", "dp", None),
            P("expert", "dp", None),
        ),
        check_vma=False,
    )
```

```python
import functools

import jax
import jax.numpy as jnp
from jax import lax
from jax.experimental import pallas as pl
from jax.experimental.pallas import tpu as pltpu
from jax.sharding import PartitionSpec as P

bucket_edges = (1, 2, 3, 4, 5, 6, 7, 8, 12, 16, 23, 32, 46, 64, 91)
levels_all = len(bucket_edges) + 1
epsilon = 1e-06
masked_score = -1000000000.0
precise = lax.Precision.HIGHEST
float32 = jnp.float32
bfloat = jnp.bfloat16
tile = 128
vmem_bytes = 56 * 1024 * 1024


def params():
    return pltpu.CompilerParams(vmem_limit_bytes=vmem_bytes)


def dot_nn(left, right):
    return lax.dot_general(left, right, (((1,), (0,)), ((), ())), preferred_element_type=float32)


def dot_nt(left, right):
    return lax.dot_general(left, right, (((1,), (1,)), ((), ())), preferred_element_type=float32)


def dot_tn(left, right):
    return lax.dot_general(left, right, (((0,), (0,)), ((), ())), preferred_element_type=float32)


def norm_rows(rows, gain):
    mean_square = jnp.mean(rows * rows, axis=-1, keepdims=True)
    return rows * lax.rsqrt(mean_square + epsilon) * gain


def norm_back(rows, gain, grad):
    scale = lax.rsqrt(jnp.mean(rows * rows, axis=-1, keepdims=True) + epsilon)
    unit = rows * scale
    weighted = grad * gain
    inner = jnp.mean(weighted * unit, axis=-1, keepdims=True)
    return scale * (weighted - unit * inner), grad * unit


def bucket_of(offset):
    distance = jnp.abs(offset)
    levels = jnp.zeros(offset.shape, jnp.int32)
    for edge_value in bucket_edges:
        levels = levels + (distance >= edge_value).astype(jnp.int32)
    return levels + levels_all * (offset > 0).astype(jnp.int32)


def near_shift(tiles):
    return min(1, tiles - 1)


def bias_kernel(stride, reach, table_ref, out_ref):
    part = 16
    row = lax.broadcasted_iota(jnp.int32, (part, tile), 0)
    lane = lax.broadcasted_iota(jnp.int32, (part, tile), 1)
    heads = out_ref.shape[0]
    edge = bucket_edges[-1]
    for shift in range(-reach, reach + 1):
        columns = slice((shift + reach) * tile, (shift + reach + 1) * tile)
        for step in range(2 * stride - 1):
            for start in range(0, tile, part):
                base = stride * (tile * shift - start) + step - (stride - 1)
                rows = slice(start, start + part)
                far = None
                if base - stride * (part - 1) >= edge:
                    far = 2 * levels_all - 1
                elif base + stride * (tile - 1) <= -edge:
                    far = levels_all - 1
                else:
                    ids = bucket_of(base + stride * (lane - row))
                for head in range(heads):
                    if far is None:
                        values = jnp.broadcast_to(table_ref[head : head + 1, :], (part, tile))
                        values = jnp.take_along_axis(values, ids, axis=1)
                    else:
                        values = jnp.broadcast_to(
                            table_ref[head : head + 1, far : far + 1], (part, tile)
                        )
                    out_ref[head, step, rows, columns] = values


def bias_tiles(table, stride, tiles):
    heads = table.shape[1]
    reach = near_shift(tiles)
    lanes = jnp.pad(table.astype(float32).T, ((0, 0), (0, tile - table.shape[0])))
    return pl.pallas_call(
        functools.partial(bias_kernel, stride, reach),
        out_shape=jax.ShapeDtypeStruct(
            (heads, 2 * stride - 1, tile, (2 * reach + 1) * tile), float32
        ),
        compiler_params=params(),
        name="bias_tiles",
    )(lanes)


def project_kernel(pairs, scale, rows_ref, gain_ref, weight_ref, normed_ref, out_ref):
    width = rows_ref.shape[2]
    depth = weight_ref.shape[1] // pairs
    lanes = weight_ref.shape[2]
    normed = norm_rows(rows_ref[0].astype(float32), gain_ref[...]).astype(bfloat)
    normed_ref[...] = normed
    for pair in range(pairs):
        weight = weight_ref[:, pair * depth : (pair + 1) * depth, :].reshape(width, lanes)
        product = dot_nn(normed, weight).astype(bfloat)
        start = pair * lanes
        out_ref[:, start : start + tile] = product[:, :tile] * bfloat(scale)
        out_ref[:, start + tile : start + lanes] = product[:, tile:]


def project(batch, rows, gain, packed, pairs, scale):
    _, count, width = rows.shape
    lanes = packed.shape[2]
    weight_shape = (packed.shape[0], pairs * width // packed.shape[0], lanes)
    step = min(512, count)
    return pl.pallas_call(
        functools.partial(project_kernel, pairs, scale),
        grid=(count // step,),
        in_specs=[
            pl.BlockSpec((1, step, width), lambda i: (batch, i, 0)),
            pl.BlockSpec((1, width), lambda i: (0, 0)),
            pl.BlockSpec(weight_shape, lambda i: (0, 0, 0)),
        ],
        out_specs=[
            pl.BlockSpec((step, width), lambda i: (i, 0)),
            pl.BlockSpec((step, pairs * lanes), lambda i: (i, 0)),
        ],
        out_shape=[
            jax.ShapeDtypeStruct((count, width), bfloat),
            jax.ShapeDtypeStruct((count, pairs * lanes), bfloat),
        ],
        compiler_params=params(),
        cost_estimate=pl.CostEstimate(
            flops=2 * count * width * lanes * pairs,
            bytes_accessed=6 * count * width,
            transcendentals=0,
        ),
        name="project",
    )(rows, gain, packed)


def count_earlier(picked, first_axis):
    size = picked.shape[1 - first_axis]
    row = lax.broadcasted_iota(jnp.int32, (size, size), 0)
    column = lax.broadcasted_iota(jnp.int32, (size, size), 1)
    if first_axis == 0:
        return dot_nn(picked, (row < column).astype(float32).astype(bfloat))
    return dot_nn((column < row).astype(float32).astype(bfloat), picked)


def tables_kernel(
    members,
    slots,
    me_ref,
    row_ref,
    column_ref,
    place_ref,
    after_ref,
    carried_ref,
    send_ref,
    back_ref,
    offset_ref,
    handed_ref,
):
    me = me_ref[0]
    batches, rows = column_ref.shape[0], column_ref.shape[1]
    names = 128
    for batch in range(batches):
        route = row_ref[batch]
        picked = lax.broadcasted_iota(jnp.int32, (names, rows), 0) == route
        earlier = count_earlier(picked.astype(float32).astype(bfloat), 0)
        slot = jnp.sum(jnp.where(picked, earlier, 0.0), axis=0, keepdims=True).astype(jnp.int32)
        target = jnp.where(route >= me, route - me, route - me + members) * slots + slot
        index = lax.broadcasted_iota(jnp.int32, (members * slots, rows), 0)
        send_ref[batch] = (index == target).astype(float32).astype(bfloat)

        route = column_ref[batch]
        picked = lax.broadcasted_iota(jnp.int32, (rows, names), 1) == route
        earlier = count_earlier(picked.astype(float32).astype(bfloat), 1)
        slot = jnp.sum(jnp.where(picked, earlier, 0.0), axis=1, keepdims=True).astype(jnp.int32)
        target = jnp.where(route >= me, route - me, route - me + members) * slots + slot
        index = lax.broadcasted_iota(jnp.int32, (rows, members * slots), 1)
        back_ref[batch] = (index == target).astype(float32).astype(bfloat)

        offsets = place_ref[batch] - members * lax.broadcasted_iota(
            jnp.int32, (rows, members), 0
        )
        lane = lax.broadcasted_iota(jnp.int32, (rows, members), 1)
        for step in range(members):
            owner = jnp.where(me >= step, me - step, me - step + members)
            chosen = jnp.sum(jnp.where(lane == owner, offsets, 0), axis=1, keepdims=True)
            offset_ref[batch, :, step : step + 1] = chosen


def row_tables(me, routes, places, after, carried, members, slots):
    batches, rows, _ = routes.shape
    vmem = pl.BlockSpec(memory_space=pltpu.VMEM)
    return pl.pallas_call(
        functools.partial(tables_kernel, members, slots),
        in_specs=[pl.BlockSpec(memory_space=pltpu.SMEM), vmem, vmem, vmem]
        + [pl.BlockSpec(memory_space=pl.ANY)] * 2,
        out_specs=[vmem, vmem, vmem, pl.BlockSpec(memory_space=pl.ANY)],
        out_shape=[
            jax.ShapeDtypeStruct((batches, members * slots, rows), bfloat),
            jax.ShapeDtypeStruct((batches, rows, members * slots), bfloat),
            jax.ShapeDtypeStruct((batches, rows, members), jnp.int32),
            jax.ShapeDtypeStruct(carried.shape, carried.dtype),
        ],
        input_output_aliases={5: 3},
        compiler_params=params(),
        name="row_tables",
    )(
        me,
        routes.reshape(batches, 1, rows),
        routes,
        jnp.transpose(places, (0, 2, 1)),
        after,
        carried,
    )


def member_rows(ordered, offset_ref, step, members):
    count = ordered.shape[0] // members
    rows = ordered[:count]
    for place in range(1, members):
        rows = jnp.where(
            offset_ref[0, :, step : step + 1] == place,
            ordered[place * count : (place + 1) * count],
            rows,
        )
    return rows


def middle_kernel(
    members,
    experts,
    me_ref,
    joined_ref,
    offset_ref,
    weight_ref,
    rows_ref,
    grad_ref,
    gain_ref,
    router_ref,
    route_ref,
    send_ref,
    after_ref,
    *refs,
):
    received = refs[: members - 1]
    mid_ref, normed_ref, probs_ref = refs[members - 1 : members + 2]
    out_refs = refs[members + 2 :]
    me = me_ref[0]
    span = joined_ref.shape[1]
    width = rows_ref.shape[2]
    slots = out_refs[0].shape[0]
    mid = rows_ref[0].astype(float32)
    for step in range(members):
        owner = jnp.where(me >= step, me - step, me - step + members)
        part = (
            member_rows(joined_ref[...], offset_ref, 0, members)
            if step == 0
            else received[step - 1][...]
        )
        mid = mid + dot_nn(part, weight_ref[pl.ds(pl.multiple_of(owner * span, span), span), :])
    mid_ref[...] = mid
    normed = norm_rows(mid, gain_ref[...]).astype(bfloat)
    normed_ref[...] = normed
    logits = dot_nn(normed, router_ref[...])
    lane = lax.broadcasted_iota(jnp.int32, logits.shape, 1)
    logits = jnp.where(lane < experts, logits, -jnp.inf)
    shifted = jnp.exp(logits - jnp.max(logits, axis=-1, keepdims=True))
    probs = shifted / jnp.sum(shifted, axis=-1, keepdims=True)
    probs_ref[...] = probs
    gate = jnp.sum(jnp.where(lane == route_ref[0], probs, 0.0), axis=1, keepdims=True)
    grad_expert = (gate * grad_ref[0].astype(float32)).astype(bfloat)
    tokens = dot_nn(send_ref[0], normed).astype(bfloat)
    grads = dot_nn(send_ref[0], grad_expert).astype(bfloat)
    for step in range(members):
        rows = slice(step * slots, (step + 1) * slots)
        out_refs[step][:, :width] = tokens[rows]
        out_refs[step][:, width:] = grads[rows]


def middle(
    batch, me, joined, received, offsets, weight, rows, grads, gain, router, routes, send, after
):
    members = offsets.shape[2]
    experts = members
    _, count, width = rows.shape
    slots = send.shape[1] // members
    row_spec = pl.BlockSpec((1, count, width), lambda i: (batch, 0, 0))

    def full(array):
        return pl.BlockSpec(array.shape, lambda i: (0,) * array.ndim)

    def own(array):
        return pl.BlockSpec((1,) + array.shape[1:], lambda i: (batch, 0, 0))

    out_shape = [
        jax.ShapeDtypeStruct((count, width), float32),
        jax.ShapeDtypeStruct((count, width), bfloat),
        jax.ShapeDtypeStruct((count, tile), float32),
    ] + [jax.ShapeDtypeStruct((slots, 2 * width), bfloat)] * members
    outs = pl.pallas_call(
        functools.partial(middle_kernel, members, experts),
        grid=(1,),
        in_specs=[
            pl.BlockSpec(memory_space=pltpu.SMEM),
            full(joined),
            own(offsets),
            full(weight),
            row_spec,
            row_spec,
            full(gain),
            full(router),
            own(routes),
            own(send),
            pl.BlockSpec(memory_space=pl.ANY),
        ]
        + [full(part) for part in received],
        out_specs=[full(shape) for shape in out_shape],
        out_shape=out_shape,
        compiler_params=params(),
        cost_estimate=pl.CostEstimate(
            flops=48 * count * width * width, bytes_accessed=12 * count * width, transcendentals=0
        ),
        name="middle",
    )(me, joined, offsets, weight, rows, grads, gain, router, routes, send, after, *received)
    return outs[0], outs[1], outs[2], list(outs[3:])


def second_kernel(
    members,
    experts,
    aliased,
    me_ref,
    back_ref,
    mid_ref,
    normed_ref,
    probs_ref,
    grad_ref,
    route_ref,
    gain_ref,
    router_ref,
    weight_ref,
    after_ref,
    *refs,
):
    returned = refs[:members]
    outs = refs[members + aliased :]
    layer_ref, grad_mid_ref, grad_attn_ref, gain_out_ref, router_out_ref = outs[:5]
    part_refs = outs[5:]
    me = me_ref[0]
    width = mid_ref.shape[1]
    span = part_refs[0].shape[1]
    blocks = jnp.concatenate([ref[...] for ref in returned], axis=0)
    home = dot_nn(back_ref[0], blocks)
    expert_back = home[:, :width]
    mid = mid_ref[...]
    gain = gain_ref[...]
    grads = grad_ref[0].astype(float32)
    probs = probs_ref[...]
    lane = lax.broadcasted_iota(jnp.int32, probs.shape, 1)
    picked = lane == route_ref[0]
    gate = jnp.sum(jnp.where(picked, probs, 0.0), axis=1, keepdims=True)
    layer_ref[0] = (mid + gate * expert_back).astype(bfloat)
    grad_gate = jnp.sum(grads * expert_back, axis=1, keepdims=True)
    grad_logits = (grad_gate * gate) * (jnp.where(picked, 1.0, 0.0) - probs)
    grad_logits = jnp.where(lane < experts, grad_logits, 0.0)
    grad_normed = home[:, width:]
    for name in range(experts):
        grad_normed = grad_normed + grad_logits[:, name : name + 1] * router_ref[name : name + 1, :]
    upper = grad_logits.astype(bfloat)
    lower = (grad_logits - upper.astype(float32)).astype(bfloat)
    normed = normed_ref[...]
    router_out_ref[...] = dot_tn(upper, normed) + dot_tn(lower, normed)
    grad_resid, terms = norm_back(mid, gain, grad_normed)
    gain_out_ref[...] = jnp.sum(terms, axis=0, keepdims=True)
    grad_mid = grads + grad_resid
    grad_mid_ref[...] = grad_mid
    grad_attn = grad_mid.astype(bfloat)
    grad_attn_ref[...] = grad_attn
    for step in range(members):
        owner = jnp.where(me >= step, me - step, me - step + members)
        rows = weight_ref[pl.ds(pl.multiple_of(owner * span, span), span), :]
        part_refs[step][...] = dot_nt(grad_attn, rows).astype(bfloat)


def second_back(
    batch,
    batches,
    me,
    returned,
    back,
    mid,
    normed,
    probs,
    grads,
    routes,
    gain,
    router,
    weight,
    members,
    span,
    after,
    layer,
):
    count, width = mid.shape
    grad_spec = pl.BlockSpec((1, count, width), lambda i: (batch, 0, 0))

    def full(array):
        return pl.BlockSpec(array.shape, lambda i: (0,) * array.ndim)

    def own(array):
        return pl.BlockSpec((1,) + array.shape[1:], lambda i: (batch, 0, 0))

    rest = [
        jax.ShapeDtypeStruct((count, width), float32),
        jax.ShapeDtypeStruct((count, width), bfloat),
        jax.ShapeDtypeStruct((1, width), float32),
        jax.ShapeDtypeStruct((tile, width), float32),
    ] + [jax.ShapeDtypeStruct((count, span), bfloat)] * members
    aliased = 0 if layer is None else 1
    outs = pl.pallas_call(
        functools.partial(second_kernel, members, members, aliased),
        grid=(1,),
        in_specs=[
            pl.BlockSpec(memory_space=pltpu.SMEM),
            own(back),
            full(mid),
            full(normed),
            full(probs),
            grad_spec,
            own(routes),
            full(gain),
            full(router),
            full(weight),
            pl.BlockSpec(memory_space=pl.ANY),
        ]
        + [full(part) for part in returned]
        + [pl.BlockSpec(memory_space=pl.ANY)] * aliased,
        out_specs=[grad_spec] + [full(shape) for shape in rest],
        out_shape=[jax.ShapeDtypeStruct((batches, count, width), bfloat)] + rest,
        input_output_aliases={11 + members: 0} if aliased else {},
        compiler_params=params(),
        cost_estimate=pl.CostEstimate(
            flops=6 * count * width * width, bytes_accessed=12 * count * width, transcendentals=0
        ),
        name="second_back",
    )(
        me,
        back,
        mid,
        normed,
        probs,
        grads,
        routes,
        gain,
        router,
        weight,
        after,
        *returned,
        *([] if layer is None else [layer]),
    )
    return outs[0], outs[1], outs[2], outs[3], outs[4], list(outs[5:])


def first_kernel(
    members,
    pairs,
    grads_ref,
    weight_ref,
    offset_ref,
    after_ref,
    *out_refs,
):
    width = out_refs[0].shape[1]
    depth = weight_ref.shape[1] // pairs
    lanes = weight_ref.shape[2]
    total = None
    for pair in range(pairs):
        weight = weight_ref[:, pair * depth : (pair + 1) * depth, :].reshape(width, lanes)
        term = dot_nt(grads_ref[:, pair * lanes : (pair + 1) * lanes], weight)
        total = term if total is None else total + term
    for step in range(members):
        out_refs[step][...] = member_rows(total, offset_ref, step, members).astype(
            out_refs[step].dtype
        )


def first_back(batch, grads, packed, pairs, width, offsets, after):
    members = offsets.shape[2]
    count = grads.shape[0]
    lanes = packed.shape[2]
    weight_shape = (packed.shape[0], pairs * width // packed.shape[0], lanes)
    own = jax.ShapeDtypeStruct((count // members, width), float32)
    sent = jax.ShapeDtypeStruct((count // members, width), bfloat)
    out_shape = [own] + [sent] * (members - 1)

    def full(array):
        return pl.BlockSpec(array.shape, lambda i: (0,) * len(array.shape))

    outs = pl.pallas_call(
        functools.partial(first_kernel, members, pairs),
        grid=(1,),
        in_specs=[
            full(grads),
            pl.BlockSpec(weight_shape, lambda i: (0, 0, 0)),
            pl.BlockSpec((1,) + offsets.shape[1:], lambda i: (batch, 0, 0)),
            pl.BlockSpec(memory_space=pl.ANY),
        ],
        out_specs=[full(shape) for shape in out_shape],
        out_shape=out_shape,
        compiler_params=params(),
        cost_estimate=pl.CostEstimate(
            flops=2 * count * width * lanes * pairs,
            bytes_accessed=8 * count * width,
            transcendentals=0,
        ),
        name="first_back",
    )(grads, packed, offsets, after)
    return outs[0], list(outs[1:])


def finish_kernel(received, own_ref, rows_ref, gain_ref, mid_ref, after_ref, *refs):
    total = own_ref[...]
    for ref in refs[:received]:
        total = total + ref[...].astype(float32)
    grad, _ = norm_back(rows_ref[0].astype(float32), gain_ref[...], total)
    refs[-1][0] = mid_ref[...] + grad


def finish(batch, own, received, rows, gain, mid, buffer, after):
    batches, count, width = rows.shape
    row_spec = pl.BlockSpec((1, count, width), lambda i: (batch, 0, 0))

    def full(array):
        return pl.BlockSpec(array.shape, lambda i: (0,) * array.ndim)

    operands = [own, rows, gain, mid, after] + received
    in_specs = [full(own), row_spec, full(gain), full(mid), pl.BlockSpec(memory_space=pl.ANY)]
    in_specs = in_specs + [full(part) for part in received]
    aliases = {}
    if buffer is not None:
        aliases = {len(operands): 0}
        operands.append(buffer)
        in_specs.append(pl.BlockSpec(memory_space=pl.ANY))
    return pl.pallas_call(
        functools.partial(finish_kernel, len(received)),
        grid=(1,),
        in_specs=in_specs,
        out_specs=row_spec,
        out_shape=jax.ShapeDtypeStruct((batches, count, width), float32),
        input_output_aliases=aliases,
        compiler_params=params(),
        name="finish",
    )(*operands)


def dense_kernel(skipped, handed, batches, weighted, blocks, *refs):
    refs = refs[skipped : len(refs) - handed]
    out_ref = refs[2 * batches + weighted]
    left = jnp.concatenate([ref[...] for ref in refs[:batches]], axis=0)
    right = jnp.concatenate([ref[...] for ref in refs[batches : 2 * batches]], axis=0)
    total = dot_tn(left, right)
    depth = out_ref.shape[1] // blocks
    lanes = out_ref.shape[2]
    term = None
    for block in range(blocks):
        part = total[:, block * lanes : (block + 1) * lanes]
        rows = slice(block * depth, (block + 1) * depth)
        out_ref[:, rows, :] = part.astype(bfloat).reshape(out_ref.shape[0], depth, lanes)
        if weighted:
            weight = refs[2 * batches][:, rows, :].reshape(part.shape).astype(float32)
            term = part * weight if term is None else term + part * weight
    if weighted:
        refs[-1][...] = jnp.sum(term, axis=1, keepdims=True)


def dense_grad(left, right, lanes, shards, direct, afters, packed=None, handed=()):
    afters = list(handed) + list(afters)
    batches = len(left)
    count, width = left[0].shape
    columns = right[0].shape[1]
    blocks = columns // lanes
    depth = width // shards
    steps = 2 if direct and width % (2 * tile) == 0 and shards % 2 == 0 else 1
    outer = shards // steps if direct else 1
    inner = depth if direct else width
    weighted = 0 if packed is None else 1
    outs = pl.pallas_call(
        functools.partial(dense_kernel, len(afters), len(handed), batches, weighted, blocks),
        grid=(steps,),
        in_specs=[pl.BlockSpec(memory_space=pl.ANY)] * len(afters)
        + [pl.BlockSpec((count, width // steps), lambda i: (0, i))] * batches
        + [pl.BlockSpec((count, columns), lambda i: (0, 0))] * batches
        + [pl.BlockSpec((outer, blocks * inner, lanes), lambda i: (i, 0, 0))] * weighted,
        out_specs=[pl.BlockSpec((outer, blocks * inner, lanes), lambda i: (i, 0, 0))]
        + [pl.BlockSpec((width // steps, 1), lambda i: (i, 0))] * weighted
        + [pl.BlockSpec(memory_space=pl.ANY)] * len(handed),
        out_shape=[jax.ShapeDtypeStruct((outer * steps, blocks * inner, lanes), bfloat)]
        + [jax.ShapeDtypeStruct((width, 1), float32)] * weighted
        + [jax.ShapeDtypeStruct(array.shape, array.dtype) for array in handed],
        input_output_aliases={idx: 1 + weighted + idx for idx in range(len(handed))},
        compiler_params=params(),
        cost_estimate=pl.CostEstimate(
            flops=2 * batches * count * width * columns,
            bytes_accessed=2 * batches * count * width,
            transcendentals=0,
        ),
        name="dense_grad",
    )(*afters, *left, *right, *([packed] if weighted else []))
    out = outs[0]
    if not direct:
        out = jnp.transpose(out.reshape(blocks, shards, depth, lanes), (1, 0, 2, 3))
        out = out.reshape(shards, blocks * depth, lanes)
    return (out,) + tuple(outs[1:])


def segment_of(positions, ends):
    segment = jnp.zeros(positions.shape, jnp.int32)
    for end in ends:
        segment = segment + (positions >= end).astype(jnp.int32)
    return segment


def masked_heads(rows, lane, per, head_dim):
    parts = []
    for sub in range(per):
        inside = (lane >= sub * head_dim) & (lane < (sub + 1) * head_dim)
        parts.append(jnp.where(inside, rows, jnp.zeros_like(rows)))
    return jnp.concatenate(parts, axis=0)


def joined_heads(rows, lane, per, head_dim):
    joined = rows[:tile]
    for sub in range(1, per):
        inside = (lane >= sub * head_dim) & (lane < (sub + 1) * head_dim)
        joined = jnp.where(inside, rows[sub * tile : (sub + 1) * tile], joined)
    return joined


def attend_kernel(
    stride,
    head_dim,
    far_ref,
    ends_ref,
    q_ref,
    k_ref,
    v_ref,
    bias_ref,
    after_ref,
    probs_ref,
    out_ref,
    inv_ref,
):
    pair = pl.program_id(0)
    rows_all = q_ref.shape[0]
    rows_part = rows_all // stride
    tiles = rows_part // tile
    reach = near_shift(tiles)
    per = tile // head_dim
    lane = lax.broadcasted_iota(jnp.int32, (tile, tile), 1)
    ends = [ends_ref[idx] for idx in range(ends_ref.shape[0])]
    keys_t = k_ref[...].T
    lane_row = lax.broadcasted_iota(jnp.int32, (1, tile), 1)
    row_column = lax.broadcasted_iota(jnp.int32, (tile, 1), 0)
    key_segments = [
        segment_of(stride * (col * tile + lane_row) + part, ends)
        for part in range(stride)
        for col in range(tiles)
    ]
    for mine in range(stride):
        for block in range(tiles):
            begin = mine * rows_part + block * tile
            rows = slice(begin, begin + tile)
            segment = segment_of(stride * (block * tile + row_column) + mine, ends)
            raw = dot_nn(masked_heads(q_ref[rows, :], lane, per, head_dim), keys_t)
            stacked = []
            inverses = []
            for sub in range(per):
                head = pair * per + sub
                pieces = []
                top = None
                for part in range(stride):
                    for col in range(tiles):
                        start = (part * tiles + col) * tile
                        piece = raw[sub * tile : (sub + 1) * tile, start : start + tile]
                        shift = col - block
                        if shift < -reach:
                            piece = piece + far_ref[0, head]
                        elif shift > reach:
                            piece = piece + far_ref[1, head]
                        else:
                            columns = slice((shift + reach) * tile, (shift + reach + 1) * tile)
                            piece = piece + bias_ref[sub, part - mine + stride - 1, :, columns]
                        same = key_segments[part * tiles + col] == segment
                        piece = jnp.where(same, piece, masked_score)
                        pieces.append(piece)
                        top = piece if top is None else jnp.maximum(top, piece)
                row_max = jnp.max(top, axis=-1, keepdims=True)
                total = None
                for idx, piece in enumerate(pieces):
                    piece = jnp.exp(piece - row_max)
                    total = piece if total is None else total + piece
                    pieces[idx] = piece.astype(bfloat)
                kept = jnp.concatenate(pieces, axis=1)
                probs_ref[sub, rows, :] = kept
                stacked.append(kept)
                inverses.append(1.0 / jnp.sum(total, axis=-1, keepdims=True))
            result = dot_nn(jnp.concatenate(stacked, axis=0), v_ref[...])
            inverse = jnp.broadcast_to(inverses[0], (tile, tile))
            for sub in range(1, per):
                inside = (lane >= sub * head_dim) & (lane < (sub + 1) * head_dim)
                inverse = jnp.where(inside, inverses[sub], inverse)
            out_ref[rows, :] = (joined_heads(result, lane, per, head_dim) * inverse).astype(bfloat)
            inv_ref[rows, :] = inverse


def kind_specs(rows_all):
    return [
        pl.BlockSpec((rows_all, tile), lambda i, kind=kind: (0, 3 * i + kind)) for kind in range(3)
    ]


def attend(qkv, ends, bias, far, after, head_dim, stride):
    rows_all, span = qkv.shape[0], qkv.shape[1] // 3
    per = tile // head_dim
    heads = span // head_dim
    row_spec = pl.BlockSpec((rows_all, tile), lambda i: (0, i))
    return pl.pallas_call(
        functools.partial(attend_kernel, stride, head_dim),
        grid=(span // tile,),
        in_specs=[
            pl.BlockSpec(memory_space=pltpu.SMEM),
            pl.BlockSpec(memory_space=pltpu.SMEM),
            *kind_specs(rows_all),
            pl.BlockSpec((per,) + bias.shape[1:], lambda i: (i, 0, 0, 0)),
            pl.BlockSpec(memory_space=pl.ANY),
        ],
        out_specs=[
            pl.BlockSpec((per, rows_all, rows_all), lambda i: (i, 0, 0)),
            row_spec,
            row_spec,
        ],
        out_shape=[
            jax.ShapeDtypeStruct((heads, rows_all, rows_all), bfloat),
            jax.ShapeDtypeStruct((rows_all, span), bfloat),
            jax.ShapeDtypeStruct((rows_all, span), float32),
        ],
        compiler_params=params(),
        cost_estimate=pl.CostEstimate(
            flops=16 * rows_all * rows_all * span,
            bytes_accessed=2 * heads * rows_all * rows_all,
            transcendentals=heads * rows_all * rows_all,
        ),
        name="attend",
    )(far, ends, qkv, qkv, qkv, bias, after)


def attend_back_kernel(
    stride,
    head_dim,
    scale,
    carried,
    skipped,
    probs_ref,
    out_ref,
    inv_ref,
    q_ref,
    k_ref,
    v_ref,
    offset_ref,
    *refs,
):
    refs = refs[skipped:]
    grad_refs = refs[:stride]
    dqkv_ref, dbias_ref, dfar_ref, ds_ref, grads_ref = refs[-5:]
    rows_all = q_ref.shape[0]
    rows_part = rows_all // stride
    tiles = rows_part // tile
    reach = near_shift(tiles)
    per = tile // head_dim
    lane = lax.broadcasted_iota(jnp.int32, (tile, tile), 1)
    queries_t = q_ref[...].T
    values_t = v_ref[...].T
    for place in range(stride):
        span = slice(place * rows_part, (place + 1) * rows_part)
        rows = grad_refs[0][...]
        for step in range(1, stride):
            rows = jnp.where(offset_ref[0, :, step : step + 1] == place, grad_refs[step][...], rows)
        grads_ref[span, :] = (rows.astype(float32) * inv_ref[span, :]).astype(bfloat)
    grads_t = grads_ref[...].T
    if carried:
        dbias_ref[...] = refs[stride][...]
        dfar_ref[...] = refs[stride + 1][...]
    else:
        dbias_ref[...] = jnp.zeros_like(dbias_ref)
        dfar_ref[...] = jnp.zeros_like(dfar_ref)
    for mine in range(stride):
        for block in range(tiles):
            begin = mine * rows_part + block * tile
            rows = slice(begin, begin + tile)
            own = masked_heads(grads_ref[rows, :], lane, per, head_dim)
            outs = out_ref[rows, :].astype(float32)
            raw = dot_nn(own, values_t)
            stacked = []
            for sub in range(per):
                span = slice(sub * tile, (sub + 1) * tile)
                row_dot = jnp.sum(own[span].astype(float32) * outs, axis=-1, keepdims=True)
                pieces = []
                for part in range(stride):
                    for col in range(tiles):
                        start = (part * tiles + col) * tile
                        piece = probs_ref[sub, rows, start : start + tile].astype(float32) * (
                            raw[span, start : start + tile] - row_dot
                        )
                        shift = col - block
                        if shift < -reach:
                            dfar_ref[sub, 0] += piece
                        elif shift > reach:
                            dfar_ref[sub, 1] += piece
                        else:
                            columns = slice((shift + reach) * tile, (shift + reach + 1) * tile)
                            dbias_ref[sub, part - mine + stride - 1, :, columns] += piece
                        pieces.append(piece.astype(bfloat))
                low_grads = jnp.concatenate(pieces, axis=1)
                ds_ref[sub, rows, :] = low_grads
                stacked.append(low_grads)
            result = dot_nn(jnp.concatenate(stacked, axis=0), k_ref[...]) * scale
            dqkv_ref[rows, :tile] = joined_heads(result, lane, per, head_dim).astype(bfloat)
    dk_parts = []
    dv_parts = []
    for sub in range(per):
        dims = slice(sub * head_dim, (sub + 1) * head_dim)
        dk_parts.append(dot_nn(queries_t[dims, :], ds_ref[sub]))
        dv_parts.append(dot_nn(grads_t[dims, :], probs_ref[sub]))
    dqkv_ref[:, tile : 2 * tile] = jnp.concatenate(dk_parts, axis=0).T.astype(bfloat)
    dqkv_ref[:, 2 * tile :] = jnp.concatenate(dv_parts, axis=0).T.astype(bfloat)


def attend_back(
    batch, probs, grads, outs, inverse, qkv, offsets, afters, sums, head_dim, stride, bias_shape
):
    rows_all, span = outs.shape
    per = tile // head_dim
    heads = span // head_dim
    row_spec = pl.BlockSpec((rows_all, tile), lambda i: (0, i))
    part_spec = pl.BlockSpec((rows_all // stride, tile), lambda i: (0, i))
    sum_specs = [
        pl.BlockSpec((per,) + bias_shape[1:], lambda i: (i, 0, 0, 0)),
        pl.BlockSpec((per, 2, tile, tile), lambda i: (i, 0, 0, 0)),
    ]
    carried = len(sums) > 0
    first = 7 + len(afters) + stride
    return pl.pallas_call(
        functools.partial(
            attend_back_kernel, stride, head_dim, head_dim ** (-0.5), carried, len(afters)
        ),
        grid=(span // tile,),
        in_specs=[pl.BlockSpec((per, rows_all, rows_all), lambda i: (i, 0, 0))]
        + [row_spec] * 2
        + kind_specs(rows_all)
        + [pl.BlockSpec((1,) + offsets.shape[1:], lambda i: (batch, 0, 0))]
        + [pl.BlockSpec(memory_space=pl.ANY)] * len(afters)
        + [part_spec] * stride
        + (sum_specs if carried else []),
        out_specs=[pl.BlockSpec((rows_all, 3 * tile), lambda i: (0, i))] + sum_specs,
        out_shape=[
            jax.ShapeDtypeStruct((rows_all, 3 * span), bfloat),
            jax.ShapeDtypeStruct(bias_shape, float32),
            jax.ShapeDtypeStruct((heads, 2, tile, tile), float32),
        ],
        scratch_shapes=[
            pltpu.VMEM((per, rows_all, rows_all), bfloat),
            pltpu.VMEM((rows_all, tile), bfloat),
        ],
        input_output_aliases={first: 1, first + 1: 2} if carried else {},
        compiler_params=params(),
        cost_estimate=pl.CostEstimate(
            flops=32 * rows_all * rows_all * span,
            bytes_accessed=2 * heads * rows_all * rows_all,
            transcendentals=0,
        ),
        name="attend_back",
    )(probs, outs, inverse, qkv, qkv, qkv, offsets, *afters, *grads, *sums)


def add_kernel(skipped, *refs):
    refs = refs[skipped:]
    out_ref = refs[-1]
    start = 0
    for left_ref, right_ref in zip(refs[:-1:2], refs[1:-1:2]):
        rows = left_ref.shape[1]
        out_ref[:, start : start + rows] = (
            left_ref[...].astype(float32) + right_ref[...].astype(float32)
        ).astype(bfloat)
        start += rows


def add_after(afters, *operands):
    vmem = pl.BlockSpec(memory_space=pltpu.VMEM)
    outer, _, lanes = operands[0].shape
    rows = sum(operand.shape[1] for operand in operands[::2])
    return pl.pallas_call(
        functools.partial(add_kernel, len(afters)),
        in_specs=[pl.BlockSpec(memory_space=pl.ANY)] * len(afters) + [vmem] * len(operands),
        out_specs=vmem,
        out_shape=jax.ShapeDtypeStruct((outer, rows, lanes), bfloat),
        compiler_params=params(),
        name="add_after",
    )(*afters, *operands)


def order_kernel(count, place_ref, *refs):
    out_ref = refs[count + 1]
    for place in range(count):
        rows = refs[0][0]
        for step in range(1, count):
            rows = jnp.where(place_ref[0, :, step : step + 1] == place, refs[step][0], rows)
        out_ref[0, place] = rows


def order_rows(parts, offsets, carried):
    batches, rows, width = parts[0].shape
    count = len(parts)
    part_spec = pl.BlockSpec((1, rows, width), lambda i: (i, 0, 0))
    return pl.pallas_call(
        functools.partial(order_kernel, count),
        grid=(batches,),
        in_specs=[pl.BlockSpec((1, rows, count), lambda i: (i, 0, 0))]
        + [part_spec] * count
        + [pl.BlockSpec(memory_space=pl.ANY)],
        out_specs=[
            pl.BlockSpec((1, count, rows, width), lambda i: (i, 0, 0, 0)),
            pl.BlockSpec(memory_space=pl.ANY),
        ],
        out_shape=[
            jax.ShapeDtypeStruct((batches, count, rows, width), bfloat),
            jax.ShapeDtypeStruct(carried.shape, carried.dtype),
        ],
        input_output_aliases={count + 1: 1},
        compiler_params=params(),
        name="order_rows",
    )(offsets, *parts, carried)


def expert_kernel(
    count, slots, width, inner_ref, outer_ref, after_ref, *refs
):
    blocks = refs[:count]
    results = refs[count : 2 * count]
    hidden_ref, grad_pre_ref, rows_ref, grads_ref, sum_ref, back_ref = refs[2 * count :]
    turn = pl.program_id(0)

    @pl.when(turn == 0)
    def _():
        for idx in range(count):
            rows = slice(idx * slots, (idx + 1) * slots)
            rows_ref[rows, :] = blocks[idx][:, :width]
            grads_ref[rows, :] = blocks[idx][:, width:]

    inner = inner_ref[...].reshape(width, width)
    outer = outer_ref[...].reshape(width, width)
    rows = rows_ref[...]
    grads = grads_ref[...]
    root = 0.7978845608028654
    pre = dot_nn(rows, inner)
    grad_hidden = dot_nt(grads, outer)
    square = pre * pre
    curve = jnp.tanh(root * pre * (1.0 + 0.044715 * square))
    half = 0.5 * (1.0 + curve)
    slope = half + (0.5 * root) * pre * (1.0 - curve * curve) * (1.0 + 0.134145 * square)
    hidden_ref[...] = (pre * half).astype(bfloat)
    grad_pre_ref[...] = (grad_hidden * slope).astype(bfloat)
    product = dot_nn(hidden_ref[...], outer)
    product_back = dot_nt(grad_pre_ref[...], inner)

    @pl.when(turn == 0)
    def _():
        sum_ref[...] = product
        back_ref[...] = product_back

    @pl.when(turn > 0)
    def _():
        sum_ref[...] += product
        back_ref[...] += product_back

    @pl.when(turn == pl.num_programs(0) - 1)
    def _():
        for idx in range(count):
            span = slice(idx * slots, (idx + 1) * slots)
            results[idx][:, :width] = sum_ref[span, :].astype(bfloat)
            results[idx][:, width:] = back_ref[span, :].astype(bfloat)


def run_expert(weights, blocks, width, after):
    (inner, inner_spec), (outer, outer_spec), turns = weights
    count = len(blocks)
    slots = blocks[0].shape[0]
    total = count * slots
    whole = pl.BlockSpec((slots, 2 * width), lambda i: (0, 0))
    chunk = pl.BlockSpec((total, width), lambda i: (0, i))
    outs = pl.pallas_call(
        functools.partial(expert_kernel, count, slots, width),
        grid=(turns,),
        in_specs=[inner_spec, outer_spec, pl.BlockSpec(memory_space=pl.ANY)] + [whole] * count,
        out_specs=[whole] * count + [chunk, chunk],
        out_shape=[jax.ShapeDtypeStruct((slots, 2 * width), bfloat)] * count
        + [jax.ShapeDtypeStruct((total, turns * width), bfloat)] * 2,
        scratch_shapes=[
            pltpu.VMEM((total, width), bfloat),
            pltpu.VMEM((total, width), bfloat),
            pltpu.VMEM((total, width), float32),
            pltpu.VMEM((total, width), float32),
        ],
        compiler_params=params(),
        cost_estimate=pl.CostEstimate(
            flops=8 * total * width * width * turns,
            bytes_accessed=4 * width * width * turns,
            transcendentals=total * width * turns,
        ),
        name="run_expert",
    )(inner, outer, after, *blocks)
    return outs[:count], outs[count], outs[count + 1]


def expert_grad_kernel(batches, count, slots, width, second, *refs):
    groups = [refs[idx * count : (idx + 1) * count] for idx in range(batches)]
    wide = refs[batches * count : batches * count + batches]
    out_ref, rows_ref = refs[-2], refs[-1]
    half = slice(width, 2 * width) if second else slice(0, width)

    @pl.when(pl.program_id(0) == 0)
    def _():
        for batch in range(batches):
            for idx in range(count):
                start = (batch * count + idx) * slots
                rows_ref[start : start + slots, :] = groups[batch][idx][:, half]

    rows = rows_ref[...]
    columns = jnp.concatenate([ref[...] for ref in wide], axis=0)
    total = dot_tn(columns, rows) if second else dot_tn(rows, columns)
    out_ref[...] = total.astype(bfloat).reshape(out_ref.shape)


def expert_grad(groups, wide, width, second, out_shape, out_spec, afters, buffer=None):
    batches = len(groups)
    count = len(groups[0])
    slots = groups[0][0].shape[0]
    total = count * slots
    turns = wide[0].shape[1] // width
    kernel = functools.partial(expert_grad_kernel, batches, count, slots, width, second)
    in_specs = [pl.BlockSpec((slots, 2 * width), lambda i: (0, 0))] * (batches * count)
    in_specs = in_specs + [pl.BlockSpec((total, width), lambda i: (0, i))] * batches
    operands = [block for group in groups for block in group] + list(wide)
    aliases = {}
    carried = list(afters)
    if buffer is not None:
        carried = [buffer] + carried
        aliases = {0: 0}
    skipped = len(carried)
    in_specs = [pl.BlockSpec(memory_space=pl.ANY)] * skipped + in_specs
    operands = carried + operands

    def body(*refs):
        kernel(*refs[skipped:])

    return pl.pallas_call(
        body,
        grid=(turns,),
        in_specs=in_specs,
        out_specs=out_spec,
        out_shape=jax.ShapeDtypeStruct(out_shape, bfloat),
        scratch_shapes=[pltpu.VMEM((batches * total, width), bfloat)],
        input_output_aliases=aliases,
        compiler_params=params(),
        cost_estimate=pl.CostEstimate(
            flops=2 * batches * total * width * width * turns,
            bytes_accessed=4 * width * width * turns,
            transcendentals=0,
        ),
        name="expert_grad_outer" if second else "expert_grad_inner",
    )(*operands)


def on_device(
    hidden_in,
    out_grad,
    places,
    lengths,
    routes,
    norm1_gain,
    w_query,
    w_key,
    w_value,
    w_output,
    rel_table,
    norm2_gain,
    w_router,
    w_in,
    w_out,
):
    batches, rows_own, width = hidden_in.shape
    heads = rel_table.shape[1]
    head_dim = width // heads
    scale = head_dim ** (-0.5)
    shards = lax.axis_size("dp")
    members = lax.axis_size("expert")
    me = lax.axis_index("expert")
    experts = w_router.shape[1]
    hidden_width = w_in.shape[2]
    turns = hidden_width // width
    tiles = rows_own // tile
    rows_group = members * rows_own
    depth = width // shards
    depth_out = hidden_width // shards
    table_rows = rel_table.shape[0]
    capacity = max(2, rows_own * 17 // (experts * 16))
    slots = -(-capacity // 16) * 16
    per = tile // head_dim
    heads_own = per * (-(-heads // (per * members)))
    span = heads_own * head_dim
    pairs = span // tile
    lanes = 3 * tile
    split = width // lanes
    me_row = me.reshape(1)

    def around(step):
        return [(idx, (idx + step) % members) for idx in range(members)]

    def columns_own(weight):
        wide = jnp.pad(weight, ((0, 0), (0, members * span - width)))
        return lax.dynamic_slice_in_dim(wide, me * span, span, axis=1)

    def in_order(parts):
        if members == 2:
            return [
                jnp.where(me == 0, parts[0], parts[1]),
                jnp.where(me == 0, parts[1], parts[0]),
            ]
        stacked = jnp.stack(parts)
        return [stacked[jnp.mod(me - idx, members)] for idx in range(members)]

    hidden_from = [hidden_in] + [
        lax.ppermute(hidden_in, "expert", around(step)) for step in range(1, members)
    ]

    small = jnp.concatenate(
        [
            norm1_gain.reshape(-1),
            norm2_gain.reshape(-1),
            w_router.reshape(-1),
            rel_table.reshape(-1),
        ]
    )
    small_used = small.shape[0]
    small_pad = -(-small_used // (16 * lanes)) * 16
    small = jnp.pad(small, (0, small_pad * lanes - small_used)).reshape(small_pad, lanes)
    kinds = [columns_own(weight) for weight in (w_query, w_key, w_value)]
    first_own = jnp.concatenate(
        [
            jnp.concatenate([kind[:, idx * tile : (idx + 1) * tile] for kind in kinds], axis=1)
            for idx in range(pairs)
        ]
        + [w_output[:, idx * lanes : (idx + 1) * lanes] for idx in range(split)]
        + [small],
        axis=0,
    )
    first = lax.all_gather(first_own, "dp", axis=0, tiled=False)
    inner_parts = [w_in[0, :, idx * width : (idx + 1) * width] for idx in range(turns)]
    second_own = jnp.concatenate(inner_parts + [w_out[0]], axis=0)
    places_in = places[:, 0].reshape(batches, members, rows_own)
    dispatch, collect, offsets, second_own = row_tables(
        me_row, routes, places_in, hidden_from[-1], second_own, members, slots
    )
    second = lax.all_gather(second_own, "dp", axis=0, tiled=False)
    ends = jnp.cumsum(lengths[:, 0], axis=-1)[:, :-1]
    ordered_in, first = order_rows(hidden_from, offsets, first)
    ordered_in = ordered_in.reshape(batches, rows_group, width)

    small_start = (pairs + split) * depth
    small_all = first[:, small_start:].reshape(shards, small_pad * lanes)
    gain_one = small_all[:, :depth].reshape(1, width).astype(float32)
    gain_two = small_all[:, depth : 2 * depth].reshape(1, width).astype(float32)
    router_end = 2 * depth + depth * experts
    router_w = small_all[:, 2 * depth : router_end].reshape(width, experts)
    table = small_all[:, router_end:small_used].reshape(shards * table_rows, heads)
    router_wide = jnp.pad(router_w, ((0, 0), (0, tile - experts)))
    router_t = router_w.astype(float32).T
    output_w = jnp.concatenate(
        [
            first[:, (pairs + idx) * depth : (pairs + idx + 1) * depth].reshape(width, lanes)
            for idx in range(split)
        ],
        axis=1,
    )
    output_w = jnp.pad(output_w, ((0, members * span - width), (0, 0)))

    direct = depth % 16 == 0 and turns * depth == depth_out and shards % turns == 0
    if direct:
        group = shards // turns
        packed = first
        inner_spec = pl.BlockSpec((shards, depth, width), lambda i: (0, i, 0))
        outer_spec = pl.BlockSpec((group, depth_out, width), lambda i: (i, 1, 0))
        weights = ((second, inner_spec), (second, outer_spec), turns)
    else:
        packed = jnp.concatenate(
            [
                first[:, idx * depth : (idx + 1) * depth].reshape(1, width, lanes)
                for idx in range(pairs)
            ],
            axis=1,
        )
        inner_w = second[:, : turns * depth].reshape(shards, turns, depth, width)
        inner_w = jnp.transpose(inner_w, (1, 0, 2, 3)).reshape(turns, width, width)
        outer_w = second[:, turns * depth : turns * depth + depth_out].reshape(
            turns, width, width
        )
        plain = pl.BlockSpec((1, width, width), lambda i: (i, 0, 0))
        weights = ((inner_w, plain), (outer_w, plain), turns)

    table_wide = jnp.pad(table, ((0, 0), (0, members * heads_own - heads)))
    table_own = lax.dynamic_slice_in_dim(table_wide, me * heads_own, heads_own, axis=1)
    bias = bias_tiles(table_own, members, tiles)
    table_f = table_own.astype(float32)
    far = jnp.stack([table_f[levels_all - 1], table_f[2 * levels_all - 1]])

    def send_rows(batch, ordered):
        arrived = []
        for step in range(1, members):
            rows = ordered[:rows_own]
            for place in range(1, members):
                rows = jnp.where(
                    offsets[batch, :, members - step : members - step + 1] == place,
                    ordered[place * rows_own : (place + 1) * rows_own],
                    rows,
                )
            arrived.append(lax.ppermute(rows, "expert", around(step)))
        return arrived

    normed_one = []
    qkv = []
    probs = []
    outs = []
    inverses = []
    arrived_heads = []
    resid_mid = []
    normed_two = []
    router_probs = []
    blocks = []
    after = table
    for batch in range(batches):
        normed, packed_rows = project(batch, ordered_in, gain_one, packed, pairs, scale)
        normed_one.append(normed)
        qkv.append(packed_rows)
        kept, joined, inverse = attend(
            packed_rows,
            ends[batch],
            bias,
            far,
            after,
            head_dim,
            members,
        )
        probs.append(kept)
        outs.append(joined)
        inverses.append(inverse)
        arrived_heads.append(send_rows(batch, joined))
        mid, normed, chances, outgoing = middle(
            batch,
            me_row,
            joined,
            arrived_heads[batch],
            offsets,
            output_w,
            hidden_in,
            out_grad,
            gain_two,
            router_wide,
            routes,
            dispatch,
            blocks[-1][-1] if blocks else table,
        )
        after = outgoing[-1]
        blocks.append(
            [outgoing[0]]
            + [
                lax.ppermute(outgoing[step], "expert", around(step))
                for step in range(1, members)
            ]
        )
        resid_mid.append(mid)
        normed_two.append(normed)
        router_probs.append(chances)

    returned = []
    hidden = []
    grad_pre = []
    for batch in range(batches):
        results, hidden_rows, grad_rows = run_expert(
            weights, blocks[batch], width, hidden[-1] if hidden else table
        )
        hidden.append(hidden_rows)
        grad_pre.append(grad_rows)
        returned.append(
            [results[0]]
            + [
                lax.ppermute(results[step], "expert", around(-step))
                for step in range(1, members)
            ]
        )

    layer_rows = [None]
    grad_mid = []
    grad_attn = []
    grad_heads = []
    gain_two_terms = []
    router_terms_all = []

    def norm_part(batch, after):
        layer, mid, attn, gain_terms, router_terms, parts = second_back(
            batch,
            batches,
            me_row,
            returned[batch],
            collect,
            resid_mid[batch],
            normed_two[batch],
            router_probs[batch],
            out_grad,
            routes,
            gain_two,
            router_t,
            output_w,
            members,
            span,
            after,
            layer_rows[-1],
        )
        grad_mid.append(mid)
        grad_attn.append(attn)
        layer_rows.append(layer)
        gain_two_terms.append(gain_terms)
        router_terms_all.append(router_terms[:experts])
        from_members = [parts[0]] + [
            lax.ppermute(parts[members - step], "expert", around(step))
            for step in range(1, members)
        ]
        grad_heads.append(from_members)

    if direct:
        buffer_shape = (shards, turns * depth + depth_out, width)
        buffer = expert_grad(
            blocks,
            grad_pre,
            width,
            False,
            buffer_shape,
            pl.BlockSpec((shards, depth, width), lambda i: (0, i, 0)),
            [returned[0][-1]],
        )
        norm_part(0, table)
        buffer = expert_grad(
            blocks,
            hidden,
            width,
            True,
            buffer_shape,
            pl.BlockSpec((group, depth_out, width), lambda i: (i, 1, 0)),
            [returned[-1][-1], grad_attn[0]],
            buffer,
        )
    else:
        plain_shape = (turns, width, width)
        inner_g = expert_grad(
            blocks, grad_pre, width, False, plain_shape, plain, [returned[0][-1]]
        )
        norm_part(0, table)
        outer_g = expert_grad(
            blocks, hidden, width, True, plain_shape, plain, [returned[-1][-1]]
        )
        inner_g = jnp.transpose(inner_g.reshape(turns, shards, depth, width), (1, 0, 2, 3))
        buffer = jnp.concatenate(
            [
                inner_g.reshape(shards, turns * depth, width),
                outer_g.reshape(shards, depth_out, width),
            ],
            axis=1,
        )
    expert_sum = lax.psum_scatter(buffer, "dp", scatter_dimension=0, tiled=False)
    for batch in range(1, batches):
        norm_part(batch, buffer)
    layer = layer_rows[-1]
    grad_gain_two = sum(gain_two_terms)
    grad_router = sum(router_terms_all)

    line = shards // 4
    my_shard = lax.axis_index("dp")

    def by_core(dense):
        dense = dense.reshape((line, 2, 2) + dense.shape[1:])
        odd = my_shard % 2 == 1
        sent = jnp.where(odd, dense[:, :, 0], dense[:, :, 1])
        held = jnp.where(odd, dense[:, :, 1], dense[:, :, 0])
        return held, lax.ppermute(sent, "dp", [(idx, idx ^ 1) for idx in range(shards)])

    def by_y(core_parts):
        held, got = core_parts
        odd = (my_shard // 2) % 2 == 1

        def half(idx):
            return held[:, idx].astype(float32) + got[:, idx].astype(float32)

        sent = jnp.where(odd, half(0), half(1)).astype(bfloat)
        kept = jnp.where(odd, half(1), half(0)).astype(bfloat)
        return kept, lax.ppermute(sent, "dp", [(idx, idx ^ 2) for idx in range(shards)])

    def own_rows_of(batch):
        joined = outs[batch]
        rows = joined[:rows_own]
        for place in range(1, members):
            rows = jnp.where(
                offsets[batch, :, 0:1] == place,
                joined[place * rows_own : (place + 1) * rows_own],
                rows,
            )
        return rows

    attended = [
        jnp.concatenate(in_order([own_rows_of(batch)] + arrived_heads[batch]), axis=1)[:, :width]
        for batch in range(batches)
    ]
    early_core = by_core(
        dense_grad(attended, grad_attn, lanes, shards, direct, [grad_heads[0][-1]])[0]
    )
    early = by_y(early_core)
    grad_qkv = []
    sums = []
    own_rows = []
    received_rows = []
    sent_last = buffer

    def first_part(batch, after):
        own, sent = first_back(batch, grad_qkv[batch], packed, pairs, width, offsets, after)
        own_rows.append(own)
        received_rows.append(
            [lax.ppermute(rows, "expert", around(-step)) for step, rows in enumerate(sent, 1)]
        )
        return sent[-1]

    for batch in range(batches):
        if batch > 0:
            sent_last = first_part(batch - 1, buffer)
        grads, *sums = attend_back(
            batch,
            probs[batch],
            grad_heads[batch],
            outs[batch],
            inverses[batch],
            qkv[batch],
            offsets,
            [buffer] if batch == 0 else [sent_last, early_core[1]],
            sums,
            head_dim,
            members,
            bias.shape,
        )
        grad_qkv.append(grads)
    grad_dense, weighted, grad_bias, grad_far = dense_grad(
        normed_one,
        grad_qkv,
        lanes,
        shards,
        direct,
        [early[1]] + [rows[-1] for rows in received_rows],
        packed,
        sums,
    )
    grad_gain_one = weighted[:, 0] / gain_one[0]
    late_core = by_core(grad_dense)
    late = by_y(late_core)
    sent_last = first_part(batches - 1, late_core[1])

    steps = 2 * members - 1
    reach = near_shift(tiles)
    shape = (steps, tile, (2 * reach + 1) * tile)
    delta = (
        members
        * (
            lax.broadcasted_iota(jnp.int32, shape, 2)
            - reach * tile
            - lax.broadcasted_iota(jnp.int32, shape, 1)
        )
        + lax.broadcasted_iota(jnp.int32, shape, 0)
        - (members - 1)
    )
    buckets = shards * table_rows
    onehot = (
        bucket_of(delta)[None] == jnp.arange(buckets, dtype=jnp.int32)[:, None, None, None]
    ).astype(bfloat)
    grad_table = jnp.einsum(
        "hsab,ksab->kh", grad_bias.astype(bfloat), onehot, preferred_element_type=float32
    )
    far_sum = jnp.sum(grad_far, axis=(2, 3))
    grad_table = grad_table.at[levels_all - 1].add(far_sum[:, 0])
    grad_table = grad_table.at[2 * levels_all - 1].add(far_sum[:, 1])
    grad_table = lax.dynamic_update_slice_in_dim(
        jnp.zeros((buckets, members * heads_own), float32), grad_table, me * heads_own, axis=1
    )[:, :heads]

    small_grad = jnp.concatenate(
        [
            grad_gain_one.reshape(shards, depth),
            grad_gain_two.reshape(shards, depth),
            grad_router.T.reshape(shards, depth * experts),
            grad_table.reshape(shards, table_rows * heads),
        ],
        axis=1,
    )
    small_grad = jnp.pad(small_grad, ((0, 0), (0, small_pad * lanes - small_used)))
    small_grad = small_grad.astype(bfloat).reshape(shards, small_pad, lanes)
    little = by_y(by_core(small_grad))
    dense_added = add_after([expert_sum, sent_last], *late, *little, *early)
    in_grad = None
    for batch in range(batches):
        in_grad = finish(
            batch,
            own_rows[batch],
            received_rows[batch],
            hidden_in,
            gain_one,
            grad_mid[batch],
            in_grad,
            buffer if batch < batches - 1 else dense_added,
        )
    dense_part = lax.psum_scatter(
        dense_added,
        "dp",
        scatter_dimension=0,
        tiled=False,
        axis_index_groups=[[rest + 4 * idx for idx in range(line)] for rest in range(4)],
    )
    parts = [dense_part] + [
        lax.ppermute(dense_part, "expert", around(step)) for step in range(1, members)
    ]
    qkv_parts = [
        part.astype(float32) for part in in_order([part[: pairs * depth] for part in parts])
    ]
    qkv_grads = [
        jnp.concatenate(
            [
                part[pair * depth : (pair + 1) * depth, kind * tile : (kind + 1) * tile]
                for part in qkv_parts
                for pair in range(pairs)
            ],
            axis=1,
        )[:, :width]
        for kind in range(3)
    ]
    rest_sum = sum(part[pairs * depth :].astype(float32) for part in parts)
    out_grad_sum = jnp.concatenate(
        [
            rest_sum[small_pad + idx * depth : small_pad + (idx + 1) * depth]
            for idx in range(split)
        ],
        axis=1,
    )
    small_sum = rest_sum[:small_pad].reshape(-1)

    expert_f = expert_sum.astype(float32)
    inner_sum = jnp.concatenate(
        [expert_f[idx * depth : (idx + 1) * depth] for idx in range(turns)], axis=1
    )[None]
    outer_sum = expert_f[turns * depth :][None]
    return (
        layer,
        in_grad,
        small_sum[:depth],
        qkv_grads[0],
        qkv_grads[1],
        qkv_grads[2],
        out_grad_sum,
        small_sum[router_end:small_used].reshape(table_rows, heads),
        small_sum[depth : 2 * depth],
        small_sum[2 * depth : router_end].reshape(depth, experts),
        inner_sum,
        outer_sum,
    )


def solution(mesh):
    return jax.shard_map(
        on_device,
        mesh=mesh,
        in_specs=(
            P(None, ("dp", "expert"), None),
            P(None, ("dp", "expert"), None),
            P(None, "dp", None),
            P(None, "dp", None),
            P(None, ("dp", "expert"), None),
            P("dp"),
            P("dp", None),
            P("dp", None),
            P("dp", None),
            P("dp", None),
            P("dp", None),
            P("dp"),
            P("dp", None),
            P("expert", "dp", None),
            P("expert", "dp", None),
        ),
        out_specs=(
            P(None, ("dp", "expert"), None),
            P(None, ("dp", "expert"), None),
            P("dp"),
            P("dp", None),
            P("dp", None),
            P("dp", None),
            P("dp", None),
            P("dp", None),
            P("dp"),
            P("dp", None),
            P("expert", "dp", None),
            P("expert", "dp", None),
        ),
        check_vma=False,
    )
```
